128 devices in a mesh: fsdp: 16 (over x, y_hi, core), sp: 8 (over z, y_lo).
Axes of the slice: x: 4, y: 4 (y_hi: 2, y_lo: 2; y = y_hi * 2 + y_lo), z: 4, core: 2. Of those that a mesh axis runs over, the one named last changes fastest.
Arguments:
- inputs: bfloat16 [16, 1024, 1536], P('fsdp', 'sp'), may hold values from -6 to 6
- norm_attn: float32 [1536], replicated, may hold values from 0.25 to 1.75
- w_query: bfloat16 [1536, 1536], P('fsdp'), may hold values from -0.15625 to 0.15625
- w_key: bfloat16 [1536, 768], P('fsdp'), may hold values from -0.15625 to 0.15625
- w_value: bfloat16 [1536, 768], P('fsdp'), may hold values from -0.15625 to 0.15625
- w_out: bfloat16 [1536, 1536], P('fsdp'), may hold values from -1.25 to 1.25
- norm_ffn: float32 [1536], replicated, may hold values from 0.25 to 1.75
- w_gate: bfloat16 [1536, 4096], P('fsdp'), may hold values from -0.15625 to 0.15625
- w_up: bfloat16 [1536, 4096], P('fsdp'), may hold values from -0.15625 to 0.15625
- w_down: bfloat16 [4096, 1536], P('fsdp'), may hold values from -0.125 to 0.125
- cotangent: bfloat16 [16, 1024, 1536], P('fsdp', 'sp'), may hold values from -6 to 6
Outputs:
- block_out: bfloat16 [16, 1024, 1536], P('fsdp', 'sp')
- input_grad: float32 [16, 1024, 1536], P('fsdp', 'sp')
- grad_norm_attn: float32 [1536], P('fsdp')
- grad_query: float32 [1536, 1536], P('fsdp')
- grad_key: float32 [1536, 768], P('fsdp')
- grad_value: float32 [1536, 768], P('fsdp')
- grad_out: float32 [1536, 1536], P('fsdp')
- grad_norm_ffn: float32 [1536], P('fsdp')
- grad_gate: float32 [1536, 4096], P('fsdp')
- grad_up: float32 [1536, 4096], P('fsdp')
- grad_down: float32 [4096, 1536], P('fsdp')
The draws below stay inside these ranges and needn't reach their ends.
All inputs are finite; a program needn't handle non-finite values.
Results may differ from the reference program's by a relative error of at most 0.024.
Values may be sent and summed in bfloat16 or wider, within the bound.
No kernel may reach another device: no remote copies, remote signals or barrier semaphores. Data moves between devices by JAX's collectives and lax.ppermute only.
A program may use at most 256 MiB of HBM per device.

```python
import math
import jax
import jax.numpy as jnp
from jax import lax

D = 1536
HEADS = 16
KV_HEADS = 8
HEAD_DIM = 96
FF = 4096
SEQ_LEN = 1024
SEQS = 16
QD = 1536
KVD = 768


def steps_of(key, shape, cuts, low, top_value):
    level = 1.0
    for dim, shards_of in cuts:
        draws = jax.random.uniform(jax.random.fold_in(jax.random.fold_in(key, 6), dim), (shards_of,), jnp.float32, low / len(cuts), top_value / len(cuts))
        level = level * jnp.repeat(jnp.exp(draws), shape[dim] // shards_of).reshape((-1,) + (1,) * (len(shape) - 1 - dim))
    return level


def normal_values(own_key, extent, scale, bound, split=(), held_as=jnp.bfloat16):
    loudness = steps_of(own_key, extent, split, -0.22, 0.18) if split else 1.0
    entries = jax.random.normal(own_key, extent, jnp.float32) * scale * loudness
    return jnp.minimum(jnp.maximum(entries, -bound), bound).astype(held_as)


def setup_inputs(seed: int = 0) -> dict:
    streams_of = jax.random.split(jax.random.key(seed), 12)
    inputs = normal_values(streams_of[0], (SEQS, SEQ_LEN, D), 1.0, 6.0, ((0, 16), (1, 8)))
    norm_attn = jnp.clip(1.0 + 0.15 * jax.random.normal(streams_of[1], (D,), jnp.float32), 0.25, 1.75)
    w_query = normal_values(streams_of[2], (D, QD), D ** -0.5, 0.15625, ((0, 16),))
    w_key = normal_values(streams_of[3], (D, KVD), D ** -0.5, 0.15625, ((0, 16),))
    w_value = normal_values(streams_of[4], (D, KVD), D ** -0.5, 0.15625, ((0, 16),))
    w_out = normal_values(streams_of[5], (QD, D), (D // 64) ** -0.5, 1.25, ((0, 16),))
    norm_ffn = jnp.clip(1.0 + 0.15 * jax.random.normal(streams_of[6], (D,), jnp.float32), 0.25, 1.75)
    w_gate = normal_values(streams_of[7], (D, FF), D ** -0.5, 0.15625, ((0, 16),))
    w_up = normal_values(streams_of[8], (D, FF), D ** -0.5, 0.15625, ((0, 16),))
    w_down = normal_values(streams_of[9], (FF, D), (FF // 2) ** -0.5, 0.125, ((0, 16),))
    cotangent = normal_values(streams_of[10], (SEQS, SEQ_LEN, D), 1.0, 6.0, ((0, 16), (1, 8)))
    return {"inputs": inputs, "norm_attn": norm_attn, "w_query": w_query, "w_key": w_key, "w_value": w_value, "w_out": w_out, "norm_ffn": norm_ffn, "w_gate": w_gate, "w_up": w_up, "w_down": w_down, "cotangent": cotangent}


@jax.custom_vjp
def low(v):
    return lax.optimization_barrier(v.astype(jnp.bfloat16)).astype(jnp.float32)

@jax.custom_vjp
def low_back(v):
    return v

def low_keep(v):
    return (low(v), None)

def low_pass(kept, grad):
    return (grad,)

def back_keep(v):
    return (v, None)

def back_low(kept, grad):
    return (low(grad),)
low.defvjp(low_keep, low_pass)
low_back.defvjp(back_keep, back_low)
EPSILON = 1e-05
ROPE_BASE = 100000.0
MASKED = -1e+30

def round_both(value):
    return low_back(low(value))

def product(left, right):
    return jnp.dot(left, right, precision=lax.Precision.HIGHEST, preferred_element_type=jnp.float32)

def rms_norm(value, gain):
    factor = lax.rsqrt(lax.optimization_barrier(jnp.mean(value * value, axis=-1, keepdims=True)) + EPSILON)
    return value * factor * gain

def rope_tables():
    half_dim = HEAD_DIM // 2
    frequency = ROPE_BASE ** (-(jnp.arange(half_dim, dtype=jnp.float32) * 2.0 / HEAD_DIM))
    angles = jnp.arange(SEQ_LEN, dtype=jnp.float32)[:, None] * frequency[None, :]
    return (jnp.cos(angles), jnp.sin(angles))

def rotate(value, cosine, sine):
    half_dim = value.shape[-1] // 2
    first = value[..., :half_dim]
    second = value[..., half_dim:]
    cos_b = cosine[:, None, :]
    sin_b = sine[:, None, :]
    return jnp.concatenate([first * cos_b - second * sin_b, second * cos_b + first * sin_b], axis=-1)

def attend_sequence(queries, keys, values):
    block_rows = min(512, SEQ_LEN)
    blocks = SEQ_LEN // block_rows
    group_size = HEADS // KV_HEADS
    grouped = queries.reshape(blocks, block_rows, KV_HEADS, group_size, HEAD_DIM)
    offsets = jnp.arange(blocks, dtype=jnp.int32) * block_rows

    def per_block(members):
        query_blk, offset = members
        scores = low_back(jnp.einsum('qhgd,khd->hgqk', query_blk, keys, precision=lax.Precision.HIGHEST) * HEAD_DIM ** (-0.5))
        row_ids = offset + jnp.arange(block_rows, dtype=jnp.int32)[:, None]
        col_ids = jnp.arange(SEQ_LEN, dtype=jnp.int32)[None, :]
        scores = jnp.where(col_ids <= row_ids, scores, MASKED)
        highest = lax.optimization_barrier(jnp.max(scores, axis=-1, keepdims=True))
        weights = jnp.exp(scores - highest)
        shares = low(weights / lax.optimization_barrier(jnp.sum(weights, axis=-1, keepdims=True)))
        return jnp.einsum('hgqk,khd->qhgd', shares, values, precision=lax.Precision.HIGHEST)
    outputs = lax.map(jax.checkpoint(per_block), (grouped, offsets))
    return outputs.reshape(SEQ_LEN, HEADS * HEAD_DIM)

def layer(inputs, params):
    norm_attn, w_query, w_key, w_value, w_out, norm_ffn, w_gate, w_up, w_down = params
    group_size = inputs.shape[0]
    cosine, sine = rope_tables()
    normed = low(rms_norm(inputs, norm_attn)).reshape(-1, D)
    query_lin = low_back(product(normed, w_query)).reshape(group_size, SEQ_LEN, HEADS, HEAD_DIM)
    key_lin = low_back(product(normed, w_key)).reshape(group_size, SEQ_LEN, KV_HEADS, HEAD_DIM)
    values = round_both(product(normed, w_value)).reshape(group_size, SEQ_LEN, KV_HEADS, HEAD_DIM)
    queries = round_both(rotate(query_lin, cosine, sine))
    keys = round_both(rotate(key_lin, cosine, sine))
    mixed = round_both(jax.vmap(attend_sequence)(queries, keys, values)).reshape(-1, HEADS * HEAD_DIM)
    branch = low_back(product(mixed, w_out))
    middle = inputs.reshape(-1, D) + branch
    normed_ffn = low(rms_norm(middle, norm_ffn))
    gate_val = low_back(product(normed_ffn, w_gate))
    up_val = low_back(product(normed_ffn, w_up))
    hidden = round_both(jax.nn.silu(gate_val) * up_val)
    result = middle + low_back(product(hidden, w_down))
    return result.reshape(group_size, SEQ_LEN, D)

def reference(inputs, norm_attn, w_query, w_key, w_value, w_out, norm_ffn, w_gate, w_up, w_down, cotangent):
    group_size = math.gcd(SEQS, max(1, 4096 // SEQ_LEN))
    params = tuple((item.astype(jnp.float32) for item in (norm_attn, w_query, w_key, w_value, w_out, norm_ffn, w_gate, w_up, w_down)))
    grouped = inputs.astype(jnp.float32).reshape(SEQS // group_size, group_size, SEQ_LEN, D)

    def forward(grouped_in, weights):
        return lax.map(jax.checkpoint(lambda piece_in: layer(piece_in, weights)), grouped_in)
    result, pull_back = jax.vjp(forward, grouped, params)
    input_grad, weight_grads = pull_back(cotangent.astype(jnp.float32).reshape(grouped.shape))
    return (result.reshape(SEQS, SEQ_LEN, D).astype(jnp.bfloat16), input_grad.reshape(SEQS, SEQ_LEN, D), weight_grads[0], weight_grads[1], weight_grads[2], weight_grads[3], weight_grads[4], weight_grads[5], weight_grads[6], weight_grads[7], weight_grads[8])
```

```python
import jax
import jax.numpy as jnp
from jax import lax
from jax.sharding import PartitionSpec as P

D = 1536
HEADS = 16
KV_HEADS = 8
HEAD_DIM = 96
FF = 4096

EPSILON = 1e-05
ROPE_BASE = 100000.0
MASKED = -1e30

NX, NZ = 4, 4
BF = jnp.bfloat16
F32 = jnp.float32


def shift_z(v, step):
    pairs = [(z * 2 + l, (z + step) % NZ * 2 + l) for z in range(NZ) for l in range(2)]
    return lax.ppermute(v, "sp", pairs)


def swap_low(v):
    return lax.ppermute(v, "sp", [(s, s ^ 1) for s in range(8)])


def shift_x(v, step):
    pairs = [(x * 4 + r, (x + step) % NX * 4 + r) for x in range(NX) for r in range(4)]
    return lax.ppermute(v, "fsdp", pairs)


def swap_core(v):
    return lax.ppermute(v, "fsdp", [(f, f ^ 1) for f in range(16)])


def mirror_y(v):
    pairs = [(f * 8 + s, (f ^ 2) * 8 + (s ^ 1)) for f in range(16) for s in range(8)]
    return lax.ppermute(v, ("fsdp", "sp"), pairs)


def places():
    f, s = lax.axis_index("fsdp"), lax.axis_index("sp")
    return f // 4, f // 2 % 2, f % 2, s // 2, s % 2


def laid(pieces, at, dim, parts):
    width = pieces[0].shape[dim]
    shape = list(pieces[0].shape)
    shape[dim] = width * parts
    out = jnp.zeros(shape, pieces[0].dtype)
    for i, piece in enumerate(pieces):
        out = lax.dynamic_update_slice_in_dim(out, piece, (at + i) % parts * width, dim)
    return out


def gather_z(v, z, dim):
    return laid([v, shift_z(v, -1), shift_z(v, 2), shift_z(v, 1)], z, dim, NZ)


def part(v, index, size, dim=0):
    return lax.dynamic_slice_in_dim(v, index * size, size, dim)


def scatter_z(v, z):
    rows = v.shape[0] // NZ
    total = part(v, z, rows)
    for step in (1, 2, 3):
        moved = shift_z(part(v, (z + step) % NZ, rows).astype(BF), step)
        total = total + moved.astype(F32)
    return total


def either(flag, own, other, axis):
    return jnp.where(flag == 0, jnp.stack([own, other], axis), jnp.stack([other, own], axis))


def gather_rows(shard, x, yh, c):
    pair = either(yh, shard, mirror_y(shard), 0)
    lane = laid([pair[None], shift_x(pair, -1)[None], shift_x(pair, 2)[None], shift_x(pair, 1)[None]], x, 0, NX)
    both = either(c, lane, swap_core(lane), 2)
    return both.reshape(16 * shard.shape[0], shard.shape[1])


def reduce_rows(grad, x, yh, c):
    rows, width = grad.shape[0] // 16, grad.shape[1]
    tiles = grad.reshape(8, 2, rows, width)
    mine = lax.dynamic_index_in_dim(tiles, c, 1, False)
    sent = lax.dynamic_index_in_dim(tiles, 1 - c, 1, False).astype(BF)
    lane = mine + swap_core(sent).astype(F32)
    lane = lane.reshape(NX, 2, rows, width)
    total = lax.dynamic_index_in_dim(lane, x, 0, False)
    for step in (1, 2, 3):
        sent = lax.dynamic_index_in_dim(lane, (x + step) % NX, 0, False).astype(BF)
        total = total + shift_x(sent, step).astype(F32)
    mine = lax.dynamic_index_in_dim(total, yh, 0, False)
    sent = lax.dynamic_index_in_dim(total, 1 - yh, 0, False).astype(BF)
    half = (mine + mirror_y(sent).astype(F32)).astype(BF)
    return (half.astype(F32) + swap_low(half).astype(F32)).astype(BF)


def rotate(value, cosine, sine):
    half = HEAD_DIM // 2
    first, second = value[..., :half], value[..., half:]
    cos_b, sin_b = cosine[:, None, :], sine[:, None, :]
    return jnp.concatenate(
        [first * cos_b - second * sin_b, second * cos_b + first * sin_b], axis=-1
    )


def project(source, whole):
    return jnp.dot(source, whole, preferred_element_type=F32)


def back(gradient, whole):
    return lax.dot_general(gradient, whole, (((1,), (1,)), ((), ())), preferred_element_type=F32)


def outer(source, gradient):
    return lax.dot_general(source, gradient, (((0,), (0,)), ((), ())), preferred_element_type=F32)


def body(
    inputs, norm_attn, w_query, w_key, w_value, w_out, norm_ffn, w_gate, w_up, w_down, cotangent
):
    x, yh, c, z, yl = places()
    rows = inputs.shape[1]
    tokens = rows * NZ
    x_own = inputs[0]
    out_grad_own = cotangent[0]

    x_all = gather_z(x_own, z, 0)
    qkv_shard = jnp.concatenate(
        [part(w_query, z, 384, 1), part(w_key, z, 192, 1), part(w_value, z, 192, 1)], axis=1
    )
    held_qkv = gather_rows(qkv_shard, x, yh, c)
    out_grad = gather_z(out_grad_own, z, 0)
    held_out = gather_rows(w_out, x, yh, c)

    def hidden_cols(w):
        return lax.dynamic_index_in_dim(w.reshape(96, 16, NZ, 64), z, 2, False).reshape(96, 1024)

    ffn_shard = jnp.concatenate([hidden_cols(w_gate), hidden_cols(w_up)], axis=1)
    held_ffn = lax.all_gather(ffn_shard, "fsdp", axis=0, tiled=True)
    held_down = lax.all_gather(part(w_down, z, 64), "fsdp", axis=0, tiled=True)

    index = jnp.arange(tokens, dtype=jnp.int32)
    positions = (index // rows * 2 + yl) * rows + index % rows
    half = HEAD_DIM // 2
    frequency = ROPE_BASE ** (-(jnp.arange(half, dtype=F32) * 2.0 / HEAD_DIM))
    angles = positions.astype(F32)[:, None] * frequency[None, :]
    cosine, sine = jnp.cos(angles), jnp.sin(angles)

    x_f = x_all.astype(F32)
    r_attn = lax.rsqrt(jnp.mean(x_f * x_f, axis=-1, keepdims=True) + EPSILON)
    normed = (x_f * r_attn * norm_attn).astype(BF)
    lin = project(normed, held_qkv)
    queries = rotate(lin[:, :384].reshape(tokens, 4, HEAD_DIM), cosine, sine).astype(BF)
    keys = rotate(lin[:, 384:576].reshape(tokens, 2, HEAD_DIM), cosine, sine).astype(BF)
    values = lin[:, 576:].reshape(tokens, 2, HEAD_DIM).astype(BF)

    kv = jnp.concatenate([keys, values], axis=1).reshape(NZ, rows, 4 * HEAD_DIM)
    kv_all = either(yl, kv, swap_low(kv), 1).reshape(2 * tokens, 4, HEAD_DIM)
    keys_all, values_all = kv_all[:, :2], kv_all[:, 2:]

    factor = HEAD_DIM ** (-0.5)
    grouped = queries.reshape(tokens, 2, 2, HEAD_DIM)
    blocks = [(0, 256, 512), (256, 512, 1024)]
    mixed_parts, share_parts = [], []
    for start, stop, seen in blocks:
        scores = jnp.einsum(
            "qhgd,khd->hgqk", grouped[start:stop], keys_all[:seen], preferred_element_type=F32
        ) * factor
        allowed = jnp.arange(seen, dtype=jnp.int32)[None, :] <= positions[start:stop, None]
        scores = jnp.where(allowed, scores, MASKED)
        weights = jnp.exp(scores - jnp.max(scores, axis=-1, keepdims=True))
        shares = (weights / jnp.sum(weights, axis=-1, keepdims=True)).astype(BF)
        share_parts.append(shares)
        mixed_parts.append(
            jnp.einsum("hgqk,khd->qhgd", shares, values_all[:seen], preferred_element_type=F32)
        )
    mixed = jnp.concatenate(mixed_parts, 0).reshape(tokens, 384).astype(BF)
    mixed_all = gather_z(mixed, z, 1)

    middle = x_f + project(mixed_all, held_out)
    r_ffn = lax.rsqrt(jnp.mean(middle * middle, axis=-1, keepdims=True) + EPSILON)
    normed_ffn = (middle * r_ffn * norm_ffn).astype(BF)
    both = project(normed_ffn, held_ffn)
    gate_val, up_val = both[:, :1024], both[:, 1024:]
    sigmoid = jax.nn.sigmoid(gate_val)
    silu = gate_val * sigmoid
    hidden = (silu * up_val).astype(BF)
    hidden_grad = back(out_grad, held_down).astype(BF).astype(F32)
    gate_grad = hidden_grad * up_val * (sigmoid * (1.0 + gate_val * (1.0 - sigmoid)))
    up_grad = hidden_grad * silu
    both_grad = jnp.concatenate([gate_grad.astype(BF), up_grad.astype(BF)], axis=1)
    ffn_in_grad = scatter_z(back(both_grad, held_ffn), z)

    middle_own = part(middle, z, rows)
    r_own = part(r_ffn, z, rows)
    pulled = ffn_in_grad * norm_ffn
    middle_grad = (
        out_grad_own.astype(F32)
        + r_own * pulled
        - middle_own * r_own**3 * jnp.mean(pulled * middle_own, axis=-1, keepdims=True)
    )
    branch_grad = middle_grad.astype(BF)
    mixed_grad_own = back(branch_grad, held_out).astype(BF)
    mixed_grad = laid(
        [part(mixed_grad_own, z, 384, 1)]
        + [
            shift_z(part(mixed_grad_own, (z - step) % NZ, 384, 1), -step)
            for step in (1, 2, 3)
        ],
        z,
        0,
        NZ,
    )

    grad_ffn_part = outer(normed_ffn, both_grad)
    grad_down_part = outer(hidden, out_grad)
    grad_ffn = lax.psum_scatter(grad_ffn_part.astype(BF), "fsdp", scatter_dimension=0, tiled=True)
    grad_down = lax.psum_scatter(grad_down_part.astype(BF), "fsdp", scatter_dimension=0, tiled=True)
    grad_ffn = (grad_ffn.astype(F32) + swap_low(grad_ffn).astype(F32)).astype(BF)
    grad_down = (grad_down.astype(F32) + swap_low(grad_down).astype(F32)).astype(BF)
    block_out = (middle_own + scatter_z(project(hidden, held_down), z)).astype(BF)

    grad_grouped = mixed_grad.reshape(tokens, 2, 2, HEAD_DIM)
    mixed_grouped = mixed.reshape(tokens, 2, 2, HEAD_DIM)
    query_parts = []
    key_acc = jnp.zeros((2 * tokens, 2, HEAD_DIM), F32)
    value_acc = jnp.zeros((2 * tokens, 2, HEAD_DIM), F32)
    for (start, stop, seen), shares in zip(blocks, share_parts):
        grad_blk = grad_grouped[start:stop]
        shares_f = shares.astype(F32)
        share_grad = jnp.einsum(
            "qhgd,khd->hgqk", grad_blk, values_all[:seen], preferred_element_type=F32
        )
        row_dot = jnp.sum(shares_f * share_grad, axis=-1, keepdims=True)
        score_grad = (shares_f * (share_grad - row_dot)).astype(BF)
        query_parts.append(
            jnp.einsum("hgqk,khd->qhgd", score_grad, keys_all[:seen], preferred_element_type=F32)
        )
        key_acc = key_acc.at[:seen].add(
            jnp.einsum("hgqk,qhgd->khd", score_grad, grouped[start:stop], preferred_element_type=F32)
        )
        value_acc = value_acc.at[:seen].add(
            jnp.einsum("hgqk,qhgd->khd", shares, grad_blk, preferred_element_type=F32)
        )
    query_grad = (jnp.concatenate(query_parts, 0).reshape(tokens, 4, HEAD_DIM) * factor).astype(BF)
    kv_acc = jnp.concatenate([key_acc * factor, value_acc], axis=1)
    kv_acc = kv_acc.reshape(NZ, 2, rows, 4 * HEAD_DIM)
    kv_mine = lax.dynamic_index_in_dim(kv_acc, yl, 1, False)
    kv_sent = lax.dynamic_index_in_dim(kv_acc, 1 - yl, 1, False).astype(BF)
    kv_grad = (kv_mine + swap_low(kv_sent).astype(F32)).astype(BF).reshape(tokens, 4, HEAD_DIM)
    query_grad = rotate(query_grad.astype(F32), cosine, -sine).astype(BF).reshape(tokens, 384)
    key_grad = rotate(kv_grad[:, :2].astype(F32), cosine, -sine).astype(BF).reshape(tokens, 192)
    value_grad = kv_grad[:, 2:].reshape(tokens, 192)
    lin_grad = jnp.concatenate([query_grad, key_grad, value_grad], axis=1)

    grad_qkv = reduce_rows(outer(normed, lin_grad), x, yh, c)
    first_grad = scatter_z(back(lin_grad, held_qkv), z)
    x_own_f = x_own.astype(F32)
    r_one = part(r_attn, z, rows)
    pulled = first_grad * norm_attn
    input_grad = (
        middle_grad
        + r_one * pulled
        - x_own_f * r_one**3 * jnp.mean(pulled * x_own_f, axis=-1, keepdims=True)
    )

    branch_all = gather_z(branch_grad, z, 0)
    grad_out_part = outer(mixed, branch_all).reshape(4, 4, 24, D)
    grad_out_part = grad_out_part.transpose(1, 0, 2, 3).reshape(384, D)
    grad_out_slice = reduce_rows(grad_out_part, x, yh, c)
    pairs = [
        (((a * 4 + r) * 8 + b * 2 + l), ((b * 4 + r) * 8 + a * 2 + l))
        for a in range(4)
        for b in range(4)
        for r in range(4)
        for l in range(2)
    ]
    grad_out = gather_z(lax.ppermute(grad_out_slice, ("fsdp", "sp"), pairs), z, 0).astype(F32)

    qkv_cols = gather_z(grad_qkv, z, 1).astype(F32).reshape(96, NZ, 768)
    grad_query = qkv_cols[:, :, :384].reshape(96, 1536)
    grad_key = qkv_cols[:, :, 384:576].reshape(96, 768)
    grad_value = qkv_cols[:, :, 576:].reshape(96, 768)

    ffn_cols = gather_z(grad_ffn, z, 1).astype(F32).reshape(96, NZ, 2, 16, 64)
    ffn_cols = ffn_cols.transpose(0, 2, 3, 1, 4).reshape(96, 2, FF)
    grad_gate, grad_up = ffn_cols[:, 0], ffn_cols[:, 1]
    grad_down = gather_z(grad_down, z, 0).astype(F32)

    def gain_grad(gain, pairs):
        total = sum(jnp.sum(w.astype(F32) * g, axis=1) for w, g in pairs)
        own = lax.dynamic_slice_in_dim(gain, lax.axis_index("fsdp") * 96, 96, 0)
        return total / own

    grad_norm_attn = gain_grad(
        norm_attn, [(w_query, grad_query), (w_key, grad_key), (w_value, grad_value)]
    )
    grad_norm_ffn = gain_grad(norm_ffn, [(w_gate, grad_gate), (w_up, grad_up)])
    return (
        block_out[None],
        input_grad[None],
        grad_norm_attn,
        grad_query,
        grad_key,
        grad_value,
        grad_out,
        grad_norm_ffn,
        grad_gate,
        grad_up,
        grad_down,
    )


def solution(mesh):
    rows = P("fsdp", None)
    tokens = P("fsdp", "sp", None)
    return jax.shard_map(
        body,
        mesh=mesh,
        in_specs=(tokens, P(), rows, rows, rows, rows, P(), rows, rows, rows, tokens),
        out_specs=(tokens, tokens, P("fsdp"), rows, rows, rows, rows, P("fsdp"), rows, rows, rows),
        check_vma=False,
    )
```

```python
import functools

import jax
import jax.numpy as jnp
import numpy as np
from jax import lax
from jax.experimental import pallas as pl
from jax.experimental.pallas import tpu as pltpu
from jax.sharding import PartitionSpec as P

D = 1536
HEADS = 16
KV_HEADS = 8
HEAD_DIM = 96
FF = 4096

EPSILON = 1e-05
ROPE_BASE = 100000.0
MASKED = -1e30

NX, NZ = 4, 4
ROWS = 128
TOKENS = ROWS * NZ
QW, KW = 384, 192
HALF = HEAD_DIM // 2
FFZ = FF // NZ
BF = jnp.bfloat16
F32 = jnp.float32
VMEM = pl.BlockSpec(memory_space=pltpu.VMEM)
SMEM = pl.BlockSpec(memory_space=pltpu.SMEM)
ANY = pl.BlockSpec(memory_space=pl.ANY)
LIMIT = pltpu.CompilerParams(vmem_limit_bytes=56 * 1024 * 1024)
X, YH, CORE, Z, YL = range(5)


def shift_z(v, step):
    pairs = [(z * 2 + l, (z + step) % NZ * 2 + l) for z in range(NZ) for l in range(2)]
    return lax.ppermute(v, "sp", pairs)


def swap_low(v):
    return lax.ppermute(v, "sp", [(s, s ^ 1) for s in range(8)])


def shift_x(v, step):
    pairs = [(x * 4 + r, (x + step) % NX * 4 + r) for x in range(NX) for r in range(4)]
    return lax.ppermute(v, "fsdp", pairs)


def swap_core(v):
    return lax.ppermute(v, "fsdp", [(f, f ^ 1) for f in range(16)])


def mirror_y(v):
    pairs = [(f * 8 + s, (f ^ 2) * 8 + (s ^ 1)) for f in range(16) for s in range(8)]
    return lax.ppermute(v, ("fsdp", "sp"), pairs)


def pieces_z(v):
    far = [shift_z(v, -1), shift_z(v, 1), shift_z(v, 2)]
    return [v, far[0], far[2], far[1]]


def pieces_x(v):
    far = [shift_x(v, -1), shift_x(v, 1), shift_x(v, 2)]
    return [v, far[0], far[2], far[1]]


def part(v, index, size, dim=0):
    return lax.dynamic_slice_in_dim(v, index * size, size, dim)


def call(kernel, outs, ins, flops, scratch=(), grid=None, in_specs=None, out_specs=None, deps=()):
    total = sum(a.size * a.dtype.itemsize for a in ins) + sum(
        int(np.prod(s)) * jnp.dtype(t).itemsize for s, t in outs
    )
    kw = {} if grid is None else {"grid": grid}

    def run(*refs):
        kernel(*refs[: len(ins)], *refs[len(ins) + len(deps) :])

    return pl.pallas_call(
        run,
        out_shape=[jax.ShapeDtypeStruct(s, t) for s, t in outs],
        in_specs=(in_specs or [SMEM] + [VMEM] * (len(ins) - 1)) + [ANY] * len(deps),
        out_specs=out_specs or [VMEM] * len(outs),
        scratch_shapes=scratch,
        compiler_params=LIMIT,
        cost_estimate=pl.CostEstimate(flops=flops, bytes_accessed=total, transcendentals=0),
        **kw,
    )(*ins, *deps)


def mm(a, b):
    return jnp.dot(a, b, preferred_element_type=F32)


def mm_t(a, b):
    return lax.dot_general(a, b, (((1,), (1,)), ((), ())), preferred_element_type=F32)


def t_mm(a, b):
    return lax.dot_general(a, b, (((0,), (0,)), ((), ())), preferred_element_type=F32)


def at_rows(index, size):
    return pl.ds(pl.multiple_of(index * size, size), size)


def put_rows(out_ref, places, mine, other, n):
    for i in range(NX):
        for k in range(2):
            base = (places[X] + i) % NX * 4 + (places[YH] + k) % 2 * 2
            for refs, core in ((mine, places[CORE]), (other, 1 - places[CORE])):
                out_ref[at_rows(base + core, n), :] = refs[i, k] if hasattr(refs, "at") else refs[i][k]


def rope(v, cosine, sine):
    width = v.shape[1]
    lane = lax.broadcasted_iota(jnp.int32, v.shape, 1) % HEAD_DIM
    partner = jnp.where(
        lane < HALF, pltpu.roll(v, width - HALF, 1), pltpu.roll(v, HALF, 1)
    )
    return v * cosine + partner * sine


def rope_keys(kv, cosine, sine):
    lane = lax.broadcasted_iota(jnp.int32, kv.shape, 1)
    return jnp.where(lane < KW, rope(kv, cosine, sine), kv)


def cut_kernel(places, wq, wk, wv, wg, wu, wd, qkv_ref, ffn_ref):
    z = places[Z]
    qkv_ref[:, :QW] = wq[:, pl.ds(pl.multiple_of(z * QW, 128), QW)]
    for t in range(3):
        ffn_ref[4 * 96 + 64 * t : 4 * 96 + 64 * (t + 1), :] = wd[
            at_rows(z, 64), t * 512 : (t + 1) * 512
        ]
    for at in range(NZ):

        @pl.when(z == at)
        def _():
            cols = slice(at * KW, (at + 1) * KW)
            qkv_ref[:, QW:] = jnp.concatenate([wk[:, cols], wv[:, cols]], axis=1)
            for k, w in enumerate((wg, wu)):
                for half in range(2):
                    starts = [(8 * half + i) * 256 + at * 64 for i in range(8)]
                    rows = slice((2 * k + half) * 96, (2 * k + half + 1) * 96)
                    ffn_ref[rows, :] = jnp.concatenate([w[:, b : b + 64] for b in starts], axis=1)


def cut(places, *weights):
    return call(cut_kernel, [((96, 768), BF), ((576, 512), BF)], [places, *weights], 0)


def copy_kernel(places, v_ref, out_ref):
    out_ref[...] = v_ref[...]


def copied(places, v, deps):
    return call(copy_kernel, [(v.shape, v.dtype)], [places, v], 0, deps=deps)[0]


def stack_kernel(places, *refs):
    for i, ref in enumerate(refs[:-1]):
        refs[-1][i] = ref[...]


def stacked(places, arrays, deps):
    shape = (len(arrays), *arrays[0].shape)
    return call(stack_kernel, [(shape, BF)], [places, *arrays], 0, deps=deps)[0]


def qkv_kernel(places, *refs):
    xs, mine, other = refs[:4], refs[4:8], refs[8:12]
    gain, cosine, sine, q_ref, kv_ref, normed_ref, x_ref, w_ref = refs[12:]
    put_rows(w_ref, places, mine, other, 96)
    for i in range(NZ):
        rows = at_rows((places[Z] + i) % NZ, ROWS)
        piece = xs[i][...]
        x_ref[rows, :] = piece
        v = piece.astype(F32)
        r = lax.rsqrt(jnp.mean(v * v, axis=1, keepdims=True) + EPSILON)
        normed_ref[rows, :] = (v * r * gain[...]).astype(BF)
    for i in range(NZ):
        rows = pl.ds(i * ROWS, ROWS)
        lin = mm(normed_ref[rows, :], w_ref[...])
        q_ref[rows, :] = rope(lin[:, :QW], cosine[rows, :], sine[rows, :]).astype(BF)
        kv_ref[rows, :] = rope_keys(lin[:, QW:], cosine[rows, :], sine[rows, :]).astype(BF)


def qkv(places, xs, mine, other, gain, cosine, sine, deps):
    return call(
        qkv_kernel,
        [
            ((TOKENS, QW), BF),
            ((TOKENS, 2 * KW), BF),
            ((TOKENS, D), BF),
            ((TOKENS, D), BF),
            ((D, QW + 2 * KW), BF),
        ],
        [places, *xs, *mine, *other, gain, cosine, sine],
        2 * TOKENS * D * 768,
        deps=deps,
    )


def head(ref, rows, index):
    return ref[rows, index * HEAD_DIM : (index + 1) * HEAD_DIM]


def two_heads(ref, j, g):
    rows = slice(j * ROWS, (j + 1) * ROWS)
    return jnp.concatenate([head(ref, rows, 2 * g), head(ref, rows, 2 * g + 1)], axis=0)


def attend_kernel(places, q_ref, own_ref, other_ref, mixed_ref, p_ref):
    late = places[YL]
    factor = HEAD_DIM ** (-0.5)
    for g in range(2):
        for j in range(NZ):
            n = (j + 1) * ROWS
            q = two_heads(q_ref, j, g)
            s_own = mm_t(q, head(own_ref, slice(0, n), g)) * factor
            s_oth = mm_t(q, head(other_ref, slice(0, n), g)) * factor
            shape = (2 * ROWS, n)
            row = lax.broadcasted_iota(jnp.int32, shape, 0) % ROWS + j * ROWS
            col = lax.broadcasted_iota(jnp.int32, shape, 1)
            s_own = jnp.where(col <= row, s_own, MASKED)
            s_oth = jnp.where(col < (j + late) * ROWS, s_oth, MASKED)
            highest = jnp.maximum(
                jnp.max(s_own, axis=1, keepdims=True), jnp.max(s_oth, axis=1, keepdims=True)
            )
            p_own, p_oth = jnp.exp(s_own - highest), jnp.exp(s_oth - highest)
            total = jnp.sum(p_own, axis=1, keepdims=True) + jnp.sum(p_oth, axis=1, keepdims=True)
            scale = 1.0 / total
            p_own, p_oth = (p_own * scale).astype(BF), (p_oth * scale).astype(BF)
            p_ref[g, j, :, :n] = p_own
            p_ref[g, j, :, n : 2 * n] = p_oth
            out = mm(p_own, head(own_ref, slice(0, n), 2 + g)) + mm(
                p_oth, head(other_ref, slice(0, n), 2 + g)
            )
            out = out.astype(BF)
            for k in range(2):
                h = 2 * g + k
                mixed_ref[j * ROWS : (j + 1) * ROWS, h * HEAD_DIM : (h + 1) * HEAD_DIM] = out[
                    k * ROWS : (k + 1) * ROWS
                ]


def attend(places, q, kv, kv_other):
    return call(
        attend_kernel,
        [((TOKENS, QW), BF), ((2, NZ, 2 * ROWS, 2 * TOKENS), BF)],
        [places, q, kv, kv_other],
        4 * TOKENS * 2 * TOKENS * HEAD_DIM * 4 * 5 // 8,
    )


def attend_back_kernel(places, *refs):
    grads = refs[:4]
    q_ref, own_ref, other_ref, p_ref = refs[4:8]
    dq_ref, down_ref, doth_ref = refs[8:11]
    do_ref, acc_own, acc_oth = refs[11:]
    factor = HEAD_DIM ** (-0.5)
    for i in range(NZ):
        do_ref[at_rows((places[Z] + i) % NZ, ROWS), :] = grads[i][...]
    for g in range(2):
        acc_own[...] = jnp.zeros_like(acc_own)
        acc_oth[...] = jnp.zeros_like(acc_oth)
        for j in range(NZ):
            n = (j + 1) * ROWS
            seen = slice(0, n)
            q = two_heads(q_ref, j, g)
            do = two_heads(do_ref, j, g)
            p_own, p_oth = p_ref[g, j, :, :n], p_ref[g, j, :, n : 2 * n]
            dp_own = mm_t(do, head(own_ref, seen, 2 + g))
            dp_oth = mm_t(do, head(other_ref, seen, 2 + g))
            f_own, f_oth = p_own.astype(F32), p_oth.astype(F32)
            dot = jnp.sum(f_own * dp_own, axis=1, keepdims=True) + jnp.sum(
                f_oth * dp_oth, axis=1, keepdims=True
            )
            ds_own = (f_own * (dp_own - dot)).astype(BF)
            ds_oth = (f_oth * (dp_oth - dot)).astype(BF)
            dq = mm(ds_own, head(own_ref, seen, g)) + mm(ds_oth, head(other_ref, seen, g))
            dq = (dq * factor).astype(BF)
            for k in range(2):
                h = 2 * g + k
                dq_ref[j * ROWS : (j + 1) * ROWS, h * HEAD_DIM : (h + 1) * HEAD_DIM] = dq[
                    k * ROWS : (k + 1) * ROWS
                ]
            acc_own[0, seen, :] += t_mm(ds_own, q)
            acc_own[1, seen, :] += t_mm(p_own, do)
            acc_oth[0, seen, :] += t_mm(ds_oth, q)
            acc_oth[1, seen, :] += t_mm(p_oth, do)
        for kind, scale in ((0, factor), (1, 1.0)):
            at = kind * KW + g * HEAD_DIM
            down_ref[:, at : at + HEAD_DIM] = acc_own[kind] * scale
            doth_ref[:, at : at + HEAD_DIM] = (acc_oth[kind] * scale).astype(BF)


def attend_back(places, grads, q, kv, kv_other, shares, deps):
    acc = pltpu.VMEM((2, TOKENS, HEAD_DIM), F32)
    return call(
        attend_back_kernel,
        [((TOKENS, QW), BF), ((TOKENS, 2 * KW), F32), ((TOKENS, 2 * KW), BF)],
        [places, *grads, q, kv, kv_other, shares],
        4 * TOKENS * 2 * TOKENS * HEAD_DIM * 8 * 5 // 8,
        scratch=[pltpu.VMEM((TOKENS, QW), BF), acc, acc],
        deps=deps,
    )


def send_chunks(refs, acc_ref, places):
    for i in range(NZ):
        rows = at_rows((places[Z] + i) % NZ, ROWS)
        refs[i][...] = acc_ref[rows, :].astype(refs[i].dtype)


CHUNKS = [((ROWS, D), F32)] + [((ROWS, D), BF)] * 3


def qkv_back_kernel(places, normed_ref, dq_ref, own_ref, got_ref, cosine, sine, w_ref, *refs):
    chunks, mine_ref, sent_ref = refs[:4], refs[4], refs[5]
    lin_ref, acc_ref, dw_ref = refs[6:]
    for i in range(NZ):
        rows = slice(i * ROWS, (i + 1) * ROWS)
        dkv = (own_ref[rows, :] + got_ref[rows, :].astype(F32)).astype(BF)
        c, s = cosine[rows, :], -sine[rows, :]
        lin_ref[rows, :QW] = rope(dq_ref[rows, :].astype(F32), c, s).astype(BF)
        lin_ref[rows, QW:] = rope_keys(dkv.astype(F32), c, s).astype(BF)
    dw_ref[...] = t_mm(normed_ref[...], lin_ref[...]).astype(BF)
    for k in range(8):
        mine_ref[k] = dw_ref[at_rows(2 * k + places[CORE], 96), :]
        sent_ref[k] = dw_ref[at_rows(2 * k + 1 - places[CORE], 96), :]
    acc_ref[...] = mm_t(lin_ref[...], w_ref[...])
    send_chunks(chunks, acc_ref, places)


def qkv_back(places, normed, dq, dkv_own, dkv_got, cosine, sine, w, deps):
    return call(
        qkv_back_kernel,
        CHUNKS + [((8, 96, 768), BF)] * 2,
        [places, normed, dq, dkv_own, dkv_got, cosine, sine, w],
        4 * TOKENS * D * 768,
        scratch=[
            pltpu.VMEM((TOKENS, 768), BF),
            pltpu.VMEM((TOKENS, D), F32),
            pltpu.VMEM((D, 768), BF),
        ],
        deps=deps,
    )


def lay_kernel(places, *refs):
    for i in range(NZ):
        refs[4][at_rows((places[Z] + i) % NZ, ROWS), :] = refs[i][...]


def lay_tokens(places, pieces, deps):
    return call(lay_kernel, [((TOKENS, D), BF)], [places, *pieces], 0, deps=deps)[0]


def lay_rows_kernel(places, mine, other, out_ref):
    put_rows(out_ref, places, mine, other, 96)


def lay_rows(places, mine, other):
    return call(lay_rows_kernel, [((D, D), BF)], [places, mine, other], 0)[0]


def middle_kernel(places, x_ref, m0, m1, m2, m3, w_ref, gain, normed_ref, own_ref, acc_ref):
    acc_ref[...] = x_ref[...].astype(F32)
    for i, ref in enumerate((m0, m1, m2, m3)):
        acc_ref[...] += mm(ref[...], w_ref[at_rows((places[Z] + i) % NZ, QW), :])
    for i in range(NZ):
        rows = slice(i * ROWS, (i + 1) * ROWS)
        v = acc_ref[rows, :]
        r = lax.rsqrt(jnp.mean(v * v, axis=1, keepdims=True) + EPSILON)
        normed_ref[rows, :] = (v * r * gain[...]).astype(BF)
    own_ref[...] = acc_ref[at_rows(places[Z], ROWS), :]


def middle_of(places, x_all, pieces, w_out, gain):
    return call(
        middle_kernel,
        [((TOKENS, D), BF), ((ROWS, D), F32)],
        [places, x_all, *pieces, w_out, gain],
        2 * TOKENS * D * D,
        scratch=[pltpu.VMEM((TOKENS, D), F32)],
    )


def ffn_kernel(places, n_ref, og_ref, gate_w, up_w, d0, d1, d2, *refs):
    hidden_ref, gg_ref, ug_ref = refs[:3]
    in_chunks, down_chunks = refs[3:7], refs[7:11]
    in_acc, down_acc = refs[11:]
    j = pl.program_id(0)
    wg = gate_w[...].reshape(D, 512)
    wu = up_w[...].reshape(D, 512)
    downs = [d[...].reshape(512, 512) for d in (d0, d1, d2)]
    gate = mm(n_ref[...], wg)
    up = mm(n_ref[...], wu)
    hg = sum(mm_t(og_ref[:, t * 512 : (t + 1) * 512], downs[t]) for t in range(3))
    hg = hg.astype(BF).astype(F32)
    sig = 1.0 / (1.0 + jnp.exp(-gate))
    silu = gate * sig
    hidden = (silu * up).astype(BF)
    gg = (hg * up * (sig * (1.0 + gate * (1.0 - sig)))).astype(BF)
    ug = (hg * silu).astype(BF)
    hidden_ref[...] = hidden
    gg_ref[...] = gg
    ug_ref[...] = ug
    into = mm_t(gg, wg) + mm_t(ug, wu)

    @pl.when(j == 0)
    def _():
        in_acc[...] = into
        for t in range(3):
            down_acc[:, t * 512 : (t + 1) * 512] = mm(hidden, downs[t])

    @pl.when(j == 1)
    def _():
        in_acc[...] += into
        for t in range(3):
            down_acc[:, t * 512 : (t + 1) * 512] += mm(hidden, downs[t])
        send_chunks(in_chunks, in_acc, places)
        send_chunks(down_chunks, down_acc, places)


def ffn(places, normed, og, packed):
    whole = pl.BlockSpec((TOKENS, D), lambda j: (0, 0))
    col = pl.BlockSpec((TOKENS, 512), lambda j: (0, j))
    chunk = pl.BlockSpec((ROWS, D), lambda j: (0, 0))
    downs = [pl.BlockSpec((8, 64, 512), lambda j, t=t: (j, 6 + t, 0)) for t in range(3)]
    gate = pl.BlockSpec((16, 96, 512), lambda j: (0, j, 0))
    up = pl.BlockSpec((16, 96, 512), lambda j: (0, 2 + j, 0))
    return call(
        ffn_kernel,
        [((TOKENS, FFZ), BF)] * 3 + CHUNKS + CHUNKS,
        [places, normed, og] + [packed] * 5,
        12 * TOKENS * D * FFZ,
        grid=(2,),
        in_specs=[SMEM, whole, whole, gate, up] + downs,
        out_specs=[col] * 3 + [chunk] * 8,
        scratch=[pltpu.VMEM((TOKENS, D), F32)] * 2,
    )


def ffn_grad_kernel(places, n_ref, g_ref, mine_ref, sent_ref, dw_ref):
    dw_ref[...] = t_mm(n_ref[...], g_ref[...]).astype(BF)
    for k in range(8):
        mine_ref[k] = dw_ref[at_rows(2 * k + places[CORE], 96), :]
        sent_ref[k] = dw_ref[at_rows(2 * k + 1 - places[CORE], 96), :]


def ffn_grad(places, normed, grad):
    out = pl.BlockSpec((8, 96, 512), lambda j: (0, 0, j))
    return call(
        ffn_grad_kernel,
        [((8, 96, FFZ), BF)] * 2,
        [places, normed, grad],
        2 * TOKENS * D * FFZ,
        grid=(2,),
        in_specs=[
            SMEM,
            pl.BlockSpec((TOKENS, D), lambda j: (0, 0)),
            pl.BlockSpec((TOKENS, 512), lambda j: (0, j)),
        ],
        out_specs=[out, out],
        scratch=[pltpu.VMEM((D, 512), BF)],
    )


def rms_back(grad, v, gain):
    r = lax.rsqrt(jnp.mean(v * v, axis=1, keepdims=True) + EPSILON)
    pulled = grad * gain
    return r * pulled - v * (r * r * r * jnp.mean(pulled * v, axis=1, keepdims=True))


def middle_back_kernel(places, own, g1, g2, g3, middle, og, gain, w_ref, mid_ref, branch_ref, *outs):
    grad = own[...] + g1[...].astype(F32) + g2[...].astype(F32) + g3[...].astype(F32)
    mid = og[...].astype(F32) + rms_back(grad, middle[...], gain[...])
    mid_ref[...] = mid
    branch = mid.astype(BF)
    branch_ref[...] = branch
    for i in range(NZ):
        outs[i][...] = mm_t(branch, w_ref[at_rows((places[Z] + i) % NZ, QW), :]).astype(BF)


def middle_back(places, chunks, middle, og, gain, w_out, deps):
    return call(
        middle_back_kernel,
        [((ROWS, D), F32), ((ROWS, D), BF)] + [((ROWS, QW), BF)] * 4,
        [places, *chunks, middle, og, gain, w_out],
        2 * ROWS * D * D,
        deps=deps,
    )


def join_kernel(places, branch, d1, d2, d3, o1, o2, o3):
    for d, o in ((d1, o1), (d2, o2), (d3, o3)):
        o[0] = branch[...]
        o[1] = d[...]


def join(places, dep, branch, downs):
    return call(join_kernel, [((2, ROWS, D), BF)] * 3, [places, branch, *downs], 0, deps=[dep])


def input_back_kernel(places, own, g1, g2, g3, x, mid, gain, out_ref):
    grad = own[...] + g1[...].astype(F32) + g2[...].astype(F32) + g3[...].astype(F32)
    out_ref[...] = mid[...] + rms_back(grad, x[...].astype(F32), gain[...])


def input_back(places, chunks, x, mid, gain, deps):
    return call(
        input_back_kernel, [((ROWS, D), F32)], [places, *chunks, x, mid, gain], 0, deps=deps
    )[0]


def scatter(chunks):
    far = [shift_z(chunks[1], 1), shift_z(chunks[3], -1), shift_z(chunks[2], 2)]
    return [chunks[0], *far]


def down_grad_kernel(places, h_ref, og_ref, mine_ref, sent_ref, dw_ref):
    dw_ref[...] = t_mm(h_ref[...], og_ref[...]).astype(BF)
    for k in range(8):
        mine_ref[k] = dw_ref[at_rows(2 * k + places[CORE], 64), :]
        sent_ref[k] = dw_ref[at_rows(2 * k + 1 - places[CORE], 64), :]


def down_grad(places, hidden, og):
    return call(
        down_grad_kernel,
        [((8, 64, D), BF)] * 2,
        [places, hidden, og],
        2 * TOKENS * D * FFZ,
        scratch=[pltpu.VMEM((FFZ, D), BF)],
    )


def ffn_core_sum_kernel(places, *refs):
    gate, up, down = refs[0:2], refs[2:4], refs[4:6]
    outs = refs[6:]
    for i in range(NX):
        for k in range(2):
            at = (places[X] + i) % NX * 2 + (places[YH] + k) % 2
            for w, (mine, got) in enumerate((gate, up)):
                total = (mine[at].astype(F32) + got[at].astype(F32)).astype(BF)
                for half in range(2):
                    r = (2 * w + half) * 96
                    outs[i][k, r : r + 96, :] = total[:, half * 512 : (half + 1) * 512]
            total = (down[0][at].astype(F32) + down[1][at].astype(F32)).astype(BF)
            for t in range(3):
                r = 384 + 64 * t
                outs[i][k, r : r + 64, :] = total[:, t * 512 : (t + 1) * 512]


def ffn_core_sum(places, gate, up, down, deps):
    return call(
        ffn_core_sum_kernel, [((2, 576, 512), BF)] * 4, [places, *gate, *up, *down], 0, deps=deps
    )


def core_sum_kernel(places, mine, got, *outs):
    for i in range(NX):
        for k in range(2):
            at = (places[X] + i) % NX * 2 + (places[YH] + k) % 2
            outs[i][k] = (mine[at].astype(F32) + got[at].astype(F32)).astype(BF)


def core_sum(places, mine, got, deps):
    shape = (2, *mine.shape[1:])
    return call(core_sum_kernel, [(shape, BF)] * 4, [places, mine, got], 0, deps=deps)


def x_sum_kernel(places, a, b, c, d, mine, sent):
    mine[...] = a[0].astype(F32) + b[0].astype(F32) + c[0].astype(F32) + d[0].astype(F32)
    total = a[1].astype(F32) + b[1].astype(F32) + c[1].astype(F32) + d[1].astype(F32)
    sent[...] = total.astype(BF)


def x_sum(places, terms, deps):
    shape = terms[0].shape[1:]
    return call(x_sum_kernel, [(shape, F32), (shape, BF)], [places, *terms], 0, deps=deps)


def add_kernel(places, a, b, out):
    out[...] = (a[...].astype(F32) + b[...].astype(F32)).astype(BF)


def added(places, a, b, deps):
    return call(add_kernel, [(a.shape, BF)], [places, a, b], 0, deps=deps)[0]


def over_x(chunks):
    far = [shift_x(chunks[1], 1), shift_x(chunks[3], -1), shift_x(chunks[2], 2)]
    return [chunks[0], *far]


def ffn_out_kernel(places, p0, p1, p2, p3, wg, wu, gate_ref, up_ref, down_ref, gain_ref, all_ref):
    for i, p in enumerate((p0, p1, p2, p3)):
        all_ref[(places[Z] + i) % NZ] = p[...]
    gain = jnp.zeros((96, 1), F32)
    for k, (w, out) in enumerate(((wg, gate_ref), (wu, up_ref))):
        for b in range(16):
            rows = slice((2 * k + b // 8) * 96, (2 * k + b // 8 + 1) * 96)
            cols = slice(b % 8 * 64, b % 8 * 64 + 64)
            tile = jnp.concatenate([all_ref[q, rows, cols].astype(F32) for q in range(NZ)], axis=1)
            out[:, b * 256 : (b + 1) * 256] = tile
            gain += jnp.sum(
                tile * w[:, b * 256 : (b + 1) * 256].astype(F32), axis=1, keepdims=True
            )
    for q in range(NZ):
        for t in range(3):
            r = 384 + 64 * t
            down_ref[q * 64 : (q + 1) * 64, t * 512 : (t + 1) * 512] = all_ref[
                q, r : r + 64, :
            ].astype(F32)
    gain_ref[...] = gain


def ffn_out(places, pieces, wg, wu, deps):
    return call(
        ffn_out_kernel,
        [((96, FF), F32), ((96, FF), F32), ((256, D), F32), ((96, 1), F32)],
        [places, *pieces, wg, wu],
        0,
        scratch=[pltpu.VMEM((NZ, 576, 512), BF)],
        deps=deps,
    )


def qkv_out_kernel(places, p0, p1, p2, p3, wq, wk, wv, q_ref, k_ref, v_ref, gain_ref, all_ref):
    for i, p in enumerate((p0, p1, p2, p3)):
        all_ref[(places[Z] + i) % NZ] = p[...]
    for q in range(NZ):
        q_ref[:, q * QW : (q + 1) * QW] = all_ref[q, :, :QW].astype(F32)
    gain = jnp.sum(q_ref[...] * wq[...].astype(F32), axis=1, keepdims=True)
    for out, w, at in ((k_ref, wk, QW), (v_ref, wv, QW + KW)):
        tile = jnp.concatenate(
            [all_ref[q, :, at : at + KW].astype(F32) for q in range(NZ)], axis=1
        )
        out[...] = tile
        gain += jnp.sum(tile * w[...].astype(F32), axis=1, keepdims=True)
    gain_ref[...] = gain


def qkv_out(places, pieces, wq, wk, wv):
    return call(
        qkv_out_kernel,
        [((96, 1536), F32), ((96, 768), F32), ((96, 768), F32), ((96, 1), F32)],
        [places, *pieces, wq, wk, wv],
        0,
        scratch=[pltpu.VMEM((NZ, 96, 768), BF)],
    )


def block_out_kernel(places, middle, own, a, b, c, out_ref):
    total = middle[...] + own[...]
    for v in (a, b, c):
        total += v[1].astype(F32)
    out_ref[...] = total.astype(BF)


def block_out_of(places, middle, own, far, deps):
    return call(
        block_out_kernel, [((ROWS, D), BF)], [places, middle, own, *far], 0, deps=deps
    )[0]


def out_grad_kernel(places, mixed, b0, b1, b2, b3, out_ref, all_ref):
    for i, b in enumerate((b0, b1, b2, b3)):
        all_ref[at_rows((places[Z] + i) % NZ, ROWS), :] = b[0] if len(b.shape) == 3 else b[...]
    out_ref[...] = t_mm(mixed[...], all_ref[...])


def out_grad(places, mixed, branches, deps):
    return call(
        out_grad_kernel,
        [((QW, D), F32)],
        [places, mixed, *branches],
        2 * TOKENS * QW * D,
        scratch=[pltpu.VMEM((TOKENS, D), BF)],
        deps=deps,
    )[0]


def sum_rows(mine, sent, x, yh):
    n, k = mine.shape[1:]
    lane = (mine.astype(F32) + swap_core(sent).astype(F32)).astype(BF).reshape(NX, 2, n, k)
    far = [
        shift_x(lax.dynamic_index_in_dim(lane, (x + step) % NX, 0, False), step)
        for step in (1, 3, 2)
    ]
    total = lax.dynamic_index_in_dim(lane, x, 0, False).astype(F32) + sum(
        v.astype(F32) for v in far
    )
    mine = lax.dynamic_index_in_dim(total, yh, 0, False)
    sent = lax.dynamic_index_in_dim(total, 1 - yh, 0, False).astype(BF)
    half = (mine + mirror_y(sent).astype(F32)).astype(BF)
    return (half.astype(F32) + swap_low(half).astype(F32)).astype(BF)


def laid(pieces, at, dim):
    width = pieces[0].shape[dim]
    shape = list(pieces[0].shape)
    shape[dim] = width * NZ
    out = jnp.zeros(shape, pieces[0].dtype)
    for i, piece in enumerate(pieces):
        out = lax.dynamic_update_slice_in_dim(out, piece, (at + i) % NZ * width, dim)
    return out


def gather_z(v, z, dim):
    return laid(pieces_z(v), z, dim)


def body(
    inputs, norm_attn, w_query, w_key, w_value, w_out, norm_ffn, w_gate, w_up, w_down, cotangent
):
    f, s = lax.axis_index("fsdp"), lax.axis_index("sp")
    x, yh, c, z, yl = f // 4, f // 2 % 2, f % 2, s // 2, s % 2
    places = jnp.stack([x, yh, c, z, yl]).astype(jnp.int32)
    x_own, og_own = inputs[0], cotangent[0]
    gain_attn, gain_ffn = norm_attn[None], norm_ffn[None]

    index = jnp.arange(TOKENS, dtype=jnp.int32)
    positions = (index // ROWS * 2 + yl) * ROWS + index % ROWS
    lane = np.arange(QW) % HEAD_DIM
    frequency = ROPE_BASE ** (-(jnp.arange(HALF, dtype=F32) * 2.0 / HEAD_DIM))
    frequency = jnp.concatenate([frequency] * (QW // HALF))
    angles = positions.astype(F32)[:, None] * frequency[None, :]
    sign = np.where(lane < HALF, -1.0, 1.0).astype(np.float32)
    cosine, sine = jnp.cos(angles), jnp.sin(angles) * sign[None, :]

    xs = pieces_z(x_own)
    qkv_shard, ffn_shard = cut(places, w_query, w_key, w_value, w_gate, w_up, w_down)
    packed = lax.all_gather(ffn_shard, "fsdp", axis=0, tiled=False)
    qkv_mirror, out_mirror = mirror_y(qkv_shard), mirror_y(w_out)
    qkv_pair = stacked(places, [qkv_shard, qkv_mirror], [cosine, sine, gain_attn])
    qkv_mine = pieces_x(qkv_pair)
    og_src = copied(places, og_own, [xs[1], xs[2], xs[3]])
    ogs = pieces_z(og_src)
    qkv_other = [swap_core(p) for p in qkv_mine]
    out_pair = stacked(places, [w_out, out_mirror], [qkv_mine[1], qkv_mine[2], qkv_mine[3]])
    out_mine = pieces_x(out_pair)

    q, kv, normed, x_all, held_qkv = qkv(
        places, xs, qkv_mine, qkv_other, gain_attn, cosine, sine, [og_src, out_pair]
    )
    kv_other = swap_low(kv)
    mixed, shares = attend(places, q, kv, kv_other)
    mixed_pieces = pieces_z(mixed)

    out_lane = stacked(places, out_mine, [mixed])
    og_all = lay_tokens(places, ogs, [out_lane])
    held_out = lay_rows(places, out_lane, swap_core(out_lane))
    normed_ffn, middle_own = middle_of(places, x_all, mixed_pieces, held_out, gain_ffn)
    outs = ffn(places, normed_ffn, og_all, packed)
    hidden, gate_grad, up_grad = outs[:3]
    in_chunks, down_chunks = outs[3:7], outs[7:11]

    in_got = scatter(in_chunks)
    gate_mine, gate_sent = ffn_grad(places, normed_ffn, gate_grad)
    up_mine, up_sent = ffn_grad(places, normed_ffn, up_grad)
    down_mine, down_sent = down_grad(places, hidden, og_all)

    back = middle_back(
        places, in_got, middle_own, og_own, gain_ffn, held_out, [gate_mine, up_mine, down_mine]
    )
    middle_grad, branch = back[:2]
    head_grads = [back[2], shift_z(back[5], -1), shift_z(back[4], 2), shift_z(back[3], 1)]
    ffn_chunks = ffn_core_sum(
        places,
        (gate_mine, swap_core(gate_sent)),
        (up_mine, swap_core(up_sent)),
        (down_mine, swap_core(down_sent)),
        [middle_grad],
    )
    ffn_terms = over_x(ffn_chunks)

    dq, dkv_own, dkv_sent = attend_back(
        places, head_grads, q, kv, kv_other, shares, [ffn_chunks[0]]
    )
    dkv_got = swap_low(dkv_sent)
    joined = join(places, dq, branch, down_chunks[1:])
    far = [shift_z(joined[0], 1), shift_z(joined[2], -1), shift_z(joined[1], 2)]

    outs = qkv_back(places, normed, dq, dkv_own, dkv_got, cosine, sine, held_qkv, [joined[0]])
    first_got = scatter(outs[:4])
    qkv_mine, qkv_sent = outs[4:]

    ffn_half, ffn_sent = x_sum(places, ffn_terms, [qkv_mine])
    ffn_got = mirror_y(ffn_sent)
    qkv_chunks = core_sum(places, qkv_mine, swap_core(qkv_sent), [ffn_sent])
    qkv_terms = over_x(qkv_chunks)

    branches = [branch, far[1], far[2], far[0]]
    out_part = out_grad(places, mixed, branches, [qkv_chunks[0]])
    block_out = block_out_of(places, middle_own, down_chunks[0], far, [qkv_chunks[0]])
    input_grad = input_back(
        places, first_got, x_own, middle_grad, gain_attn, [qkv_chunks[0], block_out]
    )
    ffn_half = added(places, ffn_half, ffn_got, [qkv_chunks[0], input_grad])
    ffn_low = swap_low(ffn_half)

    qkv_half, qkv_sent = x_sum(places, qkv_terms, [ffn_half])
    qkv_got = mirror_y(qkv_sent)
    ffn_total = added(places, ffn_half, ffn_low, [qkv_sent])
    ffn_pieces = pieces_z(ffn_total)
    qkv_half = added(places, qkv_half, qkv_got, [ffn_total])
    qkv_low = swap_low(qkv_half)
    qkv_total = added(places, qkv_half, qkv_low, [])
    qkv_pieces = pieces_z(qkv_total)

    out_part = out_part.astype(BF).reshape(2, 2, 4, 24, D)
    out_part = out_part.transpose(2, 0, 1, 3, 4).reshape(8, 2, 24, D)
    out_slice = sum_rows(
        lax.dynamic_index_in_dim(out_part, c, 1, False),
        lax.dynamic_index_in_dim(out_part, 1 - c, 1, False),
        x,
        yh,
    )
    pairs = [
        (((a * 4 + r) * 8 + b * 2 + l), ((b * 4 + r) * 8 + a * 2 + l))
        for a in range(4)
        for b in range(4)
        for r in range(4)
        for l in range(2)
    ]
    grad_out = gather_z(lax.ppermute(out_slice, ("fsdp", "sp"), pairs), z, 0).astype(F32)

    grad_gate, grad_up, grad_down, ffn_total = ffn_out(
        places, ffn_pieces, w_gate, w_up, [qkv_total]
    )
    grad_query, grad_key, grad_value, qkv_total = qkv_out(
        places, qkv_pieces, w_query, w_key, w_value
    )
    grad_norm_attn = qkv_total[:, 0] / lax.dynamic_slice_in_dim(norm_attn, f * 96, 96, 0)
    grad_norm_ffn = ffn_total[:, 0] / lax.dynamic_slice_in_dim(norm_ffn, f * 96, 96, 0)
    return (
        block_out[None],
        input_grad[None],
        grad_norm_attn,
        grad_query,
        grad_key,
        grad_value,
        grad_out,
        grad_norm_ffn,
        grad_gate,
        grad_up,
        grad_down,
    )


def solution(mesh):
    rows = P("fsdp", None)
    tokens = P("fsdp", "sp", None)
    return jax.shard_map(
        body,
        mesh=mesh,
        in_specs=(tokens, P(), rows, rows, rows, rows, P(), rows, rows, rows, tokens),
        out_specs=(tokens, tokens, P("fsdp"), rows, rows, rows, rows, P("fsdp"), rows, rows, rows),
        check_vma=False,
    )
```

```python
import functools

import jax
import jax.numpy as jnp
import numpy as np
from jax import lax
from jax.experimental import pallas as pl
from jax.experimental.pallas import tpu as pltpu
from jax.sharding import PartitionSpec as P

D = 1536
HEADS = 16
KV_HEADS = 8
HEAD_DIM = 96
FF = 4096

EPSILON = 1e-05
ROPE_BASE = 100000.0
MASKED = -1e30

NX, NZ = 4, 4
ROWS = 128
TOKENS = ROWS * NZ
QW, KW = 384, 192
HALF = HEAD_DIM // 2
FFZ = FF // NZ
BF = jnp.bfloat16
F32 = jnp.float32
VMEM = pl.BlockSpec(memory_space=pltpu.VMEM)
SMEM = pl.BlockSpec(memory_space=pltpu.SMEM)
ANY = pl.BlockSpec(memory_space=pl.ANY)
LIMIT = pltpu.CompilerParams(vmem_limit_bytes=56 * 1024 * 1024)
X, YH, CORE, Z, YL = range(5)
COST = {
    "norm": 15,
    "qkv": 0.1,
    "attend": 0.1,
    "lay_rows": 0.1,
    "middle": 0.1,
    "ffn": 17,
    "ffn_sent": 0.1,
    "middle_back": 60,
    "ffn_grad": 60,
    "attend_back": 60,
    "turn": 0.1,
    "first": 0.1,
    "x_sum": 60,
    "qkv_grad": 3,
}


Z_GROUPS = [[z * 2 + l for z in range(NZ)] for l in range(2)]


def gather_z(v):
    return lax.all_gather(v, "sp", axis=0, tiled=True, axis_index_groups=Z_GROUPS)


def shift_z(v, step):
    pairs = [(z * 2 + l, (z + step) % NZ * 2 + l) for z in range(NZ) for l in range(2)]
    return lax.ppermute(v, "sp", pairs)


def swap_low(v):
    return lax.ppermute(v, "sp", [(s, s ^ 1) for s in range(8)])


def shift_x(v, step):
    pairs = [(x * 4 + r, (x + step) % NX * 4 + r) for x in range(NX) for r in range(4)]
    return lax.ppermute(v, "fsdp", pairs)


def swap_core(v):
    return lax.ppermute(v, "fsdp", [(f, f ^ 1) for f in range(16)])


def mirror_y(v):
    pairs = [(f * 8 + s, (f ^ 2) * 8 + (s ^ 1)) for f in range(16) for s in range(8)]
    return lax.ppermute(v, ("fsdp", "sp"), pairs)


def pieces_z(v):
    far = [shift_z(v, -1), shift_z(v, 1), shift_z(v, 2)]
    return [v, far[0], far[2], far[1]]


def pieces_x(v):
    far = [shift_x(v, -1), shift_x(v, 1), shift_x(v, 2)]
    return [v, far[0], far[2], far[1]]


def part(v, index, size, dim=0):
    return lax.dynamic_slice_in_dim(v, index * size, size, dim)


def call(kernel, outs, ins, us, scratch=(), deps=()):
    def run(*refs):
        kernel(*refs[: len(ins)], *refs[len(ins) + len(deps) :])

    return pl.pallas_call(
        run,
        name=kernel.__name__.replace("_kernel", ""),
        out_shape=[jax.ShapeDtypeStruct(s, t) for s, t in outs],
        in_specs=[SMEM] + [VMEM] * (len(ins) - 1) + [ANY] * len(deps),
        out_specs=[VMEM] * len(outs),
        scratch_shapes=scratch,
        compiler_params=LIMIT,
        cost_estimate=pl.CostEstimate(
            flops=int(us * 1e9), bytes_accessed=int(us * 3e6), transcendentals=0
        ),
    )(*ins, *deps)


def mm(a, b):
    return jnp.dot(a, b, preferred_element_type=F32)


def mm_t(a, b):
    return lax.dot_general(a, b, (((1,), (1,)), ((), ())), preferred_element_type=F32)


def t_mm(a, b):
    return lax.dot_general(a, b, (((0,), (0,)), ((), ())), preferred_element_type=F32)


def at_rows(index, size):
    return pl.ds(pl.multiple_of(index * size, size), size)


def rope(v, cosine, sine):
    width = v.shape[1]
    lane = lax.broadcasted_iota(jnp.int32, v.shape, 1) % HEAD_DIM
    partner = jnp.where(
        lane < HALF, pltpu.roll(v, width - HALF, 1), pltpu.roll(v, HALF, 1)
    )
    return v * cosine + partner * sine


def rope_keys(kv, cosine, sine):
    lane = lax.broadcasted_iota(jnp.int32, kv.shape, 1)
    return jnp.where(lane < KW, rope(kv, cosine, sine), kv)


def cut_kernel(places, wq, wk, wv, wg, wu, wd, x_ref, og_ref, qkv_ref, ffn_ref, both_ref):
    z = places[Z]
    for t in range(3):
        ffn_ref[384 + 64 * t : 448 + 64 * t, :] = wd[at_rows(z, 64), t * 512 : (t + 1) * 512]
    both_ref[0] = x_ref[...]
    both_ref[1] = og_ref[...]
    qkv_ref[:, :QW] = wq[:, pl.ds(pl.multiple_of(z * QW, 128), QW)]
    for at in range(NZ):

        @pl.when(z == at)
        def _():
            cols = slice(at * KW, (at + 1) * KW)
            qkv_ref[:, QW:] = jnp.concatenate([wk[:, cols], wv[:, cols]], axis=1)
            for k, w in enumerate((wg, wu)):
                for half in range(2):
                    starts = [(8 * half + i) * 256 + at * 64 for i in range(8)]
                    rows = slice((2 * k + half) * 96, (2 * k + half + 1) * 96)
                    ffn_ref[rows, :] = jnp.concatenate([w[:, b : b + 64] for b in starts], axis=1)


def cut(places, *arrays):
    return call(
        cut_kernel,
        [((96, 768), BF), ((576, 512), BF), ((2, ROWS, D), BF)],
        [places, *arrays],
        3,
    )


def copy_kernel(places, *refs):
    n = len(refs) // 2
    for i in range(n):
        refs[n + i][...] = refs[i][...]


def copied(places, arrays, deps):
    return call(copy_kernel, [(v.shape, v.dtype) for v in arrays], [places, *arrays], 1, deps=deps)


def stack_kernel(places, *refs):
    for i, ref in enumerate(refs[:-1]):
        refs[-1][i] = ref[...]


def stacked(places, arrays, deps):
    shape = (len(arrays), *arrays[0].shape)
    return call(stack_kernel, [(shape, BF)], [places, *arrays], 1, deps=deps)[0]


def norm_kernel(places, gain, *refs):
    xs, (normed_ref, x_ref, og_ref, mine_ref, sent_ref) = refs[:4], refs[4:9]
    turned_ref = refs[9]
    for i in range(NZ):
        rows = at_rows((places[Z] + i) % NZ, ROWS)
        x_ref[rows, :] = xs[i][0]
        og_ref[rows, :] = xs[i][1]
    for i in range(NZ):
        rows = pl.ds(i * ROWS, ROWS)
        v = x_ref[rows, :].astype(F32)
        r = lax.rsqrt(jnp.mean(v * v, axis=1, keepdims=True) + EPSILON)
        normed_ref[rows, :] = (v * r * gain[...]).astype(BF)
    turned_ref[...] = normed_ref[...].T
    split_cores(places, turned_ref, mine_ref, sent_ref, 96)


def split_cores(places, turned_ref, mine_ref, sent_ref, n):
    for k in range(8):
        rows = slice(k * n, (k + 1) * n)
        mine_ref[rows, :] = turned_ref[at_rows(2 * k + places[CORE], n), :]
        sent_ref[rows, :] = turned_ref[at_rows(2 * k + 1 - places[CORE], n), :]


def norm(places, gain, boths):
    return call(
        norm_kernel,
        [((TOKENS, D), BF)] * 3 + [((D // 2, TOKENS), BF)] * 2,
        [places, gain, *boths],
        COST["norm"],
        scratch=[pltpu.VMEM((D, TOKENS), BF)],
    )


def qkv_kernel(places, normed_ref, own, own_mirror, other, other_mirror, cosine, sine, *refs):
    q_ref, kv_ref, w_ref = refs
    for i in range(NX):
        for k, (a, b) in enumerate(((own, other), (own_mirror, other_mirror))):
            base = (places[X] + i) % NX * 4 + (places[YH] + k) % 2 * 2
            w_ref[at_rows(base + places[CORE], 96), :] = a[i]
            w_ref[at_rows(base + 1 - places[CORE], 96), :] = b[i]
    for i in range(NZ):
        rows = pl.ds(i * ROWS, ROWS)
        lin = mm(normed_ref[rows, :], w_ref[...])
        q_ref[rows, :] = rope(lin[:, :QW], cosine[rows, :], sine[rows, :]).astype(BF)
        kv_ref[rows, :] = rope_keys(lin[:, QW:], cosine[rows, :], sine[rows, :]).astype(BF)


def qkv(places, normed, weights, cosine, sine):
    return call(
        qkv_kernel,
        [((TOKENS, QW), BF), ((TOKENS, 2 * KW), BF), ((D, QW + 2 * KW), BF)],
        [places, normed, *weights, cosine, sine],
        COST["qkv"],
    )


def head(ref, rows, index):
    return ref[rows, index * HEAD_DIM : (index + 1) * HEAD_DIM]


def two_heads(ref, j, g):
    rows = slice(j * ROWS, (j + 1) * ROWS)
    return jnp.concatenate([head(ref, rows, 2 * g), head(ref, rows, 2 * g + 1)], axis=0)


def attend_kernel(places, q_ref, own_ref, other_ref, mixed_ref, p_ref):
    late = places[YL]
    factor = HEAD_DIM ** (-0.5)
    for g in range(2):
        for j in range(NZ):
            n = (j + 1) * ROWS
            q = two_heads(q_ref, j, g)
            s_own = mm_t(q, head(own_ref, slice(0, n), g)) * factor
            s_oth = mm_t(q, head(other_ref, slice(0, n), g)) * factor
            shape = (2 * ROWS, n)
            row = lax.broadcasted_iota(jnp.int32, shape, 0) % ROWS + j * ROWS
            col = lax.broadcasted_iota(jnp.int32, shape, 1)
            s_own = jnp.where(col <= row, s_own, MASKED)
            s_oth = jnp.where(col < (j + late) * ROWS, s_oth, MASKED)
            highest = jnp.maximum(
                jnp.max(s_own, axis=1, keepdims=True), jnp.max(s_oth, axis=1, keepdims=True)
            )
            p_own, p_oth = jnp.exp(s_own - highest), jnp.exp(s_oth - highest)
            total = jnp.sum(p_own, axis=1, keepdims=True) + jnp.sum(p_oth, axis=1, keepdims=True)
            scale = 1.0 / total
            p_own, p_oth = (p_own * scale).astype(BF), (p_oth * scale).astype(BF)
            p_ref[g, j, :, :n] = p_own
            p_ref[g, j, :, n : 2 * n] = p_oth
            out = mm(p_own, head(own_ref, slice(0, n), 2 + g)) + mm(
                p_oth, head(other_ref, slice(0, n), 2 + g)
            )
            out = out.astype(BF)
            for k in range(2):
                h = 2 * g + k
                mixed_ref[j * ROWS : (j + 1) * ROWS, h * HEAD_DIM : (h + 1) * HEAD_DIM] = out[
                    k * ROWS : (k + 1) * ROWS
                ]


def attend(places, q, kv, kv_other, deps):
    return call(
        attend_kernel,
        [((TOKENS, QW), BF), ((2, NZ, 2 * ROWS, 2 * TOKENS), BF)],
        [places, q, kv, kv_other],
        COST["attend"],
        deps=deps,
    )


def attend_back_kernel(places, *refs):
    grads = refs[:4]
    q_ref, own_ref, other_ref, p_ref = refs[4:8]
    dq_ref, down_ref, doth_ref = refs[8:11]
    do_ref, acc_own, acc_oth = refs[11:]
    factor = HEAD_DIM ** (-0.5)
    for i in range(NZ):
        do_ref[at_rows((places[Z] + i) % NZ, ROWS), :] = grads[i][...]
    for g in range(2):
        acc_own[...] = jnp.zeros_like(acc_own)
        acc_oth[...] = jnp.zeros_like(acc_oth)
        for j in range(NZ):
            n = (j + 1) * ROWS
            seen = slice(0, n)
            q = two_heads(q_ref, j, g)
            do = two_heads(do_ref, j, g)
            p_own, p_oth = p_ref[g, j, :, :n], p_ref[g, j, :, n : 2 * n]
            dp_own = mm_t(do, head(own_ref, seen, 2 + g))
            dp_oth = mm_t(do, head(other_ref, seen, 2 + g))
            f_own, f_oth = p_own.astype(F32), p_oth.astype(F32)
            dot = jnp.sum(f_own * dp_own, axis=1, keepdims=True) + jnp.sum(
                f_oth * dp_oth, axis=1, keepdims=True
            )
            ds_own = (f_own * (dp_own - dot)).astype(BF)
            ds_oth = (f_oth * (dp_oth - dot)).astype(BF)
            dq = mm(ds_own, head(own_ref, seen, g)) + mm(ds_oth, head(other_ref, seen, g))
            dq = (dq * factor).astype(BF)
            for k in range(2):
                h = 2 * g + k
                dq_ref[j * ROWS : (j + 1) * ROWS, h * HEAD_DIM : (h + 1) * HEAD_DIM] = dq[
                    k * ROWS : (k + 1) * ROWS
                ]
            acc_own[0, seen, :] += t_mm(ds_own, q)
            acc_own[1, seen, :] += t_mm(p_own, do)
            acc_oth[0, seen, :] += t_mm(ds_oth, q)
            acc_oth[1, seen, :] += t_mm(p_oth, do)
        for kind, scale in ((0, factor), (1, 1.0)):
            at = kind * KW + g * HEAD_DIM
            down_ref[:, at : at + HEAD_DIM] = acc_own[kind] * scale
            doth_ref[:, at : at + HEAD_DIM] = (acc_oth[kind] * scale).astype(BF)


def attend_back(places, grads, q, kv, kv_other, shares, deps):
    acc = pltpu.VMEM((2, TOKENS, HEAD_DIM), F32)
    return call(
        attend_back_kernel,
        [((TOKENS, QW), BF), ((TOKENS, 2 * KW), F32), ((TOKENS, 2 * KW), BF)],
        [places, *grads, q, kv, kv_other, shares],
        COST["attend_back"],
        scratch=[pltpu.VMEM((TOKENS, QW), BF), acc, acc],
        deps=deps,
    )


def send_chunks(refs, acc_ref, places):
    for i in range(NZ):
        rows = at_rows((places[Z] + i) % NZ, ROWS)
        refs[i][...] = acc_ref[rows, :].astype(refs[i].dtype)


CHUNKS = [((ROWS, D), F32)] + [((ROWS, D), BF)] * 3


def put_out(out_ref, places, core, ref):
    for k in range(8):
        rows = pl.ds(pl.multiple_of((k % 2 * 2 + core) * 96 + k // 2 * 24, 8), 24)
        tile = out_ref[rows, :]
        ref[k, 96:, :] = jnp.concatenate([tile[:, :768], tile[:, 768:]], axis=0).astype(BF)


def turn_kernel(
    places, dq_ref, own_ref, got_ref, cosine, sine, turned_ref, mixed_ref, branch_ref, *refs
):
    lin_ref, out_ref, sent_ref = refs
    for i in range(NZ):
        rows = slice(i * ROWS, (i + 1) * ROWS)
        dkv = (own_ref[rows, :] + got_ref[rows, :].astype(F32)).astype(BF)
        c, s = cosine[rows, :], -sine[rows, :]
        lin_ref[rows, :QW] = rope(dq_ref[rows, :].astype(F32), c, s).astype(BF)
        lin_ref[rows, QW:] = rope_keys(dkv.astype(F32), c, s).astype(BF)
    for k in range(8):
        sent_ref[k, :96, :] = mm(turned_ref[k * 96 : (k + 1) * 96, :], lin_ref[...]).astype(BF)
    out_ref[...] = t_mm(mixed_ref[...], branch_ref[...])
    put_out(out_ref, places, 1 - places[CORE], sent_ref)


def turn(places, dq, dkv_own, dkv_got, cosine, sine, turned, mixed, branch):
    return call(
        turn_kernel,
        [((TOKENS, 768), BF), ((QW, D), F32), ((8, 144, 768), BF)],
        [places, dq, dkv_own, dkv_got, cosine, sine, turned, mixed, branch],
        COST["turn"],
    )


def first_kernel(places, lin_ref, w_ref, *refs):
    refs[4][...] = mm_t(lin_ref[...], w_ref[...])
    send_chunks(refs[:4], refs[4], places)


def first(places, lin, w):
    return call(
        first_kernel,
        CHUNKS,
        [places, lin, w],
        COST["first"],
        scratch=[pltpu.VMEM((TOKENS, D), F32)],
    )


def qkv_grad_kernel(places, lin_ref, turned_ref, out_ref, got_ref, *refs):
    outs, sum_ref = refs[:4], refs[4]
    for k in range(8):
        sum_ref[k, :96, :] = mm(turned_ref[k * 96 : (k + 1) * 96, :], lin_ref[...]).astype(BF)
    put_out(out_ref, places, places[CORE], sum_ref)
    for i in range(NX):
        for k in range(2):
            at = (places[X] + i) % NX * 2 + (places[YH] + k) % 2
            outs[i][k] = (sum_ref[at].astype(F32) + got_ref[at].astype(F32)).astype(BF)


def qkv_grad(places, lin, turned, out, got, deps):
    return call(
        qkv_grad_kernel,
        [((2, 144, 768), BF)] * 4,
        [places, lin, turned, out, got],
        COST["qkv_grad"],
        scratch=[pltpu.VMEM((8, 144, 768), BF)],
        deps=deps,
    )


def lay_rows_kernel(places, mine, other, out_ref):
    for i in range(NX):
        for k in range(2):
            base = (places[X] + i) % NX * 4 + (places[YH] + k) % 2 * 2
            out_ref[at_rows(base + places[CORE], 96), :] = mine[i, k]
            out_ref[at_rows(base + 1 - places[CORE], 96), :] = other[i, k]


def lay_rows(places, mine, other):
    return call(lay_rows_kernel, [((D, D), BF)], [places, mine, other], COST["lay_rows"])[0]


def middle_kernel(
    places, x_ref, m0, m1, m2, m3, w_ref, gain, normed_ref, own_ref, acc_ref, mixed_ref
):
    for i, ref in enumerate((m0, m1, m2, m3)):
        at = pl.multiple_of((places[Z] + i) % NZ * QW, QW)
        mixed_ref[:, pl.ds(at, QW)] = ref[...]
    for t in range(3):
        cols = slice(t * 512, (t + 1) * 512)
        acc_ref[:, cols] = x_ref[:, cols].astype(F32) + mm(mixed_ref[...], w_ref[:, cols])
    for i in range(NZ):
        rows = slice(i * ROWS, (i + 1) * ROWS)
        v = acc_ref[rows, :]
        r = lax.rsqrt(jnp.mean(v * v, axis=1, keepdims=True) + EPSILON)
        normed_ref[rows, :] = (v * r * gain[...]).astype(BF)
    own_ref[...] = acc_ref[at_rows(places[Z], ROWS), :]


def middle_of(places, x_all, pieces, w_out, gain):
    return call(
        middle_kernel,
        [((TOKENS, D), BF), ((ROWS, D), F32)],
        [places, x_all, *pieces, w_out, gain],
        COST["middle"],
        scratch=[pltpu.VMEM((TOKENS, D), F32), pltpu.VMEM((TOKENS, D), BF)],
    )


def ffn_kernel(places, n_ref, og_ref, packed_ref, *refs):
    hidden_ref, gg_ref, ug_ref = refs[:3]
    in_chunks, down_ref = refs[3:7], refs[7]
    in_acc, down_acc, wd = refs[8:]
    for j in range(2):
        cols = slice(j * 512, (j + 1) * 512)
        wg = packed_ref[:, j * 96 : (j + 1) * 96, :].reshape(D, 512)
        wu = packed_ref[:, (2 + j) * 96 : (3 + j) * 96, :].reshape(D, 512)
        for t in range(3):
            rows = slice(384 + 64 * t, 448 + 64 * t)
            tile = packed_ref[8 * j : 8 * j + 8, rows, :]
            wd[:, t * 512 : (t + 1) * 512] = tile.reshape(512, 512)
        gate = mm(n_ref[...], wg)
        up = mm(n_ref[...], wu)
        hg = mm_t(og_ref[...], wd[...]).astype(BF).astype(F32)
        sig = 1.0 / (1.0 + jnp.exp(-gate))
        silu = gate * sig
        hidden = (silu * up).astype(BF)
        gg = (hg * up * (sig * (1.0 + gate * (1.0 - sig)))).astype(BF)
        ug = (hg * silu).astype(BF)
        hidden_ref[:, cols] = hidden
        gg_ref[:, cols] = gg
        ug_ref[:, cols] = ug
        if j == 0:
            in_acc[...] = mm_t(gg, wg) + mm_t(ug, wu)
            down_acc[...] = mm(hidden, wd[...])
        else:
            in_acc[...] += mm_t(gg, wg) + mm_t(ug, wu)
            down_ref[...] = (down_acc[...] + mm(hidden, wd[...])).astype(BF)
    send_chunks(in_chunks, in_acc, places)


def ffn(places, normed, og, packed):
    return call(
        ffn_kernel,
        [((TOKENS, FFZ), BF)] * 3 + CHUNKS + [((TOKENS, D), BF)],
        [places, normed, og, packed],
        COST["ffn"],
        scratch=[pltpu.VMEM((TOKENS, D), F32)] * 2 + [pltpu.VMEM((512, D), BF)],
    )


def ffn_terms(places, n_ref, h_ref, gg_ref, ug_ref, og_ref, put):
    for w, ref in enumerate((gg_ref, ug_ref)):
        for half in range(2):
            tile = mm(n_ref[...], ref[:, half * 512 : (half + 1) * 512])
            put(slice((2 * w + half) * 96, (2 * w + half + 1) * 96), tile.reshape(8, 96, 512))
    for t in range(3):
        tile = mm(h_ref[...], og_ref[:, t * 512 : (t + 1) * 512])
        put(slice(384 + 64 * t, 448 + 64 * t), tile.reshape(8, 64, 512))


def ffn_sent_kernel(places, n_ref, hidden_ref, gg_ref, ug_ref, og_ref, *refs):
    sent_ref, n_mine, h_mine, n_turned, h_turned, n_sent, h_sent = refs
    n_turned[...] = n_ref[...].T
    h_turned[...] = hidden_ref[...].T
    split_cores(places, n_turned, n_mine, n_sent, 96)
    split_cores(places, h_turned, h_mine, h_sent, 64)

    def put(rows, tile):
        sent_ref[:, rows, :] = tile.astype(BF)

    ffn_terms(places, n_sent, h_sent, gg_ref, ug_ref, og_ref, put)


def ffn_sent_of(places, normed, hidden, gg, ug, og):
    return call(
        ffn_sent_kernel,
        [((8, 576, 512), BF), ((D // 2, TOKENS), BF), ((FFZ // 2, TOKENS), BF)],
        [places, normed, hidden, gg, ug, og],
        COST["ffn_sent"],
        scratch=[
            pltpu.VMEM((D, TOKENS), BF),
            pltpu.VMEM((FFZ, TOKENS), BF),
            pltpu.VMEM((D // 2, TOKENS), BF),
            pltpu.VMEM((FFZ // 2, TOKENS), BF),
        ],
    )


def ffn_grad_kernel(places, n_ref, h_ref, gg_ref, ug_ref, og_ref, got_ref, *refs):
    outs, sum_ref = refs[:4], refs[4]

    def put(rows, tile):
        sum_ref[:, rows, :] = (tile + got_ref[:, rows, :].astype(F32)).astype(BF)

    ffn_terms(places, n_ref, h_ref, gg_ref, ug_ref, og_ref, put)
    for i in range(NX):
        for k in range(2):
            at = (places[X] + i) % NX * 2 + (places[YH] + k) % 2
            outs[i][k] = sum_ref[at]


def ffn_grad(places, n_mine, h_mine, gg, ug, og, got, deps):
    return call(
        ffn_grad_kernel,
        [((2, 576, 512), BF)] * 4,
        [places, n_mine, h_mine, gg, ug, og, got],
        COST["ffn_grad"],
        scratch=[pltpu.VMEM((8, 576, 512), BF)],
        deps=deps,
    )


def rms_back(grad, v, gain):
    r = lax.rsqrt(jnp.mean(v * v, axis=1, keepdims=True) + EPSILON)
    pulled = grad * gain
    return r * pulled - v * (r * r * r * jnp.mean(pulled * v, axis=1, keepdims=True))


def middle_back_kernel(places, own, g1, g2, g3, middle, og, gain, w_ref, mid_ref, branch_ref, *outs):
    grad = own[...] + g1[...].astype(F32) + g2[...].astype(F32) + g3[...].astype(F32)
    mid = og[...].astype(F32) + rms_back(grad, middle[...], gain[...])
    mid_ref[...] = mid
    branch = mid.astype(BF)
    branch_ref[...] = branch
    for i in range(NZ):
        outs[i][...] = mm_t(branch, w_ref[at_rows((places[Z] + i) % NZ, QW), :]).astype(BF)


def middle_back(places, chunks, middle, og, gain, w_out, deps):
    return call(
        middle_back_kernel,
        [((ROWS, D), F32), ((ROWS, D), BF)] + [((ROWS, QW), BF)] * 4,
        [places, *chunks, middle, og, gain, w_out],
        COST["middle_back"],
        deps=deps,
    )


def input_back_kernel(places, own, g1, g2, g3, x, mid, gain, out_ref):
    grad = own[...] + g1[...].astype(F32) + g2[...].astype(F32) + g3[...].astype(F32)
    out_ref[...] = mid[...] + rms_back(grad, x[...].astype(F32), gain[...])


def input_back(places, chunks, x, mid, gain, deps):
    return call(
        input_back_kernel, [((ROWS, D), F32)], [places, *chunks, x, mid, gain], 2, deps=deps
    )[0]


def scatter(chunks):
    far = [shift_z(chunks[1], 1), shift_z(chunks[3], -1), shift_z(chunks[2], 2)]
    return [chunks[0], *far]


def x_sum_kernel(places, a, b, c, d, mine, sent):
    mine[...] = a[0].astype(F32) + b[0].astype(F32) + c[0].astype(F32) + d[0].astype(F32)
    total = a[1].astype(F32) + b[1].astype(F32) + c[1].astype(F32) + d[1].astype(F32)
    sent[...] = total.astype(BF)


def x_sum(places, terms, us, deps):
    shape = terms[0].shape[1:]
    return call(x_sum_kernel, [(shape, F32), (shape, BF)], [places, *terms], us, deps=deps)


def add_kernel(places, a, b, out):
    out[...] = (a[...].astype(F32) + b[...].astype(F32)).astype(BF)


def added(places, a, b, deps):
    return call(add_kernel, [(a.shape, BF)], [places, a, b], 1, deps=deps)[0]


def over_x(chunks):
    far = [shift_x(chunks[1], 1), shift_x(chunks[3], -1), shift_x(chunks[2], 2)]
    return [chunks[0], *far]


def ffn_out_kernel(places, all_ref, wg, wu, gate_ref, up_ref, down_ref, gain_ref):
    gain = jnp.zeros((96, 1), F32)
    for k, (w, out) in enumerate(((wg, gate_ref), (wu, up_ref))):
        for b in range(16):
            rows = slice((2 * k + b // 8) * 96, (2 * k + b // 8 + 1) * 96)
            cols = slice(b % 8 * 64, b % 8 * 64 + 64)
            tile = jnp.concatenate([all_ref[q, rows, cols].astype(F32) for q in range(NZ)], axis=1)
            out[:, b * 256 : (b + 1) * 256] = tile
            gain += jnp.sum(
                tile * w[:, b * 256 : (b + 1) * 256].astype(F32), axis=1, keepdims=True
            )
    for q in range(NZ):
        for t in range(3):
            r = 384 + 64 * t
            down_ref[q * 64 : (q + 1) * 64, t * 512 : (t + 1) * 512] = all_ref[
                q, r : r + 64, :
            ].astype(F32)
    gain_ref[...] = gain


def ffn_out(places, gathered, wg, wu, deps):
    return call(
        ffn_out_kernel,
        [((96, FF), F32), ((96, FF), F32), ((256, D), F32), ((96, 1), F32)],
        [places, gathered, wg, wu],
        4,
        deps=deps,
    )


def out_slices_kernel(places, p0, p1, p2, p3, *refs):
    all_ref = refs[4]
    for i, p in enumerate((p0, p1, p2, p3)):
        all_ref[(places[Z] + i) % NZ] = p[96:, :]
    for i in range(NX):
        refs[i][...] = all_ref[(places[X] + i) % NX]


def out_slices(places, pieces):
    return call(
        out_slices_kernel,
        [((48, 768), BF)] * 4,
        [places, *pieces],
        1,
        scratch=[pltpu.VMEM((NZ, 48, 768), BF)],
    )


def qkv_out_kernel(places, p0, p1, p2, p3, wq, wk, wv, q_ref, k_ref, v_ref, gain_ref, all_ref):
    for i, p in enumerate((p0, p1, p2, p3)):
        all_ref[(places[Z] + i) % NZ] = p[:96, :]
    for q in range(NZ):
        q_ref[:, q * QW : (q + 1) * QW] = all_ref[q, :, :QW].astype(F32)
    gain = jnp.sum(q_ref[...] * wq[...].astype(F32), axis=1, keepdims=True)
    for out, w, at in ((k_ref, wk, QW), (v_ref, wv, QW + KW)):
        tile = jnp.concatenate(
            [all_ref[q, :, at : at + KW].astype(F32) for q in range(NZ)], axis=1
        )
        out[...] = tile
        gain += jnp.sum(tile * w[...].astype(F32), axis=1, keepdims=True)
    gain_ref[...] = gain


def qkv_out(places, pieces, wq, wk, wv, deps):
    return call(
        qkv_out_kernel,
        [((96, 1536), F32), ((96, 768), F32), ((96, 768), F32), ((96, 1), F32)],
        [places, *pieces, wq, wk, wv],
        2,
        scratch=[pltpu.VMEM((NZ, 96, 768), BF)],
        deps=deps,
    )


def out_out_kernel(places, p0, p1, p2, p3, out_ref):
    for i, p in enumerate((p0, p1, p2, p3)):
        tile = p[...].astype(F32)
        rows = pl.ds(pl.multiple_of((places[X] + i) % NX * 24, 8), 24)
        out_ref[rows, :] = jnp.concatenate([tile[:24], tile[24:]], axis=1)


def out_out(places, pieces):
    return call(out_out_kernel, [((96, D), F32)], [places, *pieces], 1)[0]


def block_out_kernel(places, middle, down, out_ref):
    out_ref[...] = (middle[...] + down[...].astype(F32)).astype(BF)


def block_out_of(places, middle, down, deps):
    return call(block_out_kernel, [((ROWS, D), BF)], [places, middle, down], 1, deps=deps)[0]


def body(
    inputs, norm_attn, w_query, w_key, w_value, w_out, norm_ffn, w_gate, w_up, w_down, cotangent
):
    f, s = lax.axis_index("fsdp"), lax.axis_index("sp")
    x, yh, c, z, yl = f // 4, f // 2 % 2, f % 2, s // 2, s % 2
    places = jnp.stack([x, yh, c, z, yl]).astype(jnp.int32)
    x_own, og_own = inputs[0], cotangent[0]
    gain_attn, gain_ffn = norm_attn[None], norm_ffn[None]

    index = jnp.arange(TOKENS, dtype=jnp.int32)
    positions = (index // ROWS * 2 + yl) * ROWS + index % ROWS
    lane = np.arange(QW) % HEAD_DIM
    frequency = ROPE_BASE ** (-(jnp.arange(HALF, dtype=F32) * 2.0 / HEAD_DIM))
    frequency = jnp.concatenate([frequency] * (QW // HALF))
    angles = positions.astype(F32)[:, None] * frequency[None, :]
    sign = np.where(lane < HALF, -1.0, 1.0).astype(np.float32)
    cosine, sine = jnp.cos(angles), jnp.sin(angles) * sign[None, :]

    qkv_shard, ffn_shard, both_own = cut(
        places, w_query, w_key, w_value, w_gate, w_up, w_down, x_own, og_own
    )
    packed = lax.all_gather(ffn_shard, "fsdp", axis=0, tiled=False)
    boths = pieces_z(both_own)
    qkv_lane = stacked(places, pieces_x(qkv_shard), [cosine, sine, gain_attn])
    qkv_mirror = mirror_y(qkv_lane)
    qkv_other, mirror_other = swap_core(qkv_lane), swap_core(qkv_mirror)
    out_pair = stacked(places, [w_out, mirror_y(copied(places, [w_out], [qkv_shard])[0])], [])
    out_mine = pieces_x(out_pair)

    normed, x_all, og_all, turned_mine, turned_sent = norm(places, gain_attn, boths)
    q, kv, held_qkv = qkv(
        places, normed, [qkv_lane, qkv_mirror, qkv_other, mirror_other], cosine, sine
    )
    kv_other = swap_low(kv)
    out_lane = stacked(places, out_mine, [kv])
    held_out = lay_rows(places, out_lane, swap_core(out_lane))
    mixed, shares = attend(places, q, kv, kv_other, [held_out])
    mixed_pieces = pieces_z(mixed)
    normed_ffn, middle_own = middle_of(places, x_all, mixed_pieces, held_out, gain_ffn)
    outs = ffn(places, normed_ffn, og_all, packed)
    hidden, gate_grad, up_grad = outs[:3]
    in_chunks, down_part = outs[3:7], outs[7]

    in_got = scatter(in_chunks)
    ffn_sent, n_mine, h_mine = ffn_sent_of(
        places, normed_ffn, hidden, gate_grad, up_grad, og_all
    )
    back = middle_back(places, in_got, middle_own, og_own, gain_ffn, held_out, [n_mine])
    middle_grad, branch = back[:2]
    head_grads = [back[2], shift_z(back[5], -1), shift_z(back[4], 2), shift_z(back[3], 1)]
    branch_all = gather_z(branch)
    down_own = lax.psum_scatter(
        copied(places, [down_part], [branch])[0],
        "sp",
        scatter_dimension=0,
        tiled=True,
        axis_index_groups=Z_GROUPS,
    )
    ffn_chunks = ffn_grad(
        places, n_mine, h_mine, gate_grad, up_grad, og_all, swap_core(ffn_sent), [branch]
    )
    ffn_terms = over_x(ffn_chunks)

    dq, dkv_own, dkv_sent = attend_back(
        places, head_grads, q, kv, kv_other, shares, [ffn_chunks[0]]
    )
    dkv_got = swap_low(dkv_sent)
    lin, out_part, qkv_sent = turn(
        places, dq, dkv_own, dkv_got, cosine, sine, turned_sent, mixed, branch_all
    )
    qkv_got = swap_core(qkv_sent)
    first_chunks = first(places, lin, held_qkv)
    first_got = scatter(first_chunks)
    ffn_half, ffn_sent = x_sum(places, ffn_terms, COST["x_sum"], [first_chunks[0]])
    ffn_got = mirror_y(ffn_sent)
    qkv_chunks = qkv_grad(places, lin, turned_mine, out_part, qkv_got, [ffn_sent])
    qkv_terms = over_x(qkv_chunks)

    input_grad = input_back(
        places, first_got, x_own, middle_grad, gain_attn, [qkv_chunks[0]]
    )
    ffn_half = added(places, ffn_half, ffn_got, [qkv_chunks[0], input_grad])
    ffn_low = swap_low(ffn_half)

    qkv_half, qkv_sent = x_sum(places, qkv_terms, 2, [ffn_half])
    qkv_got = mirror_y(qkv_sent)
    ffn_total = added(places, ffn_half, ffn_low, [qkv_sent])
    ffn_all = gather_z(ffn_total).reshape(NZ, 576, 512)
    qkv_half = added(places, qkv_half, qkv_got, [ffn_total])
    qkv_low = swap_low(qkv_half)
    qkv_total = added(places, qkv_half, qkv_low, [])
    qkv_pieces = pieces_z(qkv_total)
    block_out = block_out_of(places, middle_own, down_own, [qkv_total])

    out_terms = over_x(out_slices(places, qkv_pieces))
    grad_query, grad_key, grad_value, qkv_gain = qkv_out(
        places, qkv_pieces, w_query, w_key, w_value, [out_terms[0]]
    )
    grad_gate, grad_up, grad_down, ffn_gain = ffn_out(
        places, ffn_all, w_gate, w_up, [qkv_gain]
    )
    grad_out = out_out(places, [out_terms[0], out_terms[2], out_terms[3], out_terms[1]])
    grad_norm_attn = qkv_gain[:, 0] / lax.dynamic_slice_in_dim(norm_attn, f * 96, 96, 0)
    grad_norm_ffn = ffn_gain[:, 0] / lax.dynamic_slice_in_dim(norm_ffn, f * 96, 96, 0)
    return (
        block_out[None],
        input_grad[None],
        grad_norm_attn,
        grad_query,
        grad_key,
        grad_value,
        grad_out,
        grad_norm_ffn,
        grad_gate,
        grad_up,
        grad_down,
    )


def solution(mesh):
    rows = P("fsdp", None)
    tokens = P("fsdp", "sp", None)
    return jax.shard_map(
        body,
        mesh=mesh,
        in_specs=(tokens, P(), rows, rows, rows, rows, P(), rows, rows, rows, tokens),
        out_specs=(tokens, tokens, P("fsdp"), rows, rows, rows, rows, P("fsdp"), rows, rows, rows),
        check_vma=False,
    )
```

```python
import functools

import jax
import jax.numpy as jnp
import numpy as np
from jax import lax
from jax.experimental import pallas as pl
from jax.experimental.pallas import tpu as pltpu
from jax.sharding import PartitionSpec as P

D = 1536
HEADS = 16
KV_HEADS = 8
HEAD_DIM = 96
FF = 4096

EPSILON = 1e-05
ROPE_BASE = 100000.0
MASKED = -1e30

NX, NZ = 4, 4
ROWS = 128
TOKENS = ROWS * NZ
QW, KW = 384, 192
HALF = HEAD_DIM // 2
FFZ = FF // NZ
BF = jnp.bfloat16
F32 = jnp.float32
VMEM = pl.BlockSpec(memory_space=pltpu.VMEM)
SMEM = pl.BlockSpec(memory_space=pltpu.SMEM)
ANY = pl.BlockSpec(memory_space=pl.ANY)
LIMIT = pltpu.CompilerParams(vmem_limit_bytes=56 * 1024 * 1024)
X, YH, CORE, Z, YL = range(5)
COST = {
    "norm": 54,
    "qkv": 0.1,
    "attend": 0.1,
    "lay_rows": 0.1,
    "middle": 0.1,
    "ffn": 17,
    "ffn_sent": 0.1,
    "middle_back": 60,
    "ffn_grad": 60,
    "attend_back": 60,
    "turn": 0.1,
    "first": 0.1,
    "x_sum": 60,
    "qkv_grad": 0.1,
    "add": 20,
}


Z_GROUPS = [[z * 2 + l for z in range(NZ)] for l in range(2)]
XC_GROUPS = [[x * 4 + h * 2 + c for x in range(NX) for c in range(2)] for h in range(2)]


def scatter_z(v):
    return lax.psum_scatter(
        v, "sp", scatter_dimension=0, tiled=True, axis_index_groups=Z_GROUPS
    )


def gather_z(v):
    return lax.all_gather(v, "sp", axis=0, tiled=True, axis_index_groups=Z_GROUPS)


def shift_z(v, step):
    pairs = [(z * 2 + l, (z + step) % NZ * 2 + l) for z in range(NZ) for l in range(2)]
    return lax.ppermute(v, "sp", pairs)


def swap_low(v):
    return lax.ppermute(v, "sp", [(s, s ^ 1) for s in range(8)])


def shift_x(v, step):
    pairs = [(x * 4 + r, (x + step) % NX * 4 + r) for x in range(NX) for r in range(4)]
    return lax.ppermute(v, "fsdp", pairs)


def swap_core(v):
    return lax.ppermute(v, "fsdp", [(f, f ^ 1) for f in range(16)])


def mirror_y(v):
    pairs = [(f * 8 + s, (f ^ 2) * 8 + (s ^ 1)) for f in range(16) for s in range(8)]
    return lax.ppermute(v, ("fsdp", "sp"), pairs)


def pieces_z(v):
    far = [shift_z(v, -1), shift_z(v, 1), shift_z(v, 2)]
    return [v, far[0], far[2], far[1]]


def pieces_x(v):
    far = [shift_x(v, -1), shift_x(v, 1), shift_x(v, 2)]
    return [v, far[0], far[2], far[1]]


def part(v, index, size, dim=0):
    return lax.dynamic_slice_in_dim(v, index * size, size, dim)


def call(kernel, outs, ins, us, scratch=(), deps=()):
    def run(*refs):
        kernel(*refs[: len(ins)], *refs[len(ins) + len(deps) :])

    return pl.pallas_call(
        run,
        name=kernel.__name__.replace("_kernel", ""),
        out_shape=[jax.ShapeDtypeStruct(s, t) for s, t in outs],
        in_specs=[SMEM] + [VMEM] * (len(ins) - 1) + [ANY] * len(deps),
        out_specs=[VMEM] * len(outs),
        scratch_shapes=scratch,
        compiler_params=LIMIT,
        cost_estimate=pl.CostEstimate(
            flops=int(us * 1e9), bytes_accessed=int(us * 3e6), transcendentals=0
        ),
    )(*ins, *deps)


def mm(a, b):
    return jnp.dot(a, b, preferred_element_type=F32)


def mm_t(a, b):
    return lax.dot_general(a, b, (((1,), (1,)), ((), ())), preferred_element_type=F32)


def t_mm(a, b):
    return lax.dot_general(a, b, (((0,), (0,)), ((), ())), preferred_element_type=F32)


def at_rows(index, size):
    return pl.ds(pl.multiple_of(index * size, size), size)


def rope(v, cosine, sine):
    width = v.shape[1]
    lane = lax.broadcasted_iota(jnp.int32, v.shape, 1) % HEAD_DIM
    partner = jnp.where(
        lane < HALF, pltpu.roll(v, width - HALF, 1), pltpu.roll(v, HALF, 1)
    )
    return v * cosine + partner * sine


def rope_keys(kv, cosine, sine):
    lane = lax.broadcasted_iota(jnp.int32, kv.shape, 1)
    return jnp.where(lane < KW, rope(kv, cosine, sine), kv)


def cut_kernel(places, wq, wk, wv, wg, wu, wd, x_ref, og_ref, qkv_ref, ffn_ref, both_ref):
    z = places[Z]
    for t in range(3):
        ffn_ref[384 + 64 * t : 448 + 64 * t, :] = wd[at_rows(z, 64), t * 512 : (t + 1) * 512]
    both_ref[0] = x_ref[...]
    both_ref[1] = og_ref[...]
    qkv_ref[:, :QW] = wq[:, pl.ds(pl.multiple_of(z * QW, 128), QW)]
    for at in range(NZ):

        @pl.when(z == at)
        def _():
            cols = slice(at * KW, (at + 1) * KW)
            qkv_ref[:, QW:] = jnp.concatenate([wk[:, cols], wv[:, cols]], axis=1)
            for k, w in enumerate((wg, wu)):
                for half in range(2):
                    starts = [(8 * half + i) * 256 + at * 64 for i in range(8)]
                    rows = slice((2 * k + half) * 96, (2 * k + half + 1) * 96)
                    ffn_ref[rows, :] = jnp.concatenate([w[:, b : b + 64] for b in starts], axis=1)


def cut(places, *arrays):
    return call(
        cut_kernel,
        [((96, 768), BF), ((576, 512), BF), ((2, ROWS, D), BF)],
        [places, *arrays],
        3,
    )


def copy_kernel(places, *refs):
    n = len(refs) // 2
    for i in range(n):
        refs[n + i][...] = refs[i][...]


def copied(places, arrays, deps):
    return call(copy_kernel, [(v.shape, v.dtype) for v in arrays], [places, *arrays], 0.1, deps=deps)


def stack_kernel(places, *refs):
    for i, ref in enumerate(refs[:-1]):
        refs[-1][i] = ref[...]


def pair_kernel(places, own, mirror, out_ref):
    out_ref[places[YH]] = own[...]
    out_ref[1 - places[YH]] = mirror[...]


def paired(places, own, mirror):
    return call(pair_kernel, [((2, *own.shape), BF)], [places, own, mirror], 1)[0]


def stacked(places, arrays, deps):
    shape = (len(arrays), *arrays[0].shape)
    return call(stack_kernel, [(shape, BF)], [places, *arrays], 0.1, deps=deps)[0]


def norm_kernel(places, gain, *refs):
    xs, (normed_ref, x_ref, og_ref, mine_ref, sent_ref) = refs[:4], refs[4:9]
    turned_ref = refs[9]
    for i in range(NZ):
        rows = at_rows((places[Z] + i) % NZ, ROWS)
        x_ref[rows, :] = xs[i][0]
        og_ref[rows, :] = xs[i][1]
    for i in range(NZ):
        rows = pl.ds(i * ROWS, ROWS)
        v = x_ref[rows, :].astype(F32)
        r = lax.rsqrt(jnp.mean(v * v, axis=1, keepdims=True) + EPSILON)
        normed_ref[rows, :] = (v * r * gain[...]).astype(BF)
    turned_ref[...] = normed_ref[...].T
    split_cores(places, turned_ref, mine_ref, sent_ref, 96)


def split_cores(places, turned_ref, mine_ref, sent_ref, n):
    for k in range(8):
        rows = slice(k * n, (k + 1) * n)
        mine_ref[rows, :] = turned_ref[at_rows(2 * k + places[CORE], n), :]
        sent_ref[rows, :] = turned_ref[at_rows(2 * k + 1 - places[CORE], n), :]


def norm(places, gain, boths):
    return call(
        norm_kernel,
        [((TOKENS, D), BF)] * 3 + [((D // 2, TOKENS), BF)] * 2,
        [places, gain, *boths],
        COST["norm"],
        scratch=[pltpu.VMEM((D, TOKENS), BF)],
    )


def qkv_kernel(places, normed_ref, own, own_mirror, other, other_mirror, cosine, sine, *refs):
    q_ref, kv_ref, w_ref = refs
    for i in range(NX):
        for k, (a, b) in enumerate(((own, other), (own_mirror, other_mirror))):
            base = (places[X] + i) % NX * 4 + (places[YH] + k) % 2 * 2
            w_ref[at_rows(base + places[CORE], 96), :] = a[i]
            w_ref[at_rows(base + 1 - places[CORE], 96), :] = b[i]
    for i in range(NZ):
        rows = pl.ds(i * ROWS, ROWS)
        lin = mm(normed_ref[rows, :], w_ref[...])
        q_ref[rows, :] = rope(lin[:, :QW], cosine[rows, :], sine[rows, :]).astype(BF)
        kv_ref[rows, :] = rope_keys(lin[:, QW:], cosine[rows, :], sine[rows, :]).astype(BF)


def qkv(places, normed, weights, cosine, sine):
    return call(
        qkv_kernel,
        [((TOKENS, QW), BF), ((TOKENS, 2 * KW), BF), ((D, QW + 2 * KW), BF)],
        [places, normed, *weights, cosine, sine],
        COST["qkv"],
    )


def head(ref, rows, index):
    return ref[rows, index * HEAD_DIM : (index + 1) * HEAD_DIM]


def two_heads(ref, j, g):
    rows = slice(j * ROWS, (j + 1) * ROWS)
    return jnp.concatenate([head(ref, rows, 2 * g), head(ref, rows, 2 * g + 1)], axis=0)


def attend_kernel(places, q_ref, own_ref, other_ref, mixed_ref, p_ref):
    late = places[YL]
    factor = HEAD_DIM ** (-0.5)
    for g in range(2):
        for j in range(NZ):
            n = (j + 1) * ROWS
            q = two_heads(q_ref, j, g)
            s_own = mm_t(q, head(own_ref, slice(0, n), g)) * factor
            s_oth = mm_t(q, head(other_ref, slice(0, n), g)) * factor
            shape = (2 * ROWS, n)
            row = lax.broadcasted_iota(jnp.int32, shape, 0) % ROWS + j * ROWS
            col = lax.broadcasted_iota(jnp.int32, shape, 1)
            s_own = jnp.where(col <= row, s_own, MASKED)
            s_oth = jnp.where(col < (j + late) * ROWS, s_oth, MASKED)
            highest = jnp.maximum(
                jnp.max(s_own, axis=1, keepdims=True), jnp.max(s_oth, axis=1, keepdims=True)
            )
            p_own, p_oth = jnp.exp(s_own - highest), jnp.exp(s_oth - highest)
            total = jnp.sum(p_own, axis=1, keepdims=True) + jnp.sum(p_oth, axis=1, keepdims=True)
            scale = 1.0 / total
            p_own, p_oth = (p_own * scale).astype(BF), (p_oth * scale).astype(BF)
            p_ref[g, j, :, :n] = p_own
            p_ref[g, j, :, n : 2 * n] = p_oth
            out = mm(p_own, head(own_ref, slice(0, n), 2 + g)) + mm(
                p_oth, head(other_ref, slice(0, n), 2 + g)
            )
            out = out.astype(BF)
            for k in range(2):
                h = 2 * g + k
                mixed_ref[j * ROWS : (j + 1) * ROWS, h * HEAD_DIM : (h + 1) * HEAD_DIM] = out[
                    k * ROWS : (k + 1) * ROWS
                ]


def attend(places, q, kv, kv_other, deps):
    return call(
        attend_kernel,
        [((TOKENS, QW), BF), ((2, NZ, 2 * ROWS, 2 * TOKENS), BF)],
        [places, q, kv, kv_other],
        COST["attend"],
        deps=deps,
    )


def attend_back_kernel(places, *refs):
    grads = refs[:4]
    q_ref, own_ref, other_ref, p_ref = refs[4:8]
    dq_ref, down_ref, doth_ref = refs[8:11]
    do_ref, acc_own, acc_oth = refs[11:]
    factor = HEAD_DIM ** (-0.5)
    for i in range(NZ):
        do_ref[at_rows((places[Z] + i) % NZ, ROWS), :] = grads[i][...]
    for g in range(2):
        acc_own[...] = jnp.zeros_like(acc_own)
        acc_oth[...] = jnp.zeros_like(acc_oth)
        for j in range(NZ):
            n = (j + 1) * ROWS
            seen = slice(0, n)
            q = two_heads(q_ref, j, g)
            do = two_heads(do_ref, j, g)
            p_own, p_oth = p_ref[g, j, :, :n], p_ref[g, j, :, n : 2 * n]
            dp_own = mm_t(do, head(own_ref, seen, 2 + g))
            dp_oth = mm_t(do, head(other_ref, seen, 2 + g))
            f_own, f_oth = p_own.astype(F32), p_oth.astype(F32)
            dot = jnp.sum(f_own * dp_own, axis=1, keepdims=True) + jnp.sum(
                f_oth * dp_oth, axis=1, keepdims=True
            )
            ds_own = (f_own * (dp_own - dot)).astype(BF)
            ds_oth = (f_oth * (dp_oth - dot)).astype(BF)
            dq = mm(ds_own, head(own_ref, seen, g)) + mm(ds_oth, head(other_ref, seen, g))
            dq = (dq * factor).astype(BF)
            for k in range(2):
                h = 2 * g + k
                dq_ref[j * ROWS : (j + 1) * ROWS, h * HEAD_DIM : (h + 1) * HEAD_DIM] = dq[
                    k * ROWS : (k + 1) * ROWS
                ]
            acc_own[0, seen, :] += t_mm(ds_own, q)
            acc_own[1, seen, :] += t_mm(p_own, do)
            acc_oth[0, seen, :] += t_mm(ds_oth, q)
            acc_oth[1, seen, :] += t_mm(p_oth, do)
        for kind, scale in ((0, factor), (1, 1.0)):
            at = kind * KW + g * HEAD_DIM
            down_ref[:, at : at + HEAD_DIM] = acc_own[kind] * scale
            doth_ref[:, at : at + HEAD_DIM] = (acc_oth[kind] * scale).astype(BF)


def attend_back(places, grads, q, kv, kv_other, shares, deps):
    acc = pltpu.VMEM((2, TOKENS, HEAD_DIM), F32)
    return call(
        attend_back_kernel,
        [((TOKENS, QW), BF), ((TOKENS, 2 * KW), F32), ((TOKENS, 2 * KW), BF)],
        [places, *grads, q, kv, kv_other, shares],
        COST["attend_back"],
        scratch=[pltpu.VMEM((TOKENS, QW), BF), acc, acc],
        deps=deps,
    )


def send_chunks(refs, acc_ref, places):
    for i in range(NZ):
        rows = at_rows((places[Z] + i) % NZ, ROWS)
        refs[i][...] = acc_ref[rows, :].astype(refs[i].dtype)


CHUNKS = [((ROWS, D), F32)] + [((ROWS, D), BF)] * 3


def put_out(out_ref, places, core, ref):
    for k in range(8):
        rows = pl.ds(pl.multiple_of((k % 2 * 2 + core) * 96 + k // 2 * 24, 8), 24)
        tile = out_ref[rows, :]
        ref[k, 96:, :] = jnp.concatenate([tile[:, :768], tile[:, 768:]], axis=0).astype(BF)


def turn_kernel(
    places, dq_ref, own_ref, got_ref, cosine, sine, turned_ref, mixed_ref, branch_ref, *refs
):
    lin_ref, out_ref, sent_ref = refs
    for i in range(NZ):
        rows = slice(i * ROWS, (i + 1) * ROWS)
        dkv = (own_ref[rows, :] + got_ref[rows, :].astype(F32)).astype(BF)
        c, s = cosine[rows, :], -sine[rows, :]
        lin_ref[rows, :QW] = rope(dq_ref[rows, :].astype(F32), c, s).astype(BF)
        lin_ref[rows, QW:] = rope_keys(dkv.astype(F32), c, s).astype(BF)
    for k in range(8):
        sent_ref[k, :96, :] = mm(turned_ref[k * 96 : (k + 1) * 96, :], lin_ref[...]).astype(BF)
    out_ref[...] = t_mm(mixed_ref[...], branch_ref[...])
    put_out(out_ref, places, 1 - places[CORE], sent_ref)


def turn(places, dq, dkv_own, dkv_got, cosine, sine, turned, mixed, branch):
    return call(
        turn_kernel,
        [((TOKENS, 768), BF), ((QW, D), F32), ((8, 144, 768), BF)],
        [places, dq, dkv_own, dkv_got, cosine, sine, turned, mixed, branch],
        COST["turn"],
    )


def first_kernel(places, lin_ref, w_ref, out_ref):
    out_ref[...] = mm_t(lin_ref[...], w_ref[...]).astype(BF)


def first(places, lin, w):
    return call(first_kernel, [((TOKENS, D), BF)], [places, lin, w], COST["first"])[0]


def qkv_grad_kernel(places, lin_ref, turned_ref, out_ref, got_ref, *refs):
    outs, sum_ref = refs[:4], refs[4]
    for k in range(8):
        sum_ref[k, :96, :] = mm(turned_ref[k * 96 : (k + 1) * 96, :], lin_ref[...]).astype(BF)
    put_out(out_ref, places, places[CORE], sum_ref)
    for i in range(NX):
        for k in range(2):
            at = (places[X] + i) % NX * 2 + (places[YH] + k) % 2
            outs[i][k] = (sum_ref[at].astype(F32) + got_ref[at].astype(F32)).astype(BF)


def qkv_grad(places, lin, turned, out, got, deps):
    return call(
        qkv_grad_kernel,
        [((2, 144, 768), BF)] * 4,
        [places, lin, turned, out, got],
        COST["qkv_grad"],
        scratch=[pltpu.VMEM((8, 144, 768), BF)],
        deps=deps,
    )


def lay_rows_kernel(places, mine, other, out_ref):
    for i in range(NX):
        for k in range(2):
            base = (places[X] + i) % NX * 4 + (places[YH] + k) % 2 * 2
            out_ref[at_rows(base + places[CORE], 96), :] = mine[i, k]
            out_ref[at_rows(base + 1 - places[CORE], 96), :] = other[i, k]


def lay_rows(places, mine, other):
    return call(lay_rows_kernel, [((D, D), BF)], [places, mine, other], COST["lay_rows"])[0]


def middle_kernel(
    places, x_ref, m0, m1, m2, m3, w_ref, gain, normed_ref, own_ref, acc_ref, mixed_ref
):
    for i, ref in enumerate((m0, m1, m2, m3)):
        at = pl.multiple_of((places[Z] + i) % NZ * QW, QW)
        mixed_ref[:, pl.ds(at, QW)] = ref[...]
    for t in range(3):
        cols = slice(t * 512, (t + 1) * 512)
        acc_ref[:, cols] = x_ref[:, cols].astype(F32) + mm(mixed_ref[...], w_ref[:, cols])
    for i in range(NZ):
        rows = slice(i * ROWS, (i + 1) * ROWS)
        v = acc_ref[rows, :]
        r = lax.rsqrt(jnp.mean(v * v, axis=1, keepdims=True) + EPSILON)
        normed_ref[rows, :] = (v * r * gain[...]).astype(BF)
    own_ref[...] = acc_ref[at_rows(places[Z], ROWS), :]


def middle_of(places, x_all, pieces, w_out, gain):
    return call(
        middle_kernel,
        [((TOKENS, D), BF), ((ROWS, D), F32)],
        [places, x_all, *pieces, w_out, gain],
        COST["middle"],
        scratch=[pltpu.VMEM((TOKENS, D), F32), pltpu.VMEM((TOKENS, D), BF)],
    )


def ffn_kernel(places, n_ref, og_ref, packed_ref, *refs):
    hidden_ref, gg_ref, ug_ref = refs[:3]
    in_chunks, down_ref = refs[3:7], refs[7]
    in_acc, down_acc, wg_ref, wu_ref, wd_ref = refs[8:]
    for j in range(2):
        cols = slice(j * 512, (j + 1) * 512)
        for b in range(16):
            at = (b // 4 * 2 + b % 2, b // 2 % 2)
            rows = slice(b * 96, (b + 1) * 96)
            wg_ref[rows, :] = packed_ref[at[0], at[1], j * 96 : (j + 1) * 96, :]
            wu_ref[rows, :] = packed_ref[at[0], at[1], (2 + j) * 96 : (3 + j) * 96, :]
            if b // 8 == j:
                rows = slice(b % 8 * 64, b % 8 * 64 + 64)
                for t in range(3):
                    wd_ref[rows, t * 512 : (t + 1) * 512] = packed_ref[
                        at[0], at[1], 384 + 64 * t : 448 + 64 * t, :
                    ]
        wg, wu, wd = wg_ref[...], wu_ref[...], wd_ref[...]
        gate = mm(n_ref[...], wg)
        up = mm(n_ref[...], wu)
        hg = mm_t(og_ref[...], wd).astype(BF).astype(F32)
        sig = 1.0 / (1.0 + jnp.exp(-gate))
        silu = gate * sig
        hidden = (silu * up).astype(BF)
        gg = (hg * up * (sig * (1.0 + gate * (1.0 - sig)))).astype(BF)
        ug = (hg * silu).astype(BF)
        hidden_ref[:, cols] = hidden
        gg_ref[:, cols] = gg
        ug_ref[:, cols] = ug
        if j == 0:
            in_acc[...] = mm_t(gg, wg) + mm_t(ug, wu)
            down_acc[...] = mm(hidden, wd)
        else:
            in_acc[...] += mm_t(gg, wg) + mm_t(ug, wu)
            down_ref[...] = (down_acc[...] + mm(hidden, wd)).astype(BF)
    send_chunks(in_chunks, in_acc, places)


def ffn(places, normed, og, packed):
    return call(
        ffn_kernel,
        [((TOKENS, FFZ), BF)] * 3 + CHUNKS + [((TOKENS, D), BF)],
        [places, normed, og, packed],
        COST["ffn"],
        scratch=[pltpu.VMEM((TOKENS, D), F32)] * 2
        + [pltpu.VMEM((D, 512), BF)] * 2
        + [pltpu.VMEM((512, D), BF)],
    )


def ffn_terms(places, n_ref, h_ref, gg_ref, ug_ref, og_ref, put):
    for w, ref in enumerate((gg_ref, ug_ref)):
        for half in range(2):
            tile = mm(n_ref[...], ref[:, half * 512 : (half + 1) * 512])
            put(slice((2 * w + half) * 96, (2 * w + half + 1) * 96), tile.reshape(8, 96, 512))
    for t in range(3):
        tile = mm(h_ref[...], og_ref[:, t * 512 : (t + 1) * 512])
        put(slice(384 + 64 * t, 448 + 64 * t), tile.reshape(8, 64, 512))


def ffn_sent_kernel(places, n_ref, hidden_ref, gg_ref, ug_ref, og_ref, *refs):
    sent_ref, n_mine, h_mine, n_turned, h_turned, n_sent, h_sent = refs
    n_turned[...] = n_ref[...].T
    h_turned[...] = hidden_ref[...].T
    split_cores(places, n_turned, n_mine, n_sent, 96)
    split_cores(places, h_turned, h_mine, h_sent, 64)

    def put(rows, tile):
        sent_ref[:, rows, :] = tile.astype(BF)

    ffn_terms(places, n_sent, h_sent, gg_ref, ug_ref, og_ref, put)


def ffn_sent_of(places, normed, hidden, gg, ug, og):
    return call(
        ffn_sent_kernel,
        [((8, 576, 512), BF), ((D // 2, TOKENS), BF), ((FFZ // 2, TOKENS), BF)],
        [places, normed, hidden, gg, ug, og],
        COST["ffn_sent"],
        scratch=[
            pltpu.VMEM((D, TOKENS), BF),
            pltpu.VMEM((FFZ, TOKENS), BF),
            pltpu.VMEM((D // 2, TOKENS), BF),
            pltpu.VMEM((FFZ // 2, TOKENS), BF),
        ],
    )


def ffn_grad_kernel(places, n_ref, h_ref, gg_ref, ug_ref, og_ref, got_ref, *refs):
    outs, sum_ref = refs[:4], refs[4]

    def put(rows, tile):
        sum_ref[:, rows, :] = (tile + got_ref[:, rows, :].astype(F32)).astype(BF)

    ffn_terms(places, n_ref, h_ref, gg_ref, ug_ref, og_ref, put)
    for i in range(NX):
        for k in range(2):
            at = (places[X] + i) % NX * 2 + (places[YH] + k) % 2
            outs[i][k] = sum_ref[at]


def ffn_grad(places, n_mine, h_mine, gg, ug, og, got, deps):
    return call(
        ffn_grad_kernel,
        [((2, 576, 512), BF)] * 4,
        [places, n_mine, h_mine, gg, ug, og, got],
        COST["ffn_grad"],
        scratch=[pltpu.VMEM((8, 576, 512), BF)],
        deps=deps,
    )


def rms_back(grad, v, gain):
    r = lax.rsqrt(jnp.mean(v * v, axis=1, keepdims=True) + EPSILON)
    pulled = grad * gain
    return r * pulled - v * (r * r * r * jnp.mean(pulled * v, axis=1, keepdims=True))


def middle_back_kernel(places, own, g1, g2, g3, middle, og, gain, w_ref, mid_ref, branch_ref, *outs):
    grad = own[...] + g1[...].astype(F32) + g2[...].astype(F32) + g3[...].astype(F32)
    mid = og[...].astype(F32) + rms_back(grad, middle[...], gain[...])
    mid_ref[...] = mid
    branch = mid.astype(BF)
    branch_ref[...] = branch
    for i in range(NZ):
        outs[i][...] = mm_t(branch, w_ref[at_rows((places[Z] + i) % NZ, QW), :]).astype(BF)


def middle_back(places, chunks, middle, og, gain, w_out, deps):
    return call(
        middle_back_kernel,
        [((ROWS, D), F32), ((ROWS, D), BF)] + [((ROWS, QW), BF)] * 4,
        [places, *chunks, middle, og, gain, w_out],
        COST["middle_back"],
        deps=deps,
    )


def input_back_kernel(places, grad, x, mid, gain, out_ref):
    out_ref[...] = mid[...] + rms_back(grad[...].astype(F32), x[...].astype(F32), gain[...])


def input_back(places, grad, x, mid, gain, deps):
    return call(
        input_back_kernel, [((ROWS, D), F32)], [places, grad, x, mid, gain], 2, deps=deps
    )[0]


def scatter(chunks):
    far = [shift_z(chunks[1], 1), shift_z(chunks[3], -1), shift_z(chunks[2], 2)]
    return [chunks[0], *far]


def x_sum_kernel(places, a, b, c, d, mine, sent):
    mine[...] = a[0].astype(F32) + b[0].astype(F32) + c[0].astype(F32) + d[0].astype(F32)
    total = a[1].astype(F32) + b[1].astype(F32) + c[1].astype(F32) + d[1].astype(F32)
    sent[...] = total.astype(BF)


def x_sum(places, terms, us, deps):
    shape = terms[0].shape[1:]
    return call(x_sum_kernel, [(shape, F32), (shape, BF)], [places, *terms], us, deps=deps)


def add_kernel(places, a, b, out):
    out[...] = (a[...].astype(F32) + b[...].astype(F32)).astype(BF)


def added(places, a, b, deps):
    return call(add_kernel, [(a.shape, BF)], [places, a, b], COST["add"], deps=deps)[0]


def add_split_kernel(places, a, b, qkv_ref, out_ref):
    total = (a[...].astype(F32) + b[...].astype(F32)).astype(BF)
    qkv_ref[...] = total[:96]
    out_ref[...] = total[96:]


def added_split(places, a, b, deps):
    return call(
        add_split_kernel, [((96, 768), BF), ((48, 768), BF)], [places, a, b], 1, deps=deps
    )


def swap_xz(v):
    pairs = [
        ((a * 4 + r) * 8 + b * 2 + l, (b * 4 + r) * 8 + a * 2 + l)
        for a in range(NX)
        for b in range(NZ)
        for r in range(4)
        for l in range(2)
    ]
    return lax.ppermute(v, ("fsdp", "sp"), pairs)


def over_x(chunks):
    far = [shift_x(chunks[1], 1), shift_x(chunks[3], -1), shift_x(chunks[2], 2)]
    return [chunks[0], *far]


def ffn_out_kernel(places, p0, p1, p2, p3, wg, wu, gate_ref, up_ref, down_ref, gain_ref, all_ref):
    for i, p in enumerate((p0, p1, p2, p3)):
        all_ref[(places[Z] + i) % NZ] = p[...]
    gain = jnp.zeros((96, 1), F32)
    for k, (w, out) in enumerate(((wg, gate_ref), (wu, up_ref))):
        for b in range(16):
            rows = slice((2 * k + b // 8) * 96, (2 * k + b // 8 + 1) * 96)
            cols = slice(b % 8 * 64, b % 8 * 64 + 64)
            tile = jnp.concatenate([all_ref[q, rows, cols].astype(F32) for q in range(NZ)], axis=1)
            out[:, b * 256 : (b + 1) * 256] = tile
            gain += jnp.sum(
                tile * w[:, b * 256 : (b + 1) * 256].astype(F32), axis=1, keepdims=True
            )
    for q in range(NZ):
        for t in range(3):
            r = 384 + 64 * t
            down_ref[q * 64 : (q + 1) * 64, t * 512 : (t + 1) * 512] = all_ref[
                q, r : r + 64, :
            ].astype(F32)
    gain_ref[...] = gain


def ffn_out(places, pieces, wg, wu, deps):
    return call(
        ffn_out_kernel,
        [((96, FF), F32), ((96, FF), F32), ((256, D), F32), ((96, 1), F32)],
        [places, *pieces, wg, wu],
        4,
        scratch=[pltpu.VMEM((NZ, 576, 512), BF)],
        deps=deps,
    )


def qkv_out_kernel(places, p0, p1, p2, p3, wq, wk, wv, q_ref, k_ref, v_ref, gain_ref, all_ref):
    for i, p in enumerate((p0, p1, p2, p3)):
        all_ref[(places[Z] + i) % NZ] = p[...]
    for q in range(NZ):
        q_ref[:, q * QW : (q + 1) * QW] = all_ref[q, :, :QW].astype(F32)
    gain = jnp.sum(q_ref[...] * wq[...].astype(F32), axis=1, keepdims=True)
    for out, w, at in ((k_ref, wk, QW), (v_ref, wv, QW + KW)):
        tile = jnp.concatenate(
            [all_ref[q, :, at : at + KW].astype(F32) for q in range(NZ)], axis=1
        )
        out[...] = tile
        gain += jnp.sum(tile * w[...].astype(F32), axis=1, keepdims=True)
    gain_ref[...] = gain


def qkv_out(places, pieces, wq, wk, wv, deps):
    return call(
        qkv_out_kernel,
        [((96, 1536), F32), ((96, 768), F32), ((96, 768), F32), ((96, 1), F32)],
        [places, *pieces, wq, wk, wv],
        2,
        scratch=[pltpu.VMEM((NZ, 96, 768), BF)],
        deps=deps,
    )


def out_out_kernel(places, p0, p1, p2, p3, out_ref):
    for i, p in enumerate((p0, p1, p2, p3)):
        tile = p[...].astype(F32)
        rows = pl.ds(pl.multiple_of((places[Z] + i) % NZ * 24, 8), 24)
        out_ref[rows, :] = jnp.concatenate([tile[:24], tile[24:]], axis=1)


def out_out(places, pieces):
    return call(out_out_kernel, [((96, D), F32)], [places, *pieces], 1)[0]


def block_out_kernel(places, middle, down, out_ref):
    out_ref[...] = (middle[...] + down[...].astype(F32)).astype(BF)


def block_out_of(places, middle, down, deps):
    return call(block_out_kernel, [((ROWS, D), BF)], [places, middle, down], 1, deps=deps)[0]


def body(
    inputs, norm_attn, w_query, w_key, w_value, w_out, norm_ffn, w_gate, w_up, w_down, cotangent
):
    f, s = lax.axis_index("fsdp"), lax.axis_index("sp")
    x, yh, c, z, yl = f // 4, f // 2 % 2, f % 2, s // 2, s % 2
    places = jnp.stack([x, yh, c, z, yl]).astype(jnp.int32)
    x_own, og_own = inputs[0], cotangent[0]
    gain_attn, gain_ffn = norm_attn[None], norm_ffn[None]

    index = jnp.arange(TOKENS, dtype=jnp.int32)
    positions = (index // ROWS * 2 + yl) * ROWS + index % ROWS
    lane = np.arange(QW) % HEAD_DIM
    frequency = ROPE_BASE ** (-(jnp.arange(HALF, dtype=F32) * 2.0 / HEAD_DIM))
    frequency = jnp.concatenate([frequency] * (QW // HALF))
    angles = positions.astype(F32)[:, None] * frequency[None, :]
    sign = np.where(lane < HALF, -1.0, 1.0).astype(np.float32)
    cosine, sine = jnp.cos(angles), jnp.sin(angles) * sign[None, :]

    qkv_shard, ffn_shard, both_own = cut(
        places, w_query, w_key, w_value, w_gate, w_up, w_down, x_own, og_own
    )
    ffn_pair = paired(places, ffn_shard, mirror_y(ffn_shard))
    packed = lax.all_gather(
        ffn_pair, "fsdp", axis=0, tiled=False, axis_index_groups=XC_GROUPS
    )
    boths = pieces_z(both_own)
    qkv_lane = stacked(places, pieces_x(qkv_shard), [cosine, sine, gain_attn])
    qkv_mirror = mirror_y(qkv_lane)
    qkv_other, mirror_other = swap_core(qkv_lane), swap_core(qkv_mirror)
    out_pair = stacked(places, [w_out, mirror_y(w_out)], [])
    out_mine = pieces_x(out_pair)

    normed, x_all, og_all, turned_mine, turned_sent = norm(places, gain_attn, boths)
    q, kv, held_qkv = qkv(
        places, normed, [qkv_lane, qkv_mirror, qkv_other, mirror_other], cosine, sine
    )
    kv_other = swap_low(kv)
    out_lane = stacked(places, out_mine, [kv])
    held_out = lay_rows(places, out_lane, swap_core(out_lane))
    mixed, shares = attend(places, q, kv, kv_other, [held_out])
    mixed_pieces = pieces_z(mixed)
    normed_ffn, middle_own = middle_of(places, x_all, mixed_pieces, held_out, gain_ffn)
    outs = ffn(places, normed_ffn, og_all, packed)
    hidden, gate_grad, up_grad = outs[:3]
    in_chunks, down_part = outs[3:7], outs[7]

    in_got = scatter(in_chunks)
    ffn_sent, n_mine, h_mine = ffn_sent_of(
        places, normed_ffn, hidden, gate_grad, up_grad, og_all
    )
    back = middle_back(places, in_got, middle_own, og_own, gain_ffn, held_out, [n_mine])
    middle_grad, branch = back[:2]
    head_grads = [back[2], shift_z(back[5], -1), shift_z(back[4], 2), shift_z(back[3], 1)]
    branch_all = gather_z(branch)
    down_own = scatter_z(copied(places, [down_part], [branch])[0])
    ffn_chunks = ffn_grad(
        places, n_mine, h_mine, gate_grad, up_grad, og_all, swap_core(ffn_sent), [branch]
    )
    ffn_terms = over_x(ffn_chunks)

    dq, dkv_own, dkv_sent = attend_back(
        places, head_grads, q, kv, kv_other, shares, [ffn_chunks[0]]
    )
    dkv_got = swap_low(dkv_sent)
    lin, out_part, qkv_sent = turn(
        places, dq, dkv_own, dkv_got, cosine, sine, turned_sent, mixed, branch_all
    )
    qkv_got = swap_core(qkv_sent)
    first_part = first(places, lin, held_qkv)
    first_got = scatter_z(first_part)
    ffn_half, ffn_sent = x_sum(places, ffn_terms, COST["x_sum"], [first_part])
    ffn_got = mirror_y(ffn_sent)
    qkv_chunks = qkv_grad(places, lin, turned_mine, out_part, qkv_got, [ffn_sent])
    qkv_terms = over_x(qkv_chunks)

    qkv_half, qkv_sent = x_sum(places, qkv_terms, 2, [])
    qkv_got = mirror_y(qkv_sent)
    ffn_half = added(places, ffn_half, ffn_got, [qkv_chunks[0]])
    ffn_low = swap_low(ffn_half)
    qkv_half = added(places, qkv_half, qkv_got, [ffn_half])
    qkv_low = swap_low(qkv_half)
    ffn_total = added(places, ffn_half, ffn_low, [qkv_half])
    ffn_pieces = pieces_z(ffn_total)
    qkv_total, out_total = added_split(places, qkv_half, qkv_low, [ffn_total])
    qkv_pieces = pieces_z(qkv_total)
    out_pieces = pieces_z(swap_xz(out_total))

    block_out = block_out_of(places, middle_own, down_own, [qkv_total])
    input_grad = input_back(places, first_got, x_own, middle_grad, gain_attn, [qkv_total])
    grad_gate, grad_up, grad_down, ffn_gain = ffn_out(
        places, ffn_pieces, w_gate, w_up, [qkv_total]
    )
    grad_query, grad_key, grad_value, qkv_gain = qkv_out(
        places, qkv_pieces, w_query, w_key, w_value, [ffn_gain]
    )
    grad_out = out_out(places, out_pieces)
    grad_norm_attn = qkv_gain[:, 0] / lax.dynamic_slice_in_dim(norm_attn, f * 96, 96, 0)
    grad_norm_ffn = ffn_gain[:, 0] / lax.dynamic_slice_in_dim(norm_ffn, f * 96, 96, 0)
    return (
        block_out[None],
        input_grad[None],
        grad_norm_attn,
        grad_query,
        grad_key,
        grad_value,
        grad_out,
        grad_norm_ffn,
        grad_gate,
        grad_up,
        grad_down,
    )


def solution(mesh):
    rows = P("fsdp", None)
    tokens = P("fsdp", "sp", None)
    return jax.shard_map(
        body,
        mesh=mesh,
        in_specs=(tokens, P(), rows, rows, rows, rows, P(), rows, rows, rows, tokens),
        out_specs=(tokens, tokens, P("fsdp"), rows, rows, rows, rows, P("fsdp"), rows, rows, rows),
        check_vma=False,
    )
```

```python
import functools

import jax
import jax.numpy as jnp
import numpy as np
from jax import lax
from jax.experimental import pallas as pl
from jax.experimental.pallas import tpu as pltpu
from jax.sharding import PartitionSpec as P

D = 1536
HEADS = 16
KV_HEADS = 8
HEAD_DIM = 96
FF = 4096

EPSILON = 1e-05
ROPE_BASE = 100000.0
MASKED = -1e30

NX, NZ = 4, 4
ROWS = 128
TOKENS = ROWS * NZ
QW, KW = 384, 192
HALF = HEAD_DIM // 2
FFZ = FF // NZ
BF = jnp.bfloat16
F32 = jnp.float32
VMEM = pl.BlockSpec(memory_space=pltpu.VMEM)
SMEM = pl.BlockSpec(memory_space=pltpu.SMEM)
ANY = pl.BlockSpec(memory_space=pl.ANY)
LIMIT = pltpu.CompilerParams(vmem_limit_bytes=56 * 1024 * 1024)
X, YH, CORE, Z, YL = range(5)
COST = {
    "norm": 54,
    "qkv": 0.1,
    "attend": 0.1,
    "lay": 0.1,
    "middle": 4,
    "ffn": 17,
    "ffn_sent": 0.1,
    "middle_back": 60,
    "ffn_grad": 60,
    "attend_back": 60,
    "turn": 0.1,
    "first": 0.1,
    "x_sum": 60,
    "y_sum": 0.1,
    "qkv_grad": 0.1,
    "add": 8,
}


Z_GROUPS = [[z * 2 + l for z in range(NZ)] for l in range(2)]
XC_GROUPS = [[x * 4 + h * 2 + c for x in range(NX) for c in range(2)] for h in range(2)]


def scatter_z(v):
    return lax.psum_scatter(
        v, "sp", scatter_dimension=0, tiled=True, axis_index_groups=Z_GROUPS
    )


def gather_xc(v):
    return lax.all_gather(v, "fsdp", axis=0, tiled=False, axis_index_groups=XC_GROUPS)


def gather_z(v):
    return lax.all_gather(v, "sp", axis=0, tiled=True, axis_index_groups=Z_GROUPS)


def shift_z(v, step):
    pairs = [(z * 2 + l, (z + step) % NZ * 2 + l) for z in range(NZ) for l in range(2)]
    return lax.ppermute(v, "sp", pairs)


def swap_low(v):
    return lax.ppermute(v, "sp", [(s, s ^ 1) for s in range(8)])


def shift_x(v, step):
    pairs = [(x * 4 + r, (x + step) % NX * 4 + r) for x in range(NX) for r in range(4)]
    return lax.ppermute(v, "fsdp", pairs)


def swap_core(v):
    return lax.ppermute(v, "fsdp", [(f, f ^ 1) for f in range(16)])


def mirror_y(v):
    pairs = [(f * 8 + s, (f ^ 2) * 8 + (s ^ 1)) for f in range(16) for s in range(8)]
    return lax.ppermute(v, ("fsdp", "sp"), pairs)


def pieces_z(v):
    far = [shift_z(v, -1), shift_z(v, 1), shift_z(v, 2)]
    return [v, far[0], far[2], far[1]]


def two_stage_z(v):
    above, below = shift_z(v, -1), shift_z(v, 1)
    return [v, above, shift_z(below, 1), below]


def two_stage_x(v):
    above, below = shift_x(v, -1), shift_x(v, 1)
    return [v, above, shift_x(below, 1), below]


def pieces_x(v):
    far = [shift_x(v, -1), shift_x(v, 1), shift_x(v, 2)]
    return [v, far[0], far[2], far[1]]


def part(v, index, size, dim=0):
    return lax.dynamic_slice_in_dim(v, index * size, size, dim)


def call(kernel, outs, ins, us, scratch=(), deps=()):
    def run(*refs):
        kernel(*refs[: len(ins)], *refs[len(ins) + len(deps) :])

    return pl.pallas_call(
        run,
        name=kernel.__name__.replace("_kernel", ""),
        out_shape=[jax.ShapeDtypeStruct(s, t) for s, t in outs],
        in_specs=[SMEM] + [VMEM] * (len(ins) - 1) + [ANY] * len(deps),
        out_specs=[VMEM] * len(outs),
        scratch_shapes=scratch,
        compiler_params=LIMIT,
        cost_estimate=pl.CostEstimate(
            flops=int(us * 1e9), bytes_accessed=int(us * 3e6), transcendentals=0
        ),
    )(*ins, *deps)


def mm(a, b):
    return jnp.dot(a, b, preferred_element_type=F32)


def mm_t(a, b):
    return lax.dot_general(a, b, (((1,), (1,)), ((), ())), preferred_element_type=F32)


def t_mm(a, b):
    return lax.dot_general(a, b, (((0,), (0,)), ((), ())), preferred_element_type=F32)


def at_rows(index, size):
    return pl.ds(pl.multiple_of(index * size, size), size)


def rope(v, cosine, sine):
    width = v.shape[1]
    lane = lax.broadcasted_iota(jnp.int32, v.shape, 1) % HEAD_DIM
    partner = jnp.where(
        lane < HALF, pltpu.roll(v, width - HALF, 1), pltpu.roll(v, HALF, 1)
    )
    return v * cosine + partner * sine


def rope_keys(kv, cosine, sine):
    lane = lax.broadcasted_iota(jnp.int32, kv.shape, 1)
    return jnp.where(lane < KW, rope(kv, cosine, sine), kv)


def cut_kernel(places, wq, wk, wv, wg, wu, wd, wo, qkv_ref, rows_ref):
    z = places[Z]
    for t in range(3):
        cols = slice(t * 512, (t + 1) * 512)
        rows_ref[384 + 64 * t : 448 + 64 * t, :] = wd[at_rows(z, 64), cols]
        rows_ref[576 + 96 * t : 672 + 96 * t, :] = wo[:, cols]
    qkv_ref[:, :QW] = wq[:, pl.ds(pl.multiple_of(z * QW, 128), QW)]
    for at in range(NZ):

        @pl.when(z == at)
        def _():
            cols = slice(at * KW, (at + 1) * KW)
            qkv_ref[:, QW:] = jnp.concatenate([wk[:, cols], wv[:, cols]], axis=1)
            for k, w in enumerate((wg, wu)):
                for half in range(2):
                    starts = [(8 * half + i) * 256 + at * 64 for i in range(8)]
                    rows = slice((2 * half + k) * 96, (2 * half + k + 1) * 96)
                    rows_ref[rows, :] = jnp.concatenate([w[:, b : b + 64] for b in starts], axis=1)


def cut(places, *arrays):
    return call(cut_kernel, [((96, 768), BF), ((864, 512), BF)], [places, *arrays], 3)


def copy_kernel(places, *refs):
    n = len(refs) // 2
    for i in range(n):
        refs[n + i][...] = refs[i][...]


def copied(places, arrays, deps):
    return call(copy_kernel, [(v.shape, v.dtype) for v in arrays], [places, *arrays], 0.1, deps=deps)


def stack_kernel(places, *refs):
    for i, ref in enumerate(refs[:-1]):
        refs[-1][i] = ref[...]


def pair_kernel(places, own, mirror, *outs):
    for i, out in enumerate(outs):
        rows = slice(288 * i, 288 * (i + 1))
        out[places[YH]] = own[rows, :]
        out[1 - places[YH]] = mirror[rows, :]


def paired(places, own, mirror, deps):
    return call(
        pair_kernel, [((2, 288, 512), BF)] * 3, [places, own, mirror], 0.1, deps=deps
    )


def stacked(places, arrays, deps):
    shape = (len(arrays), *arrays[0].shape)
    return call(stack_kernel, [(shape, BF)], [places, *arrays], 0.1, deps=deps)[0]


def norm_kernel(places, gain, *refs):
    xs, (normed_ref, x_ref, mine_ref, sent_ref, turned_ref) = refs[:4], refs[4:]
    for i in range(NZ):
        x_ref[at_rows((places[Z] + i) % NZ, ROWS), :] = xs[i][...]
    for i in range(NZ):
        rows = pl.ds(i * ROWS, ROWS)
        v = x_ref[rows, :].astype(F32)
        r = lax.rsqrt(jnp.mean(v * v, axis=1, keepdims=True) + EPSILON)
        normed_ref[rows, :] = (v * r * gain[...]).astype(BF)
    turned_ref[...] = normed_ref[...].T
    split_cores(places, turned_ref, mine_ref, sent_ref, 96)


def split_cores(places, turned_ref, mine_ref, sent_ref, n):
    for k in range(8):
        rows = slice(k * n, (k + 1) * n)
        mine_ref[rows, :] = turned_ref[at_rows(2 * k + places[CORE], n), :]
        sent_ref[rows, :] = turned_ref[at_rows(2 * k + 1 - places[CORE], n), :]


def norm(places, gain, xs):
    return call(
        norm_kernel,
        [((TOKENS, D), BF)] * 2 + [((D // 2, TOKENS), BF)] * 2,
        [places, gain, *xs],
        COST["norm"],
        scratch=[pltpu.VMEM((D, TOKENS), BF)],
    )


def qkv_kernel(places, normed_ref, own, own_mirror, other, other_mirror, cosine, sine, *refs):
    q_ref, kv_ref, w_ref = refs
    for i in range(NX):
        for k, (a, b) in enumerate(((own, other), (own_mirror, other_mirror))):
            base = (places[X] + i) % NX * 4 + (places[YH] + k) % 2 * 2
            w_ref[at_rows(base + places[CORE], 96), :] = a[i]
            w_ref[at_rows(base + 1 - places[CORE], 96), :] = b[i]
    for i in range(NZ):
        rows = pl.ds(i * ROWS, ROWS)
        lin = mm(normed_ref[rows, :], w_ref[...])
        q_ref[rows, :] = rope(lin[:, :QW], cosine[rows, :], sine[rows, :]).astype(BF)
        kv_ref[rows, :] = rope_keys(lin[:, QW:], cosine[rows, :], sine[rows, :]).astype(BF)


def qkv(places, normed, weights, cosine, sine):
    return call(
        qkv_kernel,
        [((TOKENS, QW), BF), ((TOKENS, 2 * KW), BF), ((D, QW + 2 * KW), BF)],
        [places, normed, *weights, cosine, sine],
        COST["qkv"],
    )


def head(ref, rows, index):
    return ref[rows, index * HEAD_DIM : (index + 1) * HEAD_DIM]


def two_heads(ref, j, g):
    rows = slice(j * ROWS, (j + 1) * ROWS)
    return jnp.concatenate([head(ref, rows, 2 * g), head(ref, rows, 2 * g + 1)], axis=0)


def attend_kernel(places, q_ref, own_ref, other_ref, mixed_ref, p_ref):
    late = places[YL]
    factor = HEAD_DIM ** (-0.5)
    for g in range(2):
        for j in range(NZ):
            n = (j + 1) * ROWS
            q = two_heads(q_ref, j, g)
            s_own = mm_t(q, head(own_ref, slice(0, n), g)) * factor
            s_oth = mm_t(q, head(other_ref, slice(0, n), g)) * factor
            shape = (2 * ROWS, n)
            row = lax.broadcasted_iota(jnp.int32, shape, 0) % ROWS + j * ROWS
            col = lax.broadcasted_iota(jnp.int32, shape, 1)
            s_own = jnp.where(col <= row, s_own, MASKED)
            s_oth = jnp.where(col < (j + late) * ROWS, s_oth, MASKED)
            highest = jnp.maximum(
                jnp.max(s_own, axis=1, keepdims=True), jnp.max(s_oth, axis=1, keepdims=True)
            )
            p_own, p_oth = jnp.exp(s_own - highest), jnp.exp(s_oth - highest)
            total = jnp.sum(p_own, axis=1, keepdims=True) + jnp.sum(p_oth, axis=1, keepdims=True)
            scale = 1.0 / total
            p_own, p_oth = (p_own * scale).astype(BF), (p_oth * scale).astype(BF)
            p_ref[g, j, :, :n] = p_own
            p_ref[g, j, :, n : 2 * n] = p_oth
            out = mm(p_own, head(own_ref, slice(0, n), 2 + g)) + mm(
                p_oth, head(other_ref, slice(0, n), 2 + g)
            )
            out = out.astype(BF)
            for k in range(2):
                h = 2 * g + k
                mixed_ref[j * ROWS : (j + 1) * ROWS, h * HEAD_DIM : (h + 1) * HEAD_DIM] = out[
                    k * ROWS : (k + 1) * ROWS
                ]


def attend(places, q, kv, kv_other, deps):
    return call(
        attend_kernel,
        [((TOKENS, QW), BF), ((2, NZ, 2 * ROWS, 2 * TOKENS), BF)],
        [places, q, kv, kv_other],
        COST["attend"],
        deps=deps,
    )


def attend_back_kernel(places, *refs):
    grads = refs[:4]
    q_ref, own_ref, other_ref, p_ref = refs[4:8]
    dq_ref, down_ref, doth_ref = refs[8:11]
    do_ref, acc_own, acc_oth = refs[11:]
    factor = HEAD_DIM ** (-0.5)
    for i in range(NZ):
        do_ref[at_rows((places[Z] + i) % NZ, ROWS), :] = grads[i][...]
    for g in range(2):
        acc_own[...] = jnp.zeros_like(acc_own)
        acc_oth[...] = jnp.zeros_like(acc_oth)
        for j in range(NZ):
            n = (j + 1) * ROWS
            seen = slice(0, n)
            q = two_heads(q_ref, j, g)
            do = two_heads(do_ref, j, g)
            p_own, p_oth = p_ref[g, j, :, :n], p_ref[g, j, :, n : 2 * n]
            dp_own = mm_t(do, head(own_ref, seen, 2 + g))
            dp_oth = mm_t(do, head(other_ref, seen, 2 + g))
            f_own, f_oth = p_own.astype(F32), p_oth.astype(F32)
            dot = jnp.sum(f_own * dp_own, axis=1, keepdims=True) + jnp.sum(
                f_oth * dp_oth, axis=1, keepdims=True
            )
            ds_own = (f_own * (dp_own - dot)).astype(BF)
            ds_oth = (f_oth * (dp_oth - dot)).astype(BF)
            dq = mm(ds_own, head(own_ref, seen, g)) + mm(ds_oth, head(other_ref, seen, g))
            dq = (dq * factor).astype(BF)
            for k in range(2):
                h = 2 * g + k
                dq_ref[j * ROWS : (j + 1) * ROWS, h * HEAD_DIM : (h + 1) * HEAD_DIM] = dq[
                    k * ROWS : (k + 1) * ROWS
                ]
            acc_own[0, seen, :] += t_mm(ds_own, q)
            acc_own[1, seen, :] += t_mm(p_own, do)
            acc_oth[0, seen, :] += t_mm(ds_oth, q)
            acc_oth[1, seen, :] += t_mm(p_oth, do)
        for kind, scale in ((0, factor), (1, 1.0)):
            at = kind * KW + g * HEAD_DIM
            down_ref[:, at : at + HEAD_DIM] = acc_own[kind] * scale
            doth_ref[:, at : at + HEAD_DIM] = (acc_oth[kind] * scale).astype(BF)


def attend_back(places, grads, q, kv, kv_other, shares, deps):
    acc = pltpu.VMEM((2, TOKENS, HEAD_DIM), F32)
    return call(
        attend_back_kernel,
        [((TOKENS, QW), BF), ((TOKENS, 2 * KW), F32), ((TOKENS, 2 * KW), BF)],
        [places, *grads, q, kv, kv_other, shares],
        COST["attend_back"],
        scratch=[pltpu.VMEM((TOKENS, QW), BF), acc, acc],
        deps=deps,
    )


def send_chunks(refs, acc_ref, places):
    for i in range(NZ):
        rows = at_rows((places[Z] + i) % NZ, ROWS)
        refs[i][...] = acc_ref[rows, :].astype(refs[i].dtype)


CHUNKS = [((ROWS, D), F32)] + [((ROWS, D), BF)] * 3


def put_out(out_ref, places, core, ref):
    for k in range(8):
        rows = pl.ds(pl.multiple_of((k % 2 * 2 + core) * 96 + k // 2 * 24, 8), 24)
        tile = out_ref[rows, :]
        ref[k, 96:, :] = jnp.concatenate([tile[:, :768], tile[:, 768:]], axis=0).astype(BF)


def turn_kernel(
    places, dq_ref, own_ref, got_ref, cosine, sine, turned_ref, mixed_ref, branch_ref, *refs
):
    lin_ref, out_ref, sent_ref = refs
    for i in range(NZ):
        rows = slice(i * ROWS, (i + 1) * ROWS)
        dkv = (own_ref[rows, :] + got_ref[rows, :].astype(F32)).astype(BF)
        c, s = cosine[rows, :], -sine[rows, :]
        lin_ref[rows, :QW] = rope(dq_ref[rows, :].astype(F32), c, s).astype(BF)
        lin_ref[rows, QW:] = rope_keys(dkv.astype(F32), c, s).astype(BF)
    for k in range(8):
        sent_ref[k, :96, :] = mm(turned_ref[k * 96 : (k + 1) * 96, :], lin_ref[...]).astype(BF)
    out_ref[...] = t_mm(mixed_ref[...], branch_ref[...])
    put_out(out_ref, places, 1 - places[CORE], sent_ref)


def turn(places, dq, dkv_own, dkv_got, cosine, sine, turned, mixed, branch):
    return call(
        turn_kernel,
        [((TOKENS, 768), BF), ((QW, D), F32), ((8, 144, 768), BF)],
        [places, dq, dkv_own, dkv_got, cosine, sine, turned, mixed, branch],
        COST["turn"],
    )


def first_kernel(places, lin_ref, w_ref, out_ref):
    out_ref[...] = mm_t(lin_ref[...], w_ref[...]).astype(BF)


def first(places, lin, w):
    return call(first_kernel, [((TOKENS, D), BF)], [places, lin, w], COST["first"])[0]


def qkv_grad_kernel(places, lin_ref, turned_ref, out_ref, got_ref, *refs):
    outs, sum_ref = refs[:4], refs[4]
    for k in range(8):
        sum_ref[k, :96, :] = mm(turned_ref[k * 96 : (k + 1) * 96, :], lin_ref[...]).astype(BF)
    put_out(out_ref, places, places[CORE], sum_ref)
    for i in range(NX):
        for k in range(2):
            at = (places[X] + i) % NX * 2 + (places[YH] + k) % 2
            outs[i][k] = (sum_ref[at].astype(F32) + got_ref[at].astype(F32)).astype(BF)


def qkv_grad(places, lin, turned, out, got, deps):
    return call(
        qkv_grad_kernel,
        [((2, 144, 768), BF)] * 4,
        [places, lin, turned, out, got],
        COST["qkv_grad"],
        scratch=[pltpu.VMEM((8, 144, 768), BF)],
        deps=deps,
    )


def lay_kernel(places, packed, out_ref):
    for b in range(16):
        for t in range(3):
            out_ref[b * 96 : (b + 1) * 96, t * 512 : (t + 1) * 512] = packed[
                b // 4 * 2 + b % 2, b // 2 % 2, t * 96 : (t + 1) * 96, :
            ]


def lay(places, packed, deps):
    return call(lay_kernel, [((D, D), BF)], [places, packed], COST["lay"], deps=deps)[0]


def middle_kernel(
    places, x_ref, m0, m1, m2, m3, w_ref, gain, normed_ref, own_ref, acc_ref, mixed_ref
):
    for i, ref in enumerate((m0, m1, m2, m3)):
        at = pl.multiple_of((places[Z] + i) % NZ * QW, QW)
        mixed_ref[:, pl.ds(at, QW)] = ref[...]
    for t in range(3):
        cols = slice(t * 512, (t + 1) * 512)
        acc_ref[:, cols] = x_ref[:, cols].astype(F32) + mm(mixed_ref[...], w_ref[:, cols])
    for i in range(NZ):
        rows = slice(i * ROWS, (i + 1) * ROWS)
        v = acc_ref[rows, :]
        r = lax.rsqrt(jnp.mean(v * v, axis=1, keepdims=True) + EPSILON)
        normed_ref[rows, :] = (v * r * gain[...]).astype(BF)
    own_ref[...] = acc_ref[at_rows(places[Z], ROWS), :]


def middle_of(places, x_all, pieces, w_out, gain):
    return call(
        middle_kernel,
        [((TOKENS, D), BF), ((ROWS, D), F32)],
        [places, x_all, *pieces, w_out, gain],
        COST["middle"],
        scratch=[pltpu.VMEM((TOKENS, D), F32), pltpu.VMEM((TOKENS, D), BF)],
    )


def ffn_kernel(places, n_ref, packed_ref, *refs):
    ogs, mine, other, refs = refs[:4], refs[4:8], refs[8:12], refs[12:]
    hidden_ref, gg_ref, ug_ref, og_ref = refs[:4]
    in_chunks, down_ref = refs[4:8], refs[8]
    in_acc, down_acc, wg_ref, wu_ref, wd_ref = refs[9:]
    for i, g in enumerate(ogs):
        og_ref[at_rows((places[Z] + i) % NZ, ROWS), :] = g[...]

    def from_pieces(out_ref, start):
        for i in range(NX):
            for h in range(2):
                base = (places[X] + i) % NX * 4 + h * 2
                for pieces, core in ((mine, places[CORE]), (other, 1 - places[CORE])):
                    out_ref[at_rows(base + core, 96), :] = pieces[i][h, start : start + 96, :]

    for j in range(2):
        cols = slice(j * 512, (j + 1) * 512)
        from_pieces(wg_ref, 192 * j)
        if j == 0:
            from_pieces(wu_ref, 96)
        for b in range(16):
            packed = packed_ref.at[b // 4 * 2 + b % 2, b // 2 % 2]
            if j == 1:
                wu_ref[b * 96 : (b + 1) * 96, :] = packed[:96, :]
            if b // 8 == j:
                rows = slice(b % 8 * 64, b % 8 * 64 + 64)
                for t in range(3):
                    wd_ref[rows, t * 512 : (t + 1) * 512] = packed[96 + 64 * t : 160 + 64 * t, :]
        wg, wu, wd = wg_ref[...], wu_ref[...], wd_ref[...]
        gate = mm(n_ref[...], wg)
        up = mm(n_ref[...], wu)
        hg = mm_t(og_ref[...], wd).astype(BF).astype(F32)
        sig = 1.0 / (1.0 + jnp.exp(-gate))
        silu = gate * sig
        hidden = (silu * up).astype(BF)
        gg = (hg * up * (sig * (1.0 + gate * (1.0 - sig)))).astype(BF)
        ug = (hg * silu).astype(BF)
        hidden_ref[:, cols] = hidden
        gg_ref[:, cols] = gg
        ug_ref[:, cols] = ug
        if j == 0:
            in_acc[...] = mm_t(gg, wg) + mm_t(ug, wu)
            down_acc[...] = mm(hidden, wd)
        else:
            in_acc[...] += mm_t(gg, wg) + mm_t(ug, wu)
            down_ref[...] = (down_acc[...] + mm(hidden, wd)).astype(BF)
    send_chunks(in_chunks, in_acc, places)


def ffn(places, normed, ogs, packed, mine, other):
    return call(
        ffn_kernel,
        [((TOKENS, FFZ), BF)] * 3 + [((TOKENS, D), BF)] + CHUNKS + [((TOKENS, D), BF)],
        [places, normed, packed, *ogs, *mine, *other],
        COST["ffn"],
        scratch=[pltpu.VMEM((TOKENS, D), F32)] * 2
        + [pltpu.VMEM((D, 512), BF)] * 2
        + [pltpu.VMEM((512, D), BF)],
    )


def ffn_terms(places, n_ref, h_ref, gg_ref, ug_ref, og_ref, put):
    for w, ref in enumerate((gg_ref, ug_ref)):
        for half in range(2):
            tile = mm(n_ref[...], ref[:, half * 512 : (half + 1) * 512])
            put(slice((2 * w + half) * 96, (2 * w + half + 1) * 96), tile.reshape(8, 96, 512))
    for t in range(3):
        tile = mm(h_ref[...], og_ref[:, t * 512 : (t + 1) * 512])
        put(slice(384 + 64 * t, 448 + 64 * t), tile.reshape(8, 64, 512))


def ffn_sent_kernel(places, n_ref, hidden_ref, gg_ref, ug_ref, og_ref, *refs):
    sent_ref, n_mine, h_mine, n_turned, h_turned, n_sent, h_sent = refs
    n_turned[...] = n_ref[...].T
    h_turned[...] = hidden_ref[...].T
    split_cores(places, n_turned, n_mine, n_sent, 96)
    split_cores(places, h_turned, h_mine, h_sent, 64)

    def put(rows, tile):
        sent_ref[:, rows, :] = tile.astype(BF)

    ffn_terms(places, n_sent, h_sent, gg_ref, ug_ref, og_ref, put)


def ffn_sent_of(places, normed, hidden, gg, ug, og):
    return call(
        ffn_sent_kernel,
        [((8, 576, 512), BF), ((D // 2, TOKENS), BF), ((FFZ // 2, TOKENS), BF)],
        [places, normed, hidden, gg, ug, og],
        COST["ffn_sent"],
        scratch=[
            pltpu.VMEM((D, TOKENS), BF),
            pltpu.VMEM((FFZ, TOKENS), BF),
            pltpu.VMEM((D // 2, TOKENS), BF),
            pltpu.VMEM((FFZ // 2, TOKENS), BF),
        ],
    )


def ffn_grad_kernel(places, n_ref, h_ref, gg_ref, ug_ref, og_ref, got_ref, *refs):
    outs, sum_ref = refs[:6], refs[6]

    def put(rows, tile):
        sum_ref[:, rows, :] = (tile + got_ref[:, rows, :].astype(F32)).astype(BF)

    ffn_terms(places, n_ref, h_ref, gg_ref, ug_ref, og_ref, put)
    for i in range(NX):
        for k in range(2):
            at = (places[X] + i) % NX * 2 + (places[YH] + k) % 2
            outs[i][k] = sum_ref[at, :, :256]
            outs[4 + k][i] = sum_ref[at, :, 256:]


def ffn_grad(places, n_mine, h_mine, gg, ug, og, got, deps):
    return call(
        ffn_grad_kernel,
        [((2, 576, 256), BF)] * 4 + [((4, 576, 256), BF)] * 2,
        [places, n_mine, h_mine, gg, ug, og, got],
        COST["ffn_grad"],
        scratch=[pltpu.VMEM((8, 576, 512), BF)],
        deps=deps,
    )


def y_sum_kernel(places, mine, got, *outs):
    for i in range(NX):
        outs[i][...] = (mine[i].astype(F32) + got[i].astype(F32)).astype(BF)


def y_sum(places, mine, got, deps):
    return call(
        y_sum_kernel,
        [(mine.shape[1:], BF)] * 4,
        [places, mine, got],
        COST["y_sum"],
        deps=deps,
    )


def ffn_join_kernel(places, mine, got, a, b, c, d, out):
    out[:, :256] = (mine[...] + got[...].astype(F32)).astype(BF)
    total = a[...].astype(F32) + b[...].astype(F32) + c[...].astype(F32) + d[...].astype(F32)
    out[:, 256:] = total.astype(BF)


def ffn_join(places, mine, got, terms, deps):
    return call(
        ffn_join_kernel,
        [((576, 512), BF)],
        [places, mine, got, *terms],
        COST["add"],
        deps=deps,
    )[0]


def rms_back(grad, v, gain):
    r = lax.rsqrt(jnp.mean(v * v, axis=1, keepdims=True) + EPSILON)
    pulled = grad * gain
    return r * pulled - v * (r * r * r * jnp.mean(pulled * v, axis=1, keepdims=True))


def middle_back_kernel(places, own, g1, g2, g3, middle, og, gain, w_ref, mid_ref, branch_ref, *outs):
    grad = own[...] + g1[...].astype(F32) + g2[...].astype(F32) + g3[...].astype(F32)
    mid = og[...].astype(F32) + rms_back(grad, middle[...], gain[...])
    mid_ref[...] = mid
    branch = mid.astype(BF)
    branch_ref[...] = branch
    for i in range(NZ):
        outs[i][...] = mm_t(branch, w_ref[at_rows((places[Z] + i) % NZ, QW), :]).astype(BF)


def middle_back(places, chunks, middle, og, gain, w_out, deps):
    return call(
        middle_back_kernel,
        [((ROWS, D), F32), ((ROWS, D), BF)] + [((ROWS, QW), BF)] * 4,
        [places, *chunks, middle, og, gain, w_out],
        COST["middle_back"],
        deps=deps,
    )


def input_back_kernel(places, grad, x, mid, gain, out_ref):
    out_ref[...] = mid[...] + rms_back(grad[...].astype(F32), x[...].astype(F32), gain[...])


def input_back(places, grad, x, mid, gain, deps):
    return call(
        input_back_kernel, [((ROWS, D), F32)], [places, grad, x, mid, gain], 2, deps=deps
    )[0]


def scatter(chunks):
    far = [shift_z(chunks[1], 1), shift_z(chunks[3], -1), shift_z(chunks[2], 2)]
    return [chunks[0], *far]


def x_sum_kernel(places, a, b, c, d, mine, sent):
    mine[...] = a[0].astype(F32) + b[0].astype(F32) + c[0].astype(F32) + d[0].astype(F32)
    total = a[1].astype(F32) + b[1].astype(F32) + c[1].astype(F32) + d[1].astype(F32)
    sent[...] = total.astype(BF)


def x_sum(places, terms, us, deps):
    shape = terms[0].shape[1:]
    return call(x_sum_kernel, [(shape, F32), (shape, BF)], [places, *terms], us, deps=deps)


def add_kernel(places, a, b, out):
    out[...] = (a[...].astype(F32) + b[...].astype(F32)).astype(BF)


def added(places, a, b, deps):
    return call(add_kernel, [(a.shape, BF)], [places, a, b], COST["add"], deps=deps)[0]


def over_x(chunks):
    far = [shift_x(chunks[1], 1), shift_x(chunks[3], -1), shift_x(chunks[2], 2)]
    return [chunks[0], *far]


def ffn_out_kernel(places, p0, p1, p2, p3, wg, wu, gate_ref, up_ref, down_ref, gain_ref, all_ref):
    for i, p in enumerate((p0, p1, p2, p3)):
        all_ref[(places[Z] + i) % NZ] = p[...]
    gain = jnp.zeros((96, 1), F32)
    for k, (w, out) in enumerate(((wg, gate_ref), (wu, up_ref))):
        for b in range(16):
            rows = slice((2 * k + b // 8) * 96, (2 * k + b // 8 + 1) * 96)
            cols = slice(b % 8 * 64, b % 8 * 64 + 64)
            tile = jnp.concatenate([all_ref[q, rows, cols].astype(F32) for q in range(NZ)], axis=1)
            out[:, b * 256 : (b + 1) * 256] = tile
            gain += jnp.sum(
                tile * w[:, b * 256 : (b + 1) * 256].astype(F32), axis=1, keepdims=True
            )
    for q in range(NZ):
        for t in range(3):
            r = 384 + 64 * t
            down_ref[q * 64 : (q + 1) * 64, t * 512 : (t + 1) * 512] = all_ref[
                q, r : r + 64, :
            ].astype(F32)
    gain_ref[...] = gain


def ffn_out(places, pieces, wg, wu, deps):
    return call(
        ffn_out_kernel,
        [((96, FF), F32), ((96, FF), F32), ((256, D), F32), ((96, 1), F32)],
        [places, *pieces, wg, wu],
        4,
        scratch=[pltpu.VMEM((NZ, 576, 512), BF)],
        deps=deps,
    )


def out_slices_kernel(places, p0, p1, p2, p3, *refs):
    all_ref = refs[4]
    for i, p in enumerate((p0, p1, p2, p3)):
        all_ref[(places[Z] + i) % NZ] = p[96:, :]
    for i in range(NX):
        refs[i][...] = all_ref[(places[X] + i) % NX]


def out_slices(places, pieces, deps):
    return call(
        out_slices_kernel,
        [((48, 768), BF)] * 4,
        [places, *pieces],
        1,
        scratch=[pltpu.VMEM((NZ, 48, 768), BF)],
        deps=deps,
    )


def qkv_out_kernel(places, p0, p1, p2, p3, wq, wk, wv, q_ref, k_ref, v_ref, gain_ref, all_ref):
    for i, p in enumerate((p0, p1, p2, p3)):
        all_ref[(places[Z] + i) % NZ] = p[:96, :]
    for q in range(NZ):
        q_ref[:, q * QW : (q + 1) * QW] = all_ref[q, :, :QW].astype(F32)
    gain = jnp.sum(q_ref[...] * wq[...].astype(F32), axis=1, keepdims=True)
    for out, w, at in ((k_ref, wk, QW), (v_ref, wv, QW + KW)):
        tile = jnp.concatenate(
            [all_ref[q, :, at : at + KW].astype(F32) for q in range(NZ)], axis=1
        )
        out[...] = tile
        gain += jnp.sum(tile * w[...].astype(F32), axis=1, keepdims=True)
    gain_ref[...] = gain


def qkv_out(places, pieces, wq, wk, wv, deps):
    return call(
        qkv_out_kernel,
        [((96, 1536), F32), ((96, 768), F32), ((96, 768), F32), ((96, 1), F32)],
        [places, *pieces, wq, wk, wv],
        2,
        scratch=[pltpu.VMEM((NZ, 96, 768), BF)],
        deps=deps,
    )


def out_out_kernel(places, p0, p1, p2, p3, out_ref):
    for i, p in enumerate((p0, p1, p2, p3)):
        tile = p[...].astype(F32)
        rows = pl.ds(pl.multiple_of((places[X] + i) % NX * 24, 8), 24)
        out_ref[rows, :] = jnp.concatenate([tile[:24], tile[24:]], axis=1)


def out_out(places, pieces):
    return call(out_out_kernel, [((96, D), F32)], [places, *pieces], 1)[0]


def block_out_kernel(places, middle, down, out_ref):
    out_ref[...] = (middle[...] + down[...].astype(F32)).astype(BF)


def block_out_of(places, middle, down, deps):
    return call(block_out_kernel, [((ROWS, D), BF)], [places, middle, down], 1, deps=deps)[0]


def body(
    inputs, norm_attn, w_query, w_key, w_value, w_out, norm_ffn, w_gate, w_up, w_down, cotangent
):
    f, s = lax.axis_index("fsdp"), lax.axis_index("sp")
    x, yh, c, z, yl = f // 4, f // 2 % 2, f % 2, s // 2, s % 2
    places = jnp.stack([x, yh, c, z, yl]).astype(jnp.int32)
    x_own, og_own = inputs[0], cotangent[0]
    gain_attn, gain_ffn = norm_attn[None], norm_ffn[None]

    index = jnp.arange(TOKENS, dtype=jnp.int32)
    positions = (index // ROWS * 2 + yl) * ROWS + index % ROWS
    lane = np.arange(QW) % HEAD_DIM
    frequency = ROPE_BASE ** (-(jnp.arange(HALF, dtype=F32) * 2.0 / HEAD_DIM))
    frequency = jnp.concatenate([frequency] * (QW // HALF))
    angles = positions.astype(F32)[:, None] * frequency[None, :]
    sign = np.where(lane < HALF, -1.0, 1.0).astype(np.float32)
    cosine, sine = jnp.cos(angles), jnp.sin(angles) * sign[None, :]

    qkv_shard, row_shard = cut(
        places, w_query, w_key, w_value, w_gate, w_up, w_down, w_out
    )
    row_mirror = mirror_y(row_shard)
    xs = two_stage_z(x_own)
    qkv_lane = stacked(
        places, two_stage_x(qkv_shard), [cosine, sine, gain_attn, xs[1], xs[3]]
    )
    qkv_other = swap_core(qkv_lane)
    ffn_pair, ffn_pair_all, out_pair = paired(places, row_shard, row_mirror, [qkv_lane])
    packed_out = gather_xc(out_pair)
    packed_ffn = gather_xc(ffn_pair_all)
    ffn_mine = two_stage_x(ffn_pair)

    normed, x_all, turned_mine, turned_sent = norm(places, gain_attn, xs)
    qkv_mirror = copied(places, [mirror_y(qkv_lane)], [normed])[0]
    mirror_other = swap_core(qkv_mirror)
    q, kv, held_qkv = qkv(
        places, normed, [qkv_lane, qkv_mirror, qkv_other, mirror_other], cosine, sine
    )
    kv_other = swap_low(kv)
    ogs = two_stage_z(copied(places, [og_own], [normed])[0])
    mixed, shares = attend(
        places, q, kv, kv_other, [ogs[1], ogs[3], ffn_mine[1], ffn_mine[3]]
    )
    mixed_pieces = two_stage_z(mixed)
    held_out = lay(places, packed_out, [mixed_pieces[3]])
    ffn_mine[2] = copied(
        places, [ffn_mine[2]], [mixed_pieces[1], mixed_pieces[3], held_out, ogs[2]]
    )[0]
    ffn_other = [swap_core(p) for p in ffn_mine]
    normed_ffn, middle_own = middle_of(places, x_all, mixed_pieces, held_out, gain_ffn)
    outs = ffn(places, normed_ffn, ogs, packed_ffn, ffn_mine, ffn_other)
    hidden, gate_grad, up_grad, og_all = outs[:4]
    in_chunks, down_part = outs[4:8], outs[8]

    in_got = scatter(in_chunks)
    ffn_sent, n_mine, h_mine = ffn_sent_of(
        places, normed_ffn, hidden, gate_grad, up_grad, og_all
    )
    back = middle_back(places, in_got, middle_own, og_own, gain_ffn, held_out, [n_mine])
    middle_grad, branch = back[:2]
    head_grads = [back[2], shift_z(back[5], -1), shift_z(back[4], 2), shift_z(back[3], 1)]
    branch_all = gather_z(branch)
    down_own = scatter_z(copied(places, [down_part], [branch])[0])
    ffn_chunks = ffn_grad(
        places, n_mine, h_mine, gate_grad, up_grad, og_all, swap_core(ffn_sent), [branch]
    )
    a_terms = over_x(ffn_chunks[:4])
    b_mine, b_got = ffn_chunks[4], mirror_y(ffn_chunks[5])

    dq, dkv_own, dkv_sent = attend_back(
        places, head_grads, q, kv, kv_other, shares, [ffn_chunks[0]]
    )
    dkv_got = swap_low(dkv_sent)
    lin, out_part, qkv_sent = turn(
        places, dq, dkv_own, dkv_got, cosine, sine, turned_sent, mixed, branch_all
    )
    qkv_got = swap_core(qkv_sent)
    first_part = first(places, lin, held_qkv)
    first_got = scatter_z(first_part)
    a_half, a_sent = x_sum(places, a_terms, COST["x_sum"], [first_part])
    a_got = mirror_y(a_sent)
    b_terms = over_x(y_sum(places, b_mine, b_got, [a_sent]))
    qkv_chunks = qkv_grad(places, lin, turned_mine, out_part, qkv_got, [a_sent])
    qkv_terms = over_x(qkv_chunks)

    ffn_half = ffn_join(places, a_half, a_got, b_terms, [qkv_chunks[0]])
    ffn_low = swap_low(ffn_half)
    qkv_half, qkv_sent = x_sum(places, qkv_terms, 2, [ffn_half])
    qkv_got = mirror_y(qkv_sent)
    ffn_total = added(places, ffn_half, ffn_low, [qkv_sent])
    ffn_pieces = pieces_z(ffn_total)
    qkv_half = added(places, qkv_half, qkv_got, [ffn_total])
    qkv_low = swap_low(qkv_half)
    qkv_total = added(places, qkv_half, qkv_low, [])
    qkv_pieces = pieces_z(qkv_total)

    block_out = block_out_of(places, middle_own, down_own, [qkv_total])
    input_grad = input_back(places, first_got, x_own, middle_grad, gain_attn, [qkv_total])
    grad_gate, grad_up, grad_down, ffn_gain = ffn_out(
        places, ffn_pieces, w_gate, w_up, [qkv_total, block_out, input_grad]
    )
    out_terms = over_x(out_slices(places, qkv_pieces, [ffn_gain]))
    grad_query, grad_key, grad_value, qkv_gain = qkv_out(
        places, qkv_pieces, w_query, w_key, w_value, [out_terms[0]]
    )
    grad_out = out_out(places, [out_terms[0], out_terms[2], out_terms[3], out_terms[1]])
    grad_norm_attn = qkv_gain[:, 0] / lax.dynamic_slice_in_dim(norm_attn, f * 96, 96, 0)
    grad_norm_ffn = ffn_gain[:, 0] / lax.dynamic_slice_in_dim(norm_ffn, f * 96, 96, 0)
    return (
        block_out[None],
        input_grad[None],
        grad_norm_attn,
        grad_query,
        grad_key,
        grad_value,
        grad_out,
        grad_norm_ffn,
        grad_gate,
        grad_up,
        grad_down,
    )


def solution(mesh):
    rows = P("fsdp", None)
    tokens = P("fsdp", "sp", None)
    return jax.shard_map(
        body,
        mesh=mesh,
        in_specs=(tokens, P(), rows, rows, rows, rows, P(), rows, rows, rows, tokens),
        out_specs=(tokens, tokens, P("fsdp"), rows, rows, rows, rows, P("fsdp"), rows, rows, rows),
        check_vma=False,
    )
```

```python
import functools

import jax
import jax.numpy as jnp
import numpy as np
from jax import lax
from jax.experimental import pallas as pl
from jax.experimental.pallas import tpu as pltpu
from jax.sharding import PartitionSpec as P

D = 1536
HEADS = 16
KV_HEADS = 8
HEAD_DIM = 96
FF = 4096

EPSILON = 1e-05
ROPE_BASE = 100000.0
MASKED = -1e30

NX, NZ = 4, 4
ROWS = 128
TOKENS = ROWS * NZ
QW, KW = 384, 192
HALF = HEAD_DIM // 2
FFZ = FF // NZ
BF = jnp.bfloat16
F32 = jnp.float32
VMEM = pl.BlockSpec(memory_space=pltpu.VMEM)
SMEM = pl.BlockSpec(memory_space=pltpu.SMEM)
ANY = pl.BlockSpec(memory_space=pl.ANY)
LIMIT = pltpu.CompilerParams(vmem_limit_bytes=56 * 1024 * 1024)
X, YH, CORE, Z, YL = range(5)
COST = {
    "norm": 54,
    "qkv": 0.1,
    "attend": 0.1,
    "lay": 0.1,
    "middle": 4,
    "ffn": 17,
    "ffn_sent": 0.1,
    "middle_back": 60,
    "ffn_grad": 60,
    "ffn_grad_second": 0.1,
    "attend_back": 60,
    "turn": 0.1,
    "first": 0.1,
    "x_sum": 60,
    "y_sum": 0.1,
    "qkv_grad": 0.1,
    "add": 8,
}


Z_GROUPS = [[z * 2 + l for z in range(NZ)] for l in range(2)]
XC_GROUPS = [[x * 4 + h * 2 + c for x in range(NX) for c in range(2)] for h in range(2)]


def scatter_z(v):
    return lax.psum_scatter(
        v, "sp", scatter_dimension=0, tiled=True, axis_index_groups=Z_GROUPS
    )


def gather_xc(v):
    return lax.all_gather(v, "fsdp", axis=0, tiled=False, axis_index_groups=XC_GROUPS)


def gather_z(v):
    return lax.all_gather(v, "sp", axis=0, tiled=True, axis_index_groups=Z_GROUPS)


def shift_z(v, step):
    pairs = [(z * 2 + l, (z + step) % NZ * 2 + l) for z in range(NZ) for l in range(2)]
    return lax.ppermute(v, "sp", pairs)


def swap_low(v):
    return lax.ppermute(v, "sp", [(s, s ^ 1) for s in range(8)])


def shift_x(v, step):
    pairs = [(x * 4 + r, (x + step) % NX * 4 + r) for x in range(NX) for r in range(4)]
    return lax.ppermute(v, "fsdp", pairs)


def swap_core(v):
    return lax.ppermute(v, "fsdp", [(f, f ^ 1) for f in range(16)])


def mirror_y(v):
    pairs = [(f * 8 + s, (f ^ 2) * 8 + (s ^ 1)) for f in range(16) for s in range(8)]
    return lax.ppermute(v, ("fsdp", "sp"), pairs)


def pieces_z(v):
    far = [shift_z(v, -1), shift_z(v, 1), shift_z(v, 2)]
    return [v, far[0], far[2], far[1]]


def two_stage_z(v):
    above, below = shift_z(v, -1), shift_z(v, 1)
    return [v, above, shift_z(below, 1), below]


def two_stage_x(v):
    above, below = shift_x(v, -1), shift_x(v, 1)
    return [v, above, shift_x(below, 1), below]


def pieces_x(v):
    far = [shift_x(v, -1), shift_x(v, 1), shift_x(v, 2)]
    return [v, far[0], far[2], far[1]]


def part(v, index, size, dim=0):
    return lax.dynamic_slice_in_dim(v, index * size, size, dim)


def call(kernel, outs, ins, us, scratch=(), deps=()):
    def run(*refs):
        kernel(*refs[: len(ins)], *refs[len(ins) + len(deps) :])

    return pl.pallas_call(
        run,
        name=kernel.__name__.replace("_kernel", ""),
        out_shape=[jax.ShapeDtypeStruct(s, t) for s, t in outs],
        in_specs=[SMEM] + [VMEM] * (len(ins) - 1) + [ANY] * len(deps),
        out_specs=[VMEM] * len(outs),
        scratch_shapes=scratch,
        compiler_params=LIMIT,
        cost_estimate=pl.CostEstimate(
            flops=int(us * 1e9), bytes_accessed=int(us * 3e6), transcendentals=0
        ),
    )(*ins, *deps)


def mm(a, b):
    return jnp.dot(a, b, preferred_element_type=F32)


def mm_t(a, b):
    return lax.dot_general(a, b, (((1,), (1,)), ((), ())), preferred_element_type=F32)


def t_mm(a, b):
    return lax.dot_general(a, b, (((0,), (0,)), ((), ())), preferred_element_type=F32)


def at_rows(index, size):
    return pl.ds(pl.multiple_of(index * size, size), size)


def rope(v, cosine, sine):
    width = v.shape[1]
    lane = lax.broadcasted_iota(jnp.int32, v.shape, 1) % HEAD_DIM
    partner = jnp.where(
        lane < HALF, pltpu.roll(v, width - HALF, 1), pltpu.roll(v, HALF, 1)
    )
    return v * cosine + partner * sine


def rope_keys(kv, cosine, sine):
    lane = lax.broadcasted_iota(jnp.int32, kv.shape, 1)
    return jnp.where(lane < KW, rope(kv, cosine, sine), kv)


def cut_kernel(places, wq, wk, wv, wg, wu, wd, wo, qkv_ref, rows_ref):
    z = places[Z]
    for t in range(3):
        cols = slice(t * 512, (t + 1) * 512)
        rows_ref[384 + 64 * t : 448 + 64 * t, :] = wd[at_rows(z, 64), cols]
        rows_ref[576 + 96 * t : 672 + 96 * t, :] = wo[:, cols]
    qkv_ref[:, :QW] = wq[:, pl.ds(pl.multiple_of(z * QW, 128), QW)]
    for at in range(NZ):

        @pl.when(z == at)
        def _():
            cols = slice(at * KW, (at + 1) * KW)
            qkv_ref[:, QW:] = jnp.concatenate([wk[:, cols], wv[:, cols]], axis=1)
            for k, w in enumerate((wg, wu)):
                for half in range(2):
                    starts = [(8 * half + i) * 256 + at * 64 for i in range(8)]
                    rows = slice((2 * half + k) * 96, (2 * half + k + 1) * 96)
                    rows_ref[rows, :] = jnp.concatenate([w[:, b : b + 64] for b in starts], axis=1)


def cut(places, *arrays):
    return call(cut_kernel, [((96, 768), BF), ((864, 512), BF)], [places, *arrays], 3)


def copy_kernel(places, *refs):
    n = len(refs) // 2
    for i in range(n):
        refs[n + i][...] = refs[i][...]


def copied(places, arrays, deps):
    return call(copy_kernel, [(v.shape, v.dtype) for v in arrays], [places, *arrays], 0.1, deps=deps)


def pair_kernel(places, own, mirror, *outs):
    n = outs[0].shape[1]
    for i, out in enumerate(outs):
        rows = slice(n * i, n * (i + 1))
        out[places[YH]] = own[rows, :]
        out[1 - places[YH]] = mirror[rows, :]


def paired(places, own, mirror, parts, deps):
    shape = (2, own.shape[0] // parts, own.shape[1])
    return call(pair_kernel, [(shape, BF)] * parts, [places, own, mirror], 0.1, deps=deps)


def norm_kernel(places, gain, og, *refs):
    xs, (normed_ref, x_ref, og_ref, mine_ref, sent_ref, turned_ref) = refs[:4], refs[4:]
    og_ref[...] = og[...]
    for i in range(NZ):
        x_ref[at_rows((places[Z] + i) % NZ, ROWS), :] = xs[i][...]
    for i in range(NZ):
        rows = pl.ds(i * ROWS, ROWS)
        v = x_ref[rows, :].astype(F32)
        r = lax.rsqrt(jnp.mean(v * v, axis=1, keepdims=True) + EPSILON)
        normed_ref[rows, :] = (v * r * gain[...]).astype(BF)
    turned_ref[...] = normed_ref[...].T
    split_cores(places, turned_ref, mine_ref, sent_ref, 96)


def split_cores(places, turned_ref, mine_ref, sent_ref, n):
    for k in range(8):
        rows = slice(k * n, (k + 1) * n)
        mine_ref[rows, :] = turned_ref[at_rows(2 * k + places[CORE], n), :]
        sent_ref[rows, :] = turned_ref[at_rows(2 * k + 1 - places[CORE], n), :]


def norm(places, gain, og, xs):
    return call(
        norm_kernel,
        [((TOKENS, D), BF)] * 2 + [((ROWS, D), BF)] + [((D // 2, TOKENS), BF)] * 2,
        [places, gain, og, *xs],
        COST["norm"],
        scratch=[pltpu.VMEM((D, TOKENS), BF)],
    )


def qkv_kernel(places, normed_ref, *refs):
    mine, other = refs[:4], refs[4:8]
    cosine, sine, q_ref, kv_ref, w_ref = refs[8:]
    for i in range(NX):
        for h in range(2):
            base = (places[X] + i) % NX * 4 + h * 2
            w_ref[at_rows(base + places[CORE], 96), :] = mine[i][h]
            w_ref[at_rows(base + 1 - places[CORE], 96), :] = other[i][h]
    for i in range(NZ):
        rows = pl.ds(i * ROWS, ROWS)
        lin = mm(normed_ref[rows, :], w_ref[...])
        q_ref[rows, :] = rope(lin[:, :QW], cosine[rows, :], sine[rows, :]).astype(BF)
        kv_ref[rows, :] = rope_keys(lin[:, QW:], cosine[rows, :], sine[rows, :]).astype(BF)


def qkv(places, normed, mine, other, cosine, sine):
    return call(
        qkv_kernel,
        [((TOKENS, QW), BF), ((TOKENS, 2 * KW), BF), ((D, QW + 2 * KW), BF)],
        [places, normed, *mine, *other, cosine, sine],
        COST["qkv"],
    )


def head(ref, rows, index):
    return ref[rows, index * HEAD_DIM : (index + 1) * HEAD_DIM]


def two_heads(ref, j, g):
    rows = slice(j * ROWS, (j + 1) * ROWS)
    return jnp.concatenate([head(ref, rows, 2 * g), head(ref, rows, 2 * g + 1)], axis=0)


def attend_kernel(places, q_ref, own_ref, other_ref, mixed_ref, p_ref):
    late = places[YL]
    factor = HEAD_DIM ** (-0.5)
    for g in range(2):
        for j in range(NZ):
            n = (j + 1) * ROWS
            q = two_heads(q_ref, j, g)
            s_own = mm_t(q, head(own_ref, slice(0, n), g)) * factor
            s_oth = mm_t(q, head(other_ref, slice(0, n), g)) * factor
            shape = (2 * ROWS, n)
            row = lax.broadcasted_iota(jnp.int32, shape, 0) % ROWS + j * ROWS
            col = lax.broadcasted_iota(jnp.int32, shape, 1)
            s_own = jnp.where(col <= row, s_own, MASKED)
            s_oth = jnp.where(col < (j + late) * ROWS, s_oth, MASKED)
            highest = jnp.maximum(
                jnp.max(s_own, axis=1, keepdims=True), jnp.max(s_oth, axis=1, keepdims=True)
            )
            p_own, p_oth = jnp.exp(s_own - highest), jnp.exp(s_oth - highest)
            total = jnp.sum(p_own, axis=1, keepdims=True) + jnp.sum(p_oth, axis=1, keepdims=True)
            scale = 1.0 / total
            p_own, p_oth = (p_own * scale).astype(BF), (p_oth * scale).astype(BF)
            p_ref[g, j, :, :n] = p_own
            p_ref[g, j, :, n : 2 * n] = p_oth
            out = mm(p_own, head(own_ref, slice(0, n), 2 + g)) + mm(
                p_oth, head(other_ref, slice(0, n), 2 + g)
            )
            out = out.astype(BF)
            for k in range(2):
                h = 2 * g + k
                mixed_ref[j * ROWS : (j + 1) * ROWS, h * HEAD_DIM : (h + 1) * HEAD_DIM] = out[
                    k * ROWS : (k + 1) * ROWS
                ]


def attend(places, q, kv, kv_other, deps):
    return call(
        attend_kernel,
        [((TOKENS, QW), BF), ((2, NZ, 2 * ROWS, 2 * TOKENS), BF)],
        [places, q, kv, kv_other],
        COST["attend"],
        deps=deps,
    )


def attend_back_kernel(places, *refs):
    grads = refs[:4]
    q_ref, own_ref, other_ref, p_ref = refs[4:8]
    dq_ref, down_ref, doth_ref = refs[8:11]
    do_ref, acc_own, acc_oth = refs[11:]
    factor = HEAD_DIM ** (-0.5)
    for i in range(NZ):
        do_ref[at_rows((places[Z] + i) % NZ, ROWS), :] = grads[i][...]
    for g in range(2):
        acc_own[...] = jnp.zeros_like(acc_own)
        acc_oth[...] = jnp.zeros_like(acc_oth)
        for j in range(NZ):
            n = (j + 1) * ROWS
            seen = slice(0, n)
            q = two_heads(q_ref, j, g)
            do = two_heads(do_ref, j, g)
            p_own, p_oth = p_ref[g, j, :, :n], p_ref[g, j, :, n : 2 * n]
            dp_own = mm_t(do, head(own_ref, seen, 2 + g))
            dp_oth = mm_t(do, head(other_ref, seen, 2 + g))
            f_own, f_oth = p_own.astype(F32), p_oth.astype(F32)
            dot = jnp.sum(f_own * dp_own, axis=1, keepdims=True) + jnp.sum(
                f_oth * dp_oth, axis=1, keepdims=True
            )
            ds_own = (f_own * (dp_own - dot)).astype(BF)
            ds_oth = (f_oth * (dp_oth - dot)).astype(BF)
            dq = mm(ds_own, head(own_ref, seen, g)) + mm(ds_oth, head(other_ref, seen, g))
            dq = (dq * factor).astype(BF)
            for k in range(2):
                h = 2 * g + k
                dq_ref[j * ROWS : (j + 1) * ROWS, h * HEAD_DIM : (h + 1) * HEAD_DIM] = dq[
                    k * ROWS : (k + 1) * ROWS
                ]
            acc_own[0, seen, :] += t_mm(ds_own, q)
            acc_own[1, seen, :] += t_mm(p_own, do)
            acc_oth[0, seen, :] += t_mm(ds_oth, q)
            acc_oth[1, seen, :] += t_mm(p_oth, do)
        for kind, scale in ((0, factor), (1, 1.0)):
            at = kind * KW + g * HEAD_DIM
            down_ref[:, at : at + HEAD_DIM] = acc_own[kind] * scale
            doth_ref[:, at : at + HEAD_DIM] = (acc_oth[kind] * scale).astype(BF)


def attend_back(places, grads, q, kv, kv_other, shares, deps):
    acc = pltpu.VMEM((2, TOKENS, HEAD_DIM), F32)
    return call(
        attend_back_kernel,
        [((TOKENS, QW), BF), ((TOKENS, 2 * KW), F32), ((TOKENS, 2 * KW), BF)],
        [places, *grads, q, kv, kv_other, shares],
        COST["attend_back"],
        scratch=[pltpu.VMEM((TOKENS, QW), BF), acc, acc],
        deps=deps,
    )


def send_chunks(refs, acc_ref, places):
    for i in range(NZ):
        rows = at_rows((places[Z] + i) % NZ, ROWS)
        refs[i][...] = acc_ref[rows, :].astype(refs[i].dtype)


CHUNKS = [((ROWS, D), F32)] + [((ROWS, D), BF)] * 3


def put_out(out_ref, places, core, ref):
    for k in range(8):
        rows = pl.ds(pl.multiple_of((k % 2 * 2 + core) * 96 + k // 2 * 24, 8), 24)
        tile = out_ref[rows, :]
        ref[k, 96:, :] = jnp.concatenate([tile[:, :768], tile[:, 768:]], axis=0).astype(BF)


def turn_kernel(
    places, dq_ref, own_ref, got_ref, cosine, sine, turned_ref, mixed_ref, branch_ref, *refs
):
    lin_ref, out_ref, sent_ref = refs
    for i in range(NZ):
        rows = slice(i * ROWS, (i + 1) * ROWS)
        dkv = (own_ref[rows, :] + got_ref[rows, :].astype(F32)).astype(BF)
        c, s = cosine[rows, :], -sine[rows, :]
        lin_ref[rows, :QW] = rope(dq_ref[rows, :].astype(F32), c, s).astype(BF)
        lin_ref[rows, QW:] = rope_keys(dkv.astype(F32), c, s).astype(BF)
    for k in range(8):
        sent_ref[k, :96, :] = mm(turned_ref[k * 96 : (k + 1) * 96, :], lin_ref[...]).astype(BF)
    out_ref[...] = t_mm(mixed_ref[...], branch_ref[...])
    put_out(out_ref, places, 1 - places[CORE], sent_ref)


def turn(places, dq, dkv_own, dkv_got, cosine, sine, turned, mixed, branch, deps):
    return call(
        turn_kernel,
        [((TOKENS, 768), BF), ((QW, D), F32), ((8, 144, 768), BF)],
        [places, dq, dkv_own, dkv_got, cosine, sine, turned, mixed, branch],
        COST["turn"],
        deps=deps,
    )


def first_kernel(places, lin_ref, w_ref, out_ref):
    out_ref[...] = mm_t(lin_ref[...], w_ref[...]).astype(BF)


def first(places, lin, w):
    return call(first_kernel, [((TOKENS, D), BF)], [places, lin, w], COST["first"])[0]


def qkv_grad_kernel(places, lin_ref, turned_ref, out_ref, got_ref, *refs):
    outs, sum_ref = refs[:4], refs[4]
    for k in range(8):
        sum_ref[k, :96, :] = mm(turned_ref[k * 96 : (k + 1) * 96, :], lin_ref[...]).astype(BF)
    put_out(out_ref, places, places[CORE], sum_ref)
    for i in range(NX):
        for k in range(2):
            at = (places[X] + i) % NX * 2 + (places[YH] + k) % 2
            outs[i][k] = (sum_ref[at].astype(F32) + got_ref[at].astype(F32)).astype(BF)


def qkv_grad(places, lin, turned, out, got, deps):
    return call(
        qkv_grad_kernel,
        [((2, 144, 768), BF)] * 4,
        [places, lin, turned, out, got],
        COST["qkv_grad"],
        scratch=[pltpu.VMEM((8, 144, 768), BF)],
        deps=deps,
    )


def lay_kernel(places, packed, out_ref):
    for b in range(16):
        for t in range(3):
            out_ref[b * 96 : (b + 1) * 96, t * 512 : (t + 1) * 512] = packed[
                b // 4 * 2 + b % 2, b // 2 % 2, t * 96 : (t + 1) * 96, :
            ]


def lay(places, packed, deps):
    return call(lay_kernel, [((D, D), BF)], [places, packed], COST["lay"], deps=deps)[0]


def middle_kernel(
    places, x_ref, m0, m1, m2, m3, w_ref, gain, normed_ref, own_ref, acc_ref, mixed_ref
):
    for i, ref in enumerate((m0, m1, m2, m3)):
        at = pl.multiple_of((places[Z] + i) % NZ * QW, QW)
        mixed_ref[:, pl.ds(at, QW)] = ref[...]
    for t in range(3):
        cols = slice(t * 512, (t + 1) * 512)
        acc_ref[:, cols] = x_ref[:, cols].astype(F32) + mm(mixed_ref[...], w_ref[:, cols])
    for i in range(NZ):
        rows = slice(i * ROWS, (i + 1) * ROWS)
        v = acc_ref[rows, :]
        r = lax.rsqrt(jnp.mean(v * v, axis=1, keepdims=True) + EPSILON)
        normed_ref[rows, :] = (v * r * gain[...]).astype(BF)
    own_ref[...] = acc_ref[at_rows(places[Z], ROWS), :]


def middle_of(places, x_all, pieces, w_out, gain):
    return call(
        middle_kernel,
        [((TOKENS, D), BF), ((ROWS, D), F32)],
        [places, x_all, *pieces, w_out, gain],
        COST["middle"],
        scratch=[pltpu.VMEM((TOKENS, D), F32), pltpu.VMEM((TOKENS, D), BF)],
    )


def ffn_kernel(places, n_ref, packed_ref, *refs):
    ogs, mine, other, refs = refs[:4], refs[4:8], refs[8:12], refs[12:]
    hidden_ref, gg_ref, ug_ref, og_ref = refs[:4]
    in_chunks, down_ref = refs[4:8], refs[8]
    in_acc, down_acc, wg_ref, wu_ref, wd_ref = refs[9:]
    for i, g in enumerate(ogs):
        og_ref[at_rows((places[Z] + i) % NZ, ROWS), :] = g[...]

    def from_pieces(out_ref, start):
        for i in range(NX):
            for h in range(2):
                base = (places[X] + i) % NX * 4 + h * 2
                for pieces, core in ((mine, places[CORE]), (other, 1 - places[CORE])):
                    out_ref[at_rows(base + core, 96), :] = pieces[i][h, start : start + 96, :]

    for j in range(2):
        cols = slice(j * 512, (j + 1) * 512)
        from_pieces(wg_ref, 192 * j)
        if j == 0:
            from_pieces(wu_ref, 96)
        for b in range(16):
            packed = packed_ref.at[b // 4 * 2 + b % 2, b // 2 % 2]
            if j == 1:
                wu_ref[b * 96 : (b + 1) * 96, :] = packed[:96, :]
            if b // 8 == j:
                rows = slice(b % 8 * 64, b % 8 * 64 + 64)
                for t in range(3):
                    wd_ref[rows, t * 512 : (t + 1) * 512] = packed[96 + 64 * t : 160 + 64 * t, :]
        wg, wu, wd = wg_ref[...], wu_ref[...], wd_ref[...]
        gate = mm(n_ref[...], wg)
        up = mm(n_ref[...], wu)
        hg = mm_t(og_ref[...], wd).astype(BF).astype(F32)
        sig = 1.0 / (1.0 + jnp.exp(-gate))
        silu = gate * sig
        hidden = (silu * up).astype(BF)
        gg = (hg * up * (sig * (1.0 + gate * (1.0 - sig)))).astype(BF)
        ug = (hg * silu).astype(BF)
        hidden_ref[:, cols] = hidden
        gg_ref[:, cols] = gg
        ug_ref[:, cols] = ug
        if j == 0:
            in_acc[...] = mm_t(gg, wg) + mm_t(ug, wu)
            down_acc[...] = mm(hidden, wd)
        else:
            in_acc[...] += mm_t(gg, wg) + mm_t(ug, wu)
            down_ref[...] = (down_acc[...] + mm(hidden, wd)).astype(BF)
    send_chunks(in_chunks, in_acc, places)


def ffn(places, normed, ogs, packed, mine, other):
    return call(
        ffn_kernel,
        [((TOKENS, FFZ), BF)] * 3 + [((TOKENS, D), BF)] + CHUNKS + [((TOKENS, D), BF)],
        [places, normed, packed, *ogs, *mine, *other],
        COST["ffn"],
        scratch=[pltpu.VMEM((TOKENS, D), F32)] * 2
        + [pltpu.VMEM((D, 512), BF)] * 2
        + [pltpu.VMEM((512, D), BF)],
    )


def ffn_terms(n_ref, h_ref, gg_ref, ug_ref, og_ref, cols, put):
    for w, ref in enumerate((gg_ref, ug_ref)):
        for half in range(2):
            tile = mm(n_ref[...], ref[:, half * 512 + cols.start : half * 512 + cols.stop])
            r = (2 * w + half) * 96
            put(slice(r, r + 96), tile.reshape(8, 96, -1))
    for t in range(3):
        tile = mm(h_ref[...], og_ref[:, t * 512 + cols.start : t * 512 + cols.stop])
        put(slice(384 + 64 * t, 448 + 64 * t), tile.reshape(8, 64, -1))


def ffn_sent_kernel(places, n_ref, hidden_ref, gg_ref, ug_ref, og_ref, *refs):
    sent_ref, n_mine, h_mine, n_turned, h_turned, n_sent, h_sent = refs
    n_turned[...] = n_ref[...].T
    h_turned[...] = hidden_ref[...].T
    split_cores(places, n_turned, n_mine, n_sent, 96)
    split_cores(places, h_turned, h_mine, h_sent, 64)

    def put(rows, tile):
        sent_ref[:, rows, :] = tile.astype(BF)

    ffn_terms(n_sent, h_sent, gg_ref, ug_ref, og_ref, slice(0, 512), put)


def ffn_sent_of(places, normed, hidden, gg, ug, og):
    return call(
        ffn_sent_kernel,
        [((8, 576, 512), BF), ((D // 2, TOKENS), BF), ((FFZ // 2, TOKENS), BF)],
        [places, normed, hidden, gg, ug, og],
        COST["ffn_sent"],
        scratch=[
            pltpu.VMEM((D, TOKENS), BF),
            pltpu.VMEM((FFZ, TOKENS), BF),
            pltpu.VMEM((D // 2, TOKENS), BF),
            pltpu.VMEM((FFZ // 2, TOKENS), BF),
        ],
    )


def ffn_grad_kernel(cols, places, n_ref, h_ref, gg_ref, ug_ref, og_ref, got_ref, *refs):
    outs, sum_ref = refs[:-1], refs[-1]

    def put(rows, tile):
        sum_ref[:, rows, :] = (tile + got_ref[:, rows, cols].astype(F32)).astype(BF)

    ffn_terms(n_ref, h_ref, gg_ref, ug_ref, og_ref, cols, put)
    for i in range(NX):
        for k in range(2):
            at = (places[X] + i) % NX * 2 + (places[YH] + k) % 2
            if len(outs) == 4:
                outs[i][k] = sum_ref[at]
            else:
                outs[k][i] = sum_ref[at]


def ffn_grad_first_kernel(*refs):
    ffn_grad_kernel(slice(0, 256), *refs[:7], *refs[8:12], refs[13])
    refs[12][...] = refs[7][...]


def ffn_grad_second_kernel(*refs):
    ffn_grad_kernel(slice(256, 512), *refs)


def ffn_grad_first(places, args, down_part, deps):
    return call(
        ffn_grad_first_kernel,
        [((2, 576, 256), BF)] * 4 + [((TOKENS, D), BF)],
        [places, *args, down_part],
        COST["ffn_grad"],
        scratch=[pltpu.VMEM((8, 576, 256), BF)],
        deps=deps,
    )


def ffn_grad_second(places, args, deps):
    return call(
        ffn_grad_second_kernel,
        [((4, 576, 256), BF)] * 2,
        [places, *args],
        COST["ffn_grad_second"],
        scratch=[pltpu.VMEM((8, 576, 256), BF)],
        deps=deps,
    )


def y_sum_kernel(places, mine, got, *outs):
    for i in range(NX):
        outs[i][...] = (mine[i].astype(F32) + got[i].astype(F32)).astype(BF)


def y_sum(places, mine, got, deps):
    return call(
        y_sum_kernel,
        [(mine.shape[1:], BF)] * 4,
        [places, mine, got],
        COST["y_sum"],
        deps=deps,
    )


def ffn_join_kernel(places, mine, got, a, b, c, d, out):
    out[:, :256] = (mine[...] + got[...].astype(F32)).astype(BF)
    total = a[...].astype(F32) + b[...].astype(F32) + c[...].astype(F32) + d[...].astype(F32)
    out[:, 256:] = total.astype(BF)


def ffn_join(places, mine, got, terms, deps):
    return call(
        ffn_join_kernel,
        [((576, 512), BF)],
        [places, mine, got, *terms],
        COST["add"],
        deps=deps,
    )[0]


def rms_back(grad, v, gain):
    r = lax.rsqrt(jnp.mean(v * v, axis=1, keepdims=True) + EPSILON)
    pulled = grad * gain
    return r * pulled - v * (r * r * r * jnp.mean(pulled * v, axis=1, keepdims=True))


def middle_back_kernel(places, own, g1, g2, g3, middle, og, gain, w_ref, mid_ref, branch_ref, *outs):
    grad = own[...] + g1[...].astype(F32) + g2[...].astype(F32) + g3[...].astype(F32)
    mid = og[...].astype(F32) + rms_back(grad, middle[...], gain[...])
    mid_ref[...] = mid
    branch = mid.astype(BF)
    branch_ref[...] = branch
    for i in range(NZ):
        outs[i][...] = mm_t(branch, w_ref[at_rows((places[Z] + i) % NZ, QW), :]).astype(BF)


def middle_back(places, chunks, middle, og, gain, w_out, deps):
    return call(
        middle_back_kernel,
        [((ROWS, D), F32), ((ROWS, D), BF)] + [((ROWS, QW), BF)] * 4,
        [places, *chunks, middle, og, gain, w_out],
        COST["middle_back"],
        deps=deps,
    )


def input_back_kernel(places, grad, x, mid, gain, out_ref):
    out_ref[...] = mid[...] + rms_back(grad[...].astype(F32), x[...].astype(F32), gain[...])


def input_back(places, grad, x, mid, gain, deps):
    return call(
        input_back_kernel, [((ROWS, D), F32)], [places, grad, x, mid, gain], 2, deps=deps
    )[0]


def scatter(chunks):
    far = [shift_z(chunks[1], 1), shift_z(chunks[3], -1), shift_z(chunks[2], 2)]
    return [chunks[0], *far]


def x_sum_kernel(places, a, b, c, d, mine, sent):
    mine[...] = a[0].astype(F32) + b[0].astype(F32) + c[0].astype(F32) + d[0].astype(F32)
    total = a[1].astype(F32) + b[1].astype(F32) + c[1].astype(F32) + d[1].astype(F32)
    sent[...] = total.astype(BF)


def x_sum(places, terms, us, deps):
    shape = terms[0].shape[1:]
    return call(x_sum_kernel, [(shape, F32), (shape, BF)], [places, *terms], us, deps=deps)


def add_kernel(places, a, b, out):
    out[...] = (a[...].astype(F32) + b[...].astype(F32)).astype(BF)


def added(places, a, b, deps):
    return call(add_kernel, [(a.shape, BF)], [places, a, b], COST["add"], deps=deps)[0]


def over_x(chunks):
    far = [shift_x(chunks[1], 1), shift_x(chunks[3], -1), shift_x(chunks[2], 2)]
    return [chunks[0], *far]


def ffn_out_kernel(places, p0, p1, p2, p3, wg, wu, gate_ref, up_ref, down_ref, gain_ref, all_ref):
    for i, p in enumerate((p0, p1, p2, p3)):
        all_ref[(places[Z] + i) % NZ] = p[...]
    gain = jnp.zeros((96, 1), F32)
    for k, (w, out) in enumerate(((wg, gate_ref), (wu, up_ref))):
        for b in range(16):
            rows = slice((2 * k + b // 8) * 96, (2 * k + b // 8 + 1) * 96)
            cols = slice(b % 8 * 64, b % 8 * 64 + 64)
            tile = jnp.concatenate([all_ref[q, rows, cols].astype(F32) for q in range(NZ)], axis=1)
            out[:, b * 256 : (b + 1) * 256] = tile
            gain += jnp.sum(
                tile * w[:, b * 256 : (b + 1) * 256].astype(F32), axis=1, keepdims=True
            )
    for q in range(NZ):
        for t in range(3):
            r = 384 + 64 * t
            down_ref[q * 64 : (q + 1) * 64, t * 512 : (t + 1) * 512] = all_ref[
                q, r : r + 64, :
            ].astype(F32)
    gain_ref[...] = gain


def ffn_out(places, pieces, wg, wu, deps):
    return call(
        ffn_out_kernel,
        [((96, FF), F32), ((96, FF), F32), ((256, D), F32), ((96, 1), F32)],
        [places, *pieces, wg, wu],
        4,
        scratch=[pltpu.VMEM((NZ, 576, 512), BF)],
        deps=deps,
    )


def out_slices_kernel(places, p0, p1, p2, p3, *refs):
    all_ref = refs[4]
    for i, p in enumerate((p0, p1, p2, p3)):
        all_ref[(places[Z] + i) % NZ] = p[96:, :]
    for i in range(NX):
        refs[i][...] = all_ref[(places[X] + i) % NX]


def out_slices(places, pieces, deps):
    return call(
        out_slices_kernel,
        [((48, 768), BF)] * 4,
        [places, *pieces],
        1,
        scratch=[pltpu.VMEM((NZ, 48, 768), BF)],
        deps=deps,
    )


def qkv_out_kernel(places, p0, p1, p2, p3, wq, wk, wv, q_ref, k_ref, v_ref, gain_ref, all_ref):
    for i, p in enumerate((p0, p1, p2, p3)):
        all_ref[(places[Z] + i) % NZ] = p[:96, :]
    for q in range(NZ):
        q_ref[:, q * QW : (q + 1) * QW] = all_ref[q, :, :QW].astype(F32)
    gain = jnp.sum(q_ref[...] * wq[...].astype(F32), axis=1, keepdims=True)
    for out, w, at in ((k_ref, wk, QW), (v_ref, wv, QW + KW)):
        tile = jnp.concatenate(
            [all_ref[q, :, at : at + KW].astype(F32) for q in range(NZ)], axis=1
        )
        out[...] = tile
        gain += jnp.sum(tile * w[...].astype(F32), axis=1, keepdims=True)
    gain_ref[...] = gain


def qkv_out(places, pieces, wq, wk, wv, deps):
    return call(
        qkv_out_kernel,
        [((96, 1536), F32), ((96, 768), F32), ((96, 768), F32), ((96, 1), F32)],
        [places, *pieces, wq, wk, wv],
        2,
        scratch=[pltpu.VMEM((NZ, 96, 768), BF)],
        deps=deps,
    )


def out_out_kernel(places, p0, p1, p2, p3, out_ref):
    for i, p in enumerate((p0, p1, p2, p3)):
        tile = p[...].astype(F32)
        rows = pl.ds(pl.multiple_of((places[X] + i) % NX * 24, 8), 24)
        out_ref[rows, :] = jnp.concatenate([tile[:24], tile[24:]], axis=1)


def out_out(places, pieces):
    return call(out_out_kernel, [((96, D), F32)], [places, *pieces], 1)[0]


def block_out_kernel(places, middle, down, out_ref):
    out_ref[...] = (middle[...] + down[...].astype(F32)).astype(BF)


def block_out_of(places, middle, down, deps):
    return call(block_out_kernel, [((ROWS, D), BF)], [places, middle, down], 1, deps=deps)[0]


def body(
    inputs, norm_attn, w_query, w_key, w_value, w_out, norm_ffn, w_gate, w_up, w_down, cotangent
):
    f, s = lax.axis_index("fsdp"), lax.axis_index("sp")
    x, yh, c, z, yl = f // 4, f // 2 % 2, f % 2, s // 2, s % 2
    places = jnp.stack([x, yh, c, z, yl]).astype(jnp.int32)
    x_own, og_own = inputs[0], cotangent[0]
    gain_attn, gain_ffn = norm_attn[None], norm_ffn[None]

    index = jnp.arange(TOKENS, dtype=jnp.int32)
    positions = (index // ROWS * 2 + yl) * ROWS + index % ROWS
    lane = np.arange(QW) % HEAD_DIM
    frequency = ROPE_BASE ** (-(jnp.arange(HALF, dtype=F32) * 2.0 / HEAD_DIM))
    frequency = jnp.concatenate([frequency] * (QW // HALF))
    angles = positions.astype(F32)[:, None] * frequency[None, :]
    sign = np.where(lane < HALF, -1.0, 1.0).astype(np.float32)
    cosine, sine = jnp.cos(angles), jnp.sin(angles) * sign[None, :]

    qkv_shard, row_shard = cut(
        places, w_query, w_key, w_value, w_gate, w_up, w_down, w_out
    )
    qkv_mirror, row_mirror = mirror_y(qkv_shard), mirror_y(row_shard)
    xs = two_stage_z(x_own)
    (qkv_pair,) = paired(places, qkv_shard, qkv_mirror, 1, [cosine, sine, gain_attn])
    qkv_mine = two_stage_x(qkv_pair)
    qkv_other = [swap_core(p) for p in qkv_mine]
    ffn_pair, ffn_pair_all, out_pair = paired(
        places, row_shard, row_mirror, 3, [qkv_mine[1], qkv_mine[2], xs[1], xs[2]]
    )
    packed_out = gather_xc(out_pair)
    packed_ffn = gather_xc(ffn_pair_all)
    ffn_mine = two_stage_x(ffn_pair)

    normed, x_all, og_copy, turned_mine, turned_sent = norm(places, gain_attn, og_own, xs)
    ogs = two_stage_z(og_copy)
    q, kv, held_qkv = qkv(places, normed, qkv_mine, qkv_other, cosine, sine)
    kv_other = swap_low(kv)
    mixed, shares = attend(
        places, q, kv, kv_other, [ogs[1], ogs[2], ffn_mine[1], ffn_mine[3]]
    )
    mixed_pieces = two_stage_z(mixed)
    held_out = lay(places, packed_out, [mixed_pieces[3]])
    ffn_mine[2] = copied(
        places, [ffn_mine[2]], [mixed_pieces[1], mixed_pieces[3], held_out, ogs[2]]
    )[0]
    ffn_other = [swap_core(p) for p in ffn_mine]
    normed_ffn, middle_own = middle_of(places, x_all, mixed_pieces, held_out, gain_ffn)
    outs = ffn(places, normed_ffn, ogs, packed_ffn, ffn_mine, ffn_other)
    hidden, gate_grad, up_grad, og_all = outs[:4]
    in_chunks, down_part = outs[4:8], outs[8]

    in_got = scatter(in_chunks)
    ffn_sent, n_mine, h_mine = ffn_sent_of(
        places, normed_ffn, hidden, gate_grad, up_grad, og_all
    )
    back = middle_back(places, in_got, middle_own, og_own, gain_ffn, held_out, [n_mine])
    middle_grad, branch = back[:2]
    head_grads = [back[2], shift_z(back[5], -1), shift_z(back[4], 2), shift_z(back[3], 1)]
    branch_all = gather_z(branch)
    ffn_got = swap_core(ffn_sent)
    ffn_args = (n_mine, h_mine, gate_grad, up_grad, og_all, ffn_got)
    a_chunks = ffn_grad_first(places, ffn_args, down_part, [branch])
    a_terms = over_x(a_chunks[:4])
    down_own = scatter_z(a_chunks[4])

    dq, dkv_own, dkv_sent = attend_back(
        places, head_grads, q, kv, kv_other, shares, [a_chunks[0]]
    )
    b_mine, b_sent = ffn_grad_second(places, ffn_args, [dq])
    b_got = mirror_y(b_sent)
    dkv_got = swap_low(dkv_sent)
    lin, out_part, qkv_sent = turn(
        places, dq, dkv_own, dkv_got, cosine, sine, turned_sent, mixed, branch_all, [b_sent]
    )
    qkv_got = swap_core(qkv_sent)
    first_part = first(places, lin, held_qkv)
    first_got = scatter_z(first_part)
    a_half, a_sent = x_sum(places, a_terms, COST["x_sum"], [first_part])
    a_got = mirror_y(a_sent)
    qkv_chunks = qkv_grad(places, lin, turned_mine, out_part, qkv_got, [a_sent])
    qkv_terms = over_x(qkv_chunks)
    b_terms = over_x(y_sum(places, b_mine, b_got, [qkv_chunks[0]]))

    qkv_half, qkv_sent = x_sum(places, qkv_terms, 2, [])
    qkv_got = mirror_y(qkv_sent)
    ffn_half = ffn_join(places, a_half, a_got, b_terms, [qkv_sent])
    ffn_low = swap_low(ffn_half)
    qkv_half = added(places, qkv_half, qkv_got, [ffn_half])
    qkv_low = swap_low(qkv_half)
    qkv_total = added(places, qkv_half, qkv_low, [])
    qkv_pieces = pieces_z(qkv_total)
    ffn_total = added(places, ffn_half, ffn_low, [qkv_total])
    ffn_pieces = pieces_z(ffn_total)

    block_out = block_out_of(places, middle_own, down_own, [qkv_total])
    input_grad = input_back(places, first_got, x_own, middle_grad, gain_attn, [qkv_total])
    out_terms = over_x(out_slices(places, qkv_pieces, [block_out, input_grad]))
    grad_query, grad_key, grad_value, qkv_gain = qkv_out(
        places, qkv_pieces, w_query, w_key, w_value, [out_terms[0]]
    )
    grad_gate, grad_up, grad_down, ffn_gain = ffn_out(
        places, ffn_pieces, w_gate, w_up, [qkv_gain]
    )
    grad_out = out_out(places, [out_terms[0], out_terms[2], out_terms[3], out_terms[1]])
    grad_norm_attn = qkv_gain[:, 0] / lax.dynamic_slice_in_dim(norm_attn, f * 96, 96, 0)
    grad_norm_ffn = ffn_gain[:, 0] / lax.dynamic_slice_in_dim(norm_ffn, f * 96, 96, 0)
    return (
        block_out[None],
        input_grad[None],
        grad_norm_attn,
        grad_query,
        grad_key,
        grad_value,
        grad_out,
        grad_norm_ffn,
        grad_gate,
        grad_up,
        grad_down,
    )


def solution(mesh):
    rows = P("fsdp", None)
    tokens = P("fsdp", "sp", None)
    return jax.shard_map(
        body,
        mesh=mesh,
        in_specs=(tokens, P(), rows, rows, rows, rows, P(), rows, rows, rows, tokens),
        out_specs=(tokens, tokens, P("fsdp"), rows, rows, rows, rows, P("fsdp"), rows, rows, rows),
        check_vma=False,
    )
```

```python
import functools

import jax
import jax.numpy as jnp
import numpy as np
from jax import lax
from jax.experimental import pallas as pl
from jax.experimental.pallas import tpu as pltpu
from jax.sharding import PartitionSpec as P

D = 1536
HEADS = 16
KV_HEADS = 8
HEAD_DIM = 96
FF = 4096

EPSILON = 1e-05
ROPE_BASE = 100000.0
MASKED = -1e30

NX, NZ = 4, 4
ROWS = 128
TOKENS = ROWS * NZ
QW, KW = 384, 192
HALF = HEAD_DIM // 2
FFZ = FF // NZ
BF = jnp.bfloat16
F32 = jnp.float32
VMEM = pl.BlockSpec(memory_space=pltpu.VMEM)
SMEM = pl.BlockSpec(memory_space=pltpu.SMEM)
ANY = pl.BlockSpec(memory_space=pl.ANY)
LIMIT = pltpu.CompilerParams(vmem_limit_bytes=56 * 1024 * 1024)
X, YH, CORE, Z, YL = range(5)
COST = {
    "norm": 54,
    "qkv": 0.1,
    "attend": 0.1,
    "lay": 0.1,
    "middle": 4,
    "ffn": 17,
    "ffn_sent": 0.1,
    "middle_back": 60,
    "ffn_grad": 60,
    "ffn_grad_second": 0.1,
    "attend_back": 60,
    "turn": 0.1,
    "first": 0.1,
    "x_sum": 60,
    "y_sum": 100,
    "qkv_grad": 0.1,
    "add": 8,
}


Z_GROUPS = [[z * 2 + l for z in range(NZ)] for l in range(2)]
X_GROUPS = [[x * 4 + r for x in range(NX)] for r in range(4)]
XC_GROUPS = [[x * 4 + h * 2 + c for x in range(NX) for c in range(2)] for h in range(2)]


def scatter_z(v):
    return lax.psum_scatter(
        v, "sp", scatter_dimension=0, tiled=True, axis_index_groups=Z_GROUPS
    )


def gather_xc(v):
    return lax.all_gather(v, "fsdp", axis=0, tiled=False, axis_index_groups=XC_GROUPS)


def scatter_x(v):
    return lax.psum_scatter(
        v, "fsdp", scatter_dimension=0, tiled=True, axis_index_groups=X_GROUPS
    )


def gather_z(v):
    return lax.all_gather(v, "sp", axis=0, tiled=True, axis_index_groups=Z_GROUPS)


def shift_z(v, step):
    pairs = [(z * 2 + l, (z + step) % NZ * 2 + l) for z in range(NZ) for l in range(2)]
    return lax.ppermute(v, "sp", pairs)


def swap_low(v):
    return lax.ppermute(v, "sp", [(s, s ^ 1) for s in range(8)])


def shift_x(v, step):
    pairs = [(x * 4 + r, (x + step) % NX * 4 + r) for x in range(NX) for r in range(4)]
    return lax.ppermute(v, "fsdp", pairs)


def swap_core(v):
    return lax.ppermute(v, "fsdp", [(f, f ^ 1) for f in range(16)])


def mirror_y(v):
    pairs = [(f * 8 + s, (f ^ 2) * 8 + (s ^ 1)) for f in range(16) for s in range(8)]
    return lax.ppermute(v, ("fsdp", "sp"), pairs)


def pieces_z(v):
    far = [shift_z(v, -1), shift_z(v, 1), shift_z(v, 2)]
    return [v, far[0], far[2], far[1]]


def two_stage_z(v):
    above, below = shift_z(v, -1), shift_z(v, 1)
    return [v, above, shift_z(below, 1), below]


def two_stage_x(v):
    above, below = shift_x(v, -1), shift_x(v, 1)
    return [v, above, shift_x(below, 1), below]


def pieces_x(v):
    far = [shift_x(v, -1), shift_x(v, 1), shift_x(v, 2)]
    return [v, far[0], far[2], far[1]]


def part(v, index, size, dim=0):
    return lax.dynamic_slice_in_dim(v, index * size, size, dim)


def call(kernel, outs, ins, us, scratch=(), deps=()):
    def run(*refs):
        kernel(*refs[: len(ins)], *refs[len(ins) + len(deps) :])

    return pl.pallas_call(
        run,
        name=kernel.__name__.replace("_kernel", ""),
        out_shape=[jax.ShapeDtypeStruct(s, t) for s, t in outs],
        in_specs=[SMEM] + [VMEM] * (len(ins) - 1) + [ANY] * len(deps),
        out_specs=[VMEM] * len(outs),
        scratch_shapes=scratch,
        compiler_params=LIMIT,
        cost_estimate=pl.CostEstimate(
            flops=int(us * 1e9), bytes_accessed=int(us * 3e6), transcendentals=0
        ),
    )(*ins, *deps)


def mm(a, b):
    return jnp.dot(a, b, preferred_element_type=F32)


def mm_t(a, b):
    return lax.dot_general(a, b, (((1,), (1,)), ((), ())), preferred_element_type=F32)


def t_mm(a, b):
    return lax.dot_general(a, b, (((0,), (0,)), ((), ())), preferred_element_type=F32)


def at_rows(index, size):
    return pl.ds(pl.multiple_of(index * size, size), size)


def rope(v, cosine, sine):
    width = v.shape[1]
    lane = lax.broadcasted_iota(jnp.int32, v.shape, 1) % HEAD_DIM
    partner = jnp.where(
        lane < HALF, pltpu.roll(v, width - HALF, 1), pltpu.roll(v, HALF, 1)
    )
    return v * cosine + partner * sine


def rope_keys(kv, cosine, sine):
    lane = lax.broadcasted_iota(jnp.int32, kv.shape, 1)
    return jnp.where(lane < KW, rope(kv, cosine, sine), kv)


def cut_kernel(places, wq, wk, wv, wg, wu, wd, wo, qkv_ref, rows_ref):
    z = places[Z]
    for t in range(3):
        cols = slice(t * 512, (t + 1) * 512)
        rows_ref[384 + 64 * t : 448 + 64 * t, :] = wd[at_rows(z, 64), cols]
        rows_ref[576 + 96 * t : 672 + 96 * t, :] = wo[:, cols]
    qkv_ref[:, :QW] = wq[:, pl.ds(pl.multiple_of(z * QW, 128), QW)]
    for at in range(NZ):

        @pl.when(z == at)
        def _():
            cols = slice(at * KW, (at + 1) * KW)
            qkv_ref[:, QW:] = jnp.concatenate([wk[:, cols], wv[:, cols]], axis=1)
            for k, w in enumerate((wg, wu)):
                for half in range(2):
                    starts = [(8 * half + i) * 256 + at * 64 for i in range(8)]
                    rows = slice((2 * half + k) * 96, (2 * half + k + 1) * 96)
                    rows_ref[rows, :] = jnp.concatenate([w[:, b : b + 64] for b in starts], axis=1)


def cut(places, *arrays):
    return call(cut_kernel, [((96, 768), BF), ((864, 512), BF)], [places, *arrays], 3)


def copy_kernel(places, *refs):
    n = len(refs) // 2
    for i in range(n):
        refs[n + i][...] = refs[i][...]


def copied(places, arrays, deps):
    return call(copy_kernel, [(v.shape, v.dtype) for v in arrays], [places, *arrays], 0.1, deps=deps)


def pair_kernel(places, own, mirror, *outs):
    n = outs[0].shape[1]
    for i, out in enumerate(outs):
        rows = slice(n * i, n * (i + 1))
        out[places[YH]] = own[rows, :]
        out[1 - places[YH]] = mirror[rows, :]


def paired(places, own, mirror, parts, deps):
    shape = (2, own.shape[0] // parts, own.shape[1])
    return call(pair_kernel, [(shape, BF)] * parts, [places, own, mirror], 0.1, deps=deps)


def norm_kernel(places, gain, og, *refs):
    xs, (normed_ref, x_ref, og_ref, mine_ref, sent_ref, turned_ref) = refs[:4], refs[4:]
    og_ref[...] = og[...]
    for i in range(NZ):
        x_ref[at_rows((places[Z] + i) % NZ, ROWS), :] = xs[i][...]
    for i in range(NZ):
        rows = pl.ds(i * ROWS, ROWS)
        v = x_ref[rows, :].astype(F32)
        r = lax.rsqrt(jnp.mean(v * v, axis=1, keepdims=True) + EPSILON)
        normed_ref[rows, :] = (v * r * gain[...]).astype(BF)
    turned_ref[...] = normed_ref[...].T
    split_cores(places, turned_ref, mine_ref, sent_ref, 96)


def split_cores(places, turned_ref, mine_ref, sent_ref, n):
    for k in range(8):
        rows = slice(k * n, (k + 1) * n)
        mine_ref[rows, :] = turned_ref[at_rows(2 * k + places[CORE], n), :]
        sent_ref[rows, :] = turned_ref[at_rows(2 * k + 1 - places[CORE], n), :]


def norm(places, gain, og, xs):
    return call(
        norm_kernel,
        [((TOKENS, D), BF)] * 2 + [((ROWS, D), BF)] + [((D // 2, TOKENS), BF)] * 2,
        [places, gain, og, *xs],
        COST["norm"],
        scratch=[pltpu.VMEM((D, TOKENS), BF)],
    )


def qkv_kernel(places, normed_ref, *refs):
    mine, other = refs[:4], refs[4:8]
    cosine, sine, q_ref, kv_ref, w_ref = refs[8:]
    for i in range(NX):
        for h in range(2):
            base = (places[X] + i) % NX * 4 + h * 2
            w_ref[at_rows(base + places[CORE], 96), :] = mine[i][h]
            w_ref[at_rows(base + 1 - places[CORE], 96), :] = other[i][h]
    for i in range(NZ):
        rows = pl.ds(i * ROWS, ROWS)
        lin = mm(normed_ref[rows, :], w_ref[...])
        q_ref[rows, :] = rope(lin[:, :QW], cosine[rows, :], sine[rows, :]).astype(BF)
        kv_ref[rows, :] = rope_keys(lin[:, QW:], cosine[rows, :], sine[rows, :]).astype(BF)


def qkv(places, normed, mine, other, cosine, sine):
    return call(
        qkv_kernel,
        [((TOKENS, QW), BF), ((TOKENS, 2 * KW), BF), ((D, QW + 2 * KW), BF)],
        [places, normed, *mine, *other, cosine, sine],
        COST["qkv"],
    )


def head(ref, rows, index):
    return ref[rows, index * HEAD_DIM : (index + 1) * HEAD_DIM]


def two_heads(ref, j, g):
    rows = slice(j * ROWS, (j + 1) * ROWS)
    return jnp.concatenate([head(ref, rows, 2 * g), head(ref, rows, 2 * g + 1)], axis=0)


def attend_kernel(places, q_ref, own_ref, other_ref, mixed_ref, p_ref):
    late = places[YL]
    factor = HEAD_DIM ** (-0.5)
    for g in range(2):
        for j in range(NZ):
            n = (j + 1) * ROWS
            q = two_heads(q_ref, j, g)
            s_own = mm_t(q, head(own_ref, slice(0, n), g)) * factor
            s_oth = mm_t(q, head(other_ref, slice(0, n), g)) * factor
            shape = (2 * ROWS, n)
            row = lax.broadcasted_iota(jnp.int32, shape, 0) % ROWS + j * ROWS
            col = lax.broadcasted_iota(jnp.int32, shape, 1)
            s_own = jnp.where(col <= row, s_own, MASKED)
            s_oth = jnp.where(col < (j + late) * ROWS, s_oth, MASKED)
            highest = jnp.maximum(
                jnp.max(s_own, axis=1, keepdims=True), jnp.max(s_oth, axis=1, keepdims=True)
            )
            p_own, p_oth = jnp.exp(s_own - highest), jnp.exp(s_oth - highest)
            total = jnp.sum(p_own, axis=1, keepdims=True) + jnp.sum(p_oth, axis=1, keepdims=True)
            scale = 1.0 / total
            p_own, p_oth = (p_own * scale).astype(BF), (p_oth * scale).astype(BF)
            p_ref[g, j, :, :n] = p_own
            p_ref[g, j, :, n : 2 * n] = p_oth
            out = mm(p_own, head(own_ref, slice(0, n), 2 + g)) + mm(
                p_oth, head(other_ref, slice(0, n), 2 + g)
            )
            out = out.astype(BF)
            for k in range(2):
                h = 2 * g + k
                mixed_ref[j * ROWS : (j + 1) * ROWS, h * HEAD_DIM : (h + 1) * HEAD_DIM] = out[
                    k * ROWS : (k + 1) * ROWS
                ]


def attend(places, q, kv, kv_other, deps):
    return call(
        attend_kernel,
        [((TOKENS, QW), BF), ((2, NZ, 2 * ROWS, 2 * TOKENS), BF)],
        [places, q, kv, kv_other],
        COST["attend"],
        deps=deps,
    )


def attend_back_kernel(places, *refs):
    grads = refs[:4]
    q_ref, own_ref, other_ref, p_ref = refs[4:8]
    dq_ref, down_ref, doth_ref = refs[8:11]
    do_ref, acc_own, acc_oth = refs[11:]
    factor = HEAD_DIM ** (-0.5)
    for i in range(NZ):
        do_ref[at_rows((places[Z] + i) % NZ, ROWS), :] = grads[i][...]
    for g in range(2):
        acc_own[...] = jnp.zeros_like(acc_own)
        acc_oth[...] = jnp.zeros_like(acc_oth)
        for j in range(NZ):
            n = (j + 1) * ROWS
            seen = slice(0, n)
            q = two_heads(q_ref, j, g)
            do = two_heads(do_ref, j, g)
            p_own, p_oth = p_ref[g, j, :, :n], p_ref[g, j, :, n : 2 * n]
            dp_own = mm_t(do, head(own_ref, seen, 2 + g))
            dp_oth = mm_t(do, head(other_ref, seen, 2 + g))
            f_own, f_oth = p_own.astype(F32), p_oth.astype(F32)
            dot = jnp.sum(f_own * dp_own, axis=1, keepdims=True) + jnp.sum(
                f_oth * dp_oth, axis=1, keepdims=True
            )
            ds_own = (f_own * (dp_own - dot)).astype(BF)
            ds_oth = (f_oth * (dp_oth - dot)).astype(BF)
            dq = mm(ds_own, head(own_ref, seen, g)) + mm(ds_oth, head(other_ref, seen, g))
            dq = (dq * factor).astype(BF)
            for k in range(2):
                h = 2 * g + k
                dq_ref[j * ROWS : (j + 1) * ROWS, h * HEAD_DIM : (h + 1) * HEAD_DIM] = dq[
                    k * ROWS : (k + 1) * ROWS
                ]
            acc_own[0, seen, :] += t_mm(ds_own, q)
            acc_own[1, seen, :] += t_mm(p_own, do)
            acc_oth[0, seen, :] += t_mm(ds_oth, q)
            acc_oth[1, seen, :] += t_mm(p_oth, do)
        for kind, scale in ((0, factor), (1, 1.0)):
            at = kind * KW + g * HEAD_DIM
            down_ref[:, at : at + HEAD_DIM] = acc_own[kind] * scale
            doth_ref[:, at : at + HEAD_DIM] = (acc_oth[kind] * scale).astype(BF)


def attend_back(places, grads, q, kv, kv_other, shares, deps):
    acc = pltpu.VMEM((2, TOKENS, HEAD_DIM), F32)
    return call(
        attend_back_kernel,
        [((TOKENS, QW), BF), ((TOKENS, 2 * KW), F32), ((TOKENS, 2 * KW), BF)],
        [places, *grads, q, kv, kv_other, shares],
        COST["attend_back"],
        scratch=[pltpu.VMEM((TOKENS, QW), BF), acc, acc],
        deps=deps,
    )


def send_chunks(refs, acc_ref, places):
    for i in range(NZ):
        rows = at_rows((places[Z] + i) % NZ, ROWS)
        refs[i][...] = acc_ref[rows, :].astype(refs[i].dtype)


CHUNKS = [((ROWS, D), F32)] + [((ROWS, D), BF)] * 3


def put_out(out_ref, places, core, ref):
    for k in range(8):
        rows = pl.ds(pl.multiple_of((k % 2 * 2 + core) * 96 + k // 2 * 24, 8), 24)
        tile = out_ref[rows, :]
        ref[k, 96:, :] = jnp.concatenate([tile[:, :768], tile[:, 768:]], axis=0).astype(BF)


def turn_kernel(
    places, dq_ref, own_ref, got_ref, cosine, sine, turned_ref, mixed_ref, branch_ref, *refs
):
    lin_ref, out_ref, sent_ref = refs
    for i in range(NZ):
        rows = slice(i * ROWS, (i + 1) * ROWS)
        dkv = (own_ref[rows, :] + got_ref[rows, :].astype(F32)).astype(BF)
        c, s = cosine[rows, :], -sine[rows, :]
        lin_ref[rows, :QW] = rope(dq_ref[rows, :].astype(F32), c, s).astype(BF)
        lin_ref[rows, QW:] = rope_keys(dkv.astype(F32), c, s).astype(BF)
    for k in range(8):
        sent_ref[k, :96, :] = mm(turned_ref[k * 96 : (k + 1) * 96, :], lin_ref[...]).astype(BF)
    out_ref[...] = t_mm(mixed_ref[...], branch_ref[...])
    put_out(out_ref, places, 1 - places[CORE], sent_ref)


def turn(places, dq, dkv_own, dkv_got, cosine, sine, turned, mixed, branch, deps):
    return call(
        turn_kernel,
        [((TOKENS, 768), BF), ((QW, D), F32), ((8, 144, 768), BF)],
        [places, dq, dkv_own, dkv_got, cosine, sine, turned, mixed, branch],
        COST["turn"],
        deps=deps,
    )


def first_kernel(places, lin_ref, w_ref, out_ref):
    out_ref[...] = mm_t(lin_ref[...], w_ref[...]).astype(BF)


def first(places, lin, w, deps):
    return call(first_kernel, [((TOKENS, D), BF)], [places, lin, w], COST["first"], deps=deps)[0]


def qkv_grad_kernel(places, lin_ref, turned_ref, out_ref, got_ref, total_ref, sum_ref):
    for k in range(8):
        sum_ref[k, :96, :] = mm(turned_ref[k * 96 : (k + 1) * 96, :], lin_ref[...]).astype(BF)
    put_out(out_ref, places, places[CORE], sum_ref)
    for x in range(NX):
        for k in range(2):
            at = 2 * x + (places[YH] + k) % 2
            total_ref[x, k] = (sum_ref[at].astype(F32) + got_ref[at].astype(F32)).astype(BF)


def qkv_grad(places, lin, turned, out, got, deps):
    return call(
        qkv_grad_kernel,
        [((NX, 2, 144, 768), BF)],
        [places, lin, turned, out, got],
        COST["qkv_grad"],
        scratch=[pltpu.VMEM((8, 144, 768), BF)],
        deps=deps,
    )[0]


def lay_kernel(places, packed, out_ref):
    for b in range(16):
        for t in range(3):
            out_ref[b * 96 : (b + 1) * 96, t * 512 : (t + 1) * 512] = packed[
                b // 4 * 2 + b % 2, b // 2 % 2, t * 96 : (t + 1) * 96, :
            ]


def lay(places, packed, deps):
    return call(lay_kernel, [((D, D), BF)], [places, packed], COST["lay"], deps=deps)[0]


def middle_kernel(
    places, x_ref, m0, m1, m2, m3, w_ref, gain, normed_ref, own_ref, acc_ref, mixed_ref
):
    for i, ref in enumerate((m0, m1, m2, m3)):
        at = pl.multiple_of((places[Z] + i) % NZ * QW, QW)
        mixed_ref[:, pl.ds(at, QW)] = ref[...]
    for t in range(3):
        cols = slice(t * 512, (t + 1) * 512)
        acc_ref[:, cols] = x_ref[:, cols].astype(F32) + mm(mixed_ref[...], w_ref[:, cols])
    for i in range(NZ):
        rows = slice(i * ROWS, (i + 1) * ROWS)
        v = acc_ref[rows, :]
        r = lax.rsqrt(jnp.mean(v * v, axis=1, keepdims=True) + EPSILON)
        normed_ref[rows, :] = (v * r * gain[...]).astype(BF)
    own_ref[...] = acc_ref[at_rows(places[Z], ROWS), :]


def middle_of(places, x_all, pieces, w_out, gain):
    return call(
        middle_kernel,
        [((TOKENS, D), BF), ((ROWS, D), F32)],
        [places, x_all, *pieces, w_out, gain],
        COST["middle"],
        scratch=[pltpu.VMEM((TOKENS, D), F32), pltpu.VMEM((TOKENS, D), BF)],
    )


def ffn_kernel(places, n_ref, packed_ref, *refs):
    ogs, mine, other, refs = refs[:4], refs[4:8], refs[8:12], refs[12:]
    hidden_ref, gg_ref, ug_ref, og_ref = refs[:4]
    in_chunks, down_ref = refs[4:8], refs[8]
    in_acc, down_acc, wg_ref, wu_ref, wd_ref = refs[9:]
    for i, g in enumerate(ogs):
        og_ref[at_rows((places[Z] + i) % NZ, ROWS), :] = g[...]

    def from_pieces(out_ref, start):
        for i in range(NX):
            for h in range(2):
                base = (places[X] + i) % NX * 4 + h * 2
                for pieces, core in ((mine, places[CORE]), (other, 1 - places[CORE])):
                    out_ref[at_rows(base + core, 96), :] = pieces[i][h, start : start + 96, :]

    for j in range(2):
        cols = slice(j * 512, (j + 1) * 512)
        from_pieces(wg_ref, 192 * j)
        if j == 0:
            from_pieces(wu_ref, 96)
        for b in range(16):
            packed = packed_ref.at[b // 4 * 2 + b % 2, b // 2 % 2]
            if j == 1:
                wu_ref[b * 96 : (b + 1) * 96, :] = packed[:96, :]
            if b // 8 == j:
                rows = slice(b % 8 * 64, b % 8 * 64 + 64)
                for t in range(3):
                    wd_ref[rows, t * 512 : (t + 1) * 512] = packed[96 + 64 * t : 160 + 64 * t, :]
        wg, wu, wd = wg_ref[...], wu_ref[...], wd_ref[...]
        gate = mm(n_ref[...], wg)
        up = mm(n_ref[...], wu)
        hg = mm_t(og_ref[...], wd).astype(BF).astype(F32)
        sig = 1.0 / (1.0 + jnp.exp(-gate))
        silu = gate * sig
        hidden = (silu * up).astype(BF)
        gg = (hg * up * (sig * (1.0 + gate * (1.0 - sig)))).astype(BF)
        ug = (hg * silu).astype(BF)
        hidden_ref[:, cols] = hidden
        gg_ref[:, cols] = gg
        ug_ref[:, cols] = ug
        if j == 0:
            in_acc[...] = mm_t(gg, wg) + mm_t(ug, wu)
            down_acc[...] = mm(hidden, wd)
        else:
            in_acc[...] += mm_t(gg, wg) + mm_t(ug, wu)
            down_ref[...] = (down_acc[...] + mm(hidden, wd)).astype(BF)
    send_chunks(in_chunks, in_acc, places)


def ffn(places, normed, ogs, packed, mine, other):
    return call(
        ffn_kernel,
        [((TOKENS, FFZ), BF)] * 3 + [((TOKENS, D), BF)] + CHUNKS + [((TOKENS, D), BF)],
        [places, normed, packed, *ogs, *mine, *other],
        COST["ffn"],
        scratch=[pltpu.VMEM((TOKENS, D), F32)] * 2
        + [pltpu.VMEM((D, 512), BF)] * 2
        + [pltpu.VMEM((512, D), BF)],
    )


def ffn_terms(n_ref, h_ref, gg_ref, ug_ref, og_ref, cols, put):
    for w, ref in enumerate((gg_ref, ug_ref)):
        for half in range(2):
            tile = mm(n_ref[...], ref[:, half * 512 + cols.start : half * 512 + cols.stop])
            r = (2 * w + half) * 96
            put(slice(r, r + 96), tile.reshape(8, 96, -1))
    for t in range(3):
        tile = mm(h_ref[...], og_ref[:, t * 512 + cols.start : t * 512 + cols.stop])
        put(slice(384 + 64 * t, 448 + 64 * t), tile.reshape(8, 64, -1))


def ffn_sent_kernel(places, n_ref, hidden_ref, gg_ref, ug_ref, og_ref, *refs):
    sent_ref, n_mine, h_mine, n_turned, h_turned, n_sent, h_sent = refs
    n_turned[...] = n_ref[...].T
    h_turned[...] = hidden_ref[...].T
    split_cores(places, n_turned, n_mine, n_sent, 96)
    split_cores(places, h_turned, h_mine, h_sent, 64)

    def put(rows, tile):
        sent_ref[:, rows, :] = tile.astype(BF)

    ffn_terms(n_sent, h_sent, gg_ref, ug_ref, og_ref, slice(0, 512), put)


def ffn_sent_of(places, normed, hidden, gg, ug, og):
    return call(
        ffn_sent_kernel,
        [((8, 576, 512), BF), ((D // 2, TOKENS), BF), ((FFZ // 2, TOKENS), BF)],
        [places, normed, hidden, gg, ug, og],
        COST["ffn_sent"],
        scratch=[
            pltpu.VMEM((D, TOKENS), BF),
            pltpu.VMEM((FFZ, TOKENS), BF),
            pltpu.VMEM((D // 2, TOKENS), BF),
            pltpu.VMEM((FFZ // 2, TOKENS), BF),
        ],
    )


def ffn_grad_kernel(cols, places, n_ref, h_ref, gg_ref, ug_ref, og_ref, got_ref, *refs):
    outs, sum_ref = refs[:-1], refs[-1]

    def put(rows, tile):
        sum_ref[:, rows, :] = (tile + got_ref[:, rows, cols].astype(F32)).astype(BF)

    ffn_terms(n_ref, h_ref, gg_ref, ug_ref, og_ref, cols, put)
    for i in range(NX):
        for k in range(2):
            at = (places[X] + i) % NX * 2 + (places[YH] + k) % 2
            if len(outs) == 4:
                outs[i][k] = sum_ref[at]
            else:
                outs[k][i] = sum_ref[at]


def ffn_grad_first_kernel(*refs):
    ffn_grad_kernel(slice(0, 256), *refs[:7], *refs[8:12], refs[13])
    refs[12][...] = refs[7][...]


def ffn_grad_second_kernel(*refs):
    ffn_grad_kernel(slice(256, 512), *refs)


def ffn_grad_first(places, args, down_part, deps):
    return call(
        ffn_grad_first_kernel,
        [((2, 576, 256), BF)] * 4 + [((TOKENS, D), BF)],
        [places, *args, down_part],
        COST["ffn_grad"],
        scratch=[pltpu.VMEM((8, 576, 256), BF)],
        deps=deps,
    )


def ffn_grad_second(places, args, deps):
    return call(
        ffn_grad_second_kernel,
        [((4, 576, 256), BF)] * 2,
        [places, *args],
        COST["ffn_grad_second"],
        scratch=[pltpu.VMEM((8, 576, 256), BF)],
        deps=deps,
    )


def y_sum_kernel(places, mine, got, *outs):
    for i in range(NX):
        outs[i][...] = (mine[i].astype(F32) + got[i].astype(F32)).astype(BF)


def y_sum(places, mine, got, deps):
    return call(
        y_sum_kernel,
        [(mine.shape[1:], BF)] * 4,
        [places, mine, got],
        COST["y_sum"],
        deps=deps,
    )


def ffn_join_kernel(places, mine, got, a, b, c, d, out):
    out[:, :256] = (mine[...] + got[...].astype(F32)).astype(BF)
    total = a[...].astype(F32) + b[...].astype(F32) + c[...].astype(F32) + d[...].astype(F32)
    out[:, 256:] = total.astype(BF)


def ffn_join(places, mine, got, terms, deps):
    return call(
        ffn_join_kernel,
        [((576, 512), BF)],
        [places, mine, got, *terms],
        COST["add"],
        deps=deps,
    )[0]


def rms_back(grad, v, gain):
    r = lax.rsqrt(jnp.mean(v * v, axis=1, keepdims=True) + EPSILON)
    pulled = grad * gain
    return r * pulled - v * (r * r * r * jnp.mean(pulled * v, axis=1, keepdims=True))


def middle_back_kernel(places, own, g1, g2, g3, middle, og, gain, w_ref, mid_ref, branch_ref, *outs):
    grad = own[...] + g1[...].astype(F32) + g2[...].astype(F32) + g3[...].astype(F32)
    mid = og[...].astype(F32) + rms_back(grad, middle[...], gain[...])
    mid_ref[...] = mid
    branch = mid.astype(BF)
    branch_ref[...] = branch
    for i in range(NZ):
        outs[i][...] = mm_t(branch, w_ref[at_rows((places[Z] + i) % NZ, QW), :]).astype(BF)


def middle_back(places, chunks, middle, og, gain, w_out, deps):
    return call(
        middle_back_kernel,
        [((ROWS, D), F32), ((ROWS, D), BF)] + [((ROWS, QW), BF)] * 4,
        [places, *chunks, middle, og, gain, w_out],
        COST["middle_back"],
        deps=deps,
    )


def input_back_kernel(places, grad, x, mid, gain, out_ref):
    out_ref[...] = mid[...] + rms_back(grad[...].astype(F32), x[...].astype(F32), gain[...])


def input_back(places, grad, x, mid, gain, deps):
    return call(
        input_back_kernel, [((ROWS, D), F32)], [places, grad, x, mid, gain], 2, deps=deps
    )[0]


def scatter(chunks):
    far = [shift_z(chunks[1], 1), shift_z(chunks[3], -1), shift_z(chunks[2], 2)]
    return [chunks[0], *far]


def x_sum_kernel(places, a, b, c, d, mine, sent):
    mine[...] = a[0].astype(F32) + b[0].astype(F32) + c[0].astype(F32) + d[0].astype(F32)
    total = a[1].astype(F32) + b[1].astype(F32) + c[1].astype(F32) + d[1].astype(F32)
    sent[...] = total.astype(BF)


def x_sum(places, terms, us, deps):
    shape = terms[0].shape[1:]
    return call(x_sum_kernel, [(shape, F32), (shape, BF)], [places, *terms], us, deps=deps)


def add_kernel(places, a, b, out):
    out[...] = (a[...].astype(F32) + b[...].astype(F32)).astype(BF)


def part_kernel(places, both, *refs):
    for k in range(2):
        refs[2 * k][...] = both[k, :96]
        refs[2 * k + 1][...] = both[k, 96:]


def parted(places, both, deps):
    return call(
        part_kernel,
        [((96, 768), BF), ((48, 768), BF)] * 2,
        [places, both],
        0.1,
        deps=deps,
    )


def add_parts_kernel(places, qkv, qkv_got, out_a, out_b, total):
    total[:96, :] = (qkv[...].astype(F32) + qkv_got[...].astype(F32)).astype(BF)
    total[96:, :] = (out_a[...].astype(F32) + out_b[...].astype(F32)).astype(BF)


def add_parts(places, qkv, qkv_got, out_a, out_b, deps):
    return call(
        add_parts_kernel,
        [((144, 768), BF)],
        [places, qkv, qkv_got, out_a, out_b],
        COST["add"],
        deps=deps,
    )[0]


def swap_xz(v, mirror):
    pairs = [
        (
            (a * 4 + r) * 8 + b * 2 + l,
            (b * 4 + (r ^ 2 * mirror)) * 8 + a * 2 + (l ^ mirror),
        )
        for a in range(NX)
        for b in range(NZ)
        for r in range(4)
        for l in range(2)
    ]
    return lax.ppermute(v, ("fsdp", "sp"), pairs)


def added(places, a, b, deps):
    return call(add_kernel, [(a.shape, BF)], [places, a, b], COST["add"], deps=deps)[0]


def over_x(chunks):
    far = [shift_x(chunks[1], 1), shift_x(chunks[3], -1), shift_x(chunks[2], 2)]
    return [chunks[0], *far]


def ffn_out_kernel(places, p0, p1, p2, p3, wg, wu, gate_ref, up_ref, down_ref, gain_ref, all_ref):
    for i, p in enumerate((p0, p1, p2, p3)):
        all_ref[(places[Z] + i) % NZ] = p[...]
    gain = jnp.zeros((96, 1), F32)
    for k, (w, out) in enumerate(((wg, gate_ref), (wu, up_ref))):
        for b in range(16):
            rows = slice((2 * k + b // 8) * 96, (2 * k + b // 8 + 1) * 96)
            cols = slice(b % 8 * 64, b % 8 * 64 + 64)
            tile = jnp.concatenate([all_ref[q, rows, cols].astype(F32) for q in range(NZ)], axis=1)
            out[:, b * 256 : (b + 1) * 256] = tile
            gain += jnp.sum(
                tile * w[:, b * 256 : (b + 1) * 256].astype(F32), axis=1, keepdims=True
            )
    for q in range(NZ):
        for t in range(3):
            r = 384 + 64 * t
            down_ref[q * 64 : (q + 1) * 64, t * 512 : (t + 1) * 512] = all_ref[
                q, r : r + 64, :
            ].astype(F32)
    gain_ref[...] = gain


def ffn_out(places, pieces, wg, wu, deps):
    return call(
        ffn_out_kernel,
        [((96, FF), F32), ((96, FF), F32), ((256, D), F32), ((96, 1), F32)],
        [places, *pieces, wg, wu],
        4,
        scratch=[pltpu.VMEM((NZ, 576, 512), BF)],
        deps=deps,
    )


def qkv_out_kernel(places, p0, p1, p2, p3, wq, wk, wv, q_ref, k_ref, v_ref, gain_ref, all_ref):
    for i, p in enumerate((p0, p1, p2, p3)):
        all_ref[(places[Z] + i) % NZ] = p[:96, :]
    for q in range(NZ):
        q_ref[:, q * QW : (q + 1) * QW] = all_ref[q, :, :QW].astype(F32)
    gain = jnp.sum(q_ref[...] * wq[...].astype(F32), axis=1, keepdims=True)
    for out, w, at in ((k_ref, wk, QW), (v_ref, wv, QW + KW)):
        tile = jnp.concatenate(
            [all_ref[q, :, at : at + KW].astype(F32) for q in range(NZ)], axis=1
        )
        out[...] = tile
        gain += jnp.sum(tile * w[...].astype(F32), axis=1, keepdims=True)
    gain_ref[...] = gain


def qkv_out(places, pieces, wq, wk, wv, deps):
    return call(
        qkv_out_kernel,
        [((96, 1536), F32), ((96, 768), F32), ((96, 768), F32), ((96, 1), F32)],
        [places, *pieces, wq, wk, wv],
        2,
        scratch=[pltpu.VMEM((NZ, 96, 768), BF)],
        deps=deps,
    )


def out_out_kernel(places, p0, p1, p2, p3, out_ref):
    for i, p in enumerate((p0, p1, p2, p3)):
        tile = p[96:, :].astype(F32)
        rows = pl.ds(pl.multiple_of((places[Z] + i) % NZ * 24, 8), 24)
        out_ref[rows, :] = jnp.concatenate([tile[:24], tile[24:]], axis=1)


def out_out(places, pieces):
    return call(out_out_kernel, [((96, D), F32)], [places, *pieces], 1)[0]


def block_out_kernel(places, middle, down, out_ref):
    out_ref[...] = (middle[...] + down[...].astype(F32)).astype(BF)


def block_out_of(places, middle, down, deps):
    return call(block_out_kernel, [((ROWS, D), BF)], [places, middle, down], 1, deps=deps)[0]


def body(
    inputs, norm_attn, w_query, w_key, w_value, w_out, norm_ffn, w_gate, w_up, w_down, cotangent
):
    f, s = lax.axis_index("fsdp"), lax.axis_index("sp")
    x, yh, c, z, yl = f // 4, f // 2 % 2, f % 2, s // 2, s % 2
    places = jnp.stack([x, yh, c, z, yl]).astype(jnp.int32)
    x_own, og_own = inputs[0], cotangent[0]
    gain_attn, gain_ffn = norm_attn[None], norm_ffn[None]

    index = jnp.arange(TOKENS, dtype=jnp.int32)
    positions = (index // ROWS * 2 + yl) * ROWS + index % ROWS
    lane = np.arange(QW) % HEAD_DIM
    frequency = ROPE_BASE ** (-(jnp.arange(HALF, dtype=F32) * 2.0 / HEAD_DIM))
    frequency = jnp.concatenate([frequency] * (QW // HALF))
    angles = positions.astype(F32)[:, None] * frequency[None, :]
    sign = np.where(lane < HALF, -1.0, 1.0).astype(np.float32)
    cosine, sine = jnp.cos(angles), jnp.sin(angles) * sign[None, :]

    qkv_shard, row_shard = cut(
        places, w_query, w_key, w_value, w_gate, w_up, w_down, w_out
    )
    qkv_mirror, row_mirror = mirror_y(qkv_shard), mirror_y(row_shard)
    xs = two_stage_z(x_own)
    (qkv_pair,) = paired(places, qkv_shard, qkv_mirror, 1, [cosine, sine, gain_attn])
    qkv_mine = two_stage_x(qkv_pair)
    qkv_other = [swap_core(p) for p in qkv_mine]
    ffn_pair, ffn_pair_all, out_pair = paired(
        places, row_shard, row_mirror, 3, [qkv_mine[1], qkv_mine[2], xs[1], xs[2]]
    )
    packed_out = gather_xc(out_pair)
    packed_ffn = gather_xc(ffn_pair_all)
    ffn_mine = two_stage_x(ffn_pair)

    normed, x_all, og_copy, turned_mine, turned_sent = norm(places, gain_attn, og_own, xs)
    ogs = two_stage_z(og_copy)
    q, kv, held_qkv = qkv(places, normed, qkv_mine, qkv_other, cosine, sine)
    kv_other = swap_low(kv)
    mixed, shares = attend(
        places, q, kv, kv_other, [ogs[1], ogs[2], ffn_mine[1], ffn_mine[3]]
    )
    mixed_pieces = two_stage_z(mixed)
    held_out = lay(places, packed_out, [mixed_pieces[3]])
    ffn_mine[2] = copied(
        places, [ffn_mine[2]], [mixed_pieces[1], mixed_pieces[3], held_out, ogs[2]]
    )[0]
    ffn_other = [swap_core(p) for p in ffn_mine]
    normed_ffn, middle_own = middle_of(places, x_all, mixed_pieces, held_out, gain_ffn)
    outs = ffn(places, normed_ffn, ogs, packed_ffn, ffn_mine, ffn_other)
    hidden, gate_grad, up_grad, og_all = outs[:4]
    in_chunks, down_part = outs[4:8], outs[8]

    in_got = scatter(in_chunks)
    ffn_sent, n_mine, h_mine = ffn_sent_of(
        places, normed_ffn, hidden, gate_grad, up_grad, og_all
    )
    back = middle_back(places, in_got, middle_own, og_own, gain_ffn, held_out, [n_mine])
    middle_grad, branch = back[:2]
    head_grads = [back[2], shift_z(back[5], -1), shift_z(back[4], 2), shift_z(back[3], 1)]
    branch_all = gather_z(branch)
    ffn_got = swap_core(ffn_sent)
    ffn_args = (n_mine, h_mine, gate_grad, up_grad, og_all, ffn_got)
    a_chunks = ffn_grad_first(places, ffn_args, down_part, [branch])
    a_terms = over_x(a_chunks[:4])
    down_own = scatter_z(a_chunks[4])

    dq, dkv_own, dkv_sent = attend_back(
        places, head_grads, q, kv, kv_other, shares, [a_chunks[0]]
    )
    b_mine, b_sent = ffn_grad_second(places, ffn_args, [dq])
    b_got = mirror_y(b_sent)
    dkv_got = swap_low(dkv_sent)
    lin, out_part, qkv_sent = turn(
        places, dq, dkv_own, dkv_got, cosine, sine, turned_sent, mixed, branch_all, [b_sent]
    )
    qkv_got = swap_core(qkv_sent)
    a_half, a_sent = x_sum(places, a_terms, COST["x_sum"], [qkv_sent])
    a_got = mirror_y(a_sent)
    qkv_sum = scatter_x(qkv_grad(places, lin, turned_mine, out_part, qkv_got, [a_sent]))[0]
    b_chunks = y_sum(places, b_mine, b_got, [a_sent])
    b_terms = over_x(b_chunks)

    ffn_half = ffn_join(places, a_half, a_got, b_terms, [])
    ffn_low = swap_low(ffn_half)
    qkv_half, out_half, qkv_sent, out_sent = parted(places, qkv_sum, [ffn_half])
    qkv_got = mirror_y(qkv_sent)
    out_halves = swap_xz(out_half, 0), swap_xz(out_sent, 1)
    first_part = first(places, lin, held_qkv, [qkv_sent])
    first_got = scatter_z(first_part)
    qkv_half = add_parts(places, qkv_half, qkv_got, *out_halves, [ffn_low])
    qkv_low = swap_low(qkv_half)
    ffn_total = added(places, ffn_half, ffn_low, [qkv_half])
    ffn_pieces = two_stage_z(ffn_total)
    qkv_total = added(places, qkv_half, qkv_low, [ffn_total])
    qkv_pieces = pieces_z(qkv_total)

    block_out = block_out_of(places, middle_own, down_own, [qkv_total])
    input_grad = input_back(places, first_got, x_own, middle_grad, gain_attn, [qkv_total])
    grad_out = out_out(places, qkv_pieces)
    grad_query, grad_key, grad_value, qkv_gain = qkv_out(
        places, qkv_pieces, w_query, w_key, w_value, []
    )
    grad_gate, grad_up, grad_down, ffn_gain = ffn_out(
        places, ffn_pieces, w_gate, w_up, [qkv_gain, grad_out, input_grad]
    )
    grad_norm_attn = qkv_gain[:, 0] / lax.dynamic_slice_in_dim(norm_attn, f * 96, 96, 0)
    grad_norm_ffn = ffn_gain[:, 0] / lax.dynamic_slice_in_dim(norm_ffn, f * 96, 96, 0)
    return (
        block_out[None],
        input_grad[None],
        grad_norm_attn,
        grad_query,
        grad_key,
        grad_value,
        grad_out,
        grad_norm_ffn,
        grad_gate,
        grad_up,
        grad_down,
    )


def solution(mesh):
    rows = P("fsdp", None)
    tokens = P("fsdp", "sp", None)
    return jax.shard_map(
        body,
        mesh=mesh,
        in_specs=(tokens, P(), rows, rows, rows, rows, P(), rows, rows, rows, tokens),
        out_specs=(tokens, tokens, P("fsdp"), rows, rows, rows, rows, P("fsdp"), rows, rows, rows),
        check_vma=False,
    )
```

```python
import functools

import jax
import jax.numpy as jnp
import numpy as np
from jax import lax
from jax.experimental import pallas as pl
from jax.experimental.pallas import tpu as pltpu
from jax.sharding import PartitionSpec as P

D = 1536
HEADS = 16
KV_HEADS = 8
HEAD_DIM = 96
FF = 4096

EPSILON = 1e-05
ROPE_BASE = 100000.0
MASKED = -1e30

NX, NZ = 4, 4
ROWS = 128
TOKENS = ROWS * NZ
QW, KW = 384, 192
HALF = HEAD_DIM // 2
FFZ = FF // NZ
BF = jnp.bfloat16
F32 = jnp.float32
VMEM = pl.BlockSpec(memory_space=pltpu.VMEM)
SMEM = pl.BlockSpec(memory_space=pltpu.SMEM)
ANY = pl.BlockSpec(memory_space=pl.ANY)
LIMIT = pltpu.CompilerParams(vmem_limit_bytes=56 * 1024 * 1024)
X, YH, CORE, Z, YL = range(5)
COST = {
    "norm": 54,
    "qkv": 0.1,
    "attend": 0.1,
    "lay": 0.1,
    "middle": 4,
    "ffn": 17,
    "ffn_sent": 0.1,
    "middle_back": 60,
    "ffn_grad": 60,
    "ffn_grad_second": 0.1,
    "attend_back": 60,
    "turn": 0.1,
    "first": 0.1,
    "x_sum": 60,
    "y_sum": 0.1,
    "qkv_grad": 0.1,
    "add": 8,
}


Z_GROUPS = [[z * 2 + l for z in range(NZ)] for l in range(2)]
XC_GROUPS = [[x * 4 + h * 2 + c for x in range(NX) for c in range(2)] for h in range(2)]


def scatter_z(v):
    return lax.psum_scatter(
        v, "sp", scatter_dimension=0, tiled=True, axis_index_groups=Z_GROUPS
    )


def gather_xc(v):
    return lax.all_gather(v, "fsdp", axis=0, tiled=False, axis_index_groups=XC_GROUPS)


def gather_z(v):
    return lax.all_gather(v, "sp", axis=0, tiled=True, axis_index_groups=Z_GROUPS)


def shift_z(v, step):
    pairs = [(z * 2 + l, (z + step) % NZ * 2 + l) for z in range(NZ) for l in range(2)]
    return lax.ppermute(v, "sp", pairs)


def swap_low(v):
    return lax.ppermute(v, "sp", [(s, s ^ 1) for s in range(8)])


def shift_x(v, step):
    pairs = [(x * 4 + r, (x + step) % NX * 4 + r) for x in range(NX) for r in range(4)]
    return lax.ppermute(v, "fsdp", pairs)


def swap_core(v):
    return lax.ppermute(v, "fsdp", [(f, f ^ 1) for f in range(16)])


def mirror_y(v):
    pairs = [(f * 8 + s, (f ^ 2) * 8 + (s ^ 1)) for f in range(16) for s in range(8)]
    return lax.ppermute(v, ("fsdp", "sp"), pairs)


def pieces_z(v):
    far = [shift_z(v, -1), shift_z(v, 1), shift_z(v, 2)]
    return [v, far[0], far[2], far[1]]


def two_stage_z(v):
    above, below = shift_z(v, -1), shift_z(v, 1)
    return [v, above, shift_z(below, 1), below]


def two_stage_x(v):
    above, below = shift_x(v, -1), shift_x(v, 1)
    return [v, above, shift_x(below, 1), below]


def pieces_x(v):
    far = [shift_x(v, -1), shift_x(v, 1), shift_x(v, 2)]
    return [v, far[0], far[2], far[1]]


def part(v, index, size, dim=0):
    return lax.dynamic_slice_in_dim(v, index * size, size, dim)


def call(kernel, outs, ins, us, scratch=(), deps=(), grid=(), in_specs=None, out_specs=None):
    def run(*refs):
        kernel(*refs[: len(ins)], *refs[len(ins) + len(deps) :])

    return pl.pallas_call(
        run,
        name=kernel.__name__.replace("_kernel", ""),
        grid=grid,
        out_shape=[jax.ShapeDtypeStruct(s, t) for s, t in outs],
        in_specs=(in_specs or [SMEM] + [VMEM] * (len(ins) - 1)) + [ANY] * len(deps),
        out_specs=out_specs or [VMEM] * len(outs),
        scratch_shapes=scratch,
        compiler_params=LIMIT,
        cost_estimate=pl.CostEstimate(
            flops=int(us * 1e9), bytes_accessed=int(us * 3e6), transcendentals=0
        ),
    )(*ins, *deps)


def mm(a, b):
    return jnp.dot(a, b, preferred_element_type=F32)


def mm_t(a, b):
    return lax.dot_general(a, b, (((1,), (1,)), ((), ())), preferred_element_type=F32)


def t_mm(a, b):
    return lax.dot_general(a, b, (((0,), (0,)), ((), ())), preferred_element_type=F32)


def at_rows(index, size):
    return pl.ds(pl.multiple_of(index * size, size), size)


def rope(v, cosine, sine):
    width = v.shape[1]
    lane = lax.broadcasted_iota(jnp.int32, v.shape, 1) % HEAD_DIM
    partner = jnp.where(
        lane < HALF, pltpu.roll(v, width - HALF, 1), pltpu.roll(v, HALF, 1)
    )
    return v * cosine + partner * sine


def rope_keys(kv, cosine, sine):
    lane = lax.broadcasted_iota(jnp.int32, kv.shape, 1)
    return jnp.where(lane < KW, rope(kv, cosine, sine), kv)


def cut_kernel(places, wq, wk, wv, wg, wu, wd, wo, qkv_ref, rows_ref):
    z = places[Z]
    for t in range(3):
        cols = slice(t * 512, (t + 1) * 512)
        rows_ref[384 + 64 * t : 448 + 64 * t, :] = wd[at_rows(z, 64), cols]
        rows_ref[576 + 96 * t : 672 + 96 * t, :] = wo[:, cols]
    qkv_ref[:, :QW] = wq[:, pl.ds(pl.multiple_of(z * QW, 128), QW)]
    for at in range(NZ):

        @pl.when(z == at)
        def _():
            cols = slice(at * KW, (at + 1) * KW)
            qkv_ref[:, QW:] = jnp.concatenate([wk[:, cols], wv[:, cols]], axis=1)
            for k, w in enumerate((wg, wu)):
                for half in range(2):
                    starts = [(8 * half + i) * 256 + at * 64 for i in range(8)]
                    rows = slice((2 * half + k) * 96, (2 * half + k + 1) * 96)
                    rows_ref[rows, :] = jnp.concatenate([w[:, b : b + 64] for b in starts], axis=1)


def cut(places, *arrays):
    return call(cut_kernel, [((96, 768), BF), ((864, 512), BF)], [places, *arrays], 3)


def copy_kernel(places, *refs):
    n = len(refs) // 2
    for i in range(n):
        refs[n + i][...] = refs[i][...]


def copied(places, arrays, deps):
    return call(copy_kernel, [(v.shape, v.dtype) for v in arrays], [places, *arrays], 0.1, deps=deps)


def pair_kernel(places, own, mirror, *outs):
    n = outs[0].shape[1]
    for i, out in enumerate(outs):
        rows = slice(n * i, n * (i + 1))
        out[places[YH]] = own[rows, :]
        out[1 - places[YH]] = mirror[rows, :]


def paired(places, own, mirror, parts, deps):
    shape = (2, own.shape[0] // parts, own.shape[1])
    return call(pair_kernel, [(shape, BF)] * parts, [places, own, mirror], 0.1, deps=deps)


def norm_kernel(places, gain, og, *refs):
    xs, (normed_ref, x_ref, og_ref, mine_ref, sent_ref, turned_ref) = refs[:4], refs[4:]
    og_ref[...] = og[...]
    for i in range(NZ):
        x_ref[at_rows((places[Z] + i) % NZ, ROWS), :] = xs[i][...]
    for i in range(NZ):
        rows = pl.ds(i * ROWS, ROWS)
        v = x_ref[rows, :].astype(F32)
        r = lax.rsqrt(jnp.mean(v * v, axis=1, keepdims=True) + EPSILON)
        normed_ref[rows, :] = (v * r * gain[...]).astype(BF)
    turned_ref[...] = normed_ref[...].T
    split_cores(places, turned_ref, mine_ref, sent_ref, 96)


def split_cores(places, turned_ref, mine_ref, sent_ref, n):
    for k in range(8):
        rows = slice(k * n, (k + 1) * n)
        mine_ref[rows, :] = turned_ref[at_rows(2 * k + places[CORE], n), :]
        sent_ref[rows, :] = turned_ref[at_rows(2 * k + 1 - places[CORE], n), :]


def norm(places, gain, og, xs):
    return call(
        norm_kernel,
        [((TOKENS, D), BF)] * 2 + [((ROWS, D), BF)] + [((D // 2, TOKENS), BF)] * 2,
        [places, gain, og, *xs],
        COST["norm"],
        scratch=[pltpu.VMEM((D, TOKENS), BF)],
    )


def qkv_kernel(places, normed_ref, *refs):
    mine, other = refs[:4], refs[4:8]
    cosine, sine, q_ref, kv_ref, w_ref = refs[8:]
    for i in range(NX):
        for h in range(2):
            base = (places[X] + i) % NX * 4 + h * 2
            w_ref[at_rows(base + places[CORE], 96), :] = mine[i][h]
            w_ref[at_rows(base + 1 - places[CORE], 96), :] = other[i][h]
    for i in range(NZ):
        rows = pl.ds(i * ROWS, ROWS)
        lin = mm(normed_ref[rows, :], w_ref[...])
        q_ref[rows, :] = rope(lin[:, :QW], cosine[rows, :], sine[rows, :]).astype(BF)
        kv_ref[rows, :] = rope_keys(lin[:, QW:], cosine[rows, :], sine[rows, :]).astype(BF)


def qkv(places, normed, mine, other, cosine, sine):
    return call(
        qkv_kernel,
        [((TOKENS, QW), BF), ((TOKENS, 2 * KW), BF), ((D, QW + 2 * KW), BF)],
        [places, normed, *mine, *other, cosine, sine],
        COST["qkv"],
    )


def head(ref, rows, index):
    return ref[rows, index * HEAD_DIM : (index + 1) * HEAD_DIM]


def two_heads(ref, j, g):
    rows = slice(j * ROWS, (j + 1) * ROWS)
    return jnp.concatenate([head(ref, rows, 2 * g), head(ref, rows, 2 * g + 1)], axis=0)


def attend_kernel(places, q_ref, own_ref, other_ref, mixed_ref, p_ref):
    late = places[YL]
    factor = HEAD_DIM ** (-0.5)
    for g in range(2):
        for j in range(NZ):
            n = (j + 1) * ROWS
            q = two_heads(q_ref, j, g)
            s_own = mm_t(q, head(own_ref, slice(0, n), g)) * factor
            s_oth = mm_t(q, head(other_ref, slice(0, n), g)) * factor
            shape = (2 * ROWS, n)
            row = lax.broadcasted_iota(jnp.int32, shape, 0) % ROWS + j * ROWS
            col = lax.broadcasted_iota(jnp.int32, shape, 1)
            s_own = jnp.where(col <= row, s_own, MASKED)
            s_oth = jnp.where(col < (j + late) * ROWS, s_oth, MASKED)
            highest = jnp.maximum(
                jnp.max(s_own, axis=1, keepdims=True), jnp.max(s_oth, axis=1, keepdims=True)
            )
            p_own, p_oth = jnp.exp(s_own - highest), jnp.exp(s_oth - highest)
            total = jnp.sum(p_own, axis=1, keepdims=True) + jnp.sum(p_oth, axis=1, keepdims=True)
            scale = 1.0 / total
            p_own, p_oth = (p_own * scale).astype(BF), (p_oth * scale).astype(BF)
            p_ref[g, j, :, :n] = p_own
            p_ref[g, j, :, n : 2 * n] = p_oth
            out = mm(p_own, head(own_ref, slice(0, n), 2 + g)) + mm(
                p_oth, head(other_ref, slice(0, n), 2 + g)
            )
            out = out.astype(BF)
            for k in range(2):
                h = 2 * g + k
                mixed_ref[j * ROWS : (j + 1) * ROWS, h * HEAD_DIM : (h + 1) * HEAD_DIM] = out[
                    k * ROWS : (k + 1) * ROWS
                ]


def attend(places, q, kv, kv_other, deps):
    return call(
        attend_kernel,
        [((TOKENS, QW), BF), ((2, NZ, 2 * ROWS, 2 * TOKENS), BF)],
        [places, q, kv, kv_other],
        COST["attend"],
        deps=deps,
    )


def attend_back_kernel(places, *refs):
    grads = refs[:4]
    q_ref, own_ref, other_ref, p_ref = refs[4:8]
    dq_ref, down_ref, doth_ref = refs[8:11]
    do_ref, acc_own, acc_oth = refs[11:]
    factor = HEAD_DIM ** (-0.5)
    for i in range(NZ):
        do_ref[at_rows((places[Z] + i) % NZ, ROWS), :] = grads[i][...]
    for g in range(2):
        acc_own[...] = jnp.zeros_like(acc_own)
        acc_oth[...] = jnp.zeros_like(acc_oth)
        for j in range(NZ):
            n = (j + 1) * ROWS
            seen = slice(0, n)
            q = two_heads(q_ref, j, g)
            do = two_heads(do_ref, j, g)
            p_own, p_oth = p_ref[g, j, :, :n], p_ref[g, j, :, n : 2 * n]
            dp_own = mm_t(do, head(own_ref, seen, 2 + g))
            dp_oth = mm_t(do, head(other_ref, seen, 2 + g))
            f_own, f_oth = p_own.astype(F32), p_oth.astype(F32)
            dot = jnp.sum(f_own * dp_own, axis=1, keepdims=True) + jnp.sum(
                f_oth * dp_oth, axis=1, keepdims=True
            )
            ds_own = (f_own * (dp_own - dot)).astype(BF)
            ds_oth = (f_oth * (dp_oth - dot)).astype(BF)
            dq = mm(ds_own, head(own_ref, seen, g)) + mm(ds_oth, head(other_ref, seen, g))
            dq = (dq * factor).astype(BF)
            for k in range(2):
                h = 2 * g + k
                dq_ref[j * ROWS : (j + 1) * ROWS, h * HEAD_DIM : (h + 1) * HEAD_DIM] = dq[
                    k * ROWS : (k + 1) * ROWS
                ]
            acc_own[0, seen, :] += t_mm(ds_own, q)
            acc_own[1, seen, :] += t_mm(p_own, do)
            acc_oth[0, seen, :] += t_mm(ds_oth, q)
            acc_oth[1, seen, :] += t_mm(p_oth, do)
        for kind, scale in ((0, factor), (1, 1.0)):
            at = kind * KW + g * HEAD_DIM
            down_ref[:, at : at + HEAD_DIM] = acc_own[kind] * scale
            doth_ref[:, at : at + HEAD_DIM] = (acc_oth[kind] * scale).astype(BF)


def attend_back(places, grads, q, kv, kv_other, shares, deps):
    acc = pltpu.VMEM((2, TOKENS, HEAD_DIM), F32)
    return call(
        attend_back_kernel,
        [((TOKENS, QW), BF), ((TOKENS, 2 * KW), F32), ((TOKENS, 2 * KW), BF)],
        [places, *grads, q, kv, kv_other, shares],
        COST["attend_back"],
        scratch=[pltpu.VMEM((TOKENS, QW), BF), acc, acc],
        deps=deps,
    )


def send_chunks(refs, acc_ref, places):
    for i in range(NZ):
        rows = at_rows((places[Z] + i) % NZ, ROWS)
        refs[i][...] = acc_ref[rows, :].astype(refs[i].dtype)


CHUNKS = [((ROWS, D), F32)] + [((ROWS, D), BF)] * 3


def put_out(out_ref, places, core, ref):
    for k in range(8):
        rows = pl.ds(pl.multiple_of((k % 2 * 2 + core) * 96 + k // 2 * 24, 8), 24)
        tile = out_ref[rows, :]
        ref[k, 96:, :] = jnp.concatenate([tile[:, :768], tile[:, 768:]], axis=0).astype(BF)


def turn_kernel(
    places, dq_ref, own_ref, got_ref, cosine, sine, turned_ref, mixed_ref, branch_ref, *refs
):
    lin_ref, out_ref, sent_ref = refs
    for i in range(NZ):
        rows = slice(i * ROWS, (i + 1) * ROWS)
        dkv = (own_ref[rows, :] + got_ref[rows, :].astype(F32)).astype(BF)
        c, s = cosine[rows, :], -sine[rows, :]
        lin_ref[rows, :QW] = rope(dq_ref[rows, :].astype(F32), c, s).astype(BF)
        lin_ref[rows, QW:] = rope_keys(dkv.astype(F32), c, s).astype(BF)
    for k in range(8):
        sent_ref[k, :96, :] = mm(turned_ref[k * 96 : (k + 1) * 96, :], lin_ref[...]).astype(BF)
    out_ref[...] = t_mm(mixed_ref[...], branch_ref[...])
    put_out(out_ref, places, 1 - places[CORE], sent_ref)


def turn(places, dq, dkv_own, dkv_got, cosine, sine, turned, mixed, branch, deps):
    return call(
        turn_kernel,
        [((TOKENS, 768), BF), ((QW, D), F32), ((8, 144, 768), BF)],
        [places, dq, dkv_own, dkv_got, cosine, sine, turned, mixed, branch],
        COST["turn"],
        deps=deps,
    )


def first_kernel(places, lin_ref, w_ref, out_ref):
    out_ref[...] = mm_t(lin_ref[...], w_ref[...]).astype(BF)


def first(places, lin, w, deps):
    return call(first_kernel, [((TOKENS, D), BF)], [places, lin, w], COST["first"], deps=deps)[0]


def qkv_grad_kernel(places, lin_ref, turned_ref, out_ref, got_ref, *refs):
    outs, sum_ref = refs[:4], refs[4]
    for k in range(8):
        sum_ref[k, :96, :] = mm(turned_ref[k * 96 : (k + 1) * 96, :], lin_ref[...]).astype(BF)
    put_out(out_ref, places, places[CORE], sum_ref)
    for i in range(NX):
        for k in range(2):
            at = (places[X] + i) % NX * 2 + (places[YH] + k) % 2
            outs[i][k] = (sum_ref[at].astype(F32) + got_ref[at].astype(F32)).astype(BF)


def qkv_grad(places, lin, turned, out, got, deps):
    return call(
        qkv_grad_kernel,
        [((2, 144, 768), BF)] * 4,
        [places, lin, turned, out, got],
        COST["qkv_grad"],
        scratch=[pltpu.VMEM((8, 144, 768), BF)],
        deps=deps,
    )


def lay_kernel(places, packed, out_ref):
    for b in range(16):
        for t in range(3):
            out_ref[b * 96 : (b + 1) * 96, t * 512 : (t + 1) * 512] = packed[
                b // 4 * 2 + b % 2, b // 2 % 2, t * 96 : (t + 1) * 96, :
            ]


def lay(places, packed, deps):
    return call(lay_kernel, [((D, D), BF)], [places, packed], COST["lay"], deps=deps)[0]


def middle_kernel(
    places, x_ref, m0, m1, m2, m3, w_ref, gain, normed_ref, own_ref, acc_ref, mixed_ref
):
    for i, ref in enumerate((m0, m1, m2, m3)):
        at = pl.multiple_of((places[Z] + i) % NZ * QW, QW)
        mixed_ref[:, pl.ds(at, QW)] = ref[...]
    for t in range(3):
        cols = slice(t * 512, (t + 1) * 512)
        acc_ref[:, cols] = x_ref[:, cols].astype(F32) + mm(mixed_ref[...], w_ref[:, cols])
    for i in range(NZ):
        rows = slice(i * ROWS, (i + 1) * ROWS)
        v = acc_ref[rows, :]
        r = lax.rsqrt(jnp.mean(v * v, axis=1, keepdims=True) + EPSILON)
        normed_ref[rows, :] = (v * r * gain[...]).astype(BF)
    own_ref[...] = acc_ref[at_rows(places[Z], ROWS), :]


def middle_of(places, x_all, pieces, w_out, gain):
    return call(
        middle_kernel,
        [((TOKENS, D), BF), ((ROWS, D), F32)],
        [places, x_all, *pieces, w_out, gain],
        COST["middle"],
        scratch=[pltpu.VMEM((TOKENS, D), F32), pltpu.VMEM((TOKENS, D), BF)],
    )


def ffn_kernel(places, n_ref, packed_ref, *refs):
    ogs, mine, other, refs = refs[:4], refs[4:8], refs[8:12], refs[12:]
    hidden_ref, gg_ref, ug_ref, og_ref = refs[:4]
    in_chunks = refs[4:8]
    in_acc, wg_ref, wu_ref, wd_ref = refs[8:]
    for i, g in enumerate(ogs):
        og_ref[at_rows((places[Z] + i) % NZ, ROWS), :] = g[...]

    def from_pieces(out_ref, start):
        for i in range(NX):
            for h in range(2):
                base = (places[X] + i) % NX * 4 + h * 2
                for pieces, core in ((mine, places[CORE]), (other, 1 - places[CORE])):
                    out_ref[at_rows(base + core, 96), :] = pieces[i][h, start : start + 96, :]

    for j in range(2):
        cols = slice(j * 512, (j + 1) * 512)
        from_pieces(wg_ref, 192 * j)
        if j == 0:
            from_pieces(wu_ref, 96)
        for b in range(16):
            packed = packed_ref.at[b // 4 * 2 + b % 2, b // 2 % 2]
            if j == 1:
                wu_ref[b * 96 : (b + 1) * 96, :] = packed[:96, :]
            if b // 8 == j:
                rows = slice(b % 8 * 64, b % 8 * 64 + 64)
                for t in range(3):
                    wd_ref[rows, t * 512 : (t + 1) * 512] = packed[96 + 64 * t : 160 + 64 * t, :]
        wg, wu, wd = wg_ref[...], wu_ref[...], wd_ref[...]
        gate = mm(n_ref[...], wg)
        up = mm(n_ref[...], wu)
        hg = mm_t(og_ref[...], wd).astype(BF).astype(F32)
        sig = 1.0 / (1.0 + jnp.exp(-gate))
        silu = gate * sig
        hidden = (silu * up).astype(BF)
        gg = (hg * up * (sig * (1.0 + gate * (1.0 - sig)))).astype(BF)
        ug = (hg * silu).astype(BF)
        hidden_ref[:, cols] = hidden
        gg_ref[:, cols] = gg
        ug_ref[:, cols] = ug
        if j == 0:
            in_acc[...] = mm_t(gg, wg) + mm_t(ug, wu)
        else:
            in_acc[...] += mm_t(gg, wg) + mm_t(ug, wu)
    send_chunks(in_chunks, in_acc, places)


def ffn(places, normed, ogs, packed, mine, other):
    return call(
        ffn_kernel,
        [((TOKENS, FFZ), BF)] * 3 + [((TOKENS, D), BF)] + CHUNKS,
        [places, normed, packed, *ogs, *mine, *other],
        COST["ffn"],
        scratch=[pltpu.VMEM((TOKENS, D), F32)]
        + [pltpu.VMEM((D, 512), BF)] * 2
        + [pltpu.VMEM((512, D), BF)],
    )


def ffn_terms(n_ref, h_ref, gg_ref, ug_ref, og_ref, cols, put):
    for w, ref in enumerate((gg_ref, ug_ref)):
        for half in range(2):
            tile = mm(n_ref[...], ref[:, half * 512 + cols.start : half * 512 + cols.stop])
            r = (2 * w + half) * 96
            put(slice(r, r + 96), tile.reshape(8, 96, -1))
    for t in range(3):
        tile = mm(h_ref[...], og_ref[:, t * 512 + cols.start : t * 512 + cols.stop])
        put(slice(384 + 64 * t, 448 + 64 * t), tile.reshape(8, 64, -1))


def ffn_sent_kernel(places, n_ref, hidden_ref, gg_ref, ug_ref, og_ref, packed_ref, *refs):
    sent_refs, n_mine, h_mine, down_ref = refs[:2], *refs[2:5]
    n_turned, h_turned, n_sent, h_sent, wd_ref = refs[5:]
    n_turned[...] = n_ref[...].T
    h_turned[...] = hidden_ref[...].T
    split_cores(places, n_turned, n_mine, n_sent, 96)
    split_cores(places, h_turned, h_mine, h_sent, 64)

    def put(rows, tile):
        for half, ref in enumerate(sent_refs):
            ref[:, rows, :] = tile[:, :, half * 256 : (half + 1) * 256].astype(BF)

    ffn_terms(n_sent, h_sent, gg_ref, ug_ref, og_ref, slice(0, 512), put)
    for b in range(16):
        packed = packed_ref.at[b // 4 * 2 + b % 2, b // 2 % 2]
        for t in range(3):
            rows, cols = slice(b * 64, b * 64 + 64), slice(t * 512, (t + 1) * 512)
            wd_ref[rows, cols] = packed[96 + 64 * t : 160 + 64 * t, :]
    down_ref[...] = mm(hidden_ref[...], wd_ref[...]).astype(BF)


def ffn_sent_of(places, normed, hidden, gg, ug, og, packed):
    return call(
        ffn_sent_kernel,
        [((8, 576, 256), BF)] * 2 + [((D // 2, TOKENS), BF), ((FFZ // 2, TOKENS), BF)]
        + [((TOKENS, D), BF)],
        [places, normed, hidden, gg, ug, og, packed],
        COST["ffn_sent"],
        scratch=[
            pltpu.VMEM((D, TOKENS), BF),
            pltpu.VMEM((FFZ, TOKENS), BF),
            pltpu.VMEM((D // 2, TOKENS), BF),
            pltpu.VMEM((FFZ // 2, TOKENS), BF),
            pltpu.VMEM((FFZ, D), BF),
        ],
    )


def ffn_grad_kernel(cols, places, n_ref, h_ref, gg_ref, ug_ref, og_ref, got_ref, *refs):
    outs, sum_ref = refs[:-1], refs[-1]

    def put(rows, tile):
        sum_ref[:, rows, :] = (tile + got_ref[:, rows, :].astype(F32)).astype(BF)

    ffn_terms(n_ref, h_ref, gg_ref, ug_ref, og_ref, cols, put)
    for i in range(NX):
        for k in range(2):
            at = (places[X] + i) % NX * 2 + (places[YH] + k) % 2
            if len(outs) == 4:
                outs[i][k] = sum_ref[at]
            else:
                outs[k][i] = sum_ref[at]


def ffn_grad_first_kernel(*refs):
    ffn_grad_kernel(slice(0, 256), *refs)


def ffn_grad_second_kernel(*refs):
    ffn_grad_kernel(slice(256, 512), *refs[:7], *refs[8:10], refs[11])
    refs[10][...] = refs[7][...]


def ffn_grad_first(places, args, deps):
    return call(
        ffn_grad_first_kernel,
        [((2, 576, 256), BF)] * 4,
        [places, *args],
        COST["ffn_grad"],
        scratch=[pltpu.VMEM((8, 576, 256), BF)],
        deps=deps,
    )


def ffn_grad_second(places, args, down_part, deps):
    return call(
        ffn_grad_second_kernel,
        [((4, 576, 256), BF)] * 2 + [((TOKENS, D), BF)],
        [places, *args, down_part],
        COST["ffn_grad_second"],
        scratch=[pltpu.VMEM((8, 576, 256), BF)],
        deps=deps,
    )


def y_sum_kernel(places, mine, got, *outs):
    for i in range(NX):
        outs[i][...] = (mine[i].astype(F32) + got[i].astype(F32)).astype(BF)


def y_sum(places, mine, got, deps):
    return call(
        y_sum_kernel,
        [(mine.shape[1:], BF)] * 4,
        [places, mine, got],
        COST["y_sum"],
        deps=deps,
    )


def ffn_join_kernel(places, mine, got, a, b, c, d, out):
    out[:, :256] = (mine[...] + got[...].astype(F32)).astype(BF)
    total = a[...].astype(F32) + b[...].astype(F32) + c[...].astype(F32) + d[...].astype(F32)
    out[:, 256:] = total.astype(BF)


def ffn_join(places, mine, got, terms, deps):
    return call(
        ffn_join_kernel,
        [((576, 512), BF)],
        [places, mine, got, *terms],
        COST["add"],
        deps=deps,
    )[0]


def rms_back(grad, v, gain):
    r = lax.rsqrt(jnp.mean(v * v, axis=1, keepdims=True) + EPSILON)
    pulled = grad * gain
    return r * pulled - v * (r * r * r * jnp.mean(pulled * v, axis=1, keepdims=True))


def middle_back_kernel(places, own, g1, g2, g3, middle, og, gain, w_ref, mid_ref, branch_ref, *outs):
    grad = own[...] + g1[...].astype(F32) + g2[...].astype(F32) + g3[...].astype(F32)
    mid = og[...].astype(F32) + rms_back(grad, middle[...], gain[...])
    mid_ref[...] = mid
    branch = mid.astype(BF)
    branch_ref[...] = branch
    for i in range(NZ):
        outs[i][...] = mm_t(branch, w_ref[at_rows((places[Z] + i) % NZ, QW), :]).astype(BF)


def middle_back(places, chunks, middle, og, gain, w_out, deps):
    return call(
        middle_back_kernel,
        [((ROWS, D), F32), ((ROWS, D), BF)] + [((ROWS, QW), BF)] * 4,
        [places, *chunks, middle, og, gain, w_out],
        COST["middle_back"],
        deps=deps,
    )


def input_back_kernel(places, grad, x, mid, gain, out_ref):
    out_ref[...] = mid[...] + rms_back(grad[...].astype(F32), x[...].astype(F32), gain[...])


def input_back(places, grad, x, mid, gain, deps):
    return call(
        input_back_kernel, [((ROWS, D), F32)], [places, grad, x, mid, gain], 2, deps=deps
    )[0]


def scatter(chunks):
    far = [shift_z(chunks[1], 1), shift_z(chunks[3], -1), shift_z(chunks[2], 2)]
    return [chunks[0], *far]


def x_sum_kernel(places, a, b, c, d, mine, sent):
    mine[...] = a[0].astype(F32) + b[0].astype(F32) + c[0].astype(F32) + d[0].astype(F32)
    total = a[1].astype(F32) + b[1].astype(F32) + c[1].astype(F32) + d[1].astype(F32)
    sent[...] = total.astype(BF)


def x_sum(places, terms, us, deps):
    shape = terms[0].shape[1:]
    return call(x_sum_kernel, [(shape, F32), (shape, BF)], [places, *terms], us, deps=deps)


def add_kernel(places, a, b, out):
    out[...] = (a[...].astype(F32) + b[...].astype(F32)).astype(BF)


def added(places, a, b, deps):
    return call(add_kernel, [(a.shape, BF)], [places, a, b], COST["add"], deps=deps)[0]


def over_x(chunks):
    far = [shift_x(chunks[1], 1), shift_x(chunks[3], -1), shift_x(chunks[2], 2)]
    return [chunks[0], *far]


def as_row(column):
    return jnp.broadcast_to(column, (column.shape[0], 128)).T[:1]


def ffn_out_kernel(
    places, p0, p1, p2, p3, wg, wu, gain, gate_ref, up_ref, down_ref, gain_ref, all_ref, acc_ref
):
    j = pl.program_id(0)

    @pl.when(j == 0)
    def _():
        for i, p in enumerate((p0, p1, p2, p3)):
            all_ref[(places[Z] + i) % NZ] = p[...]
        acc_ref[...] = jnp.zeros_like(acc_ref)

    cols = pl.ds(pl.multiple_of(j % 2 * 256, 256), 256)
    for k, (w, out) in enumerate(((wg, gate_ref), (wu, up_ref))):
        rows = pl.ds(pl.multiple_of((2 * k + j // 2) * 96, 96), 96)
        parts = [all_ref[q, rows, cols].astype(F32) for q in range(NZ)]
        for b in range(4):
            tile = jnp.concatenate([v[:, b * 64 : (b + 1) * 64] for v in parts], axis=1)
            at = slice(b * 256, (b + 1) * 256)
            out[:, at] = tile
            acc_ref[...] += jnp.sum(tile * w[:, at].astype(F32), axis=1, keepdims=True)
    for t in range(3):
        r = 384 + 64 * t
        down_ref[:, t * 512 : (t + 1) * 512] = all_ref[j, r : r + 64, :].astype(F32)

    @pl.when(j == 3)
    def _():
        gain_ref[...] = as_row(acc_ref[...] / gain[...])


def ffn_out(places, pieces, wg, wu, gain, deps):
    whole = lambda shape: pl.BlockSpec(shape, lambda j: (0,) * len(shape))
    cols = pl.BlockSpec((96, 1024), lambda j: (0, j))
    return call(
        ffn_out_kernel,
        [((96, FF), F32), ((96, FF), F32), ((256, D), F32), ((1, 96), F32)],
        [places, *pieces, wg, wu, gain],
        4,
        scratch=[pltpu.VMEM((NZ, 576, 512), BF), pltpu.VMEM((96, 1), F32)],
        deps=deps,
        grid=(4,),
        in_specs=[SMEM] + [whole((576, 512))] * 4 + [cols, cols, whole((96, 1))],
        out_specs=[cols, cols, pl.BlockSpec((64, D), lambda j: (j, 0)), whole((1, 96))],
    )


def out_slices_kernel(places, p0, p1, p2, p3, *refs):
    all_ref = refs[4]
    for i, p in enumerate((p0, p1, p2, p3)):
        all_ref[(places[Z] + i) % NZ] = p[96:, :]
    for i in range(NX):
        refs[i][...] = all_ref[(places[X] + i) % NX]


def out_slices(places, pieces, deps):
    return call(
        out_slices_kernel,
        [((48, 768), BF)] * 4,
        [places, *pieces],
        1,
        scratch=[pltpu.VMEM((NZ, 48, 768), BF)],
        deps=deps,
    )


def qkv_out_kernel(
    places, p0, p1, p2, p3, wq, wk, wv, own_gain, q_ref, k_ref, v_ref, gain_ref, all_ref
):
    for i, p in enumerate((p0, p1, p2, p3)):
        all_ref[(places[Z] + i) % NZ] = p[:96, :]
    for q in range(NZ):
        q_ref[:, q * QW : (q + 1) * QW] = all_ref[q, :, :QW].astype(F32)
    gain = jnp.sum(q_ref[...] * wq[...].astype(F32), axis=1, keepdims=True)
    for out, w, at in ((k_ref, wk, QW), (v_ref, wv, QW + KW)):
        tile = jnp.concatenate(
            [all_ref[q, :, at : at + KW].astype(F32) for q in range(NZ)], axis=1
        )
        out[...] = tile
        gain += jnp.sum(tile * w[...].astype(F32), axis=1, keepdims=True)
    gain_ref[...] = as_row(gain / own_gain[...])


def qkv_out(places, pieces, wq, wk, wv, gain, deps):
    return call(
        qkv_out_kernel,
        [((96, 1536), F32), ((96, 768), F32), ((96, 768), F32), ((1, 96), F32)],
        [places, *pieces, wq, wk, wv, gain],
        2,
        scratch=[pltpu.VMEM((NZ, 96, 768), BF)],
        deps=deps,
    )


def out_out_kernel(places, p0, p1, p2, p3, out_ref):
    for i, p in enumerate((p0, p1, p2, p3)):
        tile = p[...].astype(F32)
        rows = pl.ds(pl.multiple_of((places[X] + i) % NX * 24, 8), 24)
        out_ref[rows, :] = jnp.concatenate([tile[:24], tile[24:]], axis=1)


def out_out(places, pieces):
    return call(out_out_kernel, [((96, D), F32)], [places, *pieces], 1)[0]


def block_out_kernel(places, middle, down, out_ref):
    out_ref[...] = (middle[...] + down[...].astype(F32)).astype(BF)


def block_out_of(places, middle, down, deps):
    return call(block_out_kernel, [((ROWS, D), BF)], [places, middle, down], 1, deps=deps)[0]


def body(
    inputs, norm_attn, w_query, w_key, w_value, w_out, norm_ffn, w_gate, w_up, w_down, cotangent
):
    f, s = lax.axis_index("fsdp"), lax.axis_index("sp")
    x, yh, c, z, yl = f // 4, f // 2 % 2, f % 2, s // 2, s % 2
    places = jnp.stack([x, yh, c, z, yl]).astype(jnp.int32)
    x_own, og_own = inputs[0], cotangent[0]
    gain_attn, gain_ffn = norm_attn[None], norm_ffn[None]

    def column(gain):
        return lax.dynamic_slice_in_dim(gain, f * 96, 96, 0)[:, None]

    index = jnp.arange(TOKENS, dtype=jnp.int32)
    positions = (index // ROWS * 2 + yl) * ROWS + index % ROWS
    lane = np.arange(QW) % HEAD_DIM
    frequency = ROPE_BASE ** (-(jnp.arange(HALF, dtype=F32) * 2.0 / HEAD_DIM))
    frequency = jnp.concatenate([frequency] * (QW // HALF))
    angles = positions.astype(F32)[:, None] * frequency[None, :]
    sign = np.where(lane < HALF, -1.0, 1.0).astype(np.float32)
    cosine, sine = jnp.cos(angles), jnp.sin(angles) * sign[None, :]

    qkv_shard, row_shard = cut(
        places, w_query, w_key, w_value, w_gate, w_up, w_down, w_out
    )
    qkv_mirror, row_mirror = mirror_y(qkv_shard), mirror_y(row_shard)
    xs = two_stage_z(x_own)
    (qkv_pair,) = paired(places, qkv_shard, qkv_mirror, 1, [cosine, sine, gain_attn])
    qkv_mine = two_stage_x(qkv_pair)
    qkv_other = [swap_core(p) for p in qkv_mine]
    ffn_pair, ffn_pair_all, out_pair = paired(
        places, row_shard, row_mirror, 3, [qkv_mine[1], qkv_mine[3], xs[1], xs[3]]
    )
    packed_out = gather_xc(out_pair)
    packed_ffn = gather_xc(ffn_pair_all)
    ffn_mine = two_stage_x(ffn_pair)

    normed, x_all, og_copy, turned_mine, turned_sent = norm(places, gain_attn, og_own, xs)
    ogs = two_stage_z(og_copy)
    q, kv, held_qkv = qkv(places, normed, qkv_mine, qkv_other, cosine, sine)
    kv_other = swap_low(kv)
    mixed, shares = attend(
        places, q, kv, kv_other, [ogs[1], ogs[2]]
    )
    mixed_pieces = two_stage_z(mixed)
    held_out = lay(places, packed_out, [mixed_pieces[3]])
    ffn_mine[2] = copied(
        places, [ffn_mine[2]], [mixed_pieces[1], mixed_pieces[3], held_out, ogs[2]]
    )[0]
    ffn_other = [swap_core(p) for p in ffn_mine]
    normed_ffn, middle_own = middle_of(places, x_all, mixed_pieces, held_out, gain_ffn)
    outs = ffn(places, normed_ffn, ogs, packed_ffn, ffn_mine, ffn_other)
    hidden, gate_grad, up_grad, og_all = outs[:4]
    in_chunks = outs[4:8]

    in_got = scatter(in_chunks)
    a_sent, b_sent, n_mine, h_mine, down_part = ffn_sent_of(
        places, normed_ffn, hidden, gate_grad, up_grad, og_all, packed_ffn
    )
    back = middle_back(places, in_got, middle_own, og_own, gain_ffn, held_out, [n_mine])
    middle_grad, branch = back[:2]
    head_grads = [back[2], shift_z(back[5], -1), shift_z(back[4], 2), shift_z(back[3], 1)]
    branch_all = gather_z(branch)
    a_got, b_got = swap_core(a_sent), swap_core(b_sent)
    ffn_args = (n_mine, h_mine, gate_grad, up_grad, og_all)
    a_chunks = ffn_grad_first(places, (*ffn_args, a_got), [branch])
    a_terms = over_x(a_chunks)

    dq, dkv_own, dkv_sent = attend_back(
        places, head_grads, q, kv, kv_other, shares, [a_chunks[0]]
    )
    b_mine, b_sent, down_part = ffn_grad_second(places, (*ffn_args, b_got), down_part, [dq])
    down_own = scatter_z(down_part)
    b_got = mirror_y(b_sent)
    dkv_got = swap_low(dkv_sent)
    lin, out_part, qkv_sent = turn(
        places, dq, dkv_own, dkv_got, cosine, sine, turned_sent, mixed, branch_all, [b_sent]
    )
    qkv_got = swap_core(qkv_sent)
    first_part = first(places, lin, held_qkv, [])
    first_got = scatter_z(first_part)
    a_half, a_sent = x_sum(places, a_terms, COST["x_sum"], [first_part])
    a_got = mirror_y(a_sent)
    qkv_chunks = qkv_grad(places, lin, turned_mine, out_part, qkv_got, [a_sent])
    qkv_terms = over_x(qkv_chunks)
    b_terms = over_x(y_sum(places, b_mine, b_got, [qkv_chunks[0]]))

    qkv_half, qkv_sent = x_sum(places, qkv_terms, 2, [])
    qkv_got = mirror_y(qkv_sent)
    ffn_half = ffn_join(places, a_half, a_got, b_terms, [qkv_sent])
    ffn_low = swap_low(ffn_half)
    qkv_half = added(places, qkv_half, qkv_got, [ffn_half])
    qkv_low = swap_low(qkv_half)
    qkv_total = added(places, qkv_half, qkv_low, [])
    qkv_pieces = pieces_z(qkv_total)
    ffn_total = added(places, ffn_half, ffn_low, [qkv_total])
    ffn_pieces = pieces_z(ffn_total)

    block_out = block_out_of(places, middle_own, down_own, [qkv_total])
    input_grad = input_back(places, first_got, x_own, middle_grad, gain_attn, [qkv_total])
    out_terms = over_x(out_slices(places, qkv_pieces, [block_out, input_grad]))
    grad_query, grad_key, grad_value, qkv_gain = qkv_out(
        places, qkv_pieces, w_query, w_key, w_value, column(norm_attn), [out_terms[0]]
    )
    grad_gate, grad_up, grad_down, ffn_gain = ffn_out(
        places, ffn_pieces, w_gate, w_up, column(norm_ffn), [qkv_gain]
    )
    grad_out = out_out(places, [out_terms[0], out_terms[2], out_terms[3], out_terms[1]])
    grad_norm_attn, grad_norm_ffn = qkv_gain[0], ffn_gain[0]
    return (
        block_out[None],
        input_grad[None],
        grad_norm_attn,
        grad_query,
        grad_key,
        grad_value,
        grad_out,
        grad_norm_ffn,
        grad_gate,
        grad_up,
        grad_down,
    )


def solution(mesh):
    rows = P("fsdp", None)
    tokens = P("fsdp", "sp", None)
    return jax.shard_map(
        body,
        mesh=mesh,
        in_specs=(tokens, P(), rows, rows, rows, rows, P(), rows, rows, rows, tokens),
        out_specs=(tokens, tokens, P("fsdp"), rows, rows, rows, rows, P("fsdp"), rows, rows, rows),
        check_vma=False,
    )
```

```python
import functools

import jax
import jax.numpy as jnp
import numpy as np
from jax import lax
from jax.experimental import pallas as pl
from jax.experimental.pallas import tpu as pltpu
from jax.sharding import PartitionSpec as P

D = 1536
HEADS = 16
KV_HEADS = 8
HEAD_DIM = 96
FF = 4096

EPSILON = 1e-05
ROPE_BASE = 100000.0
MASKED = -1e30

NX, NZ = 4, 4
ROWS = 128
TOKENS = ROWS * NZ
QW, KW = 384, 192
HALF = HEAD_DIM // 2
FFZ = FF // NZ
BF = jnp.bfloat16
F32 = jnp.float32
VMEM = pl.BlockSpec(memory_space=pltpu.VMEM)
SMEM = pl.BlockSpec(memory_space=pltpu.SMEM)
ANY = pl.BlockSpec(memory_space=pl.ANY)
LIMIT = pltpu.CompilerParams(vmem_limit_bytes=56 * 1024 * 1024)
X, YH, CORE, Z, YL = range(5)
COST = {
    "norm": 54,
    "qkv": 0.1,
    "attend": 0.1,
    "lay": 0.1,
    "middle": 4,
    "ffn": 17,
    "ffn_sent": 0.1,
    "middle_back": 60,
    "ffn_grad": 60,
    "ffn_grad_second": 0.1,
    "attend_back": 60,
    "turn": 0.1,
    "first": 0.1,
    "x_sum": 60,
    "y_sum": 0.1,
    "qkv_grad": 0.1,
    "add": 8,
}


Z_GROUPS = [[z * 2 + l for z in range(NZ)] for l in range(2)]
XC_GROUPS = [[x * 4 + h * 2 + c for x in range(NX) for c in range(2)] for h in range(2)]


def scatter_z(v):
    return lax.psum_scatter(
        v, "sp", scatter_dimension=0, tiled=True, axis_index_groups=Z_GROUPS
    )


def gather_xc(v):
    return lax.all_gather(v, "fsdp", axis=0, tiled=False, axis_index_groups=XC_GROUPS)


def gather_z(v):
    return lax.all_gather(v, "sp", axis=0, tiled=True, axis_index_groups=Z_GROUPS)


def shift_z(v, step):
    pairs = [(z * 2 + l, (z + step) % NZ * 2 + l) for z in range(NZ) for l in range(2)]
    return lax.ppermute(v, "sp", pairs)


def swap_low(v):
    return lax.ppermute(v, "sp", [(s, s ^ 1) for s in range(8)])


def shift_x(v, step):
    pairs = [(x * 4 + r, (x + step) % NX * 4 + r) for x in range(NX) for r in range(4)]
    return lax.ppermute(v, "fsdp", pairs)


def swap_core(v):
    return lax.ppermute(v, "fsdp", [(f, f ^ 1) for f in range(16)])


def mirror_y(v):
    pairs = [(f * 8 + s, (f ^ 2) * 8 + (s ^ 1)) for f in range(16) for s in range(8)]
    return lax.ppermute(v, ("fsdp", "sp"), pairs)


def pieces_z(v):
    far = [shift_z(v, -1), shift_z(v, 1), shift_z(v, 2)]
    return [v, far[0], far[2], far[1]]


def two_stage_z(v):
    above, below = shift_z(v, -1), shift_z(v, 1)
    return [v, above, shift_z(below, 1), below]


def two_stage_x(v):
    above, below = shift_x(v, -1), shift_x(v, 1)
    return [v, above, shift_x(below, 1), below]


def pieces_x(v):
    far = [shift_x(v, -1), shift_x(v, 1), shift_x(v, 2)]
    return [v, far[0], far[2], far[1]]


def part(v, index, size, dim=0):
    return lax.dynamic_slice_in_dim(v, index * size, size, dim)


def call(kernel, outs, ins, us, scratch=(), deps=(), grid=(), in_specs=None, out_specs=None):
    def run(*refs):
        kernel(*refs[: len(ins)], *refs[len(ins) + len(deps) :])

    return pl.pallas_call(
        run,
        name=kernel.__name__.replace("_kernel", ""),
        grid=grid,
        out_shape=[jax.ShapeDtypeStruct(s, t) for s, t in outs],
        in_specs=(in_specs or [SMEM] + [VMEM] * (len(ins) - 1)) + [ANY] * len(deps),
        out_specs=out_specs or [VMEM] * len(outs),
        scratch_shapes=scratch,
        compiler_params=LIMIT,
        cost_estimate=pl.CostEstimate(
            flops=int(us * 1e9), bytes_accessed=int(us * 3e6), transcendentals=0
        ),
    )(*ins, *deps)


def mm(a, b):
    return jnp.dot(a, b, preferred_element_type=F32)


def mm_t(a, b):
    return lax.dot_general(a, b, (((1,), (1,)), ((), ())), preferred_element_type=F32)


def t_mm(a, b):
    return lax.dot_general(a, b, (((0,), (0,)), ((), ())), preferred_element_type=F32)


def at_rows(index, size):
    return pl.ds(pl.multiple_of(index * size, size), size)


def rope(v, cosine, sine):
    width = v.shape[1]
    lane = lax.broadcasted_iota(jnp.int32, v.shape, 1) % HEAD_DIM
    partner = jnp.where(
        lane < HALF, pltpu.roll(v, width - HALF, 1), pltpu.roll(v, HALF, 1)
    )
    return v * cosine + partner * sine


def rope_keys(kv, cosine, sine):
    lane = lax.broadcasted_iota(jnp.int32, kv.shape, 1)
    return jnp.where(lane < KW, rope(kv, cosine, sine), kv)


def cut_kernel(places, wq, wk, wv, wg, wu, wd, wo, qkv_ref, rows_ref):
    z = places[Z]
    for t in range(3):
        cols = slice(t * 512, (t + 1) * 512)
        rows_ref[384 + 64 * t : 448 + 64 * t, :] = wd[at_rows(z, 64), cols]
        rows_ref[576 + 96 * t : 672 + 96 * t, :] = wo[:, cols]
    qkv_ref[:, :QW] = wq[:, pl.ds(pl.multiple_of(z * QW, 128), QW)]
    for at in range(NZ):

        @pl.when(z == at)
        def _():
            cols = slice(at * KW, (at + 1) * KW)
            qkv_ref[:, QW:] = jnp.concatenate([wk[:, cols], wv[:, cols]], axis=1)
            for k, w in enumerate((wg, wu)):
                for half in range(2):
                    starts = [(8 * half + i) * 256 + at * 64 for i in range(8)]
                    rows = slice((2 * half + k) * 96, (2 * half + k + 1) * 96)
                    rows_ref[rows, :] = jnp.concatenate([w[:, b : b + 64] for b in starts], axis=1)


def cut(places, *arrays):
    return call(cut_kernel, [((96, 768), BF), ((864, 512), BF)], [places, *arrays], 3)


def copy_kernel(places, *refs):
    n = len(refs) // 2
    for i in range(n):
        refs[n + i][...] = refs[i][...]


def copied(places, arrays, deps):
    return call(copy_kernel, [(v.shape, v.dtype) for v in arrays], [places, *arrays], 0.1, deps=deps)


def pair_kernel(places, own, mirror, *outs):
    start = 0
    for out in outs:
        rows = slice(start, start + out.shape[1])
        out[places[YH]] = own[rows, :]
        out[1 - places[YH]] = mirror[rows, :]
        start += out.shape[1]


def paired(places, own, mirror, parts, deps):
    outs = [((2, n, own.shape[1]), BF) for n in parts]
    return call(pair_kernel, outs, [places, own, mirror], 0.1, deps=deps)


def norm_kernel(places, gain, og, *refs):
    xs, (normed_ref, x_ref, og_ref, mine_ref, sent_ref, turned_ref) = refs[:4], refs[4:]
    og_ref[...] = og[...]
    for i in range(NZ):
        x_ref[at_rows((places[Z] + i) % NZ, ROWS), :] = xs[i][...]
    for i in range(NZ):
        rows = pl.ds(i * ROWS, ROWS)
        v = x_ref[rows, :].astype(F32)
        r = lax.rsqrt(jnp.mean(v * v, axis=1, keepdims=True) + EPSILON)
        normed_ref[rows, :] = (v * r * gain[...]).astype(BF)
    turned_ref[...] = normed_ref[...].T
    split_cores(places, turned_ref, mine_ref, sent_ref, 96)


def split_cores(places, turned_ref, mine_ref, sent_ref, n):
    for k in range(8):
        rows = slice(k * n, (k + 1) * n)
        mine_ref[rows, :] = turned_ref[at_rows(2 * k + places[CORE], n), :]
        sent_ref[rows, :] = turned_ref[at_rows(2 * k + 1 - places[CORE], n), :]


def norm(places, gain, og, xs):
    return call(
        norm_kernel,
        [((TOKENS, D), BF)] * 2 + [((ROWS, D), BF)] + [((D // 2, TOKENS), BF)] * 2,
        [places, gain, og, *xs],
        COST["norm"],
        scratch=[pltpu.VMEM((D, TOKENS), BF)],
    )


def qkv_kernel(places, normed_ref, *refs):
    mine, other = refs[:4], refs[4:8]
    cosine, sine, q_ref, kv_ref, w_ref = refs[8:]
    for i in range(NX):
        for h in range(2):
            base = (places[X] + i) % NX * 4 + h * 2
            w_ref[at_rows(base + places[CORE], 96), :] = mine[i][h]
            w_ref[at_rows(base + 1 - places[CORE], 96), :] = other[i][h]
    for i in range(NZ):
        rows = pl.ds(i * ROWS, ROWS)
        lin = mm(normed_ref[rows, :], w_ref[...])
        q_ref[rows, :] = rope(lin[:, :QW], cosine[rows, :], sine[rows, :]).astype(BF)
        kv_ref[rows, :] = rope_keys(lin[:, QW:], cosine[rows, :], sine[rows, :]).astype(BF)


def qkv(places, normed, mine, other, cosine, sine):
    return call(
        qkv_kernel,
        [((TOKENS, QW), BF), ((TOKENS, 2 * KW), BF), ((D, QW + 2 * KW), BF)],
        [places, normed, *mine, *other, cosine, sine],
        COST["qkv"],
    )


def head(ref, rows, index):
    return ref[rows, index * HEAD_DIM : (index + 1) * HEAD_DIM]


def two_heads(ref, j, g):
    rows = slice(j * ROWS, (j + 1) * ROWS)
    return jnp.concatenate([head(ref, rows, 2 * g), head(ref, rows, 2 * g + 1)], axis=0)


def attend_kernel(places, q_ref, own_ref, other_ref, mixed_ref, p_ref):
    late = places[YL]
    factor = HEAD_DIM ** (-0.5)
    for g in range(2):
        for j in range(NZ):
            n = (j + 1) * ROWS
            q = two_heads(q_ref, j, g)
            s_own = mm_t(q, head(own_ref, slice(0, n), g)) * factor
            s_oth = mm_t(q, head(other_ref, slice(0, n), g)) * factor
            shape = (2 * ROWS, n)
            row = lax.broadcasted_iota(jnp.int32, shape, 0) % ROWS + j * ROWS
            col = lax.broadcasted_iota(jnp.int32, shape, 1)
            s_own = jnp.where(col <= row, s_own, MASKED)
            s_oth = jnp.where(col < (j + late) * ROWS, s_oth, MASKED)
            highest = jnp.maximum(
                jnp.max(s_own, axis=1, keepdims=True), jnp.max(s_oth, axis=1, keepdims=True)
            )
            p_own, p_oth = jnp.exp(s_own - highest), jnp.exp(s_oth - highest)
            total = jnp.sum(p_own, axis=1, keepdims=True) + jnp.sum(p_oth, axis=1, keepdims=True)
            scale = 1.0 / total
            p_own, p_oth = (p_own * scale).astype(BF), (p_oth * scale).astype(BF)
            p_ref[g, j, :, :n] = p_own
            p_ref[g, j, :, n : 2 * n] = p_oth
            out = mm(p_own, head(own_ref, slice(0, n), 2 + g)) + mm(
                p_oth, head(other_ref, slice(0, n), 2 + g)
            )
            out = out.astype(BF)
            for k in range(2):
                h = 2 * g + k
                mixed_ref[j * ROWS : (j + 1) * ROWS, h * HEAD_DIM : (h + 1) * HEAD_DIM] = out[
                    k * ROWS : (k + 1) * ROWS
                ]


def attend(places, q, kv, kv_other, deps):
    return call(
        attend_kernel,
        [((TOKENS, QW), BF), ((2, NZ, 2 * ROWS, 2 * TOKENS), BF)],
        [places, q, kv, kv_other],
        COST["attend"],
        deps=deps,
    )


def attend_back_kernel(places, *refs):
    grads = refs[:4]
    q_ref, own_ref, other_ref, p_ref = refs[4:8]
    dq_ref, down_ref, doth_ref = refs[8:11]
    do_ref, acc_own, acc_oth = refs[11:]
    factor = HEAD_DIM ** (-0.5)
    for i in range(NZ):
        do_ref[at_rows((places[Z] + i) % NZ, ROWS), :] = grads[i][...]
    for g in range(2):
        acc_own[...] = jnp.zeros_like(acc_own)
        acc_oth[...] = jnp.zeros_like(acc_oth)
        for j in range(NZ):
            n = (j + 1) * ROWS
            seen = slice(0, n)
            q = two_heads(q_ref, j, g)
            do = two_heads(do_ref, j, g)
            p_own, p_oth = p_ref[g, j, :, :n], p_ref[g, j, :, n : 2 * n]
            dp_own = mm_t(do, head(own_ref, seen, 2 + g))
            dp_oth = mm_t(do, head(other_ref, seen, 2 + g))
            f_own, f_oth = p_own.astype(F32), p_oth.astype(F32)
            dot = jnp.sum(f_own * dp_own, axis=1, keepdims=True) + jnp.sum(
                f_oth * dp_oth, axis=1, keepdims=True
            )
            ds_own = (f_own * (dp_own - dot)).astype(BF)
            ds_oth = (f_oth * (dp_oth - dot)).astype(BF)
            dq = mm(ds_own, head(own_ref, seen, g)) + mm(ds_oth, head(other_ref, seen, g))
            dq = (dq * factor).astype(BF)
            for k in range(2):
                h = 2 * g + k
                dq_ref[j * ROWS : (j + 1) * ROWS, h * HEAD_DIM : (h + 1) * HEAD_DIM] = dq[
                    k * ROWS : (k + 1) * ROWS
                ]
            acc_own[0, seen, :] += t_mm(ds_own, q)
            acc_own[1, seen, :] += t_mm(p_own, do)
            acc_oth[0, seen, :] += t_mm(ds_oth, q)
            acc_oth[1, seen, :] += t_mm(p_oth, do)
        for kind, scale in ((0, factor), (1, 1.0)):
            at = kind * KW + g * HEAD_DIM
            down_ref[:, at : at + HEAD_DIM] = acc_own[kind] * scale
            doth_ref[:, at : at + HEAD_DIM] = (acc_oth[kind] * scale).astype(BF)


def attend_back(places, grads, q, kv, kv_other, shares, deps):
    acc = pltpu.VMEM((2, TOKENS, HEAD_DIM), F32)
    return call(
        attend_back_kernel,
        [((TOKENS, QW), BF), ((TOKENS, 2 * KW), F32), ((TOKENS, 2 * KW), BF)],
        [places, *grads, q, kv, kv_other, shares],
        COST["attend_back"],
        scratch=[pltpu.VMEM((TOKENS, QW), BF), acc, acc],
        deps=deps,
    )


def send_chunks(refs, acc_ref, places):
    for i in range(NZ):
        rows = at_rows((places[Z] + i) % NZ, ROWS)
        refs[i][...] = acc_ref[rows, :].astype(refs[i].dtype)


CHUNKS = [((ROWS, D), F32)] + [((ROWS, D), BF)] * 3


def put_out(out_ref, places, core, ref):
    for k in range(8):
        rows = pl.ds(pl.multiple_of((k % 2 * 2 + core) * 96 + k // 2 * 24, 8), 24)
        tile = out_ref[rows, :]
        ref[k, 96:, :] = jnp.concatenate([tile[:, :768], tile[:, 768:]], axis=0).astype(BF)


def turn_kernel(
    places, dq_ref, own_ref, got_ref, cosine, sine, turned_ref, mixed_ref, branch_ref, *refs
):
    lin_ref, out_ref, sent_ref = refs
    for i in range(NZ):
        rows = slice(i * ROWS, (i + 1) * ROWS)
        dkv = (own_ref[rows, :] + got_ref[rows, :].astype(F32)).astype(BF)
        c, s = cosine[rows, :], -sine[rows, :]
        lin_ref[rows, :QW] = rope(dq_ref[rows, :].astype(F32), c, s).astype(BF)
        lin_ref[rows, QW:] = rope_keys(dkv.astype(F32), c, s).astype(BF)
    for k in range(8):
        sent_ref[k, :96, :] = mm(turned_ref[k * 96 : (k + 1) * 96, :], lin_ref[...]).astype(BF)
    out_ref[...] = t_mm(mixed_ref[...], branch_ref[...])
    put_out(out_ref, places, 1 - places[CORE], sent_ref)


def turn(places, dq, dkv_own, dkv_got, cosine, sine, turned, mixed, branch, deps):
    return call(
        turn_kernel,
        [((TOKENS, 768), BF), ((QW, D), F32), ((8, 144, 768), BF)],
        [places, dq, dkv_own, dkv_got, cosine, sine, turned, mixed, branch],
        COST["turn"],
        deps=deps,
    )


def first_kernel(places, lin_ref, w_ref, out_ref):
    out_ref[...] = mm_t(lin_ref[...], w_ref[...]).astype(BF)


def first(places, lin, w, deps):
    return call(first_kernel, [((TOKENS, D), BF)], [places, lin, w], COST["first"], deps=deps)[0]


def qkv_grad_kernel(places, lin_ref, turned_ref, out_ref, got_ref, *refs):
    outs, sum_ref = refs[:4], refs[4]
    for k in range(8):
        sum_ref[k, :96, :] = mm(turned_ref[k * 96 : (k + 1) * 96, :], lin_ref[...]).astype(BF)
    put_out(out_ref, places, places[CORE], sum_ref)
    for i in range(NX):
        for k in range(2):
            at = (places[X] + i) % NX * 2 + (places[YH] + k) % 2
            outs[i][k] = (sum_ref[at].astype(F32) + got_ref[at].astype(F32)).astype(BF)


def qkv_grad(places, lin, turned, out, got, deps):
    return call(
        qkv_grad_kernel,
        [((2, 144, 768), BF)] * 4,
        [places, lin, turned, out, got],
        COST["qkv_grad"],
        scratch=[pltpu.VMEM((8, 144, 768), BF)],
        deps=deps,
    )


def lay_out(packed, out_ref, cols):
    for b in range(16):
        for t in cols:
            out_ref[b * 96 : (b + 1) * 96, t * 512 : (t + 1) * 512] = packed[
                b // 4 * 2 + b % 2, b // 2 % 2, 288 + t * 96 : 384 + t * 96, :
            ]


def lay_kernel(places, packed, out_ref):
    lay_out(packed, out_ref, range(3))


def lay(places, packed, deps):
    return call(lay_kernel, [((D, D), BF)], [places, packed], COST["lay"], deps=deps)[0]


def middle_kernel(
    places, x_ref, m0, m1, m2, m3, packed, gain, normed_ref, own_ref, acc_ref, mixed_ref, w_ref
):
    lay_out(packed, w_ref, range(3))
    for i, ref in enumerate((m0, m1, m2, m3)):
        at = pl.multiple_of((places[Z] + i) % NZ * QW, QW)
        mixed_ref[:, pl.ds(at, QW)] = ref[...]
    for t in range(3):
        cols = slice(t * 512, (t + 1) * 512)
        acc_ref[:, cols] = x_ref[:, cols].astype(F32) + mm(mixed_ref[...], w_ref[:, cols])
    for i in range(NZ):
        rows = slice(i * ROWS, (i + 1) * ROWS)
        v = acc_ref[rows, :]
        r = lax.rsqrt(jnp.mean(v * v, axis=1, keepdims=True) + EPSILON)
        normed_ref[rows, :] = (v * r * gain[...]).astype(BF)
    own_ref[...] = acc_ref[at_rows(places[Z], ROWS), :]


def middle_of(places, x_all, pieces, w_out, gain):
    return call(
        middle_kernel,
        [((TOKENS, D), BF), ((ROWS, D), F32)],
        [places, x_all, *pieces, w_out, gain],
        COST["middle"],
        scratch=[
            pltpu.VMEM((TOKENS, D), F32),
            pltpu.VMEM((TOKENS, D), BF),
            pltpu.VMEM((D, D), BF),
        ],
    )


def ffn_kernel(places, n_ref, packed_ref, *refs):
    ogs, mine, other, refs = refs[:4], refs[4:8], refs[8:12], refs[12:]
    hidden_ref, gg_ref, ug_ref, og_ref = refs[:4]
    in_chunks = refs[4:8]
    in_acc, wg_ref, wu_ref, wd_ref = refs[8:]
    for i, g in enumerate(ogs):
        og_ref[at_rows((places[Z] + i) % NZ, ROWS), :] = g[...]

    def from_pieces(out_ref, start):
        for i in range(NX):
            for h in range(2):
                base = (places[X] + i) % NX * 4 + h * 2
                for pieces, core in ((mine, places[CORE]), (other, 1 - places[CORE])):
                    out_ref[at_rows(base + core, 96), :] = pieces[i][h, start : start + 96, :]

    for j in range(2):
        cols = slice(j * 512, (j + 1) * 512)
        from_pieces(wg_ref, 192 * j)
        if j == 0:
            from_pieces(wu_ref, 96)
        for b in range(16):
            packed = packed_ref.at[b // 4 * 2 + b % 2, b // 2 % 2]
            if j == 1:
                wu_ref[b * 96 : (b + 1) * 96, :] = packed[:96, :]
            if b // 8 == j:
                rows = slice(b % 8 * 64, b % 8 * 64 + 64)
                for t in range(3):
                    wd_ref[rows, t * 512 : (t + 1) * 512] = packed[96 + 64 * t : 160 + 64 * t, :]
        wg, wu, wd = wg_ref[...], wu_ref[...], wd_ref[...]
        gate = mm(n_ref[...], wg)
        up = mm(n_ref[...], wu)
        hg = mm_t(og_ref[...], wd).astype(BF).astype(F32)
        sig = 1.0 / (1.0 + jnp.exp(-gate))
        silu = gate * sig
        hidden = (silu * up).astype(BF)
        gg = (hg * up * (sig * (1.0 + gate * (1.0 - sig)))).astype(BF)
        ug = (hg * silu).astype(BF)
        hidden_ref[:, cols] = hidden
        gg_ref[:, cols] = gg
        ug_ref[:, cols] = ug
        if j == 0:
            in_acc[...] = mm_t(gg, wg) + mm_t(ug, wu)
        else:
            in_acc[...] += mm_t(gg, wg) + mm_t(ug, wu)
    send_chunks(in_chunks, in_acc, places)


def ffn(places, normed, ogs, packed, mine, other):
    return call(
        ffn_kernel,
        [((TOKENS, FFZ), BF)] * 3 + [((TOKENS, D), BF)] + CHUNKS,
        [places, normed, packed, *ogs, *mine, *other],
        COST["ffn"],
        scratch=[pltpu.VMEM((TOKENS, D), F32)]
        + [pltpu.VMEM((D, 512), BF)] * 2
        + [pltpu.VMEM((512, D), BF)],
    )


def ffn_terms(n_ref, h_ref, gg_ref, ug_ref, og_ref, cols, put):
    for w, ref in enumerate((gg_ref, ug_ref)):
        for half in range(2):
            tile = mm(n_ref[...], ref[:, half * 512 + cols.start : half * 512 + cols.stop])
            r = (2 * w + half) * 96
            put(slice(r, r + 96), tile.reshape(8, 96, -1))
    for t in range(3):
        tile = mm(h_ref[...], og_ref[:, t * 512 + cols.start : t * 512 + cols.stop])
        put(slice(384 + 64 * t, 448 + 64 * t), tile.reshape(8, 64, -1))


def ffn_sent_kernel(places, n_ref, hidden_ref, gg_ref, ug_ref, og_ref, packed_ref, *refs):
    sent_refs, n_mine, h_mine, down_ref = refs[:2], *refs[2:5]
    n_turned, h_turned, n_sent, h_sent, wd_ref = refs[5:]
    n_turned[...] = n_ref[...].T
    h_turned[...] = hidden_ref[...].T
    split_cores(places, n_turned, n_mine, n_sent, 96)
    split_cores(places, h_turned, h_mine, h_sent, 64)

    def put(rows, tile):
        for half, ref in enumerate(sent_refs):
            ref[:, rows, :] = tile[:, :, half * 256 : (half + 1) * 256].astype(BF)

    ffn_terms(n_sent, h_sent, gg_ref, ug_ref, og_ref, slice(0, 512), put)
    for b in range(16):
        packed = packed_ref.at[b // 4 * 2 + b % 2, b // 2 % 2]
        for t in range(3):
            rows, cols = slice(b * 64, b * 64 + 64), slice(t * 512, (t + 1) * 512)
            wd_ref[rows, cols] = packed[96 + 64 * t : 160 + 64 * t, :]
    down_ref[...] = mm(hidden_ref[...], wd_ref[...]).astype(BF)


def ffn_sent_of(places, normed, hidden, gg, ug, og, packed):
    return call(
        ffn_sent_kernel,
        [((8, 576, 256), BF)] * 2 + [((D // 2, TOKENS), BF), ((FFZ // 2, TOKENS), BF)]
        + [((TOKENS, D), BF)],
        [places, normed, hidden, gg, ug, og, packed],
        COST["ffn_sent"],
        scratch=[
            pltpu.VMEM((D, TOKENS), BF),
            pltpu.VMEM((FFZ, TOKENS), BF),
            pltpu.VMEM((D // 2, TOKENS), BF),
            pltpu.VMEM((FFZ // 2, TOKENS), BF),
            pltpu.VMEM((FFZ, D), BF),
        ],
    )


def ffn_grad_kernel(cols, places, n_ref, h_ref, gg_ref, ug_ref, og_ref, got_ref, *refs):
    outs, sum_ref = refs[:-1], refs[-1]

    def put(rows, tile):
        sum_ref[:, rows, :] = (tile + got_ref[:, rows, :].astype(F32)).astype(BF)

    ffn_terms(n_ref, h_ref, gg_ref, ug_ref, og_ref, cols, put)
    for i in range(NX):
        for k in range(2):
            at = (places[X] + i) % NX * 2 + (places[YH] + k) % 2
            if len(outs) == 4:
                outs[i][k] = sum_ref[at]
            else:
                outs[k][i] = sum_ref[at]


def ffn_grad_first_kernel(*refs):
    ffn_grad_kernel(slice(0, 256), *refs)


def ffn_grad_second_kernel(*refs):
    ffn_grad_kernel(slice(256, 512), *refs[:7], *refs[8:10], refs[11])
    refs[10][...] = refs[7][...]


def ffn_grad_first(places, args, deps):
    return call(
        ffn_grad_first_kernel,
        [((2, 576, 256), BF)] * 4,
        [places, *args],
        COST["ffn_grad"],
        scratch=[pltpu.VMEM((8, 576, 256), BF)],
        deps=deps,
    )


def ffn_grad_second(places, args, down_part, deps):
    return call(
        ffn_grad_second_kernel,
        [((4, 576, 256), BF)] * 2 + [((TOKENS, D), BF)],
        [places, *args, down_part],
        COST["ffn_grad_second"],
        scratch=[pltpu.VMEM((8, 576, 256), BF)],
        deps=deps,
    )


def y_sum_kernel(places, mine, got, *outs):
    for i in range(NX):
        outs[i][...] = (mine[i].astype(F32) + got[i].astype(F32)).astype(BF)


def y_sum(places, mine, got, deps):
    return call(
        y_sum_kernel,
        [(mine.shape[1:], BF)] * 4,
        [places, mine, got],
        COST["y_sum"],
        deps=deps,
    )


def ffn_join_kernel(places, mine, got, a, b, c, d, out):
    out[:, :256] = (mine[...] + got[...].astype(F32)).astype(BF)
    total = a[...].astype(F32) + b[...].astype(F32) + c[...].astype(F32) + d[...].astype(F32)
    out[:, 256:] = total.astype(BF)


def ffn_join(places, mine, got, terms, deps):
    return call(
        ffn_join_kernel,
        [((576, 512), BF)],
        [places, mine, got, *terms],
        COST["add"],
        deps=deps,
    )[0]


def rms_back(grad, v, gain):
    r = lax.rsqrt(jnp.mean(v * v, axis=1, keepdims=True) + EPSILON)
    pulled = grad * gain
    return r * pulled - v * (r * r * r * jnp.mean(pulled * v, axis=1, keepdims=True))


def middle_back_kernel(places, own, g1, g2, g3, middle, og, gain, w_ref, mid_ref, branch_ref, *outs):
    grad = own[...] + g1[...].astype(F32) + g2[...].astype(F32) + g3[...].astype(F32)
    mid = og[...].astype(F32) + rms_back(grad, middle[...], gain[...])
    mid_ref[...] = mid
    branch = mid.astype(BF)
    branch_ref[...] = branch
    for i in range(NZ):
        outs[i][...] = mm_t(branch, w_ref[at_rows((places[Z] + i) % NZ, QW), :]).astype(BF)


def middle_back(places, chunks, middle, og, gain, w_out, deps):
    return call(
        middle_back_kernel,
        [((ROWS, D), F32), ((ROWS, D), BF)] + [((ROWS, QW), BF)] * 4,
        [places, *chunks, middle, og, gain, w_out],
        COST["middle_back"],
        deps=deps,
    )


def input_back_kernel(places, grad, x, mid, gain, out_ref):
    out_ref[...] = mid[...] + rms_back(grad[...].astype(F32), x[...].astype(F32), gain[...])


def input_back(places, grad, x, mid, gain, deps):
    return call(
        input_back_kernel, [((ROWS, D), F32)], [places, grad, x, mid, gain], 2, deps=deps
    )[0]


def scatter(chunks):
    far = [shift_z(chunks[1], 1), shift_z(chunks[3], -1), shift_z(chunks[2], 2)]
    return [chunks[0], *far]


def x_sum_kernel(places, a, b, c, d, mine, sent):
    mine[...] = a[0].astype(F32) + b[0].astype(F32) + c[0].astype(F32) + d[0].astype(F32)
    total = a[1].astype(F32) + b[1].astype(F32) + c[1].astype(F32) + d[1].astype(F32)
    sent[...] = total.astype(BF)


def x_sum(places, terms, us, deps):
    shape = terms[0].shape[1:]
    return call(x_sum_kernel, [(shape, F32), (shape, BF)], [places, *terms], us, deps=deps)


def add_kernel(places, a, b, out):
    out[...] = (a[...].astype(F32) + b[...].astype(F32)).astype(BF)


def added(places, a, b, deps):
    return call(add_kernel, [(a.shape, BF)], [places, a, b], COST["add"], deps=deps)[0]


def over_x(chunks):
    far = [shift_x(chunks[1], 1), shift_x(chunks[3], -1), shift_x(chunks[2], 2)]
    return [chunks[0], *far]


def as_row(column):
    return jnp.broadcast_to(column, (column.shape[0], 128)).T[:1]


def ffn_out_kernel(
    places, p0, p1, p2, p3, wg, wu, gain, gate_ref, up_ref, down_ref, gain_ref, all_ref, acc_ref
):
    j = pl.program_id(0)

    @pl.when(j == 0)
    def _():
        for i, p in enumerate((p0, p1, p2, p3)):
            all_ref[(places[Z] + i) % NZ] = p[...]
        acc_ref[...] = jnp.zeros_like(acc_ref)

    cols = pl.ds(pl.multiple_of(j % 2 * 256, 256), 256)
    for k, (w, out) in enumerate(((wg, gate_ref), (wu, up_ref))):
        rows = pl.ds(pl.multiple_of((2 * k + j // 2) * 96, 96), 96)
        parts = [all_ref[q, rows, cols].astype(F32) for q in range(NZ)]
        for b in range(4):
            tile = jnp.concatenate([v[:, b * 64 : (b + 1) * 64] for v in parts], axis=1)
            at = slice(b * 256, (b + 1) * 256)
            out[:, at] = tile
            acc_ref[...] += jnp.sum(tile * w[:, at].astype(F32), axis=1, keepdims=True)
    for t in range(3):
        r = 384 + 64 * t
        down_ref[:, t * 512 : (t + 1) * 512] = all_ref[j, r : r + 64, :].astype(F32)

    @pl.when(j == 3)
    def _():
        gain_ref[...] = as_row(acc_ref[...] / gain[...])


def ffn_out(places, pieces, wg, wu, gain, deps):
    whole = lambda shape: pl.BlockSpec(shape, lambda j: (0,) * len(shape))
    cols = pl.BlockSpec((96, 1024), lambda j: (0, j))
    return call(
        ffn_out_kernel,
        [((96, FF), F32), ((96, FF), F32), ((256, D), F32), ((1, 96), F32)],
        [places, *pieces, wg, wu, gain],
        4,
        scratch=[pltpu.VMEM((NZ, 576, 512), BF), pltpu.VMEM((96, 1), F32)],
        deps=deps,
        grid=(4,),
        in_specs=[SMEM] + [whole((576, 512))] * 4 + [cols, cols, whole((96, 1))],
        out_specs=[cols, cols, pl.BlockSpec((64, D), lambda j: (j, 0)), whole((1, 96))],
    )


def out_slices_kernel(places, p0, p1, p2, p3, *refs):
    all_ref = refs[4]
    for i, p in enumerate((p0, p1, p2, p3)):
        all_ref[(places[Z] + i) % NZ] = p[96:, :]
    for i in range(NX):
        refs[i][...] = all_ref[(places[X] + i) % NX]


def out_slices(places, pieces, deps):
    return call(
        out_slices_kernel,
        [((48, 768), BF)] * 4,
        [places, *pieces],
        1,
        scratch=[pltpu.VMEM((NZ, 48, 768), BF)],
        deps=deps,
    )


def qkv_out_kernel(
    places, p0, p1, p2, p3, wq, wk, wv, own_gain, q_ref, k_ref, v_ref, gain_ref, all_ref
):
    for i, p in enumerate((p0, p1, p2, p3)):
        all_ref[(places[Z] + i) % NZ] = p[:96, :]
    for q in range(NZ):
        q_ref[:, q * QW : (q + 1) * QW] = all_ref[q, :, :QW].astype(F32)
    gain = jnp.sum(q_ref[...] * wq[...].astype(F32), axis=1, keepdims=True)
    for out, w, at in ((k_ref, wk, QW), (v_ref, wv, QW + KW)):
        tile = jnp.concatenate(
            [all_ref[q, :, at : at + KW].astype(F32) for q in range(NZ)], axis=1
        )
        out[...] = tile
        gain += jnp.sum(tile * w[...].astype(F32), axis=1, keepdims=True)
    gain_ref[...] = as_row(gain / own_gain[...])


def qkv_out(places, pieces, wq, wk, wv, gain, deps):
    return call(
        qkv_out_kernel,
        [((96, 1536), F32), ((96, 768), F32), ((96, 768), F32), ((1, 96), F32)],
        [places, *pieces, wq, wk, wv, gain],
        2,
        scratch=[pltpu.VMEM((NZ, 96, 768), BF)],
        deps=deps,
    )


def out_out_kernel(places, p0, p1, p2, p3, out_ref):
    for i, p in enumerate((p0, p1, p2, p3)):
        tile = p[...].astype(F32)
        rows = pl.ds(pl.multiple_of((places[X] + i) % NX * 24, 8), 24)
        out_ref[rows, :] = jnp.concatenate([tile[:24], tile[24:]], axis=1)


def out_out(places, pieces):
    return call(out_out_kernel, [((96, D), F32)], [places, *pieces], 1)[0]


def block_out_kernel(places, middle, down, out_ref):
    out_ref[...] = (middle[...] + down[...].astype(F32)).astype(BF)


def block_out_of(places, middle, down, deps):
    return call(block_out_kernel, [((ROWS, D), BF)], [places, middle, down], 1, deps=deps)[0]


def body(
    inputs, norm_attn, w_query, w_key, w_value, w_out, norm_ffn, w_gate, w_up, w_down, cotangent
):
    f, s = lax.axis_index("fsdp"), lax.axis_index("sp")
    x, yh, c, z, yl = f // 4, f // 2 % 2, f % 2, s // 2, s % 2
    places = jnp.stack([x, yh, c, z, yl]).astype(jnp.int32)
    x_own, og_own = inputs[0], cotangent[0]
    gain_attn, gain_ffn = norm_attn[None], norm_ffn[None]

    def column(gain):
        return lax.dynamic_slice_in_dim(gain, f * 96, 96, 0)[:, None]

    index = jnp.arange(TOKENS, dtype=jnp.int32)
    positions = (index // ROWS * 2 + yl) * ROWS + index % ROWS
    lane = np.arange(QW) % HEAD_DIM
    frequency = ROPE_BASE ** (-(jnp.arange(HALF, dtype=F32) * 2.0 / HEAD_DIM))
    frequency = jnp.concatenate([frequency] * (QW // HALF))
    angles = positions.astype(F32)[:, None] * frequency[None, :]
    sign = np.where(lane < HALF, -1.0, 1.0).astype(np.float32)
    cosine, sine = jnp.cos(angles), jnp.sin(angles) * sign[None, :]

    qkv_shard, row_shard = cut(
        places, w_query, w_key, w_value, w_gate, w_up, w_down, w_out
    )
    qkv_mirror, row_mirror = mirror_y(qkv_shard), mirror_y(row_shard)
    xs = two_stage_z(x_own)
    (qkv_pair,) = paired(places, qkv_shard, qkv_mirror, [96], [cosine, sine, gain_attn])
    qkv_mine = two_stage_x(qkv_pair)
    qkv_other = [swap_core(p) for p in qkv_mine]
    ffn_pair, rest_pair = paired(
        places, row_shard, row_mirror, [288, 576], [qkv_mine[1], qkv_mine[2], xs[1], xs[2]]
    )
    packed = gather_xc(rest_pair)
    ffn_mine = two_stage_x(ffn_pair)

    normed, x_all, og_copy, turned_mine, turned_sent = norm(places, gain_attn, og_own, xs)
    ogs = two_stage_z(og_copy)
    q, kv, held_qkv = qkv(places, normed, qkv_mine, qkv_other, cosine, sine)
    kv_other = swap_low(kv)
    mixed, shares = attend(
        places, q, kv, kv_other, [ogs[1], ogs[2]]
    )
    mixed_pieces = two_stage_z(mixed)
    ffn_mine[2] = copied(places, [ffn_mine[2]], [mixed_pieces[1], mixed_pieces[3], ogs[2]])[0]
    ffn_other = [swap_core(p) for p in ffn_mine]
    normed_ffn, middle_own = middle_of(places, x_all, mixed_pieces, packed, gain_ffn)
    outs = ffn(places, normed_ffn, ogs, packed, ffn_mine, ffn_other)
    hidden, gate_grad, up_grad, og_all = outs[:4]
    in_chunks = outs[4:8]

    in_got = scatter(in_chunks)
    a_sent, b_sent, n_mine, h_mine, down_part = ffn_sent_of(
        places, normed_ffn, hidden, gate_grad, up_grad, og_all, packed
    )
    held_out = lay(places, packed, [n_mine])
    back = middle_back(places, in_got, middle_own, og_own, gain_ffn, held_out, [n_mine])
    middle_grad, branch = back[:2]
    head_grads = [back[2], shift_z(back[5], -1), shift_z(back[4], 2), shift_z(back[3], 1)]
    branch_all = gather_z(branch)
    a_got, b_got = swap_core(a_sent), swap_core(b_sent)
    ffn_args = (n_mine, h_mine, gate_grad, up_grad, og_all)
    a_chunks = ffn_grad_first(places, (*ffn_args, a_got), [branch])
    a_terms = over_x(a_chunks)

    dq, dkv_own, dkv_sent = attend_back(
        places, head_grads, q, kv, kv_other, shares, [a_chunks[0]]
    )
    b_mine, b_sent, down_part = ffn_grad_second(places, (*ffn_args, b_got), down_part, [dq])
    down_own = scatter_z(down_part)
    b_got = mirror_y(b_sent)
    dkv_got = swap_low(dkv_sent)
    lin, out_part, qkv_sent = turn(
        places, dq, dkv_own, dkv_got, cosine, sine, turned_sent, mixed, branch_all, [b_sent]
    )
    qkv_got = swap_core(qkv_sent)
    first_part = first(places, lin, held_qkv, [])
    first_got = scatter_z(first_part)
    a_half, a_sent = x_sum(places, a_terms, COST["x_sum"], [first_part])
    a_got = mirror_y(a_sent)
    qkv_chunks = qkv_grad(places, lin, turned_mine, out_part, qkv_got, [a_sent])
    qkv_terms = over_x(qkv_chunks)
    b_terms = over_x(y_sum(places, b_mine, b_got, [qkv_chunks[0]]))

    qkv_half, qkv_sent = x_sum(places, qkv_terms, 2, [])
    qkv_got = mirror_y(qkv_sent)
    ffn_half = ffn_join(places, a_half, a_got, b_terms, [qkv_sent])
    ffn_low = swap_low(ffn_half)
    qkv_half = added(places, qkv_half, qkv_got, [ffn_half])
    qkv_low = swap_low(qkv_half)
    qkv_total = added(places, qkv_half, qkv_low, [])
    qkv_pieces = pieces_z(qkv_total)
    ffn_total = added(places, ffn_half, ffn_low, [qkv_total])
    ffn_pieces = pieces_z(ffn_total)

    block_out = block_out_of(places, middle_own, down_own, [qkv_total])
    input_grad = input_back(places, first_got, x_own, middle_grad, gain_attn, [qkv_total])
    out_terms = over_x(out_slices(places, qkv_pieces, [block_out, input_grad]))
    grad_query, grad_key, grad_value, qkv_gain = qkv_out(
        places, qkv_pieces, w_query, w_key, w_value, column(norm_attn), [out_terms[0]]
    )
    grad_gate, grad_up, grad_down, ffn_gain = ffn_out(
        places, ffn_pieces, w_gate, w_up, column(norm_ffn), [qkv_gain]
    )
    grad_out = out_out(places, [out_terms[0], out_terms[2], out_terms[3], out_terms[1]])
    grad_norm_attn, grad_norm_ffn = qkv_gain[0], ffn_gain[0]
    return (
        block_out[None],
        input_grad[None],
        grad_norm_attn,
        grad_query,
        grad_key,
        grad_value,
        grad_out,
        grad_norm_ffn,
        grad_gate,
        grad_up,
        grad_down,
    )


def solution(mesh):
    rows = P("fsdp", None)
    tokens = P("fsdp", "sp", None)
    return jax.shard_map(
        body,
        mesh=mesh,
        in_specs=(tokens, P(), rows, rows, rows, rows, P(), rows, rows, rows, tokens),
        out_specs=(tokens, tokens, P("fsdp"), rows, rows, rows, rows, P("fsdp"), rows, rows, rows),
        check_vma=False,
    )
```

```python
import functools

import jax
import jax.numpy as jnp
import numpy as np
from jax import lax
from jax.experimental import pallas as pl
from jax.experimental.pallas import tpu as pltpu
from jax.sharding import PartitionSpec as P

D = 1536
HEADS = 16
KV_HEADS = 8
HEAD_DIM = 96
FF = 4096

EPSILON = 1e-05
ROPE_BASE = 100000.0
MASKED = -1e30

NX, NZ = 4, 4
ROWS = 128
TOKENS = ROWS * NZ
QW, KW = 384, 192
HALF = HEAD_DIM // 2
FFZ = FF // NZ
BF = jnp.bfloat16
F32 = jnp.float32
VMEM = pl.BlockSpec(memory_space=pltpu.VMEM)
SMEM = pl.BlockSpec(memory_space=pltpu.SMEM)
ANY = pl.BlockSpec(memory_space=pl.ANY)
LIMIT = pltpu.CompilerParams(vmem_limit_bytes=56 * 1024 * 1024)
X, YH, CORE, Z, YL = range(5)
SPLIT = 384
COST = {
    "norm": 54,
    "qkv": 0.1,
    "attend": 0.1,
    "lay": 0.1,
    "middle": 4,
    "ffn": 17,
    "ffn_sent": 0.1,
    "middle_back": 60,
    "ffn_grad": 60,
    "ffn_grad_second": 0.1,
    "attend_back": 60,
    "turn": 0.1,
    "first": 0.1,
    "x_sum": 60,
    "y_sum": 0.1,
    "qkv_grad": 0.1,
    "add": 8,
}


Z_GROUPS = [[z * 2 + l for z in range(NZ)] for l in range(2)]


def scatter_z(v):
    return lax.psum_scatter(
        v, "sp", scatter_dimension=0, tiled=True, axis_index_groups=Z_GROUPS
    )


def gather_z(v):
    return lax.all_gather(v, "sp", axis=0, tiled=True, axis_index_groups=Z_GROUPS)


def shift_z(v, step):
    pairs = [(z * 2 + l, (z + step) % NZ * 2 + l) for z in range(NZ) for l in range(2)]
    return lax.ppermute(v, "sp", pairs)


def swap_low(v):
    return lax.ppermute(v, "sp", [(s, s ^ 1) for s in range(8)])


def shift_x(v, step):
    pairs = [(x * 4 + r, (x + step) % NX * 4 + r) for x in range(NX) for r in range(4)]
    return lax.ppermute(v, "fsdp", pairs)


def swap_core(v):
    return lax.ppermute(v, "fsdp", [(f, f ^ 1) for f in range(16)])


def mirror_y(v):
    pairs = [(f * 8 + s, (f ^ 2) * 8 + (s ^ 1)) for f in range(16) for s in range(8)]
    return lax.ppermute(v, ("fsdp", "sp"), pairs)


def pieces_z(v):
    far = [shift_z(v, -1), shift_z(v, 1), shift_z(v, 2)]
    return [v, far[0], far[2], far[1]]


def two_stage_z(v):
    above, below = shift_z(v, -1), shift_z(v, 1)
    return [v, above, shift_z(below, 1), below]


def two_stage_x(v):
    above, below = shift_x(v, -1), shift_x(v, 1)
    return [v, above, shift_x(below, 1), below]


def pieces_x(v):
    far = [shift_x(v, -1), shift_x(v, 1), shift_x(v, 2)]
    return [v, far[0], far[2], far[1]]


def part(v, index, size, dim=0):
    return lax.dynamic_slice_in_dim(v, index * size, size, dim)


def call(kernel, outs, ins, us, scratch=(), deps=(), grid=(), in_specs=None, out_specs=None):
    def run(*refs):
        kernel(*refs[: len(ins)], *refs[len(ins) + len(deps) :])

    return pl.pallas_call(
        run,
        name=kernel.__name__.replace("_kernel", ""),
        grid=grid,
        out_shape=[jax.ShapeDtypeStruct(s, t) for s, t in outs],
        in_specs=(in_specs or [SMEM] + [VMEM] * (len(ins) - 1)) + [ANY] * len(deps),
        out_specs=out_specs or [VMEM] * len(outs),
        scratch_shapes=scratch,
        compiler_params=LIMIT,
        cost_estimate=pl.CostEstimate(
            flops=int(us * 1e9), bytes_accessed=int(us * 3e6), transcendentals=0
        ),
    )(*ins, *deps)


def mm(a, b):
    return jnp.dot(a, b, preferred_element_type=F32)


def mm_t(a, b):
    return lax.dot_general(a, b, (((1,), (1,)), ((), ())), preferred_element_type=F32)


def t_mm(a, b):
    return lax.dot_general(a, b, (((0,), (0,)), ((), ())), preferred_element_type=F32)


def at_rows(index, size):
    return pl.ds(pl.multiple_of(index * size, size), size)


def rope(v, cosine, sine):
    width = v.shape[1]
    lane = lax.broadcasted_iota(jnp.int32, v.shape, 1) % HEAD_DIM
    partner = jnp.where(
        lane < HALF, pltpu.roll(v, width - HALF, 1), pltpu.roll(v, HALF, 1)
    )
    return v * cosine + partner * sine


def rope_keys(kv, cosine, sine):
    lane = lax.broadcasted_iota(jnp.int32, kv.shape, 1)
    return jnp.where(lane < KW, rope(kv, cosine, sine), kv)


def cut_kernel(places, wq, wk, wv, wg, wu, wd, wo, qkv_ref, rows_ref):
    z = places[Z]
    for t in range(3):
        cols = slice(t * 512, (t + 1) * 512)
        rows_ref[96 * t : 96 * (t + 1), :] = wo[:, cols]
        rows_ref[672 + 64 * t : 736 + 64 * t, :] = wd[at_rows(z, 64), cols]
    qkv_ref[:, :QW] = wq[:, pl.ds(pl.multiple_of(z * QW, 128), QW)]
    for at in range(NZ):

        @pl.when(z == at)
        def _():
            cols = slice(at * KW, (at + 1) * KW)
            qkv_ref[:, QW:] = jnp.concatenate([wk[:, cols], wv[:, cols]], axis=1)
            for k, w in enumerate((wg, wu)):
                for half in range(2):
                    starts = [(8 * half + i) * 256 + at * 64 for i in range(8)]
                    rows = slice(288 + (2 * half + k) * 96, 384 + (2 * half + k) * 96)
                    rows_ref[rows, :] = jnp.concatenate([w[:, b : b + 64] for b in starts], axis=1)


def cut(places, *arrays):
    return call(cut_kernel, [((96, 768), BF), ((864, 512), BF)], [places, *arrays], 3)


def copy_kernel(places, *refs):
    n = len(refs) // 2
    for i in range(n):
        refs[n + i][...] = refs[i][...]


def copied(places, arrays, deps):
    return call(copy_kernel, [(v.shape, v.dtype) for v in arrays], [places, *arrays], 0.1, deps=deps)


def pair_kernel(places, own, mirror, *outs):
    start = 0
    for out in outs:
        rows = slice(start, start + out.shape[1])
        out[places[YH]] = own[rows, :]
        out[1 - places[YH]] = mirror[rows, :]
        start += out.shape[1]


def paired(places, own, mirror, parts, deps):
    outs = [((2, n, own.shape[1]), BF) for n in parts]
    return call(pair_kernel, outs, [places, own, mirror], 0.1, deps=deps)


def norm_kernel(places, gain, og, *refs):
    xs, (normed_ref, x_ref, og_ref, mine_ref, sent_ref, turned_ref) = refs[:4], refs[4:]
    og_ref[...] = og[...]
    for i in range(NZ):
        x_ref[at_rows((places[Z] + i) % NZ, ROWS), :] = xs[i][...]
    for i in range(NZ):
        rows = pl.ds(i * ROWS, ROWS)
        v = x_ref[rows, :].astype(F32)
        r = lax.rsqrt(jnp.mean(v * v, axis=1, keepdims=True) + EPSILON)
        normed_ref[rows, :] = (v * r * gain[...]).astype(BF)
    turned_ref[...] = normed_ref[...].T
    split_cores(places, turned_ref, mine_ref, sent_ref, 96)


def split_cores(places, turned_ref, mine_ref, sent_ref, n):
    for k in range(8):
        rows = slice(k * n, (k + 1) * n)
        mine_ref[rows, :] = turned_ref[at_rows(2 * k + places[CORE], n), :]
        sent_ref[rows, :] = turned_ref[at_rows(2 * k + 1 - places[CORE], n), :]


def norm(places, gain, og, xs):
    return call(
        norm_kernel,
        [((TOKENS, D), BF)] * 2 + [((ROWS, D), BF)] + [((D // 2, TOKENS), BF)] * 2,
        [places, gain, og, *xs],
        COST["norm"],
        scratch=[pltpu.VMEM((D, TOKENS), BF)],
    )


def qkv_kernel(places, normed_ref, *refs):
    mine, other = refs[:4], refs[4:8]
    cosine, sine, q_ref, kv_ref, w_ref = refs[8:]
    for i in range(NX):
        for h in range(2):
            base = (places[X] + i) % NX * 4 + h * 2
            w_ref[at_rows(base + places[CORE], 96), :] = mine[i][h]
            w_ref[at_rows(base + 1 - places[CORE], 96), :] = other[i][h]
    for i in range(NZ):
        rows = pl.ds(i * ROWS, ROWS)
        lin = mm(normed_ref[rows, :], w_ref[...])
        q_ref[rows, :] = rope(lin[:, :QW], cosine[rows, :], sine[rows, :]).astype(BF)
        kv_ref[rows, :] = rope_keys(lin[:, QW:], cosine[rows, :], sine[rows, :]).astype(BF)


def qkv(places, normed, mine, other, cosine, sine):
    return call(
        qkv_kernel,
        [((TOKENS, QW), BF), ((TOKENS, 2 * KW), BF), ((D, QW + 2 * KW), BF)],
        [places, normed, *mine, *other, cosine, sine],
        COST["qkv"],
    )


def head(ref, rows, index):
    return ref[rows, index * HEAD_DIM : (index + 1) * HEAD_DIM]


def two_heads(ref, j, g):
    rows = slice(j * ROWS, (j + 1) * ROWS)
    return jnp.concatenate([head(ref, rows, 2 * g), head(ref, rows, 2 * g + 1)], axis=0)


def attend_kernel(places, q_ref, own_ref, other_ref, mixed_ref, p_ref):
    late = places[YL]
    factor = HEAD_DIM ** (-0.5)
    for g in range(2):
        for j in range(NZ):
            n = (j + 1) * ROWS
            q = two_heads(q_ref, j, g)
            s_own = mm_t(q, head(own_ref, slice(0, n), g)) * factor
            s_oth = mm_t(q, head(other_ref, slice(0, n), g)) * factor
            shape = (2 * ROWS, n)
            row = lax.broadcasted_iota(jnp.int32, shape, 0) % ROWS + j * ROWS
            col = lax.broadcasted_iota(jnp.int32, shape, 1)
            s_own = jnp.where(col <= row, s_own, MASKED)
            s_oth = jnp.where(col < (j + late) * ROWS, s_oth, MASKED)
            highest = jnp.maximum(
                jnp.max(s_own, axis=1, keepdims=True), jnp.max(s_oth, axis=1, keepdims=True)
            )
            p_own, p_oth = jnp.exp(s_own - highest), jnp.exp(s_oth - highest)
            total = jnp.sum(p_own, axis=1, keepdims=True) + jnp.sum(p_oth, axis=1, keepdims=True)
            scale = 1.0 / total
            p_own, p_oth = (p_own * scale).astype(BF), (p_oth * scale).astype(BF)
            p_ref[g, j, :, :n] = p_own
            p_ref[g, j, :, n : 2 * n] = p_oth
            out = mm(p_own, head(own_ref, slice(0, n), 2 + g)) + mm(
                p_oth, head(other_ref, slice(0, n), 2 + g)
            )
            out = out.astype(BF)
            for k in range(2):
                h = 2 * g + k
                mixed_ref[j * ROWS : (j + 1) * ROWS, h * HEAD_DIM : (h + 1) * HEAD_DIM] = out[
                    k * ROWS : (k + 1) * ROWS
                ]


def attend(places, q, kv, kv_other, deps):
    return call(
        attend_kernel,
        [((TOKENS, QW), BF), ((2, NZ, 2 * ROWS, 2 * TOKENS), BF)],
        [places, q, kv, kv_other],
        COST["attend"],
        deps=deps,
    )


def attend_back_kernel(places, *refs):
    grads = refs[:4]
    q_ref, own_ref, other_ref, p_ref = refs[4:8]
    dq_ref, down_ref, doth_ref = refs[8:11]
    do_ref, acc_own, acc_oth = refs[11:]
    factor = HEAD_DIM ** (-0.5)
    for i in range(NZ):
        do_ref[at_rows((places[Z] + i) % NZ, ROWS), :] = grads[i][...]
    for g in range(2):
        acc_own[...] = jnp.zeros_like(acc_own)
        acc_oth[...] = jnp.zeros_like(acc_oth)
        for j in range(NZ):
            n = (j + 1) * ROWS
            seen = slice(0, n)
            q = two_heads(q_ref, j, g)
            do = two_heads(do_ref, j, g)
            p_own, p_oth = p_ref[g, j, :, :n], p_ref[g, j, :, n : 2 * n]
            dp_own = mm_t(do, head(own_ref, seen, 2 + g))
            dp_oth = mm_t(do, head(other_ref, seen, 2 + g))
            f_own, f_oth = p_own.astype(F32), p_oth.astype(F32)
            dot = jnp.sum(f_own * dp_own, axis=1, keepdims=True) + jnp.sum(
                f_oth * dp_oth, axis=1, keepdims=True
            )
            ds_own = (f_own * (dp_own - dot)).astype(BF)
            ds_oth = (f_oth * (dp_oth - dot)).astype(BF)
            dq = mm(ds_own, head(own_ref, seen, g)) + mm(ds_oth, head(other_ref, seen, g))
            dq = (dq * factor).astype(BF)
            for k in range(2):
                h = 2 * g + k
                dq_ref[j * ROWS : (j + 1) * ROWS, h * HEAD_DIM : (h + 1) * HEAD_DIM] = dq[
                    k * ROWS : (k + 1) * ROWS
                ]
            acc_own[0, seen, :] += t_mm(ds_own, q)
            acc_own[1, seen, :] += t_mm(p_own, do)
            acc_oth[0, seen, :] += t_mm(ds_oth, q)
            acc_oth[1, seen, :] += t_mm(p_oth, do)
        for kind, scale in ((0, factor), (1, 1.0)):
            at = kind * KW + g * HEAD_DIM
            down_ref[:, at : at + HEAD_DIM] = acc_own[kind] * scale
            doth_ref[:, at : at + HEAD_DIM] = (acc_oth[kind] * scale).astype(BF)


def attend_back(places, grads, q, kv, kv_other, shares, deps):
    acc = pltpu.VMEM((2, TOKENS, HEAD_DIM), F32)
    return call(
        attend_back_kernel,
        [((TOKENS, QW), BF), ((TOKENS, 2 * KW), F32), ((TOKENS, 2 * KW), BF)],
        [places, *grads, q, kv, kv_other, shares],
        COST["attend_back"],
        scratch=[pltpu.VMEM((TOKENS, QW), BF), acc, acc],
        deps=deps,
    )


def send_chunks(refs, acc_ref, places):
    for i in range(NZ):
        rows = at_rows((places[Z] + i) % NZ, ROWS)
        refs[i][...] = acc_ref[rows, :].astype(refs[i].dtype)


CHUNKS = [((ROWS, D), F32)] + [((ROWS, D), BF)] * 3


def put_out(out_ref, places, core, ref):
    for k in range(8):
        rows = pl.ds(pl.multiple_of((k % 2 * 2 + core) * 96 + k // 2 * 24, 8), 24)
        tile = out_ref[rows, :]
        ref[k, 96:, :] = jnp.concatenate([tile[:, :768], tile[:, 768:]], axis=0).astype(BF)


def turn_kernel(
    places, dq_ref, own_ref, got_ref, cosine, sine, turned_ref, mixed_ref, branch_ref, *refs
):
    lin_ref, out_ref, sent_ref = refs
    for i in range(NZ):
        rows = slice(i * ROWS, (i + 1) * ROWS)
        dkv = (own_ref[rows, :] + got_ref[rows, :].astype(F32)).astype(BF)
        c, s = cosine[rows, :], -sine[rows, :]
        lin_ref[rows, :QW] = rope(dq_ref[rows, :].astype(F32), c, s).astype(BF)
        lin_ref[rows, QW:] = rope_keys(dkv.astype(F32), c, s).astype(BF)
    for k in range(8):
        sent_ref[k, :96, :] = mm(turned_ref[k * 96 : (k + 1) * 96, :], lin_ref[...]).astype(BF)
    out_ref[...] = t_mm(mixed_ref[...], branch_ref[...])
    put_out(out_ref, places, 1 - places[CORE], sent_ref)


def turn(places, dq, dkv_own, dkv_got, cosine, sine, turned, mixed, branch, deps):
    return call(
        turn_kernel,
        [((TOKENS, 768), BF), ((QW, D), F32), ((8, 144, 768), BF)],
        [places, dq, dkv_own, dkv_got, cosine, sine, turned, mixed, branch],
        COST["turn"],
        deps=deps,
    )


def first_kernel(places, lin_ref, w_ref, out_ref):
    out_ref[...] = mm_t(lin_ref[...], w_ref[...]).astype(BF)


def first(places, lin, w, deps):
    return call(first_kernel, [((TOKENS, D), BF)], [places, lin, w], COST["first"], deps=deps)[0]


def qkv_grad_kernel(places, lin_ref, turned_ref, out_ref, got_ref, *refs):
    outs, sum_ref = refs[:4], refs[4]
    for k in range(8):
        sum_ref[k, :96, :] = mm(turned_ref[k * 96 : (k + 1) * 96, :], lin_ref[...]).astype(BF)
    put_out(out_ref, places, places[CORE], sum_ref)
    for i in range(NX):
        for k in range(2):
            at = (places[X] + i) % NX * 2 + (places[YH] + k) % 2
            outs[i][k] = (sum_ref[at].astype(F32) + got_ref[at].astype(F32)).astype(BF)


def qkv_grad(places, lin, turned, out, got, deps):
    return call(
        qkv_grad_kernel,
        [((2, 144, 768), BF)] * 4,
        [places, lin, turned, out, got],
        COST["qkv_grad"],
        scratch=[pltpu.VMEM((8, 144, 768), BF)],
        deps=deps,
    )


def piece_rows(pieces, i, h, start, n):
    if i == 2:
        ref, start = (pieces[3], start) if start < SPLIT else (pieces[4], start - SPLIT)
    else:
        ref = pieces[(0, 1, None, 2)[i]]
    return ref[h, start : start + n, :]


def each_shard(places, pieces):
    for i in range(NX):
        for h in range(2):
            base = (places[X] + i) % NX * 4 + h * 2
            yield base + places[CORE], pieces[:5], i, h
            yield base + 1 - places[CORE], pieces[5:], i, h


def halves_kernel(places, above, below, first_ref, second_ref):
    first_ref[...] = below[:, :SPLIT]
    second_ref[...] = above[:, SPLIT:]


def halves(places, above, below):
    return call(
        halves_kernel,
        [((2, SPLIT, 512), BF), ((2, 864 - SPLIT, 512), BF)],
        [places, above, below],
        0.1,
    )


def lay_output(places, all_pieces, out_ref):
    for b, pieces, i, h in each_shard(places, all_pieces):
        for t in range(3):
            out_ref[at_rows(b, 96), t * 512 : (t + 1) * 512] = piece_rows(pieces, i, h, t * 96, 96)


def lay_down(places, all_pieces, out_ref):
    for b, pieces, i, h in each_shard(places, all_pieces):
        for t in range(3):
            tile = piece_rows(pieces, i, h, 672 + 64 * t, 64)
            out_ref[at_rows(b, 64), t * 512 : (t + 1) * 512] = tile


def lay_kernel(places, hidden_ref, *refs):
    pieces, out_ref, down_ref, wd_ref = refs[:10], *refs[10:]
    lay_output(places, pieces, out_ref)
    lay_down(places, pieces, wd_ref)
    down_ref[...] = mm(hidden_ref[...], wd_ref[...]).astype(BF)


def lay(places, hidden, pieces, deps):
    return call(
        lay_kernel,
        [((D, D), BF), ((TOKENS, D), BF)],
        [places, hidden, *pieces],
        COST["lay"],
        scratch=[pltpu.VMEM((FFZ, D), BF)],
        deps=deps,
    )


def middle_kernel(places, x_ref, gain, mixed, *refs):
    pieces, (normed_ref, own_ref, acc_ref, mixed_ref, w_ref) = refs[:10], refs[10:]
    lay_output(places, pieces, w_ref)
    for z in range(NZ):
        mixed_ref[:, z * QW : (z + 1) * QW] = mixed[z]
    for t in range(3):
        cols = slice(t * 512, (t + 1) * 512)
        acc_ref[:, cols] = x_ref[:, cols].astype(F32) + mm(mixed_ref[...], w_ref[:, cols])
    for i in range(NZ):
        rows = slice(i * ROWS, (i + 1) * ROWS)
        v = acc_ref[rows, :]
        r = lax.rsqrt(jnp.mean(v * v, axis=1, keepdims=True) + EPSILON)
        normed_ref[rows, :] = (v * r * gain[...]).astype(BF)
    own_ref[...] = acc_ref[at_rows(places[Z], ROWS), :]


def middle_of(places, x_all, gain, mixed, pieces):
    return call(
        middle_kernel,
        [((TOKENS, D), BF), ((ROWS, D), F32)],
        [places, x_all, gain, mixed, *pieces],
        COST["middle"],
        scratch=[
            pltpu.VMEM((TOKENS, D), F32),
            pltpu.VMEM((TOKENS, D), BF),
            pltpu.VMEM((D, D), BF),
        ],
    )


def ffn_kernel(places, n_ref, *refs):
    ogs, pieces, refs = refs[:4], refs[4:14], refs[14:]
    hidden_ref, gg_ref, ug_ref, og_ref = refs[:4]
    in_chunks = refs[4:8]
    in_acc, wg_ref, wu_ref, wd_ref = refs[8:]
    for i, g in enumerate(ogs):
        og_ref[at_rows((places[Z] + i) % NZ, ROWS), :] = g[...]
    lay_down(places, pieces, wd_ref)
    for j in range(2):
        cols = slice(j * 512, (j + 1) * 512)
        for b, some, i, h in each_shard(places, pieces):
            wg_ref[at_rows(b, 96), :] = piece_rows(some, i, h, 288 + 192 * j, 96)
            wu_ref[at_rows(b, 96), :] = piece_rows(some, i, h, 384 + 192 * j, 96)
        wg, wu, wd = wg_ref[...], wu_ref[...], wd_ref[cols, :]
        gate = mm(n_ref[...], wg)
        up = mm(n_ref[...], wu)
        hg = mm_t(og_ref[...], wd).astype(BF).astype(F32)
        sig = 1.0 / (1.0 + jnp.exp(-gate))
        silu = gate * sig
        hidden = (silu * up).astype(BF)
        gg = (hg * up * (sig * (1.0 + gate * (1.0 - sig)))).astype(BF)
        ug = (hg * silu).astype(BF)
        hidden_ref[:, cols] = hidden
        gg_ref[:, cols] = gg
        ug_ref[:, cols] = ug
        if j == 0:
            in_acc[...] = mm_t(gg, wg) + mm_t(ug, wu)
        else:
            in_acc[...] += mm_t(gg, wg) + mm_t(ug, wu)
    send_chunks(in_chunks, in_acc, places)


def ffn(places, normed, ogs, pieces):
    return call(
        ffn_kernel,
        [((TOKENS, FFZ), BF)] * 3 + [((TOKENS, D), BF)] + CHUNKS,
        [places, normed, *ogs, *pieces],
        COST["ffn"],
        scratch=[pltpu.VMEM((TOKENS, D), F32)]
        + [pltpu.VMEM((D, 512), BF)] * 2
        + [pltpu.VMEM((FFZ, D), BF)],
    )


def ffn_terms(n_ref, h_ref, gg_ref, ug_ref, og_ref, cols, put):
    for w, ref in enumerate((gg_ref, ug_ref)):
        for half in range(2):
            tile = mm(n_ref[...], ref[:, half * 512 + cols.start : half * 512 + cols.stop])
            r = (2 * w + half) * 96
            put(slice(r, r + 96), tile.reshape(8, 96, -1))
    for t in range(3):
        tile = mm(h_ref[...], og_ref[:, t * 512 + cols.start : t * 512 + cols.stop])
        put(slice(384 + 64 * t, 448 + 64 * t), tile.reshape(8, 64, -1))


def ffn_sent_kernel(places, n_ref, hidden_ref, gg_ref, ug_ref, og_ref, *refs):
    sent_refs, (n_mine, h_mine, n_turned, h_turned, n_sent, h_sent) = refs[:2], refs[2:]
    n_turned[...] = n_ref[...].T
    h_turned[...] = hidden_ref[...].T
    split_cores(places, n_turned, n_mine, n_sent, 96)
    split_cores(places, h_turned, h_mine, h_sent, 64)

    def put(rows, tile):
        for half, ref in enumerate(sent_refs):
            ref[:, rows, :] = tile[:, :, half * 256 : (half + 1) * 256].astype(BF)

    ffn_terms(n_sent, h_sent, gg_ref, ug_ref, og_ref, slice(0, 512), put)


def ffn_sent_of(places, normed, hidden, gg, ug, og):
    return call(
        ffn_sent_kernel,
        [((8, 576, 256), BF)] * 2 + [((D // 2, TOKENS), BF), ((FFZ // 2, TOKENS), BF)],
        [places, normed, hidden, gg, ug, og],
        COST["ffn_sent"],
        scratch=[
            pltpu.VMEM((D, TOKENS), BF),
            pltpu.VMEM((FFZ, TOKENS), BF),
            pltpu.VMEM((D // 2, TOKENS), BF),
            pltpu.VMEM((FFZ // 2, TOKENS), BF),
        ],
    )


def ffn_grad_kernel(cols, places, n_ref, h_ref, gg_ref, ug_ref, og_ref, got_ref, *refs):
    outs, sum_ref = refs[:-1], refs[-1]

    def put(rows, tile):
        sum_ref[:, rows, :] = (tile + got_ref[:, rows, :].astype(F32)).astype(BF)

    ffn_terms(n_ref, h_ref, gg_ref, ug_ref, og_ref, cols, put)
    for i in range(NX):
        for k in range(2):
            at = (places[X] + i) % NX * 2 + (places[YH] + k) % 2
            if len(outs) == 4:
                outs[i][k] = sum_ref[at]
            else:
                outs[k][i] = sum_ref[at]


def ffn_grad_first_kernel(*refs):
    ffn_grad_kernel(slice(0, 256), *refs)


def ffn_grad_second_kernel(*refs):
    ffn_grad_kernel(slice(256, 512), *refs[:7], *refs[8:10], refs[11])
    refs[10][...] = refs[7][...]


def ffn_grad_first(places, args, deps):
    return call(
        ffn_grad_first_kernel,
        [((2, 576, 256), BF)] * 4,
        [places, *args],
        COST["ffn_grad"],
        scratch=[pltpu.VMEM((8, 576, 256), BF)],
        deps=deps,
    )


def ffn_grad_second(places, args, down_part, deps):
    return call(
        ffn_grad_second_kernel,
        [((4, 576, 256), BF)] * 2 + [((TOKENS, D), BF)],
        [places, *args, down_part],
        COST["ffn_grad_second"],
        scratch=[pltpu.VMEM((8, 576, 256), BF)],
        deps=deps,
    )


def y_sum_kernel(places, mine, got, *outs):
    for i in range(NX):
        outs[i][...] = (mine[i].astype(F32) + got[i].astype(F32)).astype(BF)


def y_sum(places, mine, got, deps):
    return call(
        y_sum_kernel,
        [(mine.shape[1:], BF)] * 4,
        [places, mine, got],
        COST["y_sum"],
        deps=deps,
    )


def ffn_join_kernel(places, mine, got, a, b, c, d, out):
    out[:, :256] = (mine[...] + got[...].astype(F32)).astype(BF)
    total = a[...].astype(F32) + b[...].astype(F32) + c[...].astype(F32) + d[...].astype(F32)
    out[:, 256:] = total.astype(BF)


def ffn_join(places, mine, got, terms, deps):
    return call(
        ffn_join_kernel,
        [((576, 512), BF)],
        [places, mine, got, *terms],
        COST["add"],
        deps=deps,
    )[0]


def rms_back(grad, v, gain):
    r = lax.rsqrt(jnp.mean(v * v, axis=1, keepdims=True) + EPSILON)
    pulled = grad * gain
    return r * pulled - v * (r * r * r * jnp.mean(pulled * v, axis=1, keepdims=True))


def middle_back_kernel(places, own, g1, g2, g3, middle, og, gain, w_ref, mid_ref, branch_ref, *outs):
    grad = own[...] + g1[...].astype(F32) + g2[...].astype(F32) + g3[...].astype(F32)
    mid = og[...].astype(F32) + rms_back(grad, middle[...], gain[...])
    mid_ref[...] = mid
    branch = mid.astype(BF)
    branch_ref[...] = branch
    for i in range(NZ):
        outs[i][...] = mm_t(branch, w_ref[at_rows((places[Z] + i) % NZ, QW), :]).astype(BF)


def middle_back(places, chunks, middle, og, gain, w_out, deps):
    return call(
        middle_back_kernel,
        [((ROWS, D), F32), ((ROWS, D), BF)] + [((ROWS, QW), BF)] * 4,
        [places, *chunks, middle, og, gain, w_out],
        COST["middle_back"],
        deps=deps,
    )


def input_back_kernel(places, grad, x, mid, gain, out_ref):
    out_ref[...] = mid[...] + rms_back(grad[...].astype(F32), x[...].astype(F32), gain[...])


def input_back(places, grad, x, mid, gain, deps):
    return call(
        input_back_kernel, [((ROWS, D), F32)], [places, grad, x, mid, gain], 2, deps=deps
    )[0]


def scatter(chunks):
    far = [shift_z(chunks[1], 1), shift_z(chunks[3], -1), shift_z(chunks[2], 2)]
    return [chunks[0], *far]


def x_sum_kernel(places, a, b, c, d, mine, sent):
    mine[...] = a[0].astype(F32) + b[0].astype(F32) + c[0].astype(F32) + d[0].astype(F32)
    total = a[1].astype(F32) + b[1].astype(F32) + c[1].astype(F32) + d[1].astype(F32)
    sent[...] = total.astype(BF)


def x_sum(places, terms, us, deps):
    shape = terms[0].shape[1:]
    return call(x_sum_kernel, [(shape, F32), (shape, BF)], [places, *terms], us, deps=deps)


def add_kernel(places, a, b, out):
    out[...] = (a[...].astype(F32) + b[...].astype(F32)).astype(BF)


def added(places, a, b, deps):
    return call(add_kernel, [(a.shape, BF)], [places, a, b], COST["add"], deps=deps)[0]


def over_x(chunks):
    far = [shift_x(chunks[1], 1), shift_x(chunks[3], -1), shift_x(chunks[2], 2)]
    return [chunks[0], *far]


def as_row(column):
    return jnp.broadcast_to(column, (column.shape[0], 128)).T[:1]


def ffn_out_kernel(
    places, p0, p1, p2, p3, wg, wu, gain, gate_ref, up_ref, down_ref, gain_ref, all_ref, acc_ref
):
    j = pl.program_id(0)

    @pl.when(j == 0)
    def _():
        for i, p in enumerate((p0, p1, p2, p3)):
            all_ref[(places[Z] + i) % NZ] = p[...]
        acc_ref[...] = jnp.zeros_like(acc_ref)

    cols = pl.ds(pl.multiple_of(j % 2 * 256, 256), 256)
    for k, (w, out) in enumerate(((wg, gate_ref), (wu, up_ref))):
        rows = pl.ds(pl.multiple_of((2 * k + j // 2) * 96, 96), 96)
        parts = [all_ref[q, rows, cols].astype(F32) for q in range(NZ)]
        for b in range(4):
            tile = jnp.concatenate([v[:, b * 64 : (b + 1) * 64] for v in parts], axis=1)
            at = slice(b * 256, (b + 1) * 256)
            out[:, at] = tile
            acc_ref[...] += jnp.sum(tile * w[:, at].astype(F32), axis=1, keepdims=True)
    for t in range(3):
        r = 384 + 64 * t
        down_ref[:, t * 512 : (t + 1) * 512] = all_ref[j, r : r + 64, :].astype(F32)

    @pl.when(j == 3)
    def _():
        gain_ref[...] = as_row(acc_ref[...] / gain[...])


def ffn_out(places, pieces, wg, wu, gain, deps):
    whole = lambda shape: pl.BlockSpec(shape, lambda j: (0,) * len(shape))
    cols = pl.BlockSpec((96, 1024), lambda j: (0, j))
    return call(
        ffn_out_kernel,
        [((96, FF), F32), ((96, FF), F32), ((256, D), F32), ((1, 96), F32)],
        [places, *pieces, wg, wu, gain],
        4,
        scratch=[pltpu.VMEM((NZ, 576, 512), BF), pltpu.VMEM((96, 1), F32)],
        deps=deps,
        grid=(4,),
        in_specs=[SMEM] + [whole((576, 512))] * 4 + [cols, cols, whole((96, 1))],
        out_specs=[cols, cols, pl.BlockSpec((64, D), lambda j: (j, 0)), whole((1, 96))],
    )


def out_slices_kernel(places, p0, p1, p2, p3, *refs):
    all_ref = refs[4]
    for i, p in enumerate((p0, p1, p2, p3)):
        all_ref[(places[Z] + i) % NZ] = p[96:, :]
    for i in range(NX):
        refs[i][...] = all_ref[(places[X] + i) % NX]


def out_slices(places, pieces, deps):
    return call(
        out_slices_kernel,
        [((48, 768), BF)] * 4,
        [places, *pieces],
        1,
        scratch=[pltpu.VMEM((NZ, 48, 768), BF)],
        deps=deps,
    )


def qkv_out_kernel(
    places, p0, p1, p2, p3, wq, wk, wv, own_gain, q_ref, k_ref, v_ref, gain_ref, all_ref
):
    for i, p in enumerate((p0, p1, p2, p3)):
        all_ref[(places[Z] + i) % NZ] = p[:96, :]
    for q in range(NZ):
        q_ref[:, q * QW : (q + 1) * QW] = all_ref[q, :, :QW].astype(F32)
    gain = jnp.sum(q_ref[...] * wq[...].astype(F32), axis=1, keepdims=True)
    for out, w, at in ((k_ref, wk, QW), (v_ref, wv, QW + KW)):
        tile = jnp.concatenate(
            [all_ref[q, :, at : at + KW].astype(F32) for q in range(NZ)], axis=1
        )
        out[...] = tile
        gain += jnp.sum(tile * w[...].astype(F32), axis=1, keepdims=True)
    gain_ref[...] = as_row(gain / own_gain[...])


def qkv_out(places, pieces, wq, wk, wv, gain, deps):
    return call(
        qkv_out_kernel,
        [((96, 1536), F32), ((96, 768), F32), ((96, 768), F32), ((1, 96), F32)],
        [places, *pieces, wq, wk, wv, gain],
        2,
        scratch=[pltpu.VMEM((NZ, 96, 768), BF)],
        deps=deps,
    )


def out_out_kernel(places, p0, p1, p2, p3, out_ref):
    for i, p in enumerate((p0, p1, p2, p3)):
        tile = p[...].astype(F32)
        rows = pl.ds(pl.multiple_of((places[X] + i) % NX * 24, 8), 24)
        out_ref[rows, :] = jnp.concatenate([tile[:24], tile[24:]], axis=1)


def out_out(places, pieces):
    return call(out_out_kernel, [((96, D), F32)], [places, *pieces], 1)[0]


def block_out_kernel(places, middle, down, out_ref):
    out_ref[...] = (middle[...] + down[...].astype(F32)).astype(BF)


def block_out_of(places, middle, down, deps):
    return call(block_out_kernel, [((ROWS, D), BF)], [places, middle, down], 1, deps=deps)[0]


def body(
    inputs, norm_attn, w_query, w_key, w_value, w_out, norm_ffn, w_gate, w_up, w_down, cotangent
):
    f, s = lax.axis_index("fsdp"), lax.axis_index("sp")
    x, yh, c, z, yl = f // 4, f // 2 % 2, f % 2, s // 2, s % 2
    places = jnp.stack([x, yh, c, z, yl]).astype(jnp.int32)
    x_own, og_own = inputs[0], cotangent[0]
    gain_attn, gain_ffn = norm_attn[None], norm_ffn[None]

    def column(gain):
        return lax.dynamic_slice_in_dim(gain, f * 96, 96, 0)[:, None]

    index = jnp.arange(TOKENS, dtype=jnp.int32)
    positions = (index // ROWS * 2 + yl) * ROWS + index % ROWS
    lane = np.arange(QW) % HEAD_DIM
    frequency = ROPE_BASE ** (-(jnp.arange(HALF, dtype=F32) * 2.0 / HEAD_DIM))
    frequency = jnp.concatenate([frequency] * (QW // HALF))
    angles = positions.astype(F32)[:, None] * frequency[None, :]
    sign = np.where(lane < HALF, -1.0, 1.0).astype(np.float32)
    cosine, sine = jnp.cos(angles), jnp.sin(angles) * sign[None, :]

    qkv_shard, row_shard = cut(
        places, w_query, w_key, w_value, w_gate, w_up, w_down, w_out
    )
    qkv_mirror, row_mirror = mirror_y(qkv_shard), mirror_y(row_shard)
    xs = two_stage_z(x_own)
    (qkv_pair,) = paired(places, qkv_shard, qkv_mirror, [96], [cosine, sine, gain_attn])
    qkv_mine = two_stage_x(qkv_pair)
    qkv_other = [swap_core(p) for p in qkv_mine]
    (rows_pair,) = paired(
        places, row_shard, row_mirror, [864], [qkv_mine[1], qkv_mine[2], xs[1], xs[2]]
    )
    above, below = shift_x(rows_pair, -1), shift_x(rows_pair, 1)

    normed, x_all, og_copy, turned_mine, turned_sent = norm(places, gain_attn, og_own, xs)
    ogs = two_stage_z(og_copy)
    q, kv, held_qkv = qkv(places, normed, qkv_mine, qkv_other, cosine, sine)
    kv_other = swap_low(kv)
    half_up, half_down = halves(places, above, below)
    far = [shift_x(half_up, 1), shift_x(half_down, -1)]
    mixed, shares = attend(places, q, kv, kv_other, [ogs[1], ogs[2], half_up])
    mixed_all = gather_z(mixed).reshape(NZ, TOKENS, QW)
    far = copied(places, far, [mixed])
    pieces = [rows_pair, above, below, *far]
    pieces += [swap_core(p) for p in pieces]
    normed_ffn, middle_own = middle_of(places, x_all, gain_ffn, mixed_all, pieces)
    outs = ffn(places, normed_ffn, ogs, pieces)
    hidden, gate_grad, up_grad, og_all = outs[:4]
    in_chunks = outs[4:8]

    in_got = scatter(in_chunks)
    a_sent, b_sent, n_mine, h_mine = ffn_sent_of(
        places, normed_ffn, hidden, gate_grad, up_grad, og_all
    )
    held_out, down_part = lay(places, hidden, pieces, [n_mine])
    back = middle_back(places, in_got, middle_own, og_own, gain_ffn, held_out, [n_mine])
    middle_grad, branch = back[:2]
    head_grads = [back[2], shift_z(back[5], -1), shift_z(back[4], 2), shift_z(back[3], 1)]
    branch_all = gather_z(branch)
    a_got, b_got = swap_core(a_sent), swap_core(b_sent)
    ffn_args = (n_mine, h_mine, gate_grad, up_grad, og_all)
    a_chunks = ffn_grad_first(places, (*ffn_args, a_got), [branch])
    a_terms = over_x(a_chunks)

    dq, dkv_own, dkv_sent = attend_back(
        places, head_grads, q, kv, kv_other, shares, [a_chunks[0]]
    )
    b_mine, b_sent, down_part = ffn_grad_second(places, (*ffn_args, b_got), down_part, [dq])
    down_own = scatter_z(down_part)
    b_got = mirror_y(b_sent)
    dkv_got = swap_low(dkv_sent)
    lin, out_part, qkv_sent = turn(
        places, dq, dkv_own, dkv_got, cosine, sine, turned_sent, mixed, branch_all, [b_sent]
    )
    qkv_got = swap_core(qkv_sent)
    first_part = first(places, lin, held_qkv, [])
    first_got = scatter_z(first_part)
    a_half, a_sent = x_sum(places, a_terms, COST["x_sum"], [first_part])
    a_got = mirror_y(a_sent)
    qkv_chunks = qkv_grad(places, lin, turned_mine, out_part, qkv_got, [a_sent])
    qkv_terms = over_x(qkv_chunks)
    b_terms = over_x(y_sum(places, b_mine, b_got, [qkv_chunks[0]]))

    qkv_half, qkv_sent = x_sum(places, qkv_terms, 2, [])
    qkv_got = mirror_y(qkv_sent)
    ffn_half = ffn_join(places, a_half, a_got, b_terms, [qkv_sent])
    ffn_low = swap_low(ffn_half)
    qkv_half = added(places, qkv_half, qkv_got, [ffn_half])
    qkv_low = swap_low(qkv_half)
    qkv_total = added(places, qkv_half, qkv_low, [])
    qkv_pieces = pieces_z(qkv_total)
    ffn_total = added(places, ffn_half, ffn_low, [qkv_total])
    ffn_pieces = pieces_z(ffn_total)

    block_out = block_out_of(places, middle_own, down_own, [qkv_total])
    input_grad = input_back(places, first_got, x_own, middle_grad, gain_attn, [qkv_total])
    out_terms = over_x(out_slices(places, qkv_pieces, [block_out, input_grad]))
    grad_query, grad_key, grad_value, qkv_gain = qkv_out(
        places, qkv_pieces, w_query, w_key, w_value, column(norm_attn), [out_terms[0]]
    )
    grad_gate, grad_up, grad_down, ffn_gain = ffn_out(
        places, ffn_pieces, w_gate, w_up, column(norm_ffn), [qkv_gain]
    )
    grad_out = out_out(places, [out_terms[0], out_terms[2], out_terms[3], out_terms[1]])
    grad_norm_attn, grad_norm_ffn = qkv_gain[0], ffn_gain[0]
    return (
        block_out[None],
        input_grad[None],
        grad_norm_attn,
        grad_query,
        grad_key,
        grad_value,
        grad_out,
        grad_norm_ffn,
        grad_gate,
        grad_up,
        grad_down,
    )


def solution(mesh):
    rows = P("fsdp", None)
    tokens = P("fsdp", "sp", None)
    return jax.shard_map(
        body,
        mesh=mesh,
        in_specs=(tokens, P(), rows, rows, rows, rows, P(), rows, rows, rows, tokens),
        out_specs=(tokens, tokens, P("fsdp"), rows, rows, rows, rows, P("fsdp"), rows, rows, rows),
        check_vma=False,
    )
```

```python
import functools

import jax
import jax.numpy as jnp
import numpy as np
from jax import lax
from jax.experimental import pallas as pl
from jax.experimental.pallas import tpu as pltpu
from jax.sharding import PartitionSpec as P

D = 1536
HEADS = 16
KV_HEADS = 8
HEAD_DIM = 96
FF = 4096

EPSILON = 1e-05
ROPE_BASE = 100000.0
MASKED = -1e30

NX, NZ = 4, 4
ROWS = 128
TOKENS = ROWS * NZ
QW, KW = 384, 192
HALF = HEAD_DIM // 2
FFZ = FF // NZ
BF = jnp.bfloat16
F32 = jnp.float32
VMEM = pl.BlockSpec(memory_space=pltpu.VMEM)
SMEM = pl.BlockSpec(memory_space=pltpu.SMEM)
ANY = pl.BlockSpec(memory_space=pl.ANY)
LIMIT = pltpu.CompilerParams(vmem_limit_bytes=56 * 1024 * 1024)
X, YH, CORE, Z, YL = range(5)
SPLIT = 384
COST = {
    "norm": 54,
    "qkv": 0.1,
    "attend": 0.1,
    "down": 0.1,
    "middle": 4,
    "ffn": 17,
    "ffn_sent": 0.1,
    "middle_back": 60,
    "ffn_grad": 60,
    "ffn_grad_second": 0.1,
    "attend_back": 60,
    "turn": 0.1,
    "first": 0.1,
    "x_sum": 60,
    "y_sum": 0.1,
    "qkv_grad": 0.1,
    "add": 8,
}


Z_GROUPS = [[z * 2 + l for z in range(NZ)] for l in range(2)]


def scatter_z(v):
    return lax.psum_scatter(
        v, "sp", scatter_dimension=0, tiled=True, axis_index_groups=Z_GROUPS
    )


def gather_z(v):
    return lax.all_gather(v, "sp", axis=0, tiled=True, axis_index_groups=Z_GROUPS)


def shift_z(v, step):
    pairs = [(z * 2 + l, (z + step) % NZ * 2 + l) for z in range(NZ) for l in range(2)]
    return lax.ppermute(v, "sp", pairs)


def swap_low(v):
    return lax.ppermute(v, "sp", [(s, s ^ 1) for s in range(8)])


def shift_x(v, step):
    pairs = [(x * 4 + r, (x + step) % NX * 4 + r) for x in range(NX) for r in range(4)]
    return lax.ppermute(v, "fsdp", pairs)


def swap_core(v):
    return lax.ppermute(v, "fsdp", [(f, f ^ 1) for f in range(16)])


def mirror_y(v):
    pairs = [(f * 8 + s, (f ^ 2) * 8 + (s ^ 1)) for f in range(16) for s in range(8)]
    return lax.ppermute(v, ("fsdp", "sp"), pairs)


def pieces_z(v):
    far = [shift_z(v, -1), shift_z(v, 1), shift_z(v, 2)]
    return [v, far[0], far[2], far[1]]


def two_stage_z(v):
    above, below = shift_z(v, -1), shift_z(v, 1)
    return [v, above, shift_z(below, 1), below]


def two_stage_x(v):
    above, below = shift_x(v, -1), shift_x(v, 1)
    return [v, above, shift_x(below, 1), below]


def pieces_x(v):
    far = [shift_x(v, -1), shift_x(v, 1), shift_x(v, 2)]
    return [v, far[0], far[2], far[1]]


def part(v, index, size, dim=0):
    return lax.dynamic_slice_in_dim(v, index * size, size, dim)


def call(kernel, outs, ins, us, scratch=(), deps=(), grid=(), in_specs=None, out_specs=None):
    def run(*refs):
        kernel(*refs[: len(ins)], *refs[len(ins) + len(deps) :])

    return pl.pallas_call(
        run,
        name=kernel.__name__.replace("_kernel", ""),
        grid=grid,
        out_shape=[jax.ShapeDtypeStruct(s, t) for s, t in outs],
        in_specs=(in_specs or [SMEM] + [VMEM] * (len(ins) - 1)) + [ANY] * len(deps),
        out_specs=out_specs or [VMEM] * len(outs),
        scratch_shapes=scratch,
        compiler_params=LIMIT,
        cost_estimate=pl.CostEstimate(
            flops=int(us * 1e9), bytes_accessed=int(us * 3e6), transcendentals=0
        ),
    )(*ins, *deps)


def mm(a, b):
    return jnp.dot(a, b, preferred_element_type=F32)


def mm_t(a, b):
    return lax.dot_general(a, b, (((1,), (1,)), ((), ())), preferred_element_type=F32)


def t_mm(a, b):
    return lax.dot_general(a, b, (((0,), (0,)), ((), ())), preferred_element_type=F32)


def at_rows(index, size):
    return pl.ds(pl.multiple_of(index * size, size), size)


def rope(v, cosine, sine):
    width = v.shape[1]
    lane = lax.broadcasted_iota(jnp.int32, v.shape, 1) % HEAD_DIM
    partner = jnp.where(
        lane < HALF, pltpu.roll(v, width - HALF, 1), pltpu.roll(v, HALF, 1)
    )
    return v * cosine + partner * sine


def rope_keys(kv, cosine, sine):
    lane = lax.broadcasted_iota(jnp.int32, kv.shape, 1)
    return jnp.where(lane < KW, rope(kv, cosine, sine), kv)


def cut_kernel(places, wq, wk, wv, wg, wu, wd, wo, qkv_ref, rows_ref):
    z = places[Z]
    for t in range(3):
        cols = slice(t * 512, (t + 1) * 512)
        rows_ref[96 * t : 96 * (t + 1), :] = wo[:, cols]
        rows_ref[672 + 64 * t : 736 + 64 * t, :] = wd[at_rows(z, 64), cols]
    qkv_ref[:, :QW] = wq[:, pl.ds(pl.multiple_of(z * QW, 128), QW)]
    for at in range(NZ):

        @pl.when(z == at)
        def _():
            cols = slice(at * KW, (at + 1) * KW)
            qkv_ref[:, QW:] = jnp.concatenate([wk[:, cols], wv[:, cols]], axis=1)
            for k, w in enumerate((wg, wu)):
                for half in range(2):
                    starts = [(8 * half + i) * 256 + at * 64 for i in range(8)]
                    rows = slice(288 + (2 * half + k) * 96, 384 + (2 * half + k) * 96)
                    rows_ref[rows, :] = jnp.concatenate([w[:, b : b + 64] for b in starts], axis=1)


def cut(places, *arrays):
    return call(cut_kernel, [((96, 768), BF), ((864, 512), BF)], [places, *arrays], 3)


def copy_kernel(places, *refs):
    n = len(refs) // 2
    for i in range(n):
        refs[n + i][...] = refs[i][...]


def copied(places, arrays, deps):
    return call(copy_kernel, [(v.shape, v.dtype) for v in arrays], [places, *arrays], 0.1, deps=deps)


def pair_kernel(places, own, mirror, *outs):
    start = 0
    for out in outs:
        rows = slice(start, start + out.shape[1])
        out[places[YH]] = own[rows, :]
        out[1 - places[YH]] = mirror[rows, :]
        start += out.shape[1]


def paired(places, own, mirror, parts, deps):
    outs = [((2, n, own.shape[1]), BF) for n in parts]
    return call(pair_kernel, outs, [places, own, mirror], 0.1, deps=deps)


def norm_kernel(places, gain, og, *refs):
    xs, (normed_ref, x_ref, og_ref, mine_ref, sent_ref, turned_ref) = refs[:4], refs[4:]
    og_ref[...] = og[...]
    for i in range(NZ):
        x_ref[at_rows((places[Z] + i) % NZ, ROWS), :] = xs[i][...]
    for i in range(NZ):
        rows = pl.ds(i * ROWS, ROWS)
        v = x_ref[rows, :].astype(F32)
        r = lax.rsqrt(jnp.mean(v * v, axis=1, keepdims=True) + EPSILON)
        normed_ref[rows, :] = (v * r * gain[...]).astype(BF)
    turned_ref[...] = normed_ref[...].T
    split_cores(places, turned_ref, mine_ref, sent_ref, 96)


def split_cores(places, turned_ref, mine_ref, sent_ref, n):
    for k in range(8):
        rows = slice(k * n, (k + 1) * n)
        mine_ref[rows, :] = turned_ref[at_rows(2 * k + places[CORE], n), :]
        sent_ref[rows, :] = turned_ref[at_rows(2 * k + 1 - places[CORE], n), :]


def norm(places, gain, og, xs):
    return call(
        norm_kernel,
        [((TOKENS, D), BF)] * 2 + [((ROWS, D), BF)] + [((D // 2, TOKENS), BF)] * 2,
        [places, gain, og, *xs],
        COST["norm"],
        scratch=[pltpu.VMEM((D, TOKENS), BF)],
    )


def qkv_kernel(places, normed_ref, *refs):
    mine, other = refs[:4], refs[4:8]
    cosine, sine, q_ref, kv_ref, w_ref = refs[8:]
    for i in range(NX):
        for h in range(2):
            base = (places[X] + i) % NX * 4 + h * 2
            w_ref[at_rows(base + places[CORE], 96), :] = mine[i][h]
            w_ref[at_rows(base + 1 - places[CORE], 96), :] = other[i][h]
    for i in range(NZ):
        rows = pl.ds(i * ROWS, ROWS)
        lin = mm(normed_ref[rows, :], w_ref[...])
        q_ref[rows, :] = rope(lin[:, :QW], cosine[rows, :], sine[rows, :]).astype(BF)
        kv_ref[rows, :] = rope_keys(lin[:, QW:], cosine[rows, :], sine[rows, :]).astype(BF)


def qkv(places, normed, mine, other, cosine, sine):
    return call(
        qkv_kernel,
        [((TOKENS, QW), BF), ((TOKENS, 2 * KW), BF), ((D, QW + 2 * KW), BF)],
        [places, normed, *mine, *other, cosine, sine],
        COST["qkv"],
    )


def head(ref, rows, index):
    return ref[rows, index * HEAD_DIM : (index + 1) * HEAD_DIM]


def two_heads(ref, j, g):
    rows = slice(j * ROWS, (j + 1) * ROWS)
    return jnp.concatenate([head(ref, rows, 2 * g), head(ref, rows, 2 * g + 1)], axis=0)


def attend_kernel(places, q_ref, own_ref, other_ref, mixed_ref, p_ref):
    late = places[YL]
    factor = HEAD_DIM ** (-0.5)
    for g in range(2):
        for j in range(NZ):
            n = (j + 1) * ROWS
            q = two_heads(q_ref, j, g)
            s_own = mm_t(q, head(own_ref, slice(0, n), g)) * factor
            s_oth = mm_t(q, head(other_ref, slice(0, n), g)) * factor
            shape = (2 * ROWS, n)
            row = lax.broadcasted_iota(jnp.int32, shape, 0) % ROWS + j * ROWS
            col = lax.broadcasted_iota(jnp.int32, shape, 1)
            s_own = jnp.where(col <= row, s_own, MASKED)
            s_oth = jnp.where(col < (j + late) * ROWS, s_oth, MASKED)
            highest = jnp.maximum(
                jnp.max(s_own, axis=1, keepdims=True), jnp.max(s_oth, axis=1, keepdims=True)
            )
            p_own, p_oth = jnp.exp(s_own - highest), jnp.exp(s_oth - highest)
            total = jnp.sum(p_own, axis=1, keepdims=True) + jnp.sum(p_oth, axis=1, keepdims=True)
            scale = 1.0 / total
            p_own, p_oth = (p_own * scale).astype(BF), (p_oth * scale).astype(BF)
            p_ref[g, j, :, :n] = p_own
            p_ref[g, j, :, n : 2 * n] = p_oth
            out = mm(p_own, head(own_ref, slice(0, n), 2 + g)) + mm(
                p_oth, head(other_ref, slice(0, n), 2 + g)
            )
            out = out.astype(BF)
            for k in range(2):
                h = 2 * g + k
                mixed_ref[j * ROWS : (j + 1) * ROWS, h * HEAD_DIM : (h + 1) * HEAD_DIM] = out[
                    k * ROWS : (k + 1) * ROWS
                ]


def attend(places, q, kv, kv_other, deps):
    return call(
        attend_kernel,
        [((TOKENS, QW), BF), ((2, NZ, 2 * ROWS, 2 * TOKENS), BF)],
        [places, q, kv, kv_other],
        COST["attend"],
        deps=deps,
    )


def attend_back_kernel(places, *refs):
    grads = refs[:4]
    q_ref, own_ref, other_ref, p_ref = refs[4:8]
    dq_ref, down_ref, doth_ref = refs[8:11]
    do_ref, acc_own, acc_oth = refs[11:]
    factor = HEAD_DIM ** (-0.5)
    for i in range(NZ):
        do_ref[at_rows((places[Z] + i) % NZ, ROWS), :] = grads[i][...]
    for g in range(2):
        acc_own[...] = jnp.zeros_like(acc_own)
        acc_oth[...] = jnp.zeros_like(acc_oth)
        for j in range(NZ):
            n = (j + 1) * ROWS
            seen = slice(0, n)
            q = two_heads(q_ref, j, g)
            do = two_heads(do_ref, j, g)
            p_own, p_oth = p_ref[g, j, :, :n], p_ref[g, j, :, n : 2 * n]
            dp_own = mm_t(do, head(own_ref, seen, 2 + g))
            dp_oth = mm_t(do, head(other_ref, seen, 2 + g))
            f_own, f_oth = p_own.astype(F32), p_oth.astype(F32)
            dot = jnp.sum(f_own * dp_own, axis=1, keepdims=True) + jnp.sum(
                f_oth * dp_oth, axis=1, keepdims=True
            )
            ds_own = (f_own * (dp_own - dot)).astype(BF)
            ds_oth = (f_oth * (dp_oth - dot)).astype(BF)
            dq = mm(ds_own, head(own_ref, seen, g)) + mm(ds_oth, head(other_ref, seen, g))
            dq = (dq * factor).astype(BF)
            for k in range(2):
                h = 2 * g + k
                dq_ref[j * ROWS : (j + 1) * ROWS, h * HEAD_DIM : (h + 1) * HEAD_DIM] = dq[
                    k * ROWS : (k + 1) * ROWS
                ]
            acc_own[0, seen, :] += t_mm(ds_own, q)
            acc_own[1, seen, :] += t_mm(p_own, do)
            acc_oth[0, seen, :] += t_mm(ds_oth, q)
            acc_oth[1, seen, :] += t_mm(p_oth, do)
        for kind, scale in ((0, factor), (1, 1.0)):
            at = kind * KW + g * HEAD_DIM
            down_ref[:, at : at + HEAD_DIM] = acc_own[kind] * scale
            doth_ref[:, at : at + HEAD_DIM] = (acc_oth[kind] * scale).astype(BF)


def attend_back(places, grads, q, kv, kv_other, shares, deps):
    acc = pltpu.VMEM((2, TOKENS, HEAD_DIM), F32)
    return call(
        attend_back_kernel,
        [((TOKENS, QW), BF), ((TOKENS, 2 * KW), F32), ((TOKENS, 2 * KW), BF)],
        [places, *grads, q, kv, kv_other, shares],
        COST["attend_back"],
        scratch=[pltpu.VMEM((TOKENS, QW), BF), acc, acc],
        deps=deps,
    )


def send_chunks(refs, acc_ref, places):
    for i in range(NZ):
        rows = at_rows((places[Z] + i) % NZ, ROWS)
        refs[i][...] = acc_ref[rows, :].astype(refs[i].dtype)


CHUNKS = [((ROWS, D), F32)] + [((ROWS, D), BF)] * 3


def put_out(out_ref, places, core, ref):
    for k in range(8):
        rows = pl.ds(pl.multiple_of((k % 2 * 2 + core) * 96 + k // 2 * 24, 8), 24)
        tile = out_ref[rows, :]
        ref[k, 96:, :] = jnp.concatenate([tile[:, :768], tile[:, 768:]], axis=0).astype(BF)


def turn_kernel(
    places, dq_ref, own_ref, got_ref, cosine, sine, turned_ref, mixed_ref, branch_ref, *refs
):
    lin_ref, out_ref, sent_ref = refs
    for i in range(NZ):
        rows = slice(i * ROWS, (i + 1) * ROWS)
        dkv = (own_ref[rows, :] + got_ref[rows, :].astype(F32)).astype(BF)
        c, s = cosine[rows, :], -sine[rows, :]
        lin_ref[rows, :QW] = rope(dq_ref[rows, :].astype(F32), c, s).astype(BF)
        lin_ref[rows, QW:] = rope_keys(dkv.astype(F32), c, s).astype(BF)
    for k in range(8):
        sent_ref[k, :96, :] = mm(turned_ref[k * 96 : (k + 1) * 96, :], lin_ref[...]).astype(BF)
    out_ref[...] = t_mm(mixed_ref[...], branch_ref[...])
    put_out(out_ref, places, 1 - places[CORE], sent_ref)


def turn(places, dq, dkv_own, dkv_got, cosine, sine, turned, mixed, branch, deps):
    return call(
        turn_kernel,
        [((TOKENS, 768), BF), ((QW, D), F32), ((8, 144, 768), BF)],
        [places, dq, dkv_own, dkv_got, cosine, sine, turned, mixed, branch],
        COST["turn"],
        deps=deps,
    )


def first_kernel(places, lin_ref, w_ref, out_ref):
    out_ref[...] = mm_t(lin_ref[...], w_ref[...]).astype(BF)


def first(places, lin, w, deps):
    return call(first_kernel, [((TOKENS, D), BF)], [places, lin, w], COST["first"], deps=deps)[0]


def qkv_grad_kernel(places, lin_ref, turned_ref, out_ref, got_ref, *refs):
    outs, sum_ref = refs[:4], refs[4]
    for k in range(8):
        sum_ref[k, :96, :] = mm(turned_ref[k * 96 : (k + 1) * 96, :], lin_ref[...]).astype(BF)
    put_out(out_ref, places, places[CORE], sum_ref)
    for i in range(NX):
        for k in range(2):
            at = (places[X] + i) % NX * 2 + (places[YH] + k) % 2
            outs[i][k] = (sum_ref[at].astype(F32) + got_ref[at].astype(F32)).astype(BF)


def qkv_grad(places, lin, turned, out, got, deps):
    return call(
        qkv_grad_kernel,
        [((2, 144, 768), BF)] * 4,
        [places, lin, turned, out, got],
        COST["qkv_grad"],
        scratch=[pltpu.VMEM((8, 144, 768), BF)],
        deps=deps,
    )


def piece_rows(pieces, i, h, start, n):
    if i == 2:
        ref, start = (pieces[3], start) if start < SPLIT else (pieces[4], start - SPLIT)
    else:
        ref = pieces[(0, 1, None, 2)[i]]
    return ref[h, start : start + n, :]


def each_shard(places, pieces):
    for i in range(NX):
        for h in range(2):
            base = (places[X] + i) % NX * 4 + h * 2
            yield base + places[CORE], pieces[:5], i, h
            yield base + 1 - places[CORE], pieces[5:], i, h


def halves_kernel(places, above, below, first_ref, second_ref):
    first_ref[...] = below[:, :SPLIT]
    second_ref[...] = above[:, SPLIT:]


def halves(places, above, below, deps):
    return call(
        halves_kernel,
        [((2, SPLIT, 512), BF), ((2, 864 - SPLIT, 512), BF)],
        [places, above, below],
        0.1,
        deps=deps,
    )


def lay_output(places, all_pieces, out_ref):
    for b, pieces, i, h in each_shard(places, all_pieces):
        for t in range(3):
            out_ref[at_rows(b, 96), t * 512 : (t + 1) * 512] = piece_rows(pieces, i, h, t * 96, 96)


def lay_down(places, all_pieces, out_ref):
    for b, pieces, i, h in each_shard(places, all_pieces):
        for t in range(3):
            tile = piece_rows(pieces, i, h, 672 + 64 * t, 64)
            out_ref[at_rows(b, 64), t * 512 : (t + 1) * 512] = tile


def down_kernel(places, hidden_ref, *refs):
    pieces, down_ref, wd_ref = refs[:10], *refs[10:]
    lay_down(places, pieces, wd_ref)
    down_ref[...] = mm(hidden_ref[...], wd_ref[...]).astype(BF)


def down_of(places, hidden, pieces, deps):
    return call(
        down_kernel,
        [((TOKENS, D), BF)],
        [places, hidden, *pieces],
        COST["down"],
        scratch=[pltpu.VMEM((FFZ, D), BF)],
        deps=deps,
    )[0]


def middle_kernel(places, x_ref, gain, mixed, *refs):
    pieces, (normed_ref, own_ref, w_ref, acc_ref, mixed_ref) = refs[:10], refs[10:]
    lay_output(places, pieces, w_ref)
    for z in range(NZ):
        mixed_ref[:, z * QW : (z + 1) * QW] = mixed[z]
    for t in range(3):
        cols = slice(t * 512, (t + 1) * 512)
        acc_ref[:, cols] = x_ref[:, cols].astype(F32) + mm(mixed_ref[...], w_ref[:, cols])
    for i in range(NZ):
        rows = slice(i * ROWS, (i + 1) * ROWS)
        v = acc_ref[rows, :]
        r = lax.rsqrt(jnp.mean(v * v, axis=1, keepdims=True) + EPSILON)
        normed_ref[rows, :] = (v * r * gain[...]).astype(BF)
    own_ref[...] = acc_ref[at_rows(places[Z], ROWS), :]


def middle_of(places, x_all, gain, mixed, pieces):
    def rows(n):
        return pl.BlockSpec((2, n, 512), lambda j: (0, 0, 0))

    used = [rows(288)] * 4 + [rows(16)]
    return call(
        middle_kernel,
        [((TOKENS, D), BF), ((ROWS, D), F32), ((D, D), BF)],
        [places, x_all, gain, mixed, *pieces],
        COST["middle"],
        scratch=[pltpu.VMEM((TOKENS, D), F32), pltpu.VMEM((TOKENS, D), BF)],
        grid=(1,),
        in_specs=[SMEM, VMEM, VMEM, VMEM] + used * 2,
    )


def ffn_kernel(places, n_ref, *refs):
    ogs, pieces, refs = refs[:4], refs[4:14], refs[14:]
    hidden_ref, gg_ref, ug_ref, og_ref = refs[:4]
    in_chunks = refs[4:8]
    in_acc, wg_ref, wu_ref, wd_ref = refs[8:]
    for i, g in enumerate(ogs):
        og_ref[at_rows((places[Z] + i) % NZ, ROWS), :] = g[...]
    lay_down(places, pieces, wd_ref)
    for j in range(2):
        cols = slice(j * 512, (j + 1) * 512)
        for b, some, i, h in each_shard(places, pieces):
            wg_ref[at_rows(b, 96), :] = piece_rows(some, i, h, 288 + 192 * j, 96)
            wu_ref[at_rows(b, 96), :] = piece_rows(some, i, h, 384 + 192 * j, 96)
        wg, wu, wd = wg_ref[...], wu_ref[...], wd_ref[cols, :]
        gate = mm(n_ref[...], wg)
        up = mm(n_ref[...], wu)
        hg = mm_t(og_ref[...], wd).astype(BF).astype(F32)
        sig = 1.0 / (1.0 + jnp.exp(-gate))
        silu = gate * sig
        hidden = (silu * up).astype(BF)
        gg = (hg * up * (sig * (1.0 + gate * (1.0 - sig)))).astype(BF)
        ug = (hg * silu).astype(BF)
        hidden_ref[:, cols] = hidden
        gg_ref[:, cols] = gg
        ug_ref[:, cols] = ug
        if j == 0:
            in_acc[...] = mm_t(gg, wg) + mm_t(ug, wu)
        else:
            in_acc[...] += mm_t(gg, wg) + mm_t(ug, wu)
    send_chunks(in_chunks, in_acc, places)


def ffn(places, normed, ogs, pieces):
    return call(
        ffn_kernel,
        [((TOKENS, FFZ), BF)] * 3 + [((TOKENS, D), BF)] + CHUNKS,
        [places, normed, *ogs, *pieces],
        COST["ffn"],
        scratch=[pltpu.VMEM((TOKENS, D), F32)]
        + [pltpu.VMEM((D, 512), BF)] * 2
        + [pltpu.VMEM((FFZ, D), BF)],
    )


def ffn_terms(n_ref, h_ref, gg_ref, ug_ref, og_ref, cols, put):
    for w, ref in enumerate((gg_ref, ug_ref)):
        for half in range(2):
            tile = mm(n_ref[...], ref[:, half * 512 + cols.start : half * 512 + cols.stop])
            r = (2 * w + half) * 96
            put(slice(r, r + 96), tile.reshape(8, 96, -1))
    for t in range(3):
        tile = mm(h_ref[...], og_ref[:, t * 512 + cols.start : t * 512 + cols.stop])
        put(slice(384 + 64 * t, 448 + 64 * t), tile.reshape(8, 64, -1))


def ffn_sent_kernel(places, n_ref, hidden_ref, gg_ref, ug_ref, og_ref, *refs):
    sent_refs, (n_mine, h_mine, n_turned, h_turned, n_sent, h_sent) = refs[:2], refs[2:]
    n_turned[...] = n_ref[...].T
    h_turned[...] = hidden_ref[...].T
    split_cores(places, n_turned, n_mine, n_sent, 96)
    split_cores(places, h_turned, h_mine, h_sent, 64)

    def put(rows, tile):
        for half, ref in enumerate(sent_refs):
            ref[:, rows, :] = tile[:, :, half * 256 : (half + 1) * 256].astype(BF)

    ffn_terms(n_sent, h_sent, gg_ref, ug_ref, og_ref, slice(0, 512), put)


def ffn_sent_of(places, normed, hidden, gg, ug, og):
    return call(
        ffn_sent_kernel,
        [((8, 576, 256), BF)] * 2 + [((D // 2, TOKENS), BF), ((FFZ // 2, TOKENS), BF)],
        [places, normed, hidden, gg, ug, og],
        COST["ffn_sent"],
        scratch=[
            pltpu.VMEM((D, TOKENS), BF),
            pltpu.VMEM((FFZ, TOKENS), BF),
            pltpu.VMEM((D // 2, TOKENS), BF),
            pltpu.VMEM((FFZ // 2, TOKENS), BF),
        ],
    )


def ffn_grad_kernel(cols, places, n_ref, h_ref, gg_ref, ug_ref, og_ref, got_ref, *refs):
    outs, sum_ref = refs[:-1], refs[-1]

    def put(rows, tile):
        sum_ref[:, rows, :] = (tile + got_ref[:, rows, :].astype(F32)).astype(BF)

    ffn_terms(n_ref, h_ref, gg_ref, ug_ref, og_ref, cols, put)
    for i in range(NX):
        for k in range(2):
            at = (places[X] + i) % NX * 2 + (places[YH] + k) % 2
            if len(outs) == 4:
                outs[i][k] = sum_ref[at]
            else:
                outs[k][i] = sum_ref[at]


def ffn_grad_first_kernel(*refs):
    ffn_grad_kernel(slice(0, 256), *refs)


def ffn_grad_second_kernel(*refs):
    ffn_grad_kernel(slice(256, 512), *refs[:7], *refs[8:10], refs[11])
    refs[10][...] = refs[7][...]


def ffn_grad_first(places, args, deps):
    return call(
        ffn_grad_first_kernel,
        [((2, 576, 256), BF)] * 4,
        [places, *args],
        COST["ffn_grad"],
        scratch=[pltpu.VMEM((8, 576, 256), BF)],
        deps=deps,
    )


def ffn_grad_second(places, args, down_part, deps):
    return call(
        ffn_grad_second_kernel,
        [((4, 576, 256), BF)] * 2 + [((TOKENS, D), BF)],
        [places, *args, down_part],
        COST["ffn_grad_second"],
        scratch=[pltpu.VMEM((8, 576, 256), BF)],
        deps=deps,
    )


def y_sum_kernel(places, mine, got, *outs):
    for i in range(NX):
        outs[i][...] = (mine[i].astype(F32) + got[i].astype(F32)).astype(BF)


def y_sum(places, mine, got, deps):
    return call(
        y_sum_kernel,
        [(mine.shape[1:], BF)] * 4,
        [places, mine, got],
        COST["y_sum"],
        deps=deps,
    )


def ffn_join_kernel(places, mine, got, a, b, c, d, out):
    out[:, :256] = (mine[...] + got[...].astype(F32)).astype(BF)
    total = a[...].astype(F32) + b[...].astype(F32) + c[...].astype(F32) + d[...].astype(F32)
    out[:, 256:] = total.astype(BF)


def ffn_join(places, mine, got, terms, deps):
    return call(
        ffn_join_kernel,
        [((576, 512), BF)],
        [places, mine, got, *terms],
        COST["add"],
        deps=deps,
    )[0]


def rms_back(grad, v, gain):
    r = lax.rsqrt(jnp.mean(v * v, axis=1, keepdims=True) + EPSILON)
    pulled = grad * gain
    return r * pulled - v * (r * r * r * jnp.mean(pulled * v, axis=1, keepdims=True))


def middle_back_kernel(places, own, g1, g2, g3, middle, og, gain, w_ref, mid_ref, branch_ref, *outs):
    grad = own[...] + g1[...].astype(F32) + g2[...].astype(F32) + g3[...].astype(F32)
    mid = og[...].astype(F32) + rms_back(grad, middle[...], gain[...])
    mid_ref[...] = mid
    branch = mid.astype(BF)
    branch_ref[...] = branch
    for i in range(NZ):
        outs[i][...] = mm_t(branch, w_ref[at_rows((places[Z] + i) % NZ, QW), :]).astype(BF)


def middle_back(places, chunks, middle, og, gain, w_out, deps):
    return call(
        middle_back_kernel,
        [((ROWS, D), F32), ((ROWS, D), BF)] + [((ROWS, QW), BF)] * 4,
        [places, *chunks, middle, og, gain, w_out],
        COST["middle_back"],
        deps=deps,
    )


def input_back_kernel(places, grad, x, mid, gain, out_ref):
    out_ref[...] = mid[...] + rms_back(grad[...].astype(F32), x[...].astype(F32), gain[...])


def input_back(places, grad, x, mid, gain, deps):
    return call(
        input_back_kernel, [((ROWS, D), F32)], [places, grad, x, mid, gain], 2, deps=deps
    )[0]


def scatter(chunks):
    far = [shift_z(chunks[1], 1), shift_z(chunks[3], -1), shift_z(chunks[2], 2)]
    return [chunks[0], *far]


def x_sum_kernel(places, a, b, c, d, mine, sent):
    mine[...] = a[0].astype(F32) + b[0].astype(F32) + c[0].astype(F32) + d[0].astype(F32)
    total = a[1].astype(F32) + b[1].astype(F32) + c[1].astype(F32) + d[1].astype(F32)
    sent[...] = total.astype(BF)


def x_sum(places, terms, us, deps):
    shape = terms[0].shape[1:]
    return call(x_sum_kernel, [(shape, F32), (shape, BF)], [places, *terms], us, deps=deps)


def add_kernel(places, a, b, out):
    out[...] = (a[...].astype(F32) + b[...].astype(F32)).astype(BF)


def added(places, a, b, deps):
    return call(add_kernel, [(a.shape, BF)], [places, a, b], COST["add"], deps=deps)[0]


def over_x(chunks):
    far = [shift_x(chunks[1], 1), shift_x(chunks[3], -1), shift_x(chunks[2], 2)]
    return [chunks[0], *far]


def as_row(column):
    return jnp.broadcast_to(column, (column.shape[0], 128)).T[:1]


def ffn_out_kernel(
    places, p0, p1, p2, p3, wg, wu, gain, gate_ref, up_ref, down_ref, gain_ref, all_ref, acc_ref
):
    j = pl.program_id(0)

    @pl.when(j == 0)
    def _():
        for i, p in enumerate((p0, p1, p2, p3)):
            all_ref[(places[Z] + i) % NZ] = p[...]
        acc_ref[...] = jnp.zeros_like(acc_ref)

    cols = pl.ds(pl.multiple_of(j % 2 * 256, 256), 256)
    for k, (w, out) in enumerate(((wg, gate_ref), (wu, up_ref))):
        rows = pl.ds(pl.multiple_of((2 * k + j // 2) * 96, 96), 96)
        parts = [all_ref[q, rows, cols].astype(F32) for q in range(NZ)]
        for b in range(4):
            tile = jnp.concatenate([v[:, b * 64 : (b + 1) * 64] for v in parts], axis=1)
            at = slice(b * 256, (b + 1) * 256)
            out[:, at] = tile
            acc_ref[...] += jnp.sum(tile * w[:, at].astype(F32), axis=1, keepdims=True)
    for t in range(3):
        r = 384 + 64 * t
        down_ref[:, t * 512 : (t + 1) * 512] = all_ref[j, r : r + 64, :].astype(F32)

    @pl.when(j == 3)
    def _():
        gain_ref[...] = as_row(acc_ref[...] / gain[...])


def ffn_out(places, pieces, wg, wu, gain, deps):
    whole = lambda shape: pl.BlockSpec(shape, lambda j: (0,) * len(shape))
    cols = pl.BlockSpec((96, 1024), lambda j: (0, j))
    return call(
        ffn_out_kernel,
        [((96, FF), F32), ((96, FF), F32), ((256, D), F32), ((1, 96), F32)],
        [places, *pieces, wg, wu, gain],
        4,
        scratch=[pltpu.VMEM((NZ, 576, 512), BF), pltpu.VMEM((96, 1), F32)],
        deps=deps,
        grid=(4,),
        in_specs=[SMEM] + [whole((576, 512))] * 4 + [cols, cols, whole((96, 1))],
        out_specs=[cols, cols, pl.BlockSpec((64, D), lambda j: (j, 0)), whole((1, 96))],
    )


def out_slices_kernel(places, p0, p1, p2, p3, *refs):
    all_ref = refs[4]
    for i, p in enumerate((p0, p1, p2, p3)):
        all_ref[(places[Z] + i) % NZ] = p[96:, :]
    for i in range(NX):
        refs[i][...] = all_ref[(places[X] + i) % NX]


def out_slices(places, pieces, deps):
    return call(
        out_slices_kernel,
        [((48, 768), BF)] * 4,
        [places, *pieces],
        1,
        scratch=[pltpu.VMEM((NZ, 48, 768), BF)],
        deps=deps,
    )


def qkv_out_kernel(
    places, p0, p1, p2, p3, wq, wk, wv, own_gain, q_ref, k_ref, v_ref, gain_ref, all_ref
):
    for i, p in enumerate((p0, p1, p2, p3)):
        all_ref[(places[Z] + i) % NZ] = p[:96, :]
    for q in range(NZ):
        q_ref[:, q * QW : (q + 1) * QW] = all_ref[q, :, :QW].astype(F32)
    gain = jnp.sum(q_ref[...] * wq[...].astype(F32), axis=1, keepdims=True)
    for out, w, at in ((k_ref, wk, QW), (v_ref, wv, QW + KW)):
        tile = jnp.concatenate(
            [all_ref[q, :, at : at + KW].astype(F32) for q in range(NZ)], axis=1
        )
        out[...] = tile
        gain += jnp.sum(tile * w[...].astype(F32), axis=1, keepdims=True)
    gain_ref[...] = as_row(gain / own_gain[...])


def qkv_out(places, pieces, wq, wk, wv, gain, deps):
    return call(
        qkv_out_kernel,
        [((96, 1536), F32), ((96, 768), F32), ((96, 768), F32), ((1, 96), F32)],
        [places, *pieces, wq, wk, wv, gain],
        2,
        scratch=[pltpu.VMEM((NZ, 96, 768), BF)],
        deps=deps,
    )


def out_out_kernel(places, p0, p1, p2, p3, out_ref):
    for i, p in enumerate((p0, p1, p2, p3)):
        tile = p[...].astype(F32)
        rows = pl.ds(pl.multiple_of((places[X] + i) % NX * 24, 8), 24)
        out_ref[rows, :] = jnp.concatenate([tile[:24], tile[24:]], axis=1)


def out_out(places, pieces):
    return call(out_out_kernel, [((96, D), F32)], [places, *pieces], 1)[0]


def block_out_kernel(places, middle, down, out_ref):
    out_ref[...] = (middle[...] + down[...].astype(F32)).astype(BF)


def block_out_of(places, middle, down, deps):
    return call(block_out_kernel, [((ROWS, D), BF)], [places, middle, down], 1, deps=deps)[0]


def body(
    inputs, norm_attn, w_query, w_key, w_value, w_out, norm_ffn, w_gate, w_up, w_down, cotangent
):
    f, s = lax.axis_index("fsdp"), lax.axis_index("sp")
    x, yh, c, z, yl = f // 4, f // 2 % 2, f % 2, s // 2, s % 2
    places = jnp.stack([x, yh, c, z, yl]).astype(jnp.int32)
    x_own, og_own = inputs[0], cotangent[0]
    gain_attn, gain_ffn = norm_attn[None], norm_ffn[None]

    def column(gain):
        return lax.dynamic_slice_in_dim(gain, f * 96, 96, 0)[:, None]

    index = jnp.arange(TOKENS, dtype=jnp.int32)
    positions = (index // ROWS * 2 + yl) * ROWS + index % ROWS
    lane = np.arange(QW) % HEAD_DIM
    frequency = ROPE_BASE ** (-(jnp.arange(HALF, dtype=F32) * 2.0 / HEAD_DIM))
    frequency = jnp.concatenate([frequency] * (QW // HALF))
    angles = positions.astype(F32)[:, None] * frequency[None, :]
    sign = np.where(lane < HALF, -1.0, 1.0).astype(np.float32)
    cosine, sine = jnp.cos(angles), jnp.sin(angles) * sign[None, :]

    qkv_shard, row_shard = cut(
        places, w_query, w_key, w_value, w_gate, w_up, w_down, w_out
    )
    qkv_mirror, row_mirror = mirror_y(qkv_shard), mirror_y(row_shard)
    xs = two_stage_z(x_own)
    (qkv_pair,) = paired(places, qkv_shard, qkv_mirror, [96], [cosine, sine, gain_attn])
    qkv_mine = two_stage_x(qkv_pair)
    qkv_other = [swap_core(p) for p in qkv_mine]
    (rows_pair,) = paired(
        places, row_shard, row_mirror, [864], [qkv_mine[1], qkv_mine[2], xs[1], xs[2]]
    )
    above, below = shift_x(rows_pair, -1), shift_x(rows_pair, 1)

    normed, x_all, og_copy, turned_mine, turned_sent = norm(places, gain_attn, og_own, xs)
    ogs = two_stage_z(og_copy)
    q, kv, held_qkv = qkv(places, normed, qkv_mine, qkv_other, cosine, sine)
    kv_other = swap_low(kv)
    mixed, shares = attend(places, q, kv, kv_other, [ogs[1], ogs[2]])
    half_up, half_down = halves(places, above, below, [mixed])
    far = [shift_x(half_up, 1), shift_x(half_down, -1)]
    mixed_all = gather_z(mixed).reshape(NZ, TOKENS, QW)
    far = copied(places, far, [mixed])
    pieces = [rows_pair, above, below, *far]
    pieces += [swap_core(p) for p in pieces]
    normed_ffn, middle_own, held_out = middle_of(places, x_all, gain_ffn, mixed_all, pieces)
    outs = ffn(places, normed_ffn, ogs, pieces)
    hidden, gate_grad, up_grad, og_all = outs[:4]
    in_chunks = outs[4:8]

    in_got = scatter(in_chunks)
    a_sent, b_sent, n_mine, h_mine = ffn_sent_of(
        places, normed_ffn, hidden, gate_grad, up_grad, og_all
    )
    down_part = down_of(places, hidden, pieces, [n_mine])
    back = middle_back(
        places, in_got, middle_own, og_own, gain_ffn, held_out, [n_mine, down_part]
    )
    middle_grad, branch = back[:2]
    head_grads = [back[2], shift_z(back[5], -1), shift_z(back[4], 2), shift_z(back[3], 1)]
    branch_all = gather_z(branch)
    a_got, b_got = swap_core(a_sent), swap_core(b_sent)
    ffn_args = (n_mine, h_mine, gate_grad, up_grad, og_all)
    a_chunks = ffn_grad_first(places, (*ffn_args, a_got), [branch])
    a_terms = over_x(a_chunks)

    dq, dkv_own, dkv_sent = attend_back(
        places, head_grads, q, kv, kv_other, shares, [a_chunks[0]]
    )
    b_mine, b_sent, down_part = ffn_grad_second(places, (*ffn_args, b_got), down_part, [dq])
    down_own = scatter_z(down_part)
    b_got = mirror_y(b_sent)
    dkv_got = swap_low(dkv_sent)
    lin, out_part, qkv_sent = turn(
        places, dq, dkv_own, dkv_got, cosine, sine, turned_sent, mixed, branch_all, [b_sent]
    )
    qkv_got = swap_core(qkv_sent)
    first_part = first(places, lin, held_qkv, [])
    first_got = scatter_z(first_part)
    a_half, a_sent = x_sum(places, a_terms, COST["x_sum"], [first_part])
    a_got = mirror_y(a_sent)
    qkv_chunks = qkv_grad(places, lin, turned_mine, out_part, qkv_got, [a_sent])
    qkv_terms = over_x(qkv_chunks)
    b_terms = over_x(y_sum(places, b_mine, b_got, [qkv_chunks[0]]))

    qkv_half, qkv_sent = x_sum(places, qkv_terms, 2, [])
    qkv_got = mirror_y(qkv_sent)
    ffn_half = ffn_join(places, a_half, a_got, b_terms, [qkv_sent])
    ffn_low = swap_low(ffn_half)
    qkv_half = added(places, qkv_half, qkv_got, [ffn_half])
    qkv_low = swap_low(qkv_half)
    qkv_total = added(places, qkv_half, qkv_low, [])
    qkv_pieces = pieces_z(qkv_total)
    ffn_total = added(places, ffn_half, ffn_low, [qkv_total])
    ffn_pieces = pieces_z(ffn_total)

    block_out = block_out_of(places, middle_own, down_own, [qkv_total])
    input_grad = input_back(places, first_got, x_own, middle_grad, gain_attn, [qkv_total])
    out_terms = over_x(out_slices(places, qkv_pieces, [block_out, input_grad]))
    grad_query, grad_key, grad_value, qkv_gain = qkv_out(
        places, qkv_pieces, w_query, w_key, w_value, column(norm_attn), [out_terms[0]]
    )
    grad_gate, grad_up, grad_down, ffn_gain = ffn_out(
        places, ffn_pieces, w_gate, w_up, column(norm_ffn), [qkv_gain]
    )
    grad_out = out_out(places, [out_terms[0], out_terms[2], out_terms[3], out_terms[1]])
    grad_norm_attn, grad_norm_ffn = qkv_gain[0], ffn_gain[0]
    return (
        block_out[None],
        input_grad[None],
        grad_norm_attn,
        grad_query,
        grad_key,
        grad_value,
        grad_out,
        grad_norm_ffn,
        grad_gate,
        grad_up,
        grad_down,
    )


def solution(mesh):
    rows = P("fsdp", None)
    tokens = P("fsdp", "sp", None)
    return jax.shard_map(
        body,
        mesh=mesh,
        in_specs=(tokens, P(), rows, rows, rows, rows, P(), rows, rows, rows, tokens),
        out_specs=(tokens, tokens, P("fsdp"), rows, rows, rows, rows, P("fsdp"), rows, rows, rows),
        check_vma=False,
    )
```

```python
import functools

import jax
import jax.numpy as jnp
import numpy as np
from jax import lax
from jax.experimental import pallas as pl
from jax.experimental.pallas import tpu as pltpu
from jax.sharding import PartitionSpec as P

D = 1536
HEADS = 16
KV_HEADS = 8
HEAD_DIM = 96
FF = 4096

EPSILON = 1e-05
ROPE_BASE = 100000.0
MASKED = -1e30

NX, NZ = 4, 4
ROWS = 128
TOKENS = ROWS * NZ
QW, KW = 384, 192
HALF = HEAD_DIM // 2
FFZ = FF // NZ
BF = jnp.bfloat16
F32 = jnp.float32
VMEM = pl.BlockSpec(memory_space=pltpu.VMEM)
SMEM = pl.BlockSpec(memory_space=pltpu.SMEM)
ANY = pl.BlockSpec(memory_space=pl.ANY)
LIMIT = pltpu.CompilerParams(vmem_limit_bytes=56 * 1024 * 1024)
X, YH, CORE, Z, YL = range(5)
SPLIT = 384
FIRST = 384
COST = {
    "norm": 54,
    "qkv": 0.1,
    "attend": 0.1,
    "down": 0.1,
    "middle": 4,
    "ffn": 17,
    "ffn_sent": 0.1,
    "middle_back": 60,
    "ffn_grad": 60,
    "ffn_grad_second": 0.1,
    "attend_back": 60,
    "turn": 0.1,
    "first": 0.1,
    "x_sum": 60,
    "y_sum": 0.1,
    "qkv_grad": 0.1,
    "add": 8,
}


Z_GROUPS = [[z * 2 + l for z in range(NZ)] for l in range(2)]


def scatter_z(v):
    return lax.psum_scatter(
        v, "sp", scatter_dimension=0, tiled=True, axis_index_groups=Z_GROUPS
    )


def gather_z(v):
    return lax.all_gather(v, "sp", axis=0, tiled=True, axis_index_groups=Z_GROUPS)


def shift_z(v, step):
    pairs = [(z * 2 + l, (z + step) % NZ * 2 + l) for z in range(NZ) for l in range(2)]
    return lax.ppermute(v, "sp", pairs)


def swap_low(v):
    return lax.ppermute(v, "sp", [(s, s ^ 1) for s in range(8)])


def shift_x(v, step):
    pairs = [(x * 4 + r, (x + step) % NX * 4 + r) for x in range(NX) for r in range(4)]
    return lax.ppermute(v, "fsdp", pairs)


def swap_core(v):
    return lax.ppermute(v, "fsdp", [(f, f ^ 1) for f in range(16)])


def mirror_y(v):
    pairs = [(f * 8 + s, (f ^ 2) * 8 + (s ^ 1)) for f in range(16) for s in range(8)]
    return lax.ppermute(v, ("fsdp", "sp"), pairs)


def pieces_z(v):
    far = [shift_z(v, -1), shift_z(v, 1), shift_z(v, 2)]
    return [v, far[0], far[2], far[1]]


def two_stage_z(v):
    above, below = shift_z(v, -1), shift_z(v, 1)
    return [v, above, shift_z(below, 1), below]


def two_stage_x(v):
    above, below = shift_x(v, -1), shift_x(v, 1)
    return [v, above, shift_x(below, 1), below]


def pieces_x(v):
    far = [shift_x(v, -1), shift_x(v, 1), shift_x(v, 2)]
    return [v, far[0], far[2], far[1]]


def part(v, index, size, dim=0):
    return lax.dynamic_slice_in_dim(v, index * size, size, dim)


def call(kernel, outs, ins, us, scratch=(), deps=(), grid=(), in_specs=None, out_specs=None):
    def run(*refs):
        kernel(*refs[: len(ins)], *refs[len(ins) + len(deps) :])

    return pl.pallas_call(
        run,
        name=kernel.__name__.replace("_kernel", ""),
        grid=grid,
        out_shape=[jax.ShapeDtypeStruct(s, t) for s, t in outs],
        in_specs=(in_specs or [SMEM] + [VMEM] * (len(ins) - 1)) + [ANY] * len(deps),
        out_specs=out_specs or [VMEM] * len(outs),
        scratch_shapes=scratch,
        compiler_params=LIMIT,
        cost_estimate=pl.CostEstimate(
            flops=int(us * 1e9), bytes_accessed=int(us * 3e6), transcendentals=0
        ),
    )(*ins, *deps)


def mm(a, b):
    return jnp.dot(a, b, preferred_element_type=F32)


def mm_t(a, b):
    return lax.dot_general(a, b, (((1,), (1,)), ((), ())), preferred_element_type=F32)


def t_mm(a, b):
    return lax.dot_general(a, b, (((0,), (0,)), ((), ())), preferred_element_type=F32)


def at_rows(index, size):
    return pl.ds(pl.multiple_of(index * size, size), size)


def rope(v, cosine, sine):
    width = v.shape[1]
    lane = lax.broadcasted_iota(jnp.int32, v.shape, 1) % HEAD_DIM
    partner = jnp.where(
        lane < HALF, pltpu.roll(v, width - HALF, 1), pltpu.roll(v, HALF, 1)
    )
    return v * cosine + partner * sine


def rope_keys(kv, cosine, sine):
    lane = lax.broadcasted_iota(jnp.int32, kv.shape, 1)
    return jnp.where(lane < KW, rope(kv, cosine, sine), kv)


def cut_kernel(places, wq, wk, wv, wg, wu, wd, wo, qkv_ref, rows_ref):
    z = places[Z]
    for t in range(3):
        cols = slice(t * 512, (t + 1) * 512)
        rows_ref[96 * t : 96 * (t + 1), :] = wo[:, cols]
        rows_ref[672 + 64 * t : 736 + 64 * t, :] = wd[at_rows(z, 64), cols]
    qkv_ref[:, :QW] = wq[:, pl.ds(pl.multiple_of(z * QW, 128), QW)]
    for at in range(NZ):

        @pl.when(z == at)
        def _():
            cols = slice(at * KW, (at + 1) * KW)
            qkv_ref[:, QW:] = jnp.concatenate([wk[:, cols], wv[:, cols]], axis=1)
            for k, w in enumerate((wg, wu)):
                for half in range(2):
                    starts = [(8 * half + i) * 256 + at * 64 for i in range(8)]
                    rows = slice(288 + (2 * half + k) * 96, 384 + (2 * half + k) * 96)
                    rows_ref[rows, :] = jnp.concatenate([w[:, b : b + 64] for b in starts], axis=1)


def cut(places, *arrays):
    return call(cut_kernel, [((96, 768), BF), ((864, 512), BF)], [places, *arrays], 3)


def copy_kernel(places, *refs):
    n = len(refs) // 2
    for i in range(n):
        refs[n + i][...] = refs[i][...]


def copied(places, arrays, deps):
    return call(copy_kernel, [(v.shape, v.dtype) for v in arrays], [places, *arrays], 0.1, deps=deps)


def pair_kernel(places, own, mirror, *outs):
    start = 0
    for out in outs:
        rows = slice(start, start + out.shape[1])
        out[places[YH]] = own[rows, :]
        out[1 - places[YH]] = mirror[rows, :]
        start += out.shape[1]


def paired(places, own, mirror, parts, deps):
    outs = [((2, n, own.shape[1]), BF) for n in parts]
    return call(pair_kernel, outs, [places, own, mirror], 0.1, deps=deps)


def norm_kernel(places, gain, og, *refs):
    xs, (normed_ref, x_ref, og_ref, mine_ref, sent_ref, turned_ref) = refs[:4], refs[4:]
    og_ref[...] = og[...]
    for i in range(NZ):
        x_ref[at_rows((places[Z] + i) % NZ, ROWS), :] = xs[i][...]
    for i in range(NZ):
        rows = pl.ds(i * ROWS, ROWS)
        v = x_ref[rows, :].astype(F32)
        r = lax.rsqrt(jnp.mean(v * v, axis=1, keepdims=True) + EPSILON)
        normed_ref[rows, :] = (v * r * gain[...]).astype(BF)
    turned_ref[...] = normed_ref[...].T
    split_cores(places, turned_ref, mine_ref, sent_ref, 96)


def split_cores(places, turned_ref, mine_ref, sent_ref, n):
    for k in range(8):
        rows = slice(k * n, (k + 1) * n)
        mine_ref[rows, :] = turned_ref[at_rows(2 * k + places[CORE], n), :]
        sent_ref[rows, :] = turned_ref[at_rows(2 * k + 1 - places[CORE], n), :]


def norm(places, gain, og, xs):
    return call(
        norm_kernel,
        [((TOKENS, D), BF)] * 2 + [((ROWS, D), BF)] + [((D // 2, TOKENS), BF)] * 2,
        [places, gain, og, *xs],
        COST["norm"],
        scratch=[pltpu.VMEM((D, TOKENS), BF)],
    )


def qkv_kernel(places, normed_ref, *refs):
    mine, other = refs[:4], refs[4:8]
    cosine, sine, q_ref, kv_ref, w_ref = refs[8:]
    for i in range(NX):
        for h in range(2):
            base = (places[X] + i) % NX * 4 + h * 2
            w_ref[at_rows(base + places[CORE], 96), :] = mine[i][h]
            w_ref[at_rows(base + 1 - places[CORE], 96), :] = other[i][h]
    for i in range(NZ):
        rows = pl.ds(i * ROWS, ROWS)
        lin = mm(normed_ref[rows, :], w_ref[...])
        q_ref[rows, :] = rope(lin[:, :QW], cosine[rows, :], sine[rows, :]).astype(BF)
        kv_ref[rows, :] = rope_keys(lin[:, QW:], cosine[rows, :], sine[rows, :]).astype(BF)


def qkv(places, normed, mine, other, cosine, sine):
    return call(
        qkv_kernel,
        [((TOKENS, QW), BF), ((TOKENS, 2 * KW), BF), ((D, QW + 2 * KW), BF)],
        [places, normed, *mine, *other, cosine, sine],
        COST["qkv"],
    )


def head(ref, rows, index):
    return ref[rows, index * HEAD_DIM : (index + 1) * HEAD_DIM]


def two_heads(ref, j, g):
    rows = slice(j * ROWS, (j + 1) * ROWS)
    return jnp.concatenate([head(ref, rows, 2 * g), head(ref, rows, 2 * g + 1)], axis=0)


def attend_kernel(places, q_ref, own_ref, other_ref, mixed_ref, p_ref):
    late = places[YL]
    factor = HEAD_DIM ** (-0.5)
    for g in range(2):
        for j in range(NZ):
            n = (j + 1) * ROWS
            q = two_heads(q_ref, j, g)
            s_own = mm_t(q, head(own_ref, slice(0, n), g)) * factor
            s_oth = mm_t(q, head(other_ref, slice(0, n), g)) * factor
            shape = (2 * ROWS, n)
            row = lax.broadcasted_iota(jnp.int32, shape, 0) % ROWS + j * ROWS
            col = lax.broadcasted_iota(jnp.int32, shape, 1)
            s_own = jnp.where(col <= row, s_own, MASKED)
            s_oth = jnp.where(col < (j + late) * ROWS, s_oth, MASKED)
            highest = jnp.maximum(
                jnp.max(s_own, axis=1, keepdims=True), jnp.max(s_oth, axis=1, keepdims=True)
            )
            p_own, p_oth = jnp.exp(s_own - highest), jnp.exp(s_oth - highest)
            total = jnp.sum(p_own, axis=1, keepdims=True) + jnp.sum(p_oth, axis=1, keepdims=True)
            scale = 1.0 / total
            p_own, p_oth = (p_own * scale).astype(BF), (p_oth * scale).astype(BF)
            p_ref[g, j, :, :n] = p_own
            p_ref[g, j, :, n : 2 * n] = p_oth
            out = mm(p_own, head(own_ref, slice(0, n), 2 + g)) + mm(
                p_oth, head(other_ref, slice(0, n), 2 + g)
            )
            out = out.astype(BF)
            for k in range(2):
                h = 2 * g + k
                mixed_ref[j * ROWS : (j + 1) * ROWS, h * HEAD_DIM : (h + 1) * HEAD_DIM] = out[
                    k * ROWS : (k + 1) * ROWS
                ]


def attend(places, q, kv, kv_other, deps):
    return call(
        attend_kernel,
        [((TOKENS, QW), BF), ((2, NZ, 2 * ROWS, 2 * TOKENS), BF)],
        [places, q, kv, kv_other],
        COST["attend"],
        deps=deps,
    )


def attend_back_kernel(places, *refs):
    grads = refs[:4]
    q_ref, own_ref, other_ref, p_ref = refs[4:8]
    dq_ref, down_ref, doth_ref = refs[8:11]
    do_ref, acc_own, acc_oth = refs[11:]
    factor = HEAD_DIM ** (-0.5)
    for i in range(NZ):
        do_ref[at_rows((places[Z] + i) % NZ, ROWS), :] = grads[i][...]
    for g in range(2):
        acc_own[...] = jnp.zeros_like(acc_own)
        acc_oth[...] = jnp.zeros_like(acc_oth)
        for j in range(NZ):
            n = (j + 1) * ROWS
            seen = slice(0, n)
            q = two_heads(q_ref, j, g)
            do = two_heads(do_ref, j, g)
            p_own, p_oth = p_ref[g, j, :, :n], p_ref[g, j, :, n : 2 * n]
            dp_own = mm_t(do, head(own_ref, seen, 2 + g))
            dp_oth = mm_t(do, head(other_ref, seen, 2 + g))
            f_own, f_oth = p_own.astype(F32), p_oth.astype(F32)
            dot = jnp.sum(f_own * dp_own, axis=1, keepdims=True) + jnp.sum(
                f_oth * dp_oth, axis=1, keepdims=True
            )
            ds_own = (f_own * (dp_own - dot)).astype(BF)
            ds_oth = (f_oth * (dp_oth - dot)).astype(BF)
            dq = mm(ds_own, head(own_ref, seen, g)) + mm(ds_oth, head(other_ref, seen, g))
            dq = (dq * factor).astype(BF)
            for k in range(2):
                h = 2 * g + k
                dq_ref[j * ROWS : (j + 1) * ROWS, h * HEAD_DIM : (h + 1) * HEAD_DIM] = dq[
                    k * ROWS : (k + 1) * ROWS
                ]
            acc_own[0, seen, :] += t_mm(ds_own, q)
            acc_own[1, seen, :] += t_mm(p_own, do)
            acc_oth[0, seen, :] += t_mm(ds_oth, q)
            acc_oth[1, seen, :] += t_mm(p_oth, do)
        for kind, scale in ((0, factor), (1, 1.0)):
            at = kind * KW + g * HEAD_DIM
            down_ref[:, at : at + HEAD_DIM] = acc_own[kind] * scale
            doth_ref[:, at : at + HEAD_DIM] = (acc_oth[kind] * scale).astype(BF)


def attend_back(places, grads, q, kv, kv_other, shares, deps):
    acc = pltpu.VMEM((2, TOKENS, HEAD_DIM), F32)
    return call(
        attend_back_kernel,
        [((TOKENS, QW), BF), ((TOKENS, 2 * KW), F32), ((TOKENS, 2 * KW), BF)],
        [places, *grads, q, kv, kv_other, shares],
        COST["attend_back"],
        scratch=[pltpu.VMEM((TOKENS, QW), BF), acc, acc],
        deps=deps,
    )


def send_chunks(refs, acc_ref, places):
    for i in range(NZ):
        rows = at_rows((places[Z] + i) % NZ, ROWS)
        refs[i][...] = acc_ref[rows, :].astype(refs[i].dtype)


CHUNKS = [((ROWS, D), F32)] + [((ROWS, D), BF)] * 3


def put_out(out_ref, places, core, ref):
    for k in range(8):
        rows = pl.ds(pl.multiple_of((k % 2 * 2 + core) * 96 + k // 2 * 24, 8), 24)
        tile = out_ref[rows, :]
        ref[k, 96:, :] = jnp.concatenate([tile[:, :768], tile[:, 768:]], axis=0).astype(BF)


def turn_kernel(
    places, dq_ref, own_ref, got_ref, cosine, sine, turned_ref, mixed_ref, branch_ref, *refs
):
    lin_ref, out_ref, sent_ref = refs
    for i in range(NZ):
        rows = slice(i * ROWS, (i + 1) * ROWS)
        dkv = (own_ref[rows, :] + got_ref[rows, :].astype(F32)).astype(BF)
        c, s = cosine[rows, :], -sine[rows, :]
        lin_ref[rows, :QW] = rope(dq_ref[rows, :].astype(F32), c, s).astype(BF)
        lin_ref[rows, QW:] = rope_keys(dkv.astype(F32), c, s).astype(BF)
    for k in range(8):
        sent_ref[k, :96, :] = mm(turned_ref[k * 96 : (k + 1) * 96, :], lin_ref[...]).astype(BF)
    out_ref[...] = t_mm(mixed_ref[...], branch_ref[...])
    put_out(out_ref, places, 1 - places[CORE], sent_ref)


def turn(places, dq, dkv_own, dkv_got, cosine, sine, turned, mixed, branch, deps):
    return call(
        turn_kernel,
        [((TOKENS, 768), BF), ((QW, D), F32), ((8, 144, 768), BF)],
        [places, dq, dkv_own, dkv_got, cosine, sine, turned, mixed, branch],
        COST["turn"],
        deps=deps,
    )


def first_kernel(places, lin_ref, w_ref, out_ref):
    out_ref[...] = mm_t(lin_ref[...], w_ref[...]).astype(BF)


def first(places, lin, w, deps):
    return call(first_kernel, [((TOKENS, D), BF)], [places, lin, w], COST["first"], deps=deps)[0]


def qkv_grad_kernel(places, lin_ref, turned_ref, out_ref, got_ref, *refs):
    outs, sum_ref = refs[:4], refs[4]
    for k in range(8):
        sum_ref[k, :96, :] = mm(turned_ref[k * 96 : (k + 1) * 96, :], lin_ref[...]).astype(BF)
    put_out(out_ref, places, places[CORE], sum_ref)
    for i in range(NX):
        for k in range(2):
            at = (places[X] + i) % NX * 2 + (places[YH] + k) % 2
            outs[i][k] = (sum_ref[at].astype(F32) + got_ref[at].astype(F32)).astype(BF)


def qkv_grad(places, lin, turned, out, got, deps):
    return call(
        qkv_grad_kernel,
        [((2, 144, 768), BF)] * 4,
        [places, lin, turned, out, got],
        COST["qkv_grad"],
        scratch=[pltpu.VMEM((8, 144, 768), BF)],
        deps=deps,
    )


def piece_rows(pieces, i, h, start, n):
    if i == 2:
        ref, start = (pieces[3], start) if start < SPLIT else (pieces[4], start - SPLIT)
    else:
        ref = pieces[(0, 1, None, 2)[i]]
    return ref[h, start : start + n, :]


def each_shard(places, pieces):
    for i in range(NX):
        for h in range(2):
            base = (places[X] + i) % NX * 4 + h * 2
            yield base + places[CORE], pieces[:5], i, h
            yield base + 1 - places[CORE], pieces[5:], i, h


def halves_kernel(places, above, below, first_ref, second_ref):
    first_ref[...] = below[:, :SPLIT]
    second_ref[...] = above[:, SPLIT:]


def halves(places, above, below, deps):
    return call(
        halves_kernel,
        [((2, SPLIT, 512), BF), ((2, 864 - SPLIT, 512), BF)],
        [places, above, below],
        0.1,
        deps=deps,
    )


def lay_output(places, all_pieces, out_ref):
    for b, pieces, i, h in each_shard(places, all_pieces):
        for t in range(3):
            out_ref[at_rows(b, 96), t * 512 : (t + 1) * 512] = piece_rows(pieces, i, h, t * 96, 96)


def lay_down(places, all_pieces, out_ref):
    for b, pieces, i, h in each_shard(places, all_pieces):
        for t in range(3):
            tile = piece_rows(pieces, i, h, 672 + 64 * t, 64)
            out_ref[at_rows(b, 64), t * 512 : (t + 1) * 512] = tile


def down_kernel(places, hidden_ref, gain_a, gain_b, *refs):
    pieces, down_ref, col_a, col_b, wd_ref, turned_ref = refs[:10], *refs[10:]
    own = pl.ds(pl.multiple_of((places[X] * 4 + places[YH] * 2 + places[CORE]) * 96, 8), 96)
    for gain, col in ((gain_a, col_a), (gain_b, col_b)):
        turned_ref[...] = jnp.broadcast_to(gain[...], (128, D)).T
        col[...] = turned_ref[own, :1]
    lay_down(places, pieces, wd_ref)
    down_ref[...] = mm(hidden_ref[...], wd_ref[...]).astype(BF)


def down_of(places, hidden, gain_a, gain_b, pieces, deps):
    return call(
        down_kernel,
        [((TOKENS, D), BF), ((96, 1), F32), ((96, 1), F32)],
        [places, hidden, gain_a, gain_b, *pieces],
        COST["down"],
        scratch=[pltpu.VMEM((FFZ, D), BF), pltpu.VMEM((D, 128), F32)],
        deps=deps,
    )


def middle_kernel(places, x_ref, gain, mixed, *refs):
    pieces, (normed_ref, own_ref, w_ref, acc_ref, mixed_ref) = refs[:10], refs[10:]
    lay_output(places, pieces, w_ref)
    for z in range(NZ):
        mixed_ref[:, z * QW : (z + 1) * QW] = mixed[z]
    for t in range(3):
        cols = slice(t * 512, (t + 1) * 512)
        acc_ref[:, cols] = x_ref[:, cols].astype(F32) + mm(mixed_ref[...], w_ref[:, cols])
    for i in range(NZ):
        rows = slice(i * ROWS, (i + 1) * ROWS)
        v = acc_ref[rows, :]
        r = lax.rsqrt(jnp.mean(v * v, axis=1, keepdims=True) + EPSILON)
        normed_ref[rows, :] = (v * r * gain[...]).astype(BF)
    own_ref[...] = acc_ref[at_rows(places[Z], ROWS), :]


def middle_of(places, x_all, gain, mixed, pieces):
    def rows(n):
        return pl.BlockSpec((2, n, 512), lambda j: (0, 0, 0))

    used = [rows(288)] * 4 + [rows(16)]
    return call(
        middle_kernel,
        [((TOKENS, D), BF), ((ROWS, D), F32), ((D, D), BF)],
        [places, x_all, gain, mixed, *pieces],
        COST["middle"],
        scratch=[pltpu.VMEM((TOKENS, D), F32), pltpu.VMEM((TOKENS, D), BF)],
        grid=(1,),
        in_specs=[SMEM, VMEM, VMEM, VMEM] + used * 2,
    )


def ffn_kernel(places, n_ref, *refs):
    ogs, pieces, refs = refs[:4], refs[4:14], refs[14:]
    hidden_ref, gg_ref, ug_ref, og_ref = refs[:4]
    in_chunks = refs[4:8]
    in_acc, wg_ref, wu_ref, wd_ref = refs[8:]
    for i, g in enumerate(ogs):
        og_ref[at_rows((places[Z] + i) % NZ, ROWS), :] = g[...]
    lay_down(places, pieces, wd_ref)
    for j in range(2):
        cols = slice(j * 512, (j + 1) * 512)
        for b, some, i, h in each_shard(places, pieces):
            wg_ref[at_rows(b, 96), :] = piece_rows(some, i, h, 288 + 192 * j, 96)
            wu_ref[at_rows(b, 96), :] = piece_rows(some, i, h, 384 + 192 * j, 96)
        wg, wu, wd = wg_ref[...], wu_ref[...], wd_ref[cols, :]
        gate = mm(n_ref[...], wg)
        up = mm(n_ref[...], wu)
        hg = mm_t(og_ref[...], wd).astype(BF).astype(F32)
        sig = 1.0 / (1.0 + jnp.exp(-gate))
        silu = gate * sig
        hidden = (silu * up).astype(BF)
        gg = (hg * up * (sig * (1.0 + gate * (1.0 - sig)))).astype(BF)
        ug = (hg * silu).astype(BF)
        hidden_ref[:, cols] = hidden
        gg_ref[:, cols] = gg
        ug_ref[:, cols] = ug
        if j == 0:
            in_acc[...] = mm_t(gg, wg) + mm_t(ug, wu)
        else:
            in_acc[...] += mm_t(gg, wg) + mm_t(ug, wu)
    send_chunks(in_chunks, in_acc, places)


def ffn(places, normed, ogs, pieces):
    return call(
        ffn_kernel,
        [((TOKENS, FFZ), BF)] * 3 + [((TOKENS, D), BF)] + CHUNKS,
        [places, normed, *ogs, *pieces],
        COST["ffn"],
        scratch=[pltpu.VMEM((TOKENS, D), F32)]
        + [pltpu.VMEM((D, 512), BF)] * 2
        + [pltpu.VMEM((FFZ, D), BF)],
    )


def ffn_terms(n_ref, h_ref, gg_ref, ug_ref, og_ref, cols, put):
    for w, ref in enumerate((gg_ref, ug_ref)):
        for half in range(2):
            tile = mm(n_ref[...], ref[:, half * 512 + cols.start : half * 512 + cols.stop])
            r = (2 * w + half) * 96
            put(slice(r, r + 96), tile.reshape(8, 96, -1))
    for t in range(3):
        tile = mm(h_ref[...], og_ref[:, t * 512 + cols.start : t * 512 + cols.stop])
        put(slice(384 + 64 * t, 448 + 64 * t), tile.reshape(8, 64, -1))


def ffn_sent_kernel(places, n_ref, hidden_ref, gg_ref, ug_ref, og_ref, *refs):
    sent_refs, (n_mine, h_mine, n_turned, h_turned, n_sent, h_sent) = refs[:2], refs[2:]
    n_turned[...] = n_ref[...].T
    h_turned[...] = hidden_ref[...].T
    split_cores(places, n_turned, n_mine, n_sent, 96)
    split_cores(places, h_turned, h_mine, h_sent, 64)

    def put(rows, tile):
        for half, ref in enumerate(sent_refs):
            ref[:, rows, :] = tile[:, :, (0, FIRST)[half] : (FIRST, 512)[half]].astype(BF)

    ffn_terms(n_sent, h_sent, gg_ref, ug_ref, og_ref, slice(0, 512), put)


def ffn_sent_of(places, normed, hidden, gg, ug, og):
    return call(
        ffn_sent_kernel,
        [
            ((8, 576, FIRST), BF),
            ((8, 576, 512 - FIRST), BF),
            ((D // 2, TOKENS), BF),
            ((FFZ // 2, TOKENS), BF),
        ],
        [places, normed, hidden, gg, ug, og],
        COST["ffn_sent"],
        scratch=[
            pltpu.VMEM((D, TOKENS), BF),
            pltpu.VMEM((FFZ, TOKENS), BF),
            pltpu.VMEM((D // 2, TOKENS), BF),
            pltpu.VMEM((FFZ // 2, TOKENS), BF),
        ],
    )


def ffn_grad_kernel(cols, places, n_ref, h_ref, gg_ref, ug_ref, og_ref, got_ref, *refs):
    outs, sum_ref = refs[:-1], refs[-1]

    def put(rows, tile):
        sum_ref[:, rows, :] = (tile + got_ref[:, rows, :].astype(F32)).astype(BF)

    ffn_terms(n_ref, h_ref, gg_ref, ug_ref, og_ref, cols, put)
    for i in range(NX):
        for k in range(2):
            at = (places[X] + i) % NX * 2 + (places[YH] + k) % 2
            if len(outs) == 4:
                outs[i][k] = sum_ref[at]
            else:
                outs[k][i] = sum_ref[at]


def ffn_grad_first_kernel(*refs):
    ffn_grad_kernel(slice(0, FIRST), *refs)


def ffn_grad_second_kernel(*refs):
    ffn_grad_kernel(slice(FIRST, 512), *refs[:7], *refs[8:10], refs[11])
    refs[10][...] = refs[7][...]


def ffn_grad_first(places, args, deps):
    return call(
        ffn_grad_first_kernel,
        [((2, 576, FIRST), BF)] * 4,
        [places, *args],
        COST["ffn_grad"],
        scratch=[pltpu.VMEM((8, 576, FIRST), BF)],
        deps=deps,
    )


def ffn_grad_second(places, args, down_part, deps):
    return call(
        ffn_grad_second_kernel,
        [((4, 576, 512 - FIRST), BF)] * 2 + [((TOKENS, D), BF)],
        [places, *args, down_part],
        COST["ffn_grad_second"],
        scratch=[pltpu.VMEM((8, 576, 512 - FIRST), BF)],
        deps=deps,
    )


def y_sum_kernel(places, mine, got, *outs):
    for i in range(NX):
        outs[i][...] = (mine[i].astype(F32) + got[i].astype(F32)).astype(BF)


def y_sum(places, mine, got, deps):
    return call(
        y_sum_kernel,
        [(mine.shape[1:], BF)] * 4,
        [places, mine, got],
        COST["y_sum"],
        deps=deps,
    )


def ffn_join_kernel(places, mine, got, a, b, c, d, out):
    out[:, :FIRST] = (mine[...] + got[...].astype(F32)).astype(BF)
    total = a[...].astype(F32) + b[...].astype(F32) + c[...].astype(F32) + d[...].astype(F32)
    out[:, FIRST:] = total.astype(BF)


def ffn_join(places, mine, got, terms, deps):
    return call(
        ffn_join_kernel,
        [((576, 512), BF)],
        [places, mine, got, *terms],
        COST["add"],
        deps=deps,
    )[0]


def rms_back(grad, v, gain):
    r = lax.rsqrt(jnp.mean(v * v, axis=1, keepdims=True) + EPSILON)
    pulled = grad * gain
    return r * pulled - v * (r * r * r * jnp.mean(pulled * v, axis=1, keepdims=True))


def middle_back_kernel(places, own, g1, g2, g3, middle, og, gain, w_ref, mid_ref, branch_ref, *outs):
    grad = own[...] + g1[...].astype(F32) + g2[...].astype(F32) + g3[...].astype(F32)
    mid = og[...].astype(F32) + rms_back(grad, middle[...], gain[...])
    mid_ref[...] = mid
    branch = mid.astype(BF)
    branch_ref[...] = branch
    for i in range(NZ):
        outs[i][...] = mm_t(branch, w_ref[at_rows((places[Z] + i) % NZ, QW), :]).astype(BF)


def middle_back(places, chunks, middle, og, gain, w_out, deps):
    return call(
        middle_back_kernel,
        [((ROWS, D), F32), ((ROWS, D), BF)] + [((ROWS, QW), BF)] * 4,
        [places, *chunks, middle, og, gain, w_out],
        COST["middle_back"],
        deps=deps,
    )


def input_back_kernel(places, grad, x, mid, gain, out_ref):
    out_ref[...] = mid[...] + rms_back(grad[...].astype(F32), x[...].astype(F32), gain[...])


def input_back(places, grad, x, mid, gain, deps):
    return call(
        input_back_kernel, [((ROWS, D), F32)], [places, grad, x, mid, gain], 2, deps=deps
    )[0]


def scatter(chunks):
    far = [shift_z(chunks[1], 1), shift_z(chunks[3], -1), shift_z(chunks[2], 2)]
    return [chunks[0], *far]


def x_sum_kernel(places, a, b, c, d, mine, sent):
    mine[...] = a[0].astype(F32) + b[0].astype(F32) + c[0].astype(F32) + d[0].astype(F32)
    total = a[1].astype(F32) + b[1].astype(F32) + c[1].astype(F32) + d[1].astype(F32)
    sent[...] = total.astype(BF)


def x_sum(places, terms, us, deps):
    shape = terms[0].shape[1:]
    return call(x_sum_kernel, [(shape, F32), (shape, BF)], [places, *terms], us, deps=deps)


def add_kernel(places, a, b, out):
    out[...] = (a[...].astype(F32) + b[...].astype(F32)).astype(BF)


def added(places, a, b, deps):
    return call(add_kernel, [(a.shape, BF)], [places, a, b], COST["add"], deps=deps)[0]


def over_x(chunks):
    far = [shift_x(chunks[1], 1), shift_x(chunks[3], -1), shift_x(chunks[2], 2)]
    return [chunks[0], *far]


def as_row(column):
    return jnp.broadcast_to(column, (column.shape[0], 128)).T[:1]


def ffn_out_kernel(
    places, p0, p1, p2, p3, wg, wu, gain, gate_ref, up_ref, down_ref, gain_ref, all_ref, acc_ref
):
    j = pl.program_id(0)

    @pl.when(j == 0)
    def _():
        for i, p in enumerate((p0, p1, p2, p3)):
            all_ref[(places[Z] + i) % NZ] = p[...]
        acc_ref[...] = jnp.zeros_like(acc_ref)

    cols = pl.ds(pl.multiple_of(j % 2 * 256, 256), 256)
    for k, (w, out) in enumerate(((wg, gate_ref), (wu, up_ref))):
        rows = pl.ds(pl.multiple_of((2 * k + j // 2) * 96, 96), 96)
        parts = [all_ref[q, rows, cols].astype(F32) for q in range(NZ)]
        for b in range(4):
            tile = jnp.concatenate([v[:, b * 64 : (b + 1) * 64] for v in parts], axis=1)
            at = slice(b * 256, (b + 1) * 256)
            out[:, at] = tile
            acc_ref[...] += jnp.sum(tile * w[:, at].astype(F32), axis=1, keepdims=True)
    for t in range(3):
        r = 384 + 64 * t
        down_ref[:, t * 512 : (t + 1) * 512] = all_ref[j, r : r + 64, :].astype(F32)

    @pl.when(j == 3)
    def _():
        gain_ref[...] = as_row(acc_ref[...] / gain[...])


def ffn_out(places, pieces, wg, wu, gain, deps):
    whole = lambda shape: pl.BlockSpec(shape, lambda j: (0,) * len(shape))
    cols = pl.BlockSpec((96, 1024), lambda j: (0, j))
    return call(
        ffn_out_kernel,
        [((96, FF), F32), ((96, FF), F32), ((256, D), F32), ((1, 96), F32)],
        [places, *pieces, wg, wu, gain],
        4,
        scratch=[pltpu.VMEM((NZ, 576, 512), BF), pltpu.VMEM((96, 1), F32)],
        deps=deps,
        grid=(4,),
        in_specs=[SMEM] + [whole((576, 512))] * 4 + [cols, cols, whole((96, 1))],
        out_specs=[cols, cols, pl.BlockSpec((64, D), lambda j: (j, 0)), whole((1, 96))],
    )


def out_slices_kernel(places, p0, p1, p2, p3, *refs):
    all_ref = refs[4]
    for i, p in enumerate((p0, p1, p2, p3)):
        all_ref[(places[Z] + i) % NZ] = p[96:, :]
    for i in range(NX):
        refs[i][...] = all_ref[(places[X] + i) % NX]


def out_slices(places, pieces, deps):
    return call(
        out_slices_kernel,
        [((48, 768), BF)] * 4,
        [places, *pieces],
        1,
        scratch=[pltpu.VMEM((NZ, 48, 768), BF)],
        deps=deps,
    )


def qkv_out_kernel(
    places, p0, p1, p2, p3, wq, wk, wv, own_gain, q_ref, k_ref, v_ref, gain_ref, all_ref
):
    for i, p in enumerate((p0, p1, p2, p3)):
        all_ref[(places[Z] + i) % NZ] = p[:96, :]
    for q in range(NZ):
        q_ref[:, q * QW : (q + 1) * QW] = all_ref[q, :, :QW].astype(F32)
    gain = jnp.sum(q_ref[...] * wq[...].astype(F32), axis=1, keepdims=True)
    for out, w, at in ((k_ref, wk, QW), (v_ref, wv, QW + KW)):
        tile = jnp.concatenate(
            [all_ref[q, :, at : at + KW].astype(F32) for q in range(NZ)], axis=1
        )
        out[...] = tile
        gain += jnp.sum(tile * w[...].astype(F32), axis=1, keepdims=True)
    gain_ref[...] = as_row(gain / own_gain[...])


def qkv_out(places, pieces, wq, wk, wv, gain, deps):
    return call(
        qkv_out_kernel,
        [((96, 1536), F32), ((96, 768), F32), ((96, 768), F32), ((1, 96), F32)],
        [places, *pieces, wq, wk, wv, gain],
        2,
        scratch=[pltpu.VMEM((NZ, 96, 768), BF)],
        deps=deps,
    )


def out_out_kernel(places, p0, p1, p2, p3, out_ref):
    for i, p in enumerate((p0, p1, p2, p3)):
        tile = p[...].astype(F32)
        rows = pl.ds(pl.multiple_of((places[X] + i) % NX * 24, 8), 24)
        out_ref[rows, :] = jnp.concatenate([tile[:24], tile[24:]], axis=1)


def out_out(places, pieces):
    return call(out_out_kernel, [((96, D), F32)], [places, *pieces], 1)[0]


def block_out_kernel(places, middle, down, out_ref):
    out_ref[...] = (middle[...] + down[...].astype(F32)).astype(BF)


def block_out_of(places, middle, down, deps):
    return call(block_out_kernel, [((ROWS, D), BF)], [places, middle, down], 1, deps=deps)[0]


def body(
    inputs, norm_attn, w_query, w_key, w_value, w_out, norm_ffn, w_gate, w_up, w_down, cotangent
):
    f, s = lax.axis_index("fsdp"), lax.axis_index("sp")
    x, yh, c, z, yl = f // 4, f // 2 % 2, f % 2, s // 2, s % 2
    places = jnp.stack([x, yh, c, z, yl]).astype(jnp.int32)
    x_own, og_own = inputs[0], cotangent[0]
    gain_attn, gain_ffn = norm_attn[None], norm_ffn[None]

    index = jnp.arange(TOKENS, dtype=jnp.int32)
    positions = (index // ROWS * 2 + yl) * ROWS + index % ROWS
    lane = np.arange(QW) % HEAD_DIM
    frequency = ROPE_BASE ** (-(jnp.arange(HALF, dtype=F32) * 2.0 / HEAD_DIM))
    frequency = jnp.concatenate([frequency] * (QW // HALF))
    angles = positions.astype(F32)[:, None] * frequency[None, :]
    sign = np.where(lane < HALF, -1.0, 1.0).astype(np.float32)
    cosine, sine = jnp.cos(angles), jnp.sin(angles) * sign[None, :]

    qkv_shard, row_shard = cut(
        places, w_query, w_key, w_value, w_gate, w_up, w_down, w_out
    )
    qkv_mirror, row_mirror = mirror_y(qkv_shard), mirror_y(row_shard)
    xs = two_stage_z(x_own)
    (qkv_pair,) = paired(places, qkv_shard, qkv_mirror, [96], [cosine, sine, gain_attn])
    qkv_mine = two_stage_x(qkv_pair)
    qkv_other = [swap_core(p) for p in qkv_mine]
    (rows_pair,) = paired(
        places, row_shard, row_mirror, [864], [qkv_mine[1], qkv_mine[2], xs[1], xs[2]]
    )
    above, below = shift_x(rows_pair, -1), shift_x(rows_pair, 1)

    normed, x_all, og_copy, turned_mine, turned_sent = norm(places, gain_attn, og_own, xs)
    ogs = two_stage_z(og_copy)
    q, kv, held_qkv = qkv(places, normed, qkv_mine, qkv_other, cosine, sine)
    kv_other = swap_low(kv)
    mixed, shares = attend(places, q, kv, kv_other, [ogs[1], ogs[2]])
    half_up, half_down = halves(places, above, below, [mixed])
    far = [shift_x(half_up, 1), shift_x(half_down, -1)]
    mixed_all = gather_z(mixed).reshape(NZ, TOKENS, QW)
    far = copied(places, far, [mixed])
    pieces = [rows_pair, above, below, *far]
    pieces += [swap_core(p) for p in pieces]
    normed_ffn, middle_own, held_out = middle_of(places, x_all, gain_ffn, mixed_all, pieces)
    outs = ffn(places, normed_ffn, ogs, pieces)
    hidden, gate_grad, up_grad, og_all = outs[:4]
    in_chunks = outs[4:8]

    in_got = scatter(in_chunks)
    a_sent, b_sent, n_mine, h_mine = ffn_sent_of(
        places, normed_ffn, hidden, gate_grad, up_grad, og_all
    )
    down_part, column_attn, column_ffn = down_of(
        places, hidden, gain_attn, gain_ffn, pieces, [n_mine]
    )
    back = middle_back(
        places, in_got, middle_own, og_own, gain_ffn, held_out, [n_mine, down_part]
    )
    middle_grad, branch = back[:2]
    head_grads = [back[2], shift_z(back[5], -1), shift_z(back[4], 2), shift_z(back[3], 1)]
    branch_all = gather_z(branch)
    a_got, b_got = swap_core(a_sent), swap_core(b_sent)
    ffn_args = (n_mine, h_mine, gate_grad, up_grad, og_all)
    a_chunks = ffn_grad_first(places, (*ffn_args, a_got), [branch])
    a_terms = over_x(a_chunks)

    dq, dkv_own, dkv_sent = attend_back(
        places, head_grads, q, kv, kv_other, shares, [a_chunks[0]]
    )
    b_mine, b_sent, down_part = ffn_grad_second(places, (*ffn_args, b_got), down_part, [dq])
    down_own = scatter_z(down_part)
    b_got = mirror_y(b_sent)
    dkv_got = swap_low(dkv_sent)
    lin, out_part, qkv_sent = turn(
        places, dq, dkv_own, dkv_got, cosine, sine, turned_sent, mixed, branch_all, [b_sent]
    )
    qkv_got = swap_core(qkv_sent)
    first_part = first(places, lin, held_qkv, [])
    first_got = scatter_z(first_part)
    a_half, a_sent = x_sum(places, a_terms, COST["x_sum"], [first_part])
    a_got = mirror_y(a_sent)
    qkv_chunks = qkv_grad(places, lin, turned_mine, out_part, qkv_got, [a_sent])
    qkv_terms = over_x(qkv_chunks)
    b_terms = over_x(y_sum(places, b_mine, b_got, [qkv_chunks[0]]))

    qkv_half, qkv_sent = x_sum(places, qkv_terms, 2, [])
    qkv_got = mirror_y(qkv_sent)
    ffn_half = ffn_join(places, a_half, a_got, b_terms, [qkv_sent])
    ffn_low = swap_low(ffn_half)
    qkv_half = added(places, qkv_half, qkv_got, [ffn_half])
    qkv_low = swap_low(qkv_half)
    qkv_total = added(places, qkv_half, qkv_low, [])
    qkv_pieces = pieces_z(qkv_total)
    ffn_total = added(places, ffn_half, ffn_low, [qkv_total])
    ffn_pieces = pieces_z(ffn_total)

    block_out = block_out_of(places, middle_own, down_own, [qkv_total])
    input_grad = input_back(places, first_got, x_own, middle_grad, gain_attn, [qkv_total])
    out_terms = over_x(out_slices(places, qkv_pieces, [block_out, input_grad]))
    grad_query, grad_key, grad_value, qkv_gain = qkv_out(
        places, qkv_pieces, w_query, w_key, w_value, column_attn, [out_terms[0]]
    )
    grad_gate, grad_up, grad_down, ffn_gain = ffn_out(
        places, ffn_pieces, w_gate, w_up, column_ffn, [qkv_gain]
    )
    grad_out = out_out(places, [out_terms[0], out_terms[2], out_terms[3], out_terms[1]])
    grad_norm_attn, grad_norm_ffn = qkv_gain[0], ffn_gain[0]
    return (
        block_out[None],
        input_grad[None],
        grad_norm_attn,
        grad_query,
        grad_key,
        grad_value,
        grad_out,
        grad_norm_ffn,
        grad_gate,
        grad_up,
        grad_down,
    )


def solution(mesh):
    rows = P("fsdp", None)
    tokens = P("fsdp", "sp", None)
    return jax.shard_map(
        body,
        mesh=mesh,
        in_specs=(tokens, P(), rows, rows, rows, rows, P(), rows, rows, rows, tokens),
        out_specs=(tokens, tokens, P("fsdp"), rows, rows, rows, rows, P("fsdp"), rows, rows, rows),
        check_vma=False,
    )
```

```python
import functools

import jax
import jax.numpy as jnp
import numpy as np
from jax import lax
from jax.experimental import pallas as pl
from jax.experimental.pallas import tpu as pltpu
from jax.sharding import PartitionSpec as P

D = 1536
HEADS = 16
KV_HEADS = 8
HEAD_DIM = 96
FF = 4096

EPSILON = 1e-05
ROPE_BASE = 100000.0
MASKED = -1e30

NX, NZ = 4, 4
ROWS = 128
TOKENS = ROWS * NZ
QW, KW = 384, 192
HALF = HEAD_DIM // 2
FFZ = FF // NZ
BF = jnp.bfloat16
F32 = jnp.float32
VMEM = pl.BlockSpec(memory_space=pltpu.VMEM)
SMEM = pl.BlockSpec(memory_space=pltpu.SMEM)
ANY = pl.BlockSpec(memory_space=pl.ANY)
LIMIT = pltpu.CompilerParams(vmem_limit_bytes=56 * 1024 * 1024)
X, YH, CORE, Z, YL = range(5)
SPLIT = 384
FIRST = 384
COST = {
    "norm": 54,
    "qkv": 0.1,
    "attend": 0.1,
    "down": 0.1,
    "middle": 4,
    "ffn": 17,
    "ffn_sent": 0.1,
    "middle_back": 60,
    "ffn_grad": 60,
    "ffn_grad_second": 0.1,
    "attend_back": 60,
    "turn": 0.1,
    "first": 0.1,
    "x_sum": 60,
    "y_sum": 0.1,
    "qkv_grad": 0.1,
    "add": 8,
}


Z_GROUPS = [[z * 2 + l for z in range(NZ)] for l in range(2)]


def scatter_z(v):
    return lax.psum_scatter(
        v, "sp", scatter_dimension=0, tiled=True, axis_index_groups=Z_GROUPS
    )


def gather_z(v):
    return lax.all_gather(v, "sp", axis=0, tiled=True, axis_index_groups=Z_GROUPS)


def shift_z(v, step):
    pairs = [(z * 2 + l, (z + step) % NZ * 2 + l) for z in range(NZ) for l in range(2)]
    return lax.ppermute(v, "sp", pairs)


def swap_low(v):
    return lax.ppermute(v, "sp", [(s, s ^ 1) for s in range(8)])


def shift_x(v, step):
    pairs = [(x * 4 + r, (x + step) % NX * 4 + r) for x in range(NX) for r in range(4)]
    return lax.ppermute(v, "fsdp", pairs)


def swap_core(v):
    return lax.ppermute(v, "fsdp", [(f, f ^ 1) for f in range(16)])


def mirror_y(v):
    pairs = [(f * 8 + s, (f ^ 2) * 8 + (s ^ 1)) for f in range(16) for s in range(8)]
    return lax.ppermute(v, ("fsdp", "sp"), pairs)


def pieces_z(v):
    far = [shift_z(v, -1), shift_z(v, 1), shift_z(v, 2)]
    return [v, far[0], far[2], far[1]]


def two_stage_z(v):
    above, below = shift_z(v, -1), shift_z(v, 1)
    return [v, above, shift_z(below, 1), below]


def two_stage_x(v):
    above, below = shift_x(v, -1), shift_x(v, 1)
    return [v, above, shift_x(below, 1), below]


def pieces_x(v):
    far = [shift_x(v, -1), shift_x(v, 1), shift_x(v, 2)]
    return [v, far[0], far[2], far[1]]


def part(v, index, size, dim=0):
    return lax.dynamic_slice_in_dim(v, index * size, size, dim)


def call(kernel, outs, ins, us, scratch=(), deps=(), grid=(), in_specs=None, out_specs=None):
    def run(*refs):
        kernel(*refs[: len(ins)], *refs[len(ins) + len(deps) :])

    return pl.pallas_call(
        run,
        name=kernel.__name__.replace("_kernel", ""),
        grid=grid,
        out_shape=[jax.ShapeDtypeStruct(s, t) for s, t in outs],
        in_specs=(in_specs or [SMEM] + [VMEM] * (len(ins) - 1)) + [ANY] * len(deps),
        out_specs=out_specs or [VMEM] * len(outs),
        scratch_shapes=scratch,
        compiler_params=LIMIT,
        cost_estimate=pl.CostEstimate(
            flops=int(us * 1e9), bytes_accessed=int(us * 3e6), transcendentals=0
        ),
    )(*ins, *deps)


def mm(a, b):
    return jnp.dot(a, b, preferred_element_type=F32)


def mm_t(a, b):
    return lax.dot_general(a, b, (((1,), (1,)), ((), ())), preferred_element_type=F32)


def t_mm(a, b):
    return lax.dot_general(a, b, (((0,), (0,)), ((), ())), preferred_element_type=F32)


def at_rows(index, size):
    return pl.ds(pl.multiple_of(index * size, size), size)


def rope(v, cosine, sine):
    width = v.shape[1]
    lane = lax.broadcasted_iota(jnp.int32, v.shape, 1) % HEAD_DIM
    partner = jnp.where(
        lane < HALF, pltpu.roll(v, width - HALF, 1), pltpu.roll(v, HALF, 1)
    )
    return v * cosine + partner * sine


def rope_keys(kv, cosine, sine):
    lane = lax.broadcasted_iota(jnp.int32, kv.shape, 1)
    return jnp.where(lane < KW, rope(kv, cosine, sine), kv)


def cut_kernel(places, wq, wk, wv, wg, wu, wd, wo, qkv_ref, rows_ref):
    z = places[Z]
    for t in range(3):
        cols = slice(t * 512, (t + 1) * 512)
        rows_ref[96 * t : 96 * (t + 1), :] = wo[:, cols]
        rows_ref[672 + 64 * t : 736 + 64 * t, :] = wd[at_rows(z, 64), cols]
    qkv_ref[:, :QW] = wq[:, pl.ds(pl.multiple_of(z * QW, 128), QW)]
    for at in range(NZ):

        @pl.when(z == at)
        def _():
            cols = slice(at * KW, (at + 1) * KW)
            qkv_ref[:, QW:] = jnp.concatenate([wk[:, cols], wv[:, cols]], axis=1)
            for k, w in enumerate((wg, wu)):
                for half in range(2):
                    starts = [(8 * half + i) * 256 + at * 64 for i in range(8)]
                    rows = slice(288 + (2 * half + k) * 96, 384 + (2 * half + k) * 96)
                    rows_ref[rows, :] = jnp.concatenate([w[:, b : b + 64] for b in starts], axis=1)


def cut(places, *arrays):
    return call(cut_kernel, [((96, 768), BF), ((864, 512), BF)], [places, *arrays], 3)


def copy_kernel(places, *refs):
    n = len(refs) // 2
    for i in range(n):
        refs[n + i][...] = refs[i][...]


def copied(places, arrays, deps):
    return call(copy_kernel, [(v.shape, v.dtype) for v in arrays], [places, *arrays], 0.1, deps=deps)


def pair_kernel(places, own, mirror, *outs):
    start = 0
    for out in outs:
        rows = slice(start, start + out.shape[1])
        out[places[YH]] = own[rows, :]
        out[1 - places[YH]] = mirror[rows, :]
        start += out.shape[1]


def paired(places, own, mirror, parts, deps):
    outs = [((2, n, own.shape[1]), BF) for n in parts]
    return call(pair_kernel, outs, [places, own, mirror], 0.1, deps=deps)


def norm_kernel(places, gain, og, *refs):
    xs, (normed_ref, x_ref, og_ref, mine_ref, sent_ref, turned_ref) = refs[:4], refs[4:]
    og_ref[...] = og[...]
    for i in range(NZ):
        x_ref[at_rows((places[Z] + i) % NZ, ROWS), :] = xs[i][...]
    for i in range(NZ):
        rows = pl.ds(i * ROWS, ROWS)
        v = x_ref[rows, :].astype(F32)
        r = lax.rsqrt(jnp.mean(v * v, axis=1, keepdims=True) + EPSILON)
        normed_ref[rows, :] = (v * r * gain[...]).astype(BF)
    turned_ref[...] = normed_ref[...].T
    split_cores(places, turned_ref, mine_ref, sent_ref, 96)


def split_cores(places, turned_ref, mine_ref, sent_ref, n):
    for k in range(8):
        rows = slice(k * n, (k + 1) * n)
        mine_ref[rows, :] = turned_ref[at_rows(2 * k + places[CORE], n), :]
        sent_ref[rows, :] = turned_ref[at_rows(2 * k + 1 - places[CORE], n), :]


def norm(places, gain, og, xs):
    return call(
        norm_kernel,
        [((TOKENS, D), BF)] * 2 + [((ROWS, D), BF)] + [((D // 2, TOKENS), BF)] * 2,
        [places, gain, og, *xs],
        COST["norm"],
        scratch=[pltpu.VMEM((D, TOKENS), BF)],
    )


def qkv_kernel(places, normed_ref, *refs):
    mine, other = refs[:4], refs[4:8]
    cosine, sine, q_ref, kv_ref, w_ref = refs[8:]
    for i in range(NX):
        for h in range(2):
            base = (places[X] + i) % NX * 4 + h * 2
            w_ref[at_rows(base + places[CORE], 96), :] = mine[i][h]
            w_ref[at_rows(base + 1 - places[CORE], 96), :] = other[i][h]
    for i in range(NZ):
        rows = pl.ds(i * ROWS, ROWS)
        lin = mm(normed_ref[rows, :], w_ref[...])
        q_ref[rows, :] = rope(lin[:, :QW], cosine[rows, :], sine[rows, :]).astype(BF)
        kv_ref[rows, :] = rope_keys(lin[:, QW:], cosine[rows, :], sine[rows, :]).astype(BF)


def qkv(places, normed, mine, other, cosine, sine):
    return call(
        qkv_kernel,
        [((TOKENS, QW), BF), ((TOKENS, 2 * KW), BF), ((D, QW + 2 * KW), BF)],
        [places, normed, *mine, *other, cosine, sine],
        COST["qkv"],
    )


def head(ref, rows, index):
    return ref[rows, index * HEAD_DIM : (index + 1) * HEAD_DIM]


def two_heads(ref, j, g):
    rows = slice(j * ROWS, (j + 1) * ROWS)
    return jnp.concatenate([head(ref, rows, 2 * g), head(ref, rows, 2 * g + 1)], axis=0)


def attend_kernel(places, q_ref, own_ref, other_ref, mixed_ref, p_ref):
    late = places[YL]
    factor = HEAD_DIM ** (-0.5)
    for g in range(2):
        for j in range(NZ):
            n = (j + 1) * ROWS
            q = two_heads(q_ref, j, g)
            s_own = mm_t(q, head(own_ref, slice(0, n), g)) * factor
            s_oth = mm_t(q, head(other_ref, slice(0, n), g)) * factor
            shape = (2 * ROWS, n)
            row = lax.broadcasted_iota(jnp.int32, shape, 0) % ROWS + j * ROWS
            col = lax.broadcasted_iota(jnp.int32, shape, 1)
            s_own = jnp.where(col <= row, s_own, MASKED)
            s_oth = jnp.where(col < (j + late) * ROWS, s_oth, MASKED)
            highest = jnp.maximum(
                jnp.max(s_own, axis=1, keepdims=True), jnp.max(s_oth, axis=1, keepdims=True)
            )
            p_own, p_oth = jnp.exp(s_own - highest), jnp.exp(s_oth - highest)
            total = jnp.sum(p_own, axis=1, keepdims=True) + jnp.sum(p_oth, axis=1, keepdims=True)
            scale = 1.0 / total
            p_own, p_oth = (p_own * scale).astype(BF), (p_oth * scale).astype(BF)
            p_ref[g, j, :, :n] = p_own
            p_ref[g, j, :, n : 2 * n] = p_oth
            out = mm(p_own, head(own_ref, slice(0, n), 2 + g)) + mm(
                p_oth, head(other_ref, slice(0, n), 2 + g)
            )
            out = out.astype(BF)
            for k in range(2):
                h = 2 * g + k
                mixed_ref[j * ROWS : (j + 1) * ROWS, h * HEAD_DIM : (h + 1) * HEAD_DIM] = out[
                    k * ROWS : (k + 1) * ROWS
                ]


def attend(places, q, kv, kv_other, deps):
    return call(
        attend_kernel,
        [((TOKENS, QW), BF), ((2, NZ, 2 * ROWS, 2 * TOKENS), BF)],
        [places, q, kv, kv_other],
        COST["attend"],
        deps=deps,
    )


def attend_back_kernel(places, *refs):
    grads = refs[:4]
    q_ref, own_ref, other_ref, p_ref = refs[4:8]
    dq_ref, down_ref, doth_ref = refs[8:11]
    do_ref, acc_own, acc_oth = refs[11:]
    factor = HEAD_DIM ** (-0.5)
    for i in range(NZ):
        do_ref[at_rows((places[Z] + i) % NZ, ROWS), :] = grads[i][...]
    for g in range(2):
        acc_own[...] = jnp.zeros_like(acc_own)
        acc_oth[...] = jnp.zeros_like(acc_oth)
        for j in range(NZ):
            n = (j + 1) * ROWS
            seen = slice(0, n)
            q = two_heads(q_ref, j, g)
            do = two_heads(do_ref, j, g)
            p_own, p_oth = p_ref[g, j, :, :n], p_ref[g, j, :, n : 2 * n]
            dp_own = mm_t(do, head(own_ref, seen, 2 + g))
            dp_oth = mm_t(do, head(other_ref, seen, 2 + g))
            f_own, f_oth = p_own.astype(F32), p_oth.astype(F32)
            dot = jnp.sum(f_own * dp_own, axis=1, keepdims=True) + jnp.sum(
                f_oth * dp_oth, axis=1, keepdims=True
            )
            ds_own = (f_own * (dp_own - dot)).astype(BF)
            ds_oth = (f_oth * (dp_oth - dot)).astype(BF)
            dq = mm(ds_own, head(own_ref, seen, g)) + mm(ds_oth, head(other_ref, seen, g))
            dq = (dq * factor).astype(BF)
            for k in range(2):
                h = 2 * g + k
                dq_ref[j * ROWS : (j + 1) * ROWS, h * HEAD_DIM : (h + 1) * HEAD_DIM] = dq[
                    k * ROWS : (k + 1) * ROWS
                ]
            acc_own[0, seen, :] += t_mm(ds_own, q)
            acc_own[1, seen, :] += t_mm(p_own, do)
            acc_oth[0, seen, :] += t_mm(ds_oth, q)
            acc_oth[1, seen, :] += t_mm(p_oth, do)
        for kind, scale in ((0, factor), (1, 1.0)):
            at = kind * KW + g * HEAD_DIM
            down_ref[:, at : at + HEAD_DIM] = acc_own[kind] * scale
            doth_ref[:, at : at + HEAD_DIM] = (acc_oth[kind] * scale).astype(BF)


def attend_back(places, grads, q, kv, kv_other, shares, deps):
    acc = pltpu.VMEM((2, TOKENS, HEAD_DIM), F32)
    return call(
        attend_back_kernel,
        [((TOKENS, QW), BF), ((TOKENS, 2 * KW), F32), ((TOKENS, 2 * KW), BF)],
        [places, *grads, q, kv, kv_other, shares],
        COST["attend_back"],
        scratch=[pltpu.VMEM((TOKENS, QW), BF), acc, acc],
        deps=deps,
    )


def send_chunks(refs, acc_ref, places):
    for i in range(NZ):
        rows = at_rows((places[Z] + i) % NZ, ROWS)
        refs[i][...] = acc_ref[rows, :].astype(refs[i].dtype)


CHUNKS = [((ROWS, D), F32)] + [((ROWS, D), BF)] * 3


def put_out(out_ref, places, core, ref):
    for k in range(8):
        rows = pl.ds(pl.multiple_of((k % 2 * 2 + core) * 96 + k // 2 * 24, 8), 24)
        tile = out_ref[rows, :]
        ref[k, 96:, :] = jnp.concatenate([tile[:, :768], tile[:, 768:]], axis=0).astype(BF)


def turn_kernel(
    places, dq_ref, own_ref, got_ref, cosine, sine, turned_ref, mixed_ref, branch_ref, *refs
):
    lin_ref, out_ref, sent_ref = refs
    for i in range(NZ):
        rows = slice(i * ROWS, (i + 1) * ROWS)
        dkv = (own_ref[rows, :] + got_ref[rows, :].astype(F32)).astype(BF)
        c, s = cosine[rows, :], -sine[rows, :]
        lin_ref[rows, :QW] = rope(dq_ref[rows, :].astype(F32), c, s).astype(BF)
        lin_ref[rows, QW:] = rope_keys(dkv.astype(F32), c, s).astype(BF)
    for k in range(8):
        sent_ref[k, :96, :] = mm(turned_ref[k * 96 : (k + 1) * 96, :], lin_ref[...]).astype(BF)
    out_ref[...] = t_mm(mixed_ref[...], branch_ref[...])
    put_out(out_ref, places, 1 - places[CORE], sent_ref)


def turn(places, dq, dkv_own, dkv_got, cosine, sine, turned, mixed, branch, deps):
    return call(
        turn_kernel,
        [((TOKENS, 768), BF), ((QW, D), F32), ((8, 144, 768), BF)],
        [places, dq, dkv_own, dkv_got, cosine, sine, turned, mixed, branch],
        COST["turn"],
        deps=deps,
    )


def first_kernel(places, lin_ref, w_ref, out_ref):
    out_ref[...] = mm_t(lin_ref[...], w_ref[...]).astype(BF)


def first(places, lin, w, deps):
    return call(first_kernel, [((TOKENS, D), BF)], [places, lin, w], COST["first"], deps=deps)[0]


def qkv_grad_kernel(places, lin_ref, turned_ref, out_ref, got_ref, *refs):
    outs, sum_ref = refs[:4], refs[4]
    for k in range(8):
        sum_ref[k, :96, :] = mm(turned_ref[k * 96 : (k + 1) * 96, :], lin_ref[...]).astype(BF)
    put_out(out_ref, places, places[CORE], sum_ref)
    for i in range(NX):
        for k in range(2):
            at = (places[X] + i) % NX * 2 + (places[YH] + k) % 2
            outs[i][k] = (sum_ref[at].astype(F32) + got_ref[at].astype(F32)).astype(BF)


def qkv_grad(places, lin, turned, out, got, deps):
    return call(
        qkv_grad_kernel,
        [((2, 144, 768), BF)] * 4,
        [places, lin, turned, out, got],
        COST["qkv_grad"],
        scratch=[pltpu.VMEM((8, 144, 768), BF)],
        deps=deps,
    )


def piece_rows(pieces, i, h, start, n):
    if i == 2:
        ref, start = (pieces[3], start) if start < SPLIT else (pieces[4], start - SPLIT)
    else:
        ref = pieces[(0, 1, None, 2)[i]]
    return ref[h, start : start + n, :]


def each_shard(places, pieces):
    for i in range(NX):
        for h in range(2):
            base = (places[X] + i) % NX * 4 + h * 2
            yield base + places[CORE], pieces[:5], i, h
            yield base + 1 - places[CORE], pieces[5:], i, h


def halves_kernel(places, below, *refs):
    above, first_ref, second_ref = refs[:-2], refs[-2], refs[-1]
    first_ref[...] = below[...]
    for i, ref in enumerate(above):
        second_ref[:, i * 96 : (i + 1) * 96] = ref[...]


def halves(places, above, below, deps):
    def block(n, at):
        return pl.BlockSpec((2, n, 512), lambda j: (0, at, 0))

    count = (864 - SPLIT) // 96
    return call(
        halves_kernel,
        [((2, SPLIT, 512), BF), ((2, 864 - SPLIT, 512), BF)],
        [places, below] + [above] * count,
        0.1,
        deps=deps,
        grid=(1,),
        in_specs=[SMEM, block(SPLIT, 0)] + [block(96, SPLIT // 96 + i) for i in range(count)],
    )


def lay_output(places, all_pieces, out_ref):
    for b, pieces, i, h in each_shard(places, all_pieces):
        for t in range(3):
            out_ref[at_rows(b, 96), t * 512 : (t + 1) * 512] = piece_rows(pieces, i, h, t * 96, 96)


def lay_down(places, all_pieces, out_ref):
    for b, pieces, i, h in each_shard(places, all_pieces):
        for t in range(3):
            tile = piece_rows(pieces, i, h, 672 + 64 * t, 64)
            out_ref[at_rows(b, 64), t * 512 : (t + 1) * 512] = tile


def down_kernel(places, hidden_ref, gain_a, gain_b, *refs):
    pieces, down_ref, col_a, col_b, wd_ref, turned_ref = refs[:10], *refs[10:]
    own = pl.ds(pl.multiple_of((places[X] * 4 + places[YH] * 2 + places[CORE]) * 96, 8), 96)
    for gain, col in ((gain_a, col_a), (gain_b, col_b)):
        turned_ref[...] = jnp.broadcast_to(gain[...], (128, D)).T
        col[...] = turned_ref[own, :1]
    lay_down(places, pieces, wd_ref)
    down_ref[...] = mm(hidden_ref[...], wd_ref[...]).astype(BF)


def down_of(places, hidden, gain_a, gain_b, pieces, deps):
    return call(
        down_kernel,
        [((TOKENS, D), BF), ((96, 1), F32), ((96, 1), F32)],
        [places, hidden, gain_a, gain_b, *pieces],
        COST["down"],
        scratch=[pltpu.VMEM((FFZ, D), BF), pltpu.VMEM((D, 128), F32)],
        deps=deps,
    )


def middle_kernel(places, x_ref, gain, mixed, *refs):
    pieces, (normed_ref, own_ref, w_ref, acc_ref, mixed_ref) = refs[:10], refs[10:]
    lay_output(places, pieces, w_ref)
    for z in range(NZ):
        mixed_ref[:, z * QW : (z + 1) * QW] = mixed[z]
    for t in range(3):
        cols = slice(t * 512, (t + 1) * 512)
        acc_ref[:, cols] = x_ref[:, cols].astype(F32) + mm(mixed_ref[...], w_ref[:, cols])
    for i in range(NZ):
        rows = slice(i * ROWS, (i + 1) * ROWS)
        v = acc_ref[rows, :]
        r = lax.rsqrt(jnp.mean(v * v, axis=1, keepdims=True) + EPSILON)
        normed_ref[rows, :] = (v * r * gain[...]).astype(BF)
    own_ref[...] = acc_ref[at_rows(places[Z], ROWS), :]


def middle_of(places, x_all, gain, mixed, pieces):
    def rows(n):
        return pl.BlockSpec((2, n, 512), lambda j: (0, 0, 0))

    used = [rows(288)] * 4 + [rows(16)]
    return call(
        middle_kernel,
        [((TOKENS, D), BF), ((ROWS, D), F32), ((D, D), BF)],
        [places, x_all, gain, mixed, *pieces],
        COST["middle"],
        scratch=[pltpu.VMEM((TOKENS, D), F32), pltpu.VMEM((TOKENS, D), BF)],
        grid=(1,),
        in_specs=[SMEM, VMEM, VMEM, VMEM] + used * 2,
    )


def ffn_kernel(places, n_ref, *refs):
    ogs, pieces, refs = refs[:4], refs[4:14], refs[14:]
    hidden_ref, gg_ref, ug_ref, og_ref = refs[:4]
    in_chunks = refs[4:8]
    in_acc, wg_ref, wu_ref, wd_ref = refs[8:]
    for i, g in enumerate(ogs):
        og_ref[at_rows((places[Z] + i) % NZ, ROWS), :] = g[...]
    lay_down(places, pieces, wd_ref)
    for j in range(2):
        cols = slice(j * 512, (j + 1) * 512)
        for b, some, i, h in each_shard(places, pieces):
            wg_ref[at_rows(b, 96), :] = piece_rows(some, i, h, 288 + 192 * j, 96)
            wu_ref[at_rows(b, 96), :] = piece_rows(some, i, h, 384 + 192 * j, 96)
        wg, wu, wd = wg_ref[...], wu_ref[...], wd_ref[cols, :]
        gate = mm(n_ref[...], wg)
        up = mm(n_ref[...], wu)
        hg = mm_t(og_ref[...], wd).astype(BF).astype(F32)
        sig = 1.0 / (1.0 + jnp.exp(-gate))
        silu = gate * sig
        hidden = (silu * up).astype(BF)
        gg = (hg * up * (sig * (1.0 + gate * (1.0 - sig)))).astype(BF)
        ug = (hg * silu).astype(BF)
        hidden_ref[:, cols] = hidden
        gg_ref[:, cols] = gg
        ug_ref[:, cols] = ug
        if j == 0:
            in_acc[...] = mm_t(gg, wg) + mm_t(ug, wu)
        else:
            in_acc[...] += mm_t(gg, wg) + mm_t(ug, wu)
    send_chunks(in_chunks, in_acc, places)


def ffn(places, normed, ogs, pieces):
    return call(
        ffn_kernel,
        [((TOKENS, FFZ), BF)] * 3 + [((TOKENS, D), BF)] + CHUNKS,
        [places, normed, *ogs, *pieces],
        COST["ffn"],
        scratch=[pltpu.VMEM((TOKENS, D), F32)]
        + [pltpu.VMEM((D, 512), BF)] * 2
        + [pltpu.VMEM((FFZ, D), BF)],
    )


def ffn_terms(n_ref, h_ref, gg_ref, ug_ref, og_ref, cols, put):
    for w, ref in enumerate((gg_ref, ug_ref)):
        for half in range(2):
            tile = mm(n_ref[...], ref[:, half * 512 + cols.start : half * 512 + cols.stop])
            r = (2 * w + half) * 96
            put(slice(r, r + 96), tile.reshape(8, 96, -1))
    for t in range(3):
        tile = mm(h_ref[...], og_ref[:, t * 512 + cols.start : t * 512 + cols.stop])
        put(slice(384 + 64 * t, 448 + 64 * t), tile.reshape(8, 64, -1))


def ffn_sent_kernel(places, n_ref, hidden_ref, gg_ref, ug_ref, og_ref, *refs):
    sent_refs, (n_mine, h_mine, n_turned, h_turned, n_sent, h_sent) = refs[:2], refs[2:]
    n_turned[...] = n_ref[...].T
    h_turned[...] = hidden_ref[...].T
    split_cores(places, n_turned, n_mine, n_sent, 96)
    split_cores(places, h_turned, h_mine, h_sent, 64)

    def put(rows, tile):
        for half, ref in enumerate(sent_refs):
            ref[:, rows, :] = tile[:, :, (0, FIRST)[half] : (FIRST, 512)[half]].astype(BF)

    ffn_terms(n_sent, h_sent, gg_ref, ug_ref, og_ref, slice(0, 512), put)


def ffn_sent_of(places, normed, hidden, gg, ug, og):
    return call(
        ffn_sent_kernel,
        [
            ((8, 576, FIRST), BF),
            ((8, 576, 512 - FIRST), BF),
            ((D // 2, TOKENS), BF),
            ((FFZ // 2, TOKENS), BF),
        ],
        [places, normed, hidden, gg, ug, og],
        COST["ffn_sent"],
        scratch=[
            pltpu.VMEM((D, TOKENS), BF),
            pltpu.VMEM((FFZ, TOKENS), BF),
            pltpu.VMEM((D // 2, TOKENS), BF),
            pltpu.VMEM((FFZ // 2, TOKENS), BF),
        ],
    )


def ffn_grad_kernel(cols, places, n_ref, h_ref, gg_ref, ug_ref, og_ref, got_ref, *refs):
    outs, sum_ref = refs[:-1], refs[-1]

    def put(rows, tile):
        sum_ref[:, rows, :] = (tile + got_ref[:, rows, :].astype(F32)).astype(BF)

    ffn_terms(n_ref, h_ref, gg_ref, ug_ref, og_ref, cols, put)
    for i in range(NX):
        for k in range(2):
            at = (places[X] + i) % NX * 2 + (places[YH] + k) % 2
            if len(outs) == 4:
                outs[i][k] = sum_ref[at]
            else:
                outs[k][i] = sum_ref[at]


def ffn_grad_first_kernel(*refs):
    ffn_grad_kernel(slice(0, FIRST), *refs)


def ffn_grad_second_kernel(*refs):
    ffn_grad_kernel(slice(FIRST, 512), *refs[:7], *refs[8:10], refs[11])
    refs[10][...] = refs[7][...]


def ffn_grad_first(places, args, deps):
    return call(
        ffn_grad_first_kernel,
        [((2, 576, FIRST), BF)] * 4,
        [places, *args],
        COST["ffn_grad"],
        scratch=[pltpu.VMEM((8, 576, FIRST), BF)],
        deps=deps,
    )


def ffn_grad_second(places, args, down_part, deps):
    return call(
        ffn_grad_second_kernel,
        [((4, 576, 512 - FIRST), BF)] * 2 + [((TOKENS, D), BF)],
        [places, *args, down_part],
        COST["ffn_grad_second"],
        scratch=[pltpu.VMEM((8, 576, 512 - FIRST), BF)],
        deps=deps,
    )


def y_sum_kernel(places, mine, got, *outs):
    for i in range(NX):
        outs[i][...] = (mine[i].astype(F32) + got[i].astype(F32)).astype(BF)


def y_sum(places, mine, got, deps):
    return call(
        y_sum_kernel,
        [(mine.shape[1:], BF)] * 4,
        [places, mine, got],
        COST["y_sum"],
        deps=deps,
    )


def ffn_join_kernel(places, mine, got, a, b, c, d, out):
    out[:, :FIRST] = (mine[...] + got[...].astype(F32)).astype(BF)
    total = a[...].astype(F32) + b[...].astype(F32) + c[...].astype(F32) + d[...].astype(F32)
    out[:, FIRST:] = total.astype(BF)


def ffn_join(places, mine, got, terms, deps):
    return call(
        ffn_join_kernel,
        [((576, 512), BF)],
        [places, mine, got, *terms],
        COST["add"],
        deps=deps,
    )[0]


def rms_back(grad, v, gain):
    r = lax.rsqrt(jnp.mean(v * v, axis=1, keepdims=True) + EPSILON)
    pulled = grad * gain
    return r * pulled - v * (r * r * r * jnp.mean(pulled * v, axis=1, keepdims=True))


def middle_back_kernel(places, own, g1, g2, g3, middle, og, gain, w_ref, mid_ref, branch_ref, *outs):
    grad = own[...] + g1[...].astype(F32) + g2[...].astype(F32) + g3[...].astype(F32)
    mid = og[...].astype(F32) + rms_back(grad, middle[...], gain[...])
    mid_ref[...] = mid
    branch = mid.astype(BF)
    branch_ref[...] = branch
    for i in range(NZ):
        outs[i][...] = mm_t(branch, w_ref[at_rows((places[Z] + i) % NZ, QW), :]).astype(BF)


def middle_back(places, chunks, middle, og, gain, w_out, deps):
    return call(
        middle_back_kernel,
        [((ROWS, D), F32), ((ROWS, D), BF)] + [((ROWS, QW), BF)] * 4,
        [places, *chunks, middle, og, gain, w_out],
        COST["middle_back"],
        deps=deps,
    )


def input_back_kernel(places, grad, x, mid, gain, out_ref):
    out_ref[...] = mid[...] + rms_back(grad[...].astype(F32), x[...].astype(F32), gain[...])


def input_back(places, grad, x, mid, gain, deps):
    return call(
        input_back_kernel, [((ROWS, D), F32)], [places, grad, x, mid, gain], 2, deps=deps
    )[0]


def scatter(chunks):
    far = [shift_z(chunks[1], 1), shift_z(chunks[3], -1), shift_z(chunks[2], 2)]
    return [chunks[0], *far]


def x_sum_kernel(places, a, b, c, d, mine, sent):
    mine[...] = a[0].astype(F32) + b[0].astype(F32) + c[0].astype(F32) + d[0].astype(F32)
    total = a[1].astype(F32) + b[1].astype(F32) + c[1].astype(F32) + d[1].astype(F32)
    sent[...] = total.astype(BF)


def x_sum(places, terms, us, deps):
    shape = terms[0].shape[1:]
    return call(x_sum_kernel, [(shape, F32), (shape, BF)], [places, *terms], us, deps=deps)


def qkv_x_sum_kernel(places, a, b, c, d, mine, sent, out_mine, out_sent):
    for k, (ref, out_ref) in enumerate(((mine, out_mine), (sent, out_sent))):
        total = a[k].astype(F32) + b[k].astype(F32) + c[k].astype(F32) + d[k].astype(F32)
        ref[...] = total[:96].astype(ref.dtype)
        out_ref[...] = total[96:].astype(BF)


def qkv_x_sum(places, terms):
    return call(
        qkv_x_sum_kernel,
        [((96, 768), F32), ((96, 768), BF), ((48, 768), BF), ((48, 768), BF)],
        [places, *terms],
        2,
    )


def add_parts_kernel(places, qkv, qkv_got, out_a, out_b, total):
    total[:96, :] = (qkv[...] + qkv_got[...].astype(F32)).astype(BF)
    total[96:, :] = (out_a[...].astype(F32) + out_b[...].astype(F32)).astype(BF)


def add_parts(places, qkv, qkv_got, out_a, out_b, deps):
    return call(
        add_parts_kernel,
        [((144, 768), BF)],
        [places, qkv, qkv_got, out_a, out_b],
        COST["add"],
        deps=deps,
    )[0]


def swap_xz(v, mirror):
    pairs = [
        (
            (a * 4 + r) * 8 + b * 2 + l,
            (b * 4 + (r ^ 2 * mirror)) * 8 + a * 2 + (l ^ mirror),
        )
        for a in range(NX)
        for b in range(NZ)
        for r in range(4)
        for l in range(2)
    ]
    return lax.ppermute(v, ("fsdp", "sp"), pairs)


def add_kernel(places, a, b, out):
    out[...] = (a[...].astype(F32) + b[...].astype(F32)).astype(BF)


def added(places, a, b, deps):
    return call(add_kernel, [(a.shape, BF)], [places, a, b], COST["add"], deps=deps)[0]


def over_x(chunks):
    far = [shift_x(chunks[1], 1), shift_x(chunks[3], -1), shift_x(chunks[2], 2)]
    return [chunks[0], *far]


def as_row(column):
    return jnp.broadcast_to(column, (column.shape[0], 128)).T[:1]


def ffn_out_kernel(
    places, p0, p1, p2, p3, wg, wu, gain, gate_ref, up_ref, down_ref, gain_ref, all_ref, acc_ref
):
    j = pl.program_id(0)

    @pl.when(j == 0)
    def _():
        for i, p in enumerate((p0, p1, p2, p3)):
            all_ref[(places[Z] + i) % NZ] = p[...]
        acc_ref[...] = jnp.zeros_like(acc_ref)

    cols = pl.ds(pl.multiple_of(j % 2 * 256, 256), 256)
    for k, (w, out) in enumerate(((wg, gate_ref), (wu, up_ref))):
        rows = pl.ds(pl.multiple_of((2 * k + j // 2) * 96, 96), 96)
        parts = [all_ref[q, rows, cols].astype(F32) for q in range(NZ)]
        for b in range(4):
            tile = jnp.concatenate([v[:, b * 64 : (b + 1) * 64] for v in parts], axis=1)
            at = slice(b * 256, (b + 1) * 256)
            out[:, at] = tile
            acc_ref[...] += jnp.sum(tile * w[:, at].astype(F32), axis=1, keepdims=True)
    for t in range(3):
        r = 384 + 64 * t
        down_ref[:, t * 512 : (t + 1) * 512] = all_ref[j, r : r + 64, :].astype(F32)

    @pl.when(j == 3)
    def _():
        gain_ref[...] = as_row(acc_ref[...] / gain[...])


def ffn_out(places, pieces, wg, wu, gain, deps):
    whole = lambda shape: pl.BlockSpec(shape, lambda j: (0,) * len(shape))
    cols = pl.BlockSpec((96, 1024), lambda j: (0, j))
    return call(
        ffn_out_kernel,
        [((96, FF), F32), ((96, FF), F32), ((256, D), F32), ((1, 96), F32)],
        [places, *pieces, wg, wu, gain],
        4,
        scratch=[pltpu.VMEM((NZ, 576, 512), BF), pltpu.VMEM((96, 1), F32)],
        deps=deps,
        grid=(4,),
        in_specs=[SMEM] + [whole((576, 512))] * 4 + [cols, cols, whole((96, 1))],
        out_specs=[cols, cols, pl.BlockSpec((64, D), lambda j: (j, 0)), whole((1, 96))],
    )


def qkv_out_kernel(
    places, p0, p1, p2, p3, wq, wk, wv, own_gain, q_ref, k_ref, v_ref, gain_ref, all_ref
):
    for i, p in enumerate((p0, p1, p2, p3)):
        all_ref[(places[Z] + i) % NZ] = p[:96, :]
    for q in range(NZ):
        q_ref[:, q * QW : (q + 1) * QW] = all_ref[q, :, :QW].astype(F32)
    gain = jnp.sum(q_ref[...] * wq[...].astype(F32), axis=1, keepdims=True)
    for out, w, at in ((k_ref, wk, QW), (v_ref, wv, QW + KW)):
        tile = jnp.concatenate(
            [all_ref[q, :, at : at + KW].astype(F32) for q in range(NZ)], axis=1
        )
        out[...] = tile
        gain += jnp.sum(tile * w[...].astype(F32), axis=1, keepdims=True)
    gain_ref[...] = as_row(gain / own_gain[...])


def qkv_out(places, pieces, wq, wk, wv, gain, deps):
    return call(
        qkv_out_kernel,
        [((96, 1536), F32), ((96, 768), F32), ((96, 768), F32), ((1, 96), F32)],
        [places, *pieces, wq, wk, wv, gain],
        2,
        scratch=[pltpu.VMEM((NZ, 96, 768), BF)],
        deps=deps,
    )


def out_out_kernel(places, p0, p1, p2, p3, out_ref):
    for i, p in enumerate((p0, p1, p2, p3)):
        tile = p[96:, :].astype(F32)
        rows = pl.ds(pl.multiple_of((places[Z] + i) % NZ * 24, 8), 24)
        out_ref[rows, :] = jnp.concatenate([tile[:24], tile[24:]], axis=1)


def out_out(places, pieces):
    return call(out_out_kernel, [((96, D), F32)], [places, *pieces], 1)[0]


def block_out_kernel(places, middle, down, out_ref):
    out_ref[...] = (middle[...] + down[...].astype(F32)).astype(BF)


def block_out_of(places, middle, down, deps):
    return call(block_out_kernel, [((ROWS, D), BF)], [places, middle, down], 1, deps=deps)[0]


def body(
    inputs, norm_attn, w_query, w_key, w_value, w_out, norm_ffn, w_gate, w_up, w_down, cotangent
):
    f, s = lax.axis_index("fsdp"), lax.axis_index("sp")
    x, yh, c, z, yl = f // 4, f // 2 % 2, f % 2, s // 2, s % 2
    places = jnp.stack([x, yh, c, z, yl]).astype(jnp.int32)
    x_own, og_own = inputs[0], cotangent[0]
    gain_attn, gain_ffn = norm_attn[None], norm_ffn[None]

    index = jnp.arange(TOKENS, dtype=jnp.int32)
    positions = (index // ROWS * 2 + yl) * ROWS + index % ROWS
    lane = np.arange(QW) % HEAD_DIM
    frequency = ROPE_BASE ** (-(jnp.arange(HALF, dtype=F32) * 2.0 / HEAD_DIM))
    frequency = jnp.concatenate([frequency] * (QW // HALF))
    angles = positions.astype(F32)[:, None] * frequency[None, :]
    sign = np.where(lane < HALF, -1.0, 1.0).astype(np.float32)
    cosine, sine = jnp.cos(angles), jnp.sin(angles) * sign[None, :]

    qkv_shard, row_shard = cut(
        places, w_query, w_key, w_value, w_gate, w_up, w_down, w_out
    )
    qkv_mirror, row_mirror = mirror_y(qkv_shard), mirror_y(row_shard)
    xs = two_stage_z(x_own)
    (qkv_pair,) = paired(places, qkv_shard, qkv_mirror, [96], [cosine, sine, gain_attn])
    qkv_mine = two_stage_x(qkv_pair)
    qkv_other = [swap_core(p) for p in qkv_mine]
    (rows_pair,) = paired(
        places, row_shard, row_mirror, [864], [qkv_mine[1], qkv_mine[2], xs[1], xs[2]]
    )
    above, below = shift_x(rows_pair, -1), shift_x(rows_pair, 1)

    normed, x_all, og_copy, turned_mine, turned_sent = norm(places, gain_attn, og_own, xs)
    ogs = two_stage_z(og_copy)
    q, kv, held_qkv = qkv(places, normed, qkv_mine, qkv_other, cosine, sine)
    kv_other = swap_low(kv)
    mixed, shares = attend(places, q, kv, kv_other, [ogs[1], ogs[2]])
    half_up, half_down = halves(places, above, below, [mixed])
    far = [shift_x(half_up, 1), shift_x(half_down, -1)]
    mixed_all = gather_z(mixed).reshape(NZ, TOKENS, QW)
    pieces = [rows_pair, above, below, *far]
    pieces += [swap_core(p) for p in pieces]
    normed_ffn, middle_own, held_out = middle_of(places, x_all, gain_ffn, mixed_all, pieces)
    outs = ffn(places, normed_ffn, ogs, pieces)
    hidden, gate_grad, up_grad, og_all = outs[:4]
    in_chunks = outs[4:8]

    in_got = scatter(in_chunks)
    a_sent, b_sent, n_mine, h_mine = ffn_sent_of(
        places, normed_ffn, hidden, gate_grad, up_grad, og_all
    )
    down_part, column_attn, column_ffn = down_of(
        places, hidden, gain_attn, gain_ffn, pieces, [n_mine]
    )
    back = middle_back(
        places, in_got, middle_own, og_own, gain_ffn, held_out, [n_mine, down_part]
    )
    middle_grad, branch = back[:2]
    head_grads = [back[2], shift_z(back[5], -1), shift_z(back[4], 2), shift_z(back[3], 1)]
    branch_all = gather_z(branch)
    a_got, b_got = swap_core(a_sent), swap_core(b_sent)
    ffn_args = (n_mine, h_mine, gate_grad, up_grad, og_all)
    a_chunks = ffn_grad_first(places, (*ffn_args, a_got), [branch])
    a_terms = over_x(a_chunks)

    dq, dkv_own, dkv_sent = attend_back(
        places, head_grads, q, kv, kv_other, shares, [a_chunks[0]]
    )
    b_mine, b_sent, down_part = ffn_grad_second(places, (*ffn_args, b_got), down_part, [dq])
    down_own = scatter_z(down_part)
    b_got = mirror_y(b_sent)
    dkv_got = swap_low(dkv_sent)
    lin, out_part, qkv_sent = turn(
        places, dq, dkv_own, dkv_got, cosine, sine, turned_sent, mixed, branch_all, [b_sent]
    )
    qkv_got = swap_core(qkv_sent)
    first_part = first(places, lin, held_qkv, [])
    first_got = scatter_z(first_part)
    a_half, a_sent = x_sum(places, a_terms, COST["x_sum"], [first_part])
    a_got = mirror_y(a_sent)
    qkv_chunks = qkv_grad(places, lin, turned_mine, out_part, qkv_got, [a_sent])
    qkv_terms = over_x(qkv_chunks)
    b_terms = over_x(y_sum(places, b_mine, b_got, [qkv_chunks[0]]))

    qkv_half, qkv_sent, out_half, out_sent = qkv_x_sum(places, qkv_terms)
    qkv_got = mirror_y(qkv_sent)
    out_halves = swap_xz(out_half, 0), swap_xz(out_sent, 1)
    ffn_half = ffn_join(places, a_half, a_got, b_terms, [qkv_sent])
    ffn_low = swap_low(ffn_half)
    qkv_half = add_parts(places, qkv_half, qkv_got, *out_halves, [ffn_half])
    qkv_low = swap_low(qkv_half)
    qkv_total = added(places, qkv_half, qkv_low, [])
    qkv_pieces = pieces_z(qkv_total)
    ffn_total = added(places, ffn_half, ffn_low, [qkv_total])
    ffn_pieces = pieces_z(ffn_total)

    block_out = block_out_of(places, middle_own, down_own, [qkv_total])
    input_grad = input_back(places, first_got, x_own, middle_grad, gain_attn, [qkv_total])
    grad_out = out_out(places, qkv_pieces)
    grad_query, grad_key, grad_value, qkv_gain = qkv_out(
        places, qkv_pieces, w_query, w_key, w_value, column_attn, []
    )
    grad_gate, grad_up, grad_down, ffn_gain = ffn_out(
        places, ffn_pieces, w_gate, w_up, column_ffn, [qkv_gain]
    )
    grad_norm_attn, grad_norm_ffn = qkv_gain[0], ffn_gain[0]
    return (
        block_out[None],
        input_grad[None],
        grad_norm_attn,
        grad_query,
        grad_key,
        grad_value,
        grad_out,
        grad_norm_ffn,
        grad_gate,
        grad_up,
        grad_down,
    )


def solution(mesh):
    rows = P("fsdp", None)
    tokens = P("fsdp", "sp", None)
    return jax.shard_map(
        body,
        mesh=mesh,
        in_specs=(tokens, P(), rows, rows, rows, rows, P(), rows, rows, rows, tokens),
        out_specs=(tokens, tokens, P("fsdp"), rows, rows, rows, rows, P("fsdp"), rows, rows, rows),
        check_vma=False,
    )
```

```python
import functools

import jax
import jax.numpy as jnp
import numpy as np
from jax import lax
from jax.experimental import pallas as pl
from jax.experimental.pallas import tpu as pltpu
from jax.sharding import PartitionSpec as P

D = 1536
HEADS = 16
KV_HEADS = 8
HEAD_DIM = 96
FF = 4096

EPSILON = 1e-05
ROPE_BASE = 100000.0
MASKED = -1e30

NX, NZ = 4, 4
ROWS = 128
TOKENS = ROWS * NZ
QW, KW = 384, 192
HALF = HEAD_DIM // 2
FFZ = FF // NZ
BF = jnp.bfloat16
F32 = jnp.float32
VMEM = pl.BlockSpec(memory_space=pltpu.VMEM)
SMEM = pl.BlockSpec(memory_space=pltpu.SMEM)
ANY = pl.BlockSpec(memory_space=pl.ANY)
LIMIT = pltpu.CompilerParams(vmem_limit_bytes=56 * 1024 * 1024)
X, YH, CORE, Z, YL = range(5)
SPLIT = 384
FIRST = 384
COST = {
    "norm": 54,
    "qkv": 0.1,
    "attend": 0.1,
    "down": 0.1,
    "middle": 4,
    "ffn": 17,
    "ffn_sent": 0.1,
    "middle_back": 60,
    "ffn_grad": 60,
    "ffn_grad_second": 0.1,
    "attend_back": 60,
    "turn": 0.1,
    "first": 0.1,
    "x_sum": 60,
    "y_sum": 0.1,
    "qkv_grad": 0.1,
    "add": 8,
}


Z_GROUPS = [[z * 2 + l for z in range(NZ)] for l in range(2)]


def scatter_z(v):
    return lax.psum_scatter(
        v, "sp", scatter_dimension=0, tiled=True, axis_index_groups=Z_GROUPS
    )


def gather_z(v):
    return lax.all_gather(v, "sp", axis=0, tiled=True, axis_index_groups=Z_GROUPS)


def shift_z(v, step):
    pairs = [(z * 2 + l, (z + step) % NZ * 2 + l) for z in range(NZ) for l in range(2)]
    return lax.ppermute(v, "sp", pairs)


def swap_low(v):
    return lax.ppermute(v, "sp", [(s, s ^ 1) for s in range(8)])


def shift_x(v, step):
    pairs = [(x * 4 + r, (x + step) % NX * 4 + r) for x in range(NX) for r in range(4)]
    return lax.ppermute(v, "fsdp", pairs)


def swap_core(v):
    return lax.ppermute(v, "fsdp", [(f, f ^ 1) for f in range(16)])


def mirror_y(v):
    pairs = [(f * 8 + s, (f ^ 2) * 8 + (s ^ 1)) for f in range(16) for s in range(8)]
    return lax.ppermute(v, ("fsdp", "sp"), pairs)


def pieces_z(v):
    far = [shift_z(v, -1), shift_z(v, 1), shift_z(v, 2)]
    return [v, far[0], far[2], far[1]]


def two_stage_z(v):
    above, below = shift_z(v, -1), shift_z(v, 1)
    return [v, above, shift_z(below, 1), below]


def two_stage_x(v):
    above, below = shift_x(v, -1), shift_x(v, 1)
    return [v, above, shift_x(below, 1), below]


def pieces_x(v):
    far = [shift_x(v, -1), shift_x(v, 1), shift_x(v, 2)]
    return [v, far[0], far[2], far[1]]


def part(v, index, size, dim=0):
    return lax.dynamic_slice_in_dim(v, index * size, size, dim)


def call(kernel, outs, ins, us, scratch=(), deps=(), grid=(), in_specs=None, out_specs=None):
    def run(*refs):
        kernel(*refs[: len(ins)], *refs[len(ins) + len(deps) :])

    return pl.pallas_call(
        run,
        name=kernel.__name__.replace("_kernel", ""),
        grid=grid,
        out_shape=[jax.ShapeDtypeStruct(s, t) for s, t in outs],
        in_specs=(in_specs or [SMEM] + [VMEM] * (len(ins) - 1)) + [ANY] * len(deps),
        out_specs=out_specs or [VMEM] * len(outs),
        scratch_shapes=scratch,
        compiler_params=LIMIT,
        cost_estimate=pl.CostEstimate(
            flops=int(us * 1e9), bytes_accessed=int(us * 3e6), transcendentals=0
        ),
    )(*ins, *deps)


def mm(a, b):
    return jnp.dot(a, b, preferred_element_type=F32)


def mm_t(a, b):
    return lax.dot_general(a, b, (((1,), (1,)), ((), ())), preferred_element_type=F32)


def t_mm(a, b):
    return lax.dot_general(a, b, (((0,), (0,)), ((), ())), preferred_element_type=F32)


def at_rows(index, size):
    return pl.ds(pl.multiple_of(index * size, size), size)


def rope(v, cosine, sine):
    width = v.shape[1]
    lane = lax.broadcasted_iota(jnp.int32, v.shape, 1) % HEAD_DIM
    partner = jnp.where(
        lane < HALF, pltpu.roll(v, width - HALF, 1), pltpu.roll(v, HALF, 1)
    )
    return v * cosine + partner * sine


def rope_keys(kv, cosine, sine):
    lane = lax.broadcasted_iota(jnp.int32, kv.shape, 1)
    return jnp.where(lane < KW, rope(kv, cosine, sine), kv)


def cut_kernel(places, wq, wk, wv, wg, wu, wd, wo, qkv_ref, rows_ref):
    z = places[Z]
    for t in range(3):
        cols = slice(t * 512, (t + 1) * 512)
        rows_ref[96 * t : 96 * (t + 1), :] = wo[:, cols]
        rows_ref[672 + 64 * t : 736 + 64 * t, :] = wd[at_rows(z, 64), cols]
    qkv_ref[:, :QW] = wq[:, pl.ds(pl.multiple_of(z * QW, 128), QW)]
    for at in range(NZ):

        @pl.when(z == at)
        def _():
            cols = slice(at * KW, (at + 1) * KW)
            qkv_ref[:, QW:] = jnp.concatenate([wk[:, cols], wv[:, cols]], axis=1)
            for k, w in enumerate((wg, wu)):
                for half in range(2):
                    starts = [(8 * half + i) * 256 + at * 64 for i in range(8)]
                    rows = slice(288 + (2 * half + k) * 96, 384 + (2 * half + k) * 96)
                    rows_ref[rows, :] = jnp.concatenate([w[:, b : b + 64] for b in starts], axis=1)


def cut(places, *arrays):
    return call(cut_kernel, [((96, 768), BF), ((864, 512), BF)], [places, *arrays], 3)


def copy_kernel(places, *refs):
    n = len(refs) // 2
    for i in range(n):
        refs[n + i][...] = refs[i][...]


def copied(places, arrays, deps):
    return call(copy_kernel, [(v.shape, v.dtype) for v in arrays], [places, *arrays], 0.1, deps=deps)


def pair_kernel(places, own, mirror, *outs):
    start = 0
    for out in outs:
        rows = slice(start, start + out.shape[1])
        out[places[YH]] = own[rows, :]
        out[1 - places[YH]] = mirror[rows, :]
        start += out.shape[1]


def paired(places, own, mirror, parts, deps):
    outs = [((2, n, own.shape[1]), BF) for n in parts]
    return call(pair_kernel, outs, [places, own, mirror], 0.1, deps=deps)


def norm_kernel(places, gain, og, *refs):
    xs, (normed_ref, x_ref, og_ref, mine_ref, sent_ref, turned_ref) = refs[:4], refs[4:]
    og_ref[...] = og[...]
    for i in range(NZ):
        x_ref[at_rows((places[Z] + i) % NZ, ROWS), :] = xs[i][...]
    for i in range(NZ):
        rows = pl.ds(i * ROWS, ROWS)
        v = x_ref[rows, :].astype(F32)
        r = lax.rsqrt(jnp.mean(v * v, axis=1, keepdims=True) + EPSILON)
        normed_ref[rows, :] = (v * r * gain[...]).astype(BF)
    turned_ref[...] = normed_ref[...].T
    split_cores(places, turned_ref, mine_ref, sent_ref, 96)


def split_cores(places, turned_ref, mine_ref, sent_ref, n):
    for k in range(8):
        rows = slice(k * n, (k + 1) * n)
        mine_ref[rows, :] = turned_ref[at_rows(2 * k + places[CORE], n), :]
        sent_ref[rows, :] = turned_ref[at_rows(2 * k + 1 - places[CORE], n), :]


def norm(places, gain, og, xs):
    return call(
        norm_kernel,
        [((TOKENS, D), BF)] * 2 + [((ROWS, D), BF)] + [((D // 2, TOKENS), BF)] * 2,
        [places, gain, og, *xs],
        COST["norm"],
        scratch=[pltpu.VMEM((D, TOKENS), BF)],
    )


def qkv_kernel(places, normed_ref, *refs):
    mine, other = refs[:4], refs[4:8]
    cosine, sine, q_ref, kv_ref, w_ref = refs[8:]
    for i in range(NX):
        for h in range(2):
            base = (places[X] + i) % NX * 4 + h * 2
            w_ref[at_rows(base + places[CORE], 96), :] = mine[i][h]
            w_ref[at_rows(base + 1 - places[CORE], 96), :] = other[i][h]
    for i in range(NZ):
        rows = pl.ds(i * ROWS, ROWS)
        lin = mm(normed_ref[rows, :], w_ref[...])
        q_ref[rows, :] = rope(lin[:, :QW], cosine[rows, :], sine[rows, :]).astype(BF)
        kv_ref[rows, :] = rope_keys(lin[:, QW:], cosine[rows, :], sine[rows, :]).astype(BF)


def qkv(places, normed, mine, other, cosine, sine):
    return call(
        qkv_kernel,
        [((TOKENS, QW), BF), ((TOKENS, 2 * KW), BF), ((D, QW + 2 * KW), BF)],
        [places, normed, *mine, *other, cosine, sine],
        COST["qkv"],
    )


def head(ref, rows, index):
    return ref[rows, index * HEAD_DIM : (index + 1) * HEAD_DIM]


def two_heads(ref, j, g):
    rows = slice(j * ROWS, (j + 1) * ROWS)
    return jnp.concatenate([head(ref, rows, 2 * g), head(ref, rows, 2 * g + 1)], axis=0)


def attend_kernel(places, q_ref, own_ref, other_ref, mixed_ref, p_ref):
    late = places[YL]
    factor = HEAD_DIM ** (-0.5)
    for g in range(2):
        for j in range(NZ):
            n = (j + 1) * ROWS
            q = two_heads(q_ref, j, g)
            s_own = mm_t(q, head(own_ref, slice(0, n), g)) * factor
            s_oth = mm_t(q, head(other_ref, slice(0, n), g)) * factor
            shape = (2 * ROWS, n)
            row = lax.broadcasted_iota(jnp.int32, shape, 0) % ROWS + j * ROWS
            col = lax.broadcasted_iota(jnp.int32, shape, 1)
            s_own = jnp.where(col <= row, s_own, MASKED)
            s_oth = jnp.where(col < (j + late) * ROWS, s_oth, MASKED)
            highest = jnp.maximum(
                jnp.max(s_own, axis=1, keepdims=True), jnp.max(s_oth, axis=1, keepdims=True)
            )
            p_own, p_oth = jnp.exp(s_own - highest), jnp.exp(s_oth - highest)
            total = jnp.sum(p_own, axis=1, keepdims=True) + jnp.sum(p_oth, axis=1, keepdims=True)
            scale = 1.0 / total
            p_own, p_oth = (p_own * scale).astype(BF), (p_oth * scale).astype(BF)
            p_ref[g, j, :, :n] = p_own
            p_ref[g, j, :, n : 2 * n] = p_oth
            out = mm(p_own, head(own_ref, slice(0, n), 2 + g)) + mm(
                p_oth, head(other_ref, slice(0, n), 2 + g)
            )
            out = out.astype(BF)
            for k in range(2):
                h = 2 * g + k
                mixed_ref[j * ROWS : (j + 1) * ROWS, h * HEAD_DIM : (h + 1) * HEAD_DIM] = out[
                    k * ROWS : (k + 1) * ROWS
                ]


def attend(places, q, kv, kv_other, deps):
    return call(
        attend_kernel,
        [((TOKENS, QW), BF), ((2, NZ, 2 * ROWS, 2 * TOKENS), BF)],
        [places, q, kv, kv_other],
        COST["attend"],
        deps=deps,
    )


def attend_back_kernel(places, *refs):
    grads = refs[:4]
    q_ref, own_ref, other_ref, p_ref = refs[4:8]
    dq_ref, down_ref, doth_ref = refs[8:11]
    do_ref, acc_own, acc_oth = refs[11:]
    factor = HEAD_DIM ** (-0.5)
    for i in range(NZ):
        do_ref[at_rows((places[Z] + i) % NZ, ROWS), :] = grads[i][...]
    for g in range(2):
        acc_own[...] = jnp.zeros_like(acc_own)
        acc_oth[...] = jnp.zeros_like(acc_oth)
        for j in range(NZ):
            n = (j + 1) * ROWS
            seen = slice(0, n)
            q = two_heads(q_ref, j, g)
            do = two_heads(do_ref, j, g)
            p_own, p_oth = p_ref[g, j, :, :n], p_ref[g, j, :, n : 2 * n]
            dp_own = mm_t(do, head(own_ref, seen, 2 + g))
            dp_oth = mm_t(do, head(other_ref, seen, 2 + g))
            f_own, f_oth = p_own.astype(F32), p_oth.astype(F32)
            dot = jnp.sum(f_own * dp_own, axis=1, keepdims=True) + jnp.sum(
                f_oth * dp_oth, axis=1, keepdims=True
            )
            ds_own = (f_own * (dp_own - dot)).astype(BF)
            ds_oth = (f_oth * (dp_oth - dot)).astype(BF)
            dq = mm(ds_own, head(own_ref, seen, g)) + mm(ds_oth, head(other_ref, seen, g))
            dq = (dq * factor).astype(BF)
            for k in range(2):
                h = 2 * g + k
                dq_ref[j * ROWS : (j + 1) * ROWS, h * HEAD_DIM : (h + 1) * HEAD_DIM] = dq[
                    k * ROWS : (k + 1) * ROWS
                ]
            acc_own[0, seen, :] += t_mm(ds_own, q)
            acc_own[1, seen, :] += t_mm(p_own, do)
            acc_oth[0, seen, :] += t_mm(ds_oth, q)
            acc_oth[1, seen, :] += t_mm(p_oth, do)
        for kind, scale in ((0, factor), (1, 1.0)):
            at = kind * KW + g * HEAD_DIM
            down_ref[:, at : at + HEAD_DIM] = acc_own[kind] * scale
            doth_ref[:, at : at + HEAD_DIM] = (acc_oth[kind] * scale).astype(BF)


def attend_back(places, grads, q, kv, kv_other, shares, deps):
    acc = pltpu.VMEM((2, TOKENS, HEAD_DIM), F32)
    return call(
        attend_back_kernel,
        [((TOKENS, QW), BF), ((TOKENS, 2 * KW), F32), ((TOKENS, 2 * KW), BF)],
        [places, *grads, q, kv, kv_other, shares],
        COST["attend_back"],
        scratch=[pltpu.VMEM((TOKENS, QW), BF), acc, acc],
        deps=deps,
    )


def send_chunks(refs, acc_ref, places):
    for i in range(NZ):
        rows = at_rows((places[Z] + i) % NZ, ROWS)
        refs[i][...] = acc_ref[rows, :].astype(refs[i].dtype)


CHUNKS = [((ROWS, D), F32)] + [((ROWS, D), BF)] * 3


def put_out(out_ref, places, core, ref):
    for k in range(8):
        rows = pl.ds(pl.multiple_of((k % 2 * 2 + core) * 96 + k // 2 * 24, 8), 24)
        tile = out_ref[rows, :]
        ref[k, 96:, :] = jnp.concatenate([tile[:, :768], tile[:, 768:]], axis=0).astype(BF)


def turn_kernel(
    places, dq_ref, own_ref, got_ref, cosine, sine, turned_ref, mixed_ref, branch_ref, *refs
):
    lin_ref, out_ref, sent_ref = refs
    for i in range(NZ):
        rows = slice(i * ROWS, (i + 1) * ROWS)
        dkv = (own_ref[rows, :] + got_ref[rows, :].astype(F32)).astype(BF)
        c, s = cosine[rows, :], -sine[rows, :]
        lin_ref[rows, :QW] = rope(dq_ref[rows, :].astype(F32), c, s).astype(BF)
        lin_ref[rows, QW:] = rope_keys(dkv.astype(F32), c, s).astype(BF)
    for k in range(8):
        sent_ref[k, :96, :] = mm(turned_ref[k * 96 : (k + 1) * 96, :], lin_ref[...]).astype(BF)
    out_ref[...] = t_mm(mixed_ref[...], branch_ref[...])
    put_out(out_ref, places, 1 - places[CORE], sent_ref)


def turn(places, dq, dkv_own, dkv_got, cosine, sine, turned, mixed, branch, deps):
    return call(
        turn_kernel,
        [((TOKENS, 768), BF), ((QW, D), F32), ((8, 144, 768), BF)],
        [places, dq, dkv_own, dkv_got, cosine, sine, turned, mixed, branch],
        COST["turn"],
        deps=deps,
    )


def first_kernel(places, lin_ref, w_ref, out_ref):
    out_ref[...] = mm_t(lin_ref[...], w_ref[...]).astype(BF)


def first(places, lin, w, deps):
    return call(first_kernel, [((TOKENS, D), BF)], [places, lin, w], COST["first"], deps=deps)[0]


def qkv_grad_kernel(places, lin_ref, turned_ref, out_ref, got_ref, *refs):
    outs, sum_ref = refs[:4], refs[4]
    for k in range(8):
        sum_ref[k, :96, :] = mm(turned_ref[k * 96 : (k + 1) * 96, :], lin_ref[...]).astype(BF)
    put_out(out_ref, places, places[CORE], sum_ref)
    for i in range(NX):
        for k in range(2):
            at = (places[X] + i) % NX * 2 + (places[YH] + k) % 2
            outs[i][k] = (sum_ref[at].astype(F32) + got_ref[at].astype(F32)).astype(BF)


def qkv_grad(places, lin, turned, out, got, deps):
    return call(
        qkv_grad_kernel,
        [((2, 144, 768), BF)] * 4,
        [places, lin, turned, out, got],
        COST["qkv_grad"],
        scratch=[pltpu.VMEM((8, 144, 768), BF)],
        deps=deps,
    )


def piece_rows(pieces, i, h, start, n):
    if i == 2:
        ref, start = (pieces[3], start) if start < SPLIT else (pieces[4], start - SPLIT)
    else:
        ref = pieces[(0, 1, None, 2)[i]]
    return ref[h, start : start + n, :]


def each_shard(places, pieces):
    for i in range(NX):
        for h in range(2):
            base = (places[X] + i) % NX * 4 + h * 2
            yield base + places[CORE], pieces[:5], i, h
            yield base + 1 - places[CORE], pieces[5:], i, h


def halves_kernel(places, below, *refs):
    above, first_ref, second_ref = refs[:-2], refs[-2], refs[-1]
    first_ref[...] = below[...]
    for i, ref in enumerate(above):
        second_ref[:, i * 96 : (i + 1) * 96] = ref[...]


def halves(places, above, below, deps):
    def block(n, at):
        return pl.BlockSpec((2, n, 512), lambda j: (0, at, 0))

    count = (864 - SPLIT) // 96
    return call(
        halves_kernel,
        [((2, SPLIT, 512), BF), ((2, 864 - SPLIT, 512), BF)],
        [places, below] + [above] * count,
        0.1,
        deps=deps,
        grid=(1,),
        in_specs=[SMEM, block(SPLIT, 0)] + [block(96, SPLIT // 96 + i) for i in range(count)],
    )


def lay_output(places, all_pieces, out_ref):
    for b, pieces, i, h in each_shard(places, all_pieces):
        for t in range(3):
            out_ref[at_rows(b, 96), t * 512 : (t + 1) * 512] = piece_rows(pieces, i, h, t * 96, 96)


def lay_down(places, all_pieces, out_ref):
    for b, pieces, i, h in each_shard(places, all_pieces):
        for t in range(3):
            tile = piece_rows(pieces, i, h, 672 + 64 * t, 64)
            out_ref[at_rows(b, 64), t * 512 : (t + 1) * 512] = tile


def down_kernel(places, hidden_ref, gain_a, gain_b, *refs):
    pieces, down_ref, col_a, col_b, wd_ref, turned_ref = refs[:10], *refs[10:]
    own = pl.ds(pl.multiple_of((places[X] * 4 + places[YH] * 2 + places[CORE]) * 96, 8), 96)
    for gain, col in ((gain_a, col_a), (gain_b, col_b)):
        turned_ref[...] = jnp.broadcast_to(gain[...], (128, D)).T
        col[...] = turned_ref[own, :1]
    lay_down(places, pieces, wd_ref)
    down_ref[...] = mm(hidden_ref[...], wd_ref[...]).astype(BF)


def down_of(places, hidden, gain_a, gain_b, pieces, deps):
    return call(
        down_kernel,
        [((TOKENS, D), BF), ((96, 1), F32), ((96, 1), F32)],
        [places, hidden, gain_a, gain_b, *pieces],
        COST["down"],
        scratch=[pltpu.VMEM((FFZ, D), BF), pltpu.VMEM((D, 128), F32)],
        deps=deps,
    )


def middle_kernel(places, x_ref, gain, mixed, *refs):
    pieces, (normed_ref, own_ref, w_ref, acc_ref, mixed_ref) = refs[:10], refs[10:]
    lay_output(places, pieces, w_ref)
    for z in range(NZ):
        mixed_ref[:, z * QW : (z + 1) * QW] = mixed[z]
    for t in range(3):
        cols = slice(t * 512, (t + 1) * 512)
        acc_ref[:, cols] = x_ref[:, cols].astype(F32) + mm(mixed_ref[...], w_ref[:, cols])
    for i in range(NZ):
        rows = slice(i * ROWS, (i + 1) * ROWS)
        v = acc_ref[rows, :]
        r = lax.rsqrt(jnp.mean(v * v, axis=1, keepdims=True) + EPSILON)
        normed_ref[rows, :] = (v * r * gain[...]).astype(BF)
    own_ref[...] = acc_ref[at_rows(places[Z], ROWS), :]


def middle_of(places, x_all, gain, mixed, pieces):
    def rows(n):
        return pl.BlockSpec((2, n, 512), lambda j: (0, 0, 0))

    used = [rows(288)] * 4 + [rows(16)]
    return call(
        middle_kernel,
        [((TOKENS, D), BF), ((ROWS, D), F32), ((D, D), BF)],
        [places, x_all, gain, mixed, *pieces],
        COST["middle"],
        scratch=[pltpu.VMEM((TOKENS, D), F32), pltpu.VMEM((TOKENS, D), BF)],
        grid=(1,),
        in_specs=[SMEM, VMEM, VMEM, VMEM] + used * 2,
    )


def ffn_kernel(places, n_ref, *refs):
    ogs, pieces, refs = refs[:4], refs[4:14], refs[14:]
    hidden_ref, gg_ref, ug_ref, og_ref = refs[:4]
    in_chunks = refs[4:8]
    in_acc, wg_ref, wu_ref, wd_ref = refs[8:]
    for i, g in enumerate(ogs):
        og_ref[at_rows((places[Z] + i) % NZ, ROWS), :] = g[...]
    lay_down(places, pieces, wd_ref)
    for j in range(2):
        cols = slice(j * 512, (j + 1) * 512)
        for b, some, i, h in each_shard(places, pieces):
            wg_ref[at_rows(b, 96), :] = piece_rows(some, i, h, 288 + 192 * j, 96)
            wu_ref[at_rows(b, 96), :] = piece_rows(some, i, h, 384 + 192 * j, 96)
        wg, wu, wd = wg_ref[...], wu_ref[...], wd_ref[cols, :]
        gate = mm(n_ref[...], wg)
        up = mm(n_ref[...], wu)
        hg = mm_t(og_ref[...], wd).astype(BF).astype(F32)
        sig = 1.0 / (1.0 + jnp.exp(-gate))
        silu = gate * sig
        hidden = (silu * up).astype(BF)
        gg = (hg * up * (sig * (1.0 + gate * (1.0 - sig)))).astype(BF)
        ug = (hg * silu).astype(BF)
        hidden_ref[:, cols] = hidden
        gg_ref[:, cols] = gg
        ug_ref[:, cols] = ug
        if j == 0:
            in_acc[...] = mm_t(gg, wg) + mm_t(ug, wu)
        else:
            in_acc[...] += mm_t(gg, wg) + mm_t(ug, wu)
    send_chunks(in_chunks, in_acc, places)


def ffn(places, normed, ogs, pieces):
    return call(
        ffn_kernel,
        [((TOKENS, FFZ), BF)] * 3 + [((TOKENS, D), BF)] + CHUNKS,
        [places, normed, *ogs, *pieces],
        COST["ffn"],
        scratch=[pltpu.VMEM((TOKENS, D), F32)]
        + [pltpu.VMEM((D, 512), BF)] * 2
        + [pltpu.VMEM((FFZ, D), BF)],
    )


def ffn_terms(n_ref, h_ref, gg_ref, ug_ref, og_ref, cols, put):
    for w, ref in enumerate((gg_ref, ug_ref)):
        for half in range(2):
            tile = mm(n_ref[...], ref[:, half * 512 + cols.start : half * 512 + cols.stop])
            r = (2 * w + half) * 96
            put(slice(r, r + 96), tile.reshape(8, 96, -1))
    for t in range(3):
        tile = mm(h_ref[...], og_ref[:, t * 512 + cols.start : t * 512 + cols.stop])
        put(slice(384 + 64 * t, 448 + 64 * t), tile.reshape(8, 64, -1))


def ffn_sent_kernel(places, n_ref, hidden_ref, gg_ref, ug_ref, og_ref, *refs):
    sent_refs, (n_mine, h_mine, n_turned, h_turned, n_sent, h_sent) = refs[:2], refs[2:]
    n_turned[...] = n_ref[...].T
    h_turned[...] = hidden_ref[...].T
    split_cores(places, n_turned, n_mine, n_sent, 96)
    split_cores(places, h_turned, h_mine, h_sent, 64)

    def put(rows, tile):
        for half, ref in enumerate(sent_refs):
            ref[:, rows, :] = tile[:, :, (0, FIRST)[half] : (FIRST, 512)[half]].astype(BF)

    ffn_terms(n_sent, h_sent, gg_ref, ug_ref, og_ref, slice(0, 512), put)


def ffn_sent_of(places, normed, hidden, gg, ug, og):
    return call(
        ffn_sent_kernel,
        [
            ((8, 576, FIRST), BF),
            ((8, 576, 512 - FIRST), BF),
            ((D // 2, TOKENS), BF),
            ((FFZ // 2, TOKENS), BF),
        ],
        [places, normed, hidden, gg, ug, og],
        COST["ffn_sent"],
        scratch=[
            pltpu.VMEM((D, TOKENS), BF),
            pltpu.VMEM((FFZ, TOKENS), BF),
            pltpu.VMEM((D // 2, TOKENS), BF),
            pltpu.VMEM((FFZ // 2, TOKENS), BF),
        ],
    )


def ffn_grad_kernel(cols, places, n_ref, h_ref, gg_ref, ug_ref, og_ref, got_ref, *refs):
    outs, sum_ref = refs[:-1], refs[-1]

    def put(rows, tile):
        sum_ref[:, rows, :] = (tile + got_ref[:, rows, :].astype(F32)).astype(BF)

    ffn_terms(n_ref, h_ref, gg_ref, ug_ref, og_ref, cols, put)
    for i in range(NX):
        for k in range(2):
            at = (places[X] + i) % NX * 2 + (places[YH] + k) % 2
            if len(outs) == 4:
                outs[i][k] = sum_ref[at]
            else:
                outs[k][i] = sum_ref[at]


def ffn_grad_first_kernel(*refs):
    ffn_grad_kernel(slice(0, FIRST), *refs)


def ffn_grad_second_kernel(*refs):
    ffn_grad_kernel(slice(FIRST, 512), *refs[:7], *refs[8:10], refs[11])
    refs[10][...] = refs[7][...]


def ffn_grad_first(places, args, deps):
    return call(
        ffn_grad_first_kernel,
        [((2, 576, FIRST), BF)] * 4,
        [places, *args],
        COST["ffn_grad"],
        scratch=[pltpu.VMEM((8, 576, FIRST), BF)],
        deps=deps,
    )


def ffn_grad_second(places, args, down_part, deps):
    return call(
        ffn_grad_second_kernel,
        [((4, 576, 512 - FIRST), BF)] * 2 + [((TOKENS, D), BF)],
        [places, *args, down_part],
        COST["ffn_grad_second"],
        scratch=[pltpu.VMEM((8, 576, 512 - FIRST), BF)],
        deps=deps,
    )


def y_sum_kernel(places, mine, got, *outs):
    for i in range(NX):
        outs[i][...] = (mine[i].astype(F32) + got[i].astype(F32)).astype(BF)


def y_sum(places, mine, got, deps):
    return call(
        y_sum_kernel,
        [(mine.shape[1:], BF)] * 4,
        [places, mine, got],
        COST["y_sum"],
        deps=deps,
    )


def ffn_join_kernel(places, mine, got, a, b, c, d, out):
    out[:, :FIRST] = (mine[...] + got[...].astype(F32)).astype(BF)
    total = a[...].astype(F32) + b[...].astype(F32) + c[...].astype(F32) + d[...].astype(F32)
    out[:, FIRST:] = total.astype(BF)


def ffn_join(places, mine, got, terms, deps):
    return call(
        ffn_join_kernel,
        [((576, 512), BF)],
        [places, mine, got, *terms],
        COST["add"],
        deps=deps,
    )[0]


def rms_back(grad, v, gain):
    r = lax.rsqrt(jnp.mean(v * v, axis=1, keepdims=True) + EPSILON)
    pulled = grad * gain
    return r * pulled - v * (r * r * r * jnp.mean(pulled * v, axis=1, keepdims=True))


def middle_back_kernel(places, own, g1, g2, g3, middle, og, gain, w_ref, mid_ref, branch_ref, *outs):
    grad = own[...] + g1[...].astype(F32) + g2[...].astype(F32) + g3[...].astype(F32)
    mid = og[...].astype(F32) + rms_back(grad, middle[...], gain[...])
    mid_ref[...] = mid
    branch = mid.astype(BF)
    branch_ref[...] = branch
    for i in range(NZ):
        outs[i][...] = mm_t(branch, w_ref[at_rows((places[Z] + i) % NZ, QW), :]).astype(BF)


def middle_back(places, chunks, middle, og, gain, w_out, deps):
    return call(
        middle_back_kernel,
        [((ROWS, D), F32), ((ROWS, D), BF)] + [((ROWS, QW), BF)] * 4,
        [places, *chunks, middle, og, gain, w_out],
        COST["middle_back"],
        deps=deps,
    )


def input_back_kernel(places, grad, x, mid, gain, out_ref):
    out_ref[...] = mid[...] + rms_back(grad[...].astype(F32), x[...].astype(F32), gain[...])


def input_back(places, grad, x, mid, gain, deps):
    return call(
        input_back_kernel, [((ROWS, D), F32)], [places, grad, x, mid, gain], 2, deps=deps
    )[0]


def scatter(chunks):
    far = [shift_z(chunks[1], 1), shift_z(chunks[3], -1), shift_z(chunks[2], 2)]
    return [chunks[0], *far]


def x_sum_kernel(places, a, b, c, d, mine, sent):
    mine[...] = a[0].astype(F32) + b[0].astype(F32) + c[0].astype(F32) + d[0].astype(F32)
    total = a[1].astype(F32) + b[1].astype(F32) + c[1].astype(F32) + d[1].astype(F32)
    sent[...] = total.astype(BF)


def x_sum(places, terms, us, deps):
    shape = terms[0].shape[1:]
    return call(x_sum_kernel, [(shape, F32), (shape, BF)], [places, *terms], us, deps=deps)


def qkv_x_sum_kernel(places, a, b, c, d, mine, sent, out_mine, out_sent):
    for k, (ref, out_ref) in enumerate(((mine, out_mine), (sent, out_sent))):
        total = a[k].astype(F32) + b[k].astype(F32) + c[k].astype(F32) + d[k].astype(F32)
        ref[...] = total[:96].astype(ref.dtype)
        out_ref[...] = total[96:].astype(BF)


def qkv_x_sum(places, terms):
    return call(
        qkv_x_sum_kernel,
        [((96, 768), F32), ((96, 768), BF), ((48, 768), BF), ((48, 768), BF)],
        [places, *terms],
        2,
    )


def add_parts_kernel(places, qkv, qkv_got, out_a, out_b, total):
    total[:96, :] = (qkv[...] + qkv_got[...].astype(F32)).astype(BF)
    total[96:, :] = (out_a[...].astype(F32) + out_b[...].astype(F32)).astype(BF)


def add_parts(places, qkv, qkv_got, out_a, out_b, deps):
    return call(
        add_parts_kernel,
        [((144, 768), BF)],
        [places, qkv, qkv_got, out_a, out_b],
        COST["add"],
        deps=deps,
    )[0]


def swap_xz(v, mirror):
    pairs = [
        (
            (a * 4 + r) * 8 + b * 2 + l,
            (b * 4 + (r ^ 2 * mirror)) * 8 + a * 2 + (l ^ mirror),
        )
        for a in range(NX)
        for b in range(NZ)
        for r in range(4)
        for l in range(2)
    ]
    return lax.ppermute(v, ("fsdp", "sp"), pairs)


def add_kernel(places, a, b, out):
    out[...] = (a[...].astype(F32) + b[...].astype(F32)).astype(BF)


def added(places, a, b, deps):
    return call(add_kernel, [(a.shape, BF)], [places, a, b], COST["add"], deps=deps)[0]


def over_x(chunks):
    far = [shift_x(chunks[1], 1), shift_x(chunks[3], -1), shift_x(chunks[2], 2)]
    return [chunks[0], *far]


def as_row(column):
    return jnp.broadcast_to(column, (column.shape[0], 128)).T[:1]


def ffn_out_kernel(
    places, p0, p1, p2, p3, wg, wu, gain, gate_ref, up_ref, down_ref, gain_ref, all_ref, acc_ref
):
    j = pl.program_id(0)

    @pl.when(j == 0)
    def _():
        for i, p in enumerate((p0, p1, p2, p3)):
            all_ref[(places[Z] + i) % NZ] = p[...]
        acc_ref[...] = jnp.zeros_like(acc_ref)

    cols = pl.ds(pl.multiple_of(j % 2 * 256, 256), 256)
    for k, (w, out) in enumerate(((wg, gate_ref), (wu, up_ref))):
        rows = pl.ds(pl.multiple_of((2 * k + j // 2) * 96, 96), 96)
        parts = [all_ref[q, rows, cols].astype(F32) for q in range(NZ)]
        for b in range(4):
            tile = jnp.concatenate([v[:, b * 64 : (b + 1) * 64] for v in parts], axis=1)
            at = slice(b * 256, (b + 1) * 256)
            out[:, at] = tile
            acc_ref[...] += jnp.sum(tile * w[:, at].astype(F32), axis=1, keepdims=True)
    for t in range(3):
        r = 384 + 64 * t
        down_ref[:, t * 512 : (t + 1) * 512] = all_ref[j, r : r + 64, :].astype(F32)

    @pl.when(j == 3)
    def _():
        gain_ref[...] = as_row(acc_ref[...] / gain[...])


def ffn_out(places, pieces, wg, wu, gain, deps):
    whole = lambda shape: pl.BlockSpec(shape, lambda j: (0,) * len(shape))
    cols = pl.BlockSpec((96, 1024), lambda j: (0, j))
    return call(
        ffn_out_kernel,
        [((96, FF), F32), ((96, FF), F32), ((256, D), F32), ((1, 96), F32)],
        [places, *pieces, wg, wu, gain],
        4,
        scratch=[pltpu.VMEM((NZ, 576, 512), BF), pltpu.VMEM((96, 1), F32)],
        deps=deps,
        grid=(4,),
        in_specs=[SMEM] + [whole((576, 512))] * 4 + [cols, cols, whole((96, 1))],
        out_specs=[cols, cols, pl.BlockSpec((64, D), lambda j: (j, 0)), whole((1, 96))],
    )


def qkv_out_kernel(
    places, p0, p1, p2, p3, wq, wk, wv, own_gain, q_ref, k_ref, v_ref, gain_ref, all_ref
):
    for i, p in enumerate((p0, p1, p2, p3)):
        all_ref[(places[Z] + i) % NZ] = p[:96, :]
    for q in range(NZ):
        q_ref[:, q * QW : (q + 1) * QW] = all_ref[q, :, :QW].astype(F32)
    gain = jnp.sum(q_ref[...] * wq[...].astype(F32), axis=1, keepdims=True)
    for out, w, at in ((k_ref, wk, QW), (v_ref, wv, QW + KW)):
        tile = jnp.concatenate(
            [all_ref[q, :, at : at + KW].astype(F32) for q in range(NZ)], axis=1
        )
        out[...] = tile
        gain += jnp.sum(tile * w[...].astype(F32), axis=1, keepdims=True)
    gain_ref[...] = as_row(gain / own_gain[...])


def qkv_out(places, pieces, wq, wk, wv, gain, deps):
    return call(
        qkv_out_kernel,
        [((96, 1536), F32), ((96, 768), F32), ((96, 768), F32), ((1, 96), F32)],
        [places, *pieces, wq, wk, wv, gain],
        2,
        scratch=[pltpu.VMEM((NZ, 96, 768), BF)],
        deps=deps,
    )


def out_out_kernel(places, p0, p1, p2, p3, out_ref):
    for i, p in enumerate((p0, p1, p2, p3)):
        tile = p[96:, :].astype(F32)
        rows = pl.ds(pl.multiple_of((places[Z] + i) % NZ * 24, 8), 24)
        out_ref[rows, :] = jnp.concatenate([tile[:24], tile[24:]], axis=1)


def out_out(places, pieces):
    return call(out_out_kernel, [((96, D), F32)], [places, *pieces], 1)[0]


def block_out_kernel(places, middle, down, out_ref):
    out_ref[...] = (middle[...] + down[...].astype(F32)).astype(BF)


def block_out_of(places, middle, down, deps):
    return call(block_out_kernel, [((ROWS, D), BF)], [places, middle, down], 1, deps=deps)[0]


def body(
    inputs, norm_attn, w_query, w_key, w_value, w_out, norm_ffn, w_gate, w_up, w_down, cotangent
):
    f, s = lax.axis_index("fsdp"), lax.axis_index("sp")
    x, yh, c, z, yl = f // 4, f // 2 % 2, f % 2, s // 2, s % 2
    places = jnp.stack([x, yh, c, z, yl]).astype(jnp.int32)
    x_own, og_own = inputs[0], cotangent[0]
    gain_attn, gain_ffn = norm_attn[None], norm_ffn[None]

    index = jnp.arange(TOKENS, dtype=jnp.int32)
    positions = (index // ROWS * 2 + yl) * ROWS + index % ROWS
    lane = np.arange(QW) % HEAD_DIM
    frequency = ROPE_BASE ** (-(jnp.arange(HALF, dtype=F32) * 2.0 / HEAD_DIM))
    frequency = jnp.concatenate([frequency] * (QW // HALF))
    angles = positions.astype(F32)[:, None] * frequency[None, :]
    sign = np.where(lane < HALF, -1.0, 1.0).astype(np.float32)
    cosine, sine = jnp.cos(angles), jnp.sin(angles) * sign[None, :]

    qkv_shard, row_shard = cut(
        places, w_query, w_key, w_value, w_gate, w_up, w_down, w_out
    )
    qkv_mirror, row_mirror = mirror_y(qkv_shard), mirror_y(row_shard)
    xs = two_stage_z(x_own)
    (qkv_pair,) = paired(places, qkv_shard, qkv_mirror, [96], [cosine, sine, gain_attn])
    qkv_mine = two_stage_x(qkv_pair)
    qkv_other = [swap_core(p) for p in qkv_mine]
    (rows_pair,) = paired(
        places, row_shard, row_mirror, [864], [qkv_mine[1], qkv_mine[2], xs[1], xs[2]]
    )
    above, below = shift_x(rows_pair, -1), shift_x(rows_pair, 1)

    normed, x_all, og_copy, turned_mine, turned_sent = norm(places, gain_attn, og_own, xs)
    ogs = two_stage_z(og_copy)
    q, kv, held_qkv = qkv(places, normed, qkv_mine, qkv_other, cosine, sine)
    kv_other = swap_low(kv)
    mixed, shares = attend(places, q, kv, kv_other, [ogs[1], ogs[2]])
    half_up, half_down = halves(places, above, below, [mixed])
    far = [shift_x(half_up, 1), shift_x(half_down, -1)]
    mixed_all = gather_z(mixed).reshape(NZ, TOKENS, QW)
    pieces = [rows_pair, above, below, *far]
    pieces += [swap_core(p) for p in pieces]
    normed_ffn, middle_own, held_out = middle_of(places, x_all, gain_ffn, mixed_all, pieces)
    outs = ffn(places, normed_ffn, ogs, pieces)
    hidden, gate_grad, up_grad, og_all = outs[:4]
    in_chunks = outs[4:8]

    in_got = scatter(in_chunks)
    a_sent, b_sent, n_mine, h_mine = ffn_sent_of(
        places, normed_ffn, hidden, gate_grad, up_grad, og_all
    )
    down_part, column_attn, column_ffn = down_of(
        places, hidden, gain_attn, gain_ffn, pieces, [n_mine]
    )
    back = middle_back(
        places, in_got, middle_own, og_own, gain_ffn, held_out, [n_mine, down_part]
    )
    middle_grad, branch = back[:2]
    head_grads = [back[2], shift_z(back[5], -1), shift_z(back[4], 2), shift_z(back[3], 1)]
    branch_all = gather_z(branch)
    a_got, b_got = swap_core(a_sent), swap_core(b_sent)
    ffn_args = (n_mine, h_mine, gate_grad, up_grad, og_all)
    a_chunks = ffn_grad_first(places, (*ffn_args, a_got), [branch])
    a_terms = over_x(a_chunks)

    dq, dkv_own, dkv_sent = attend_back(
        places, head_grads, q, kv, kv_other, shares, [a_chunks[0]]
    )
    b_mine, b_sent, down_part = ffn_grad_second(places, (*ffn_args, b_got), down_part, [dq])
    down_own = scatter_z(down_part)
    b_got = mirror_y(b_sent)
    dkv_got = swap_low(dkv_sent)
    lin, out_part, qkv_sent = turn(
        places, dq, dkv_own, dkv_got, cosine, sine, turned_sent, mixed, branch_all, [b_sent]
    )
    qkv_got = swap_core(qkv_sent)
    first_part = first(places, lin, held_qkv, [])
    first_got = scatter_z(first_part)
    a_half, a_sent = x_sum(places, a_terms, COST["x_sum"], [first_part])
    a_got = mirror_y(a_sent)
    qkv_chunks = qkv_grad(places, lin, turned_mine, out_part, qkv_got, [a_sent])
    qkv_terms = over_x(qkv_chunks)
    b_terms = over_x(y_sum(places, b_mine, b_got, [qkv_chunks[0]]))

    qkv_half, qkv_sent, out_half, out_sent = qkv_x_sum(places, qkv_terms)
    qkv_got = mirror_y(qkv_sent)
    out_halves = swap_xz(out_half, 0), swap_xz(out_sent, 1)
    ffn_half = ffn_join(places, a_half, a_got, b_terms, [qkv_got])
    ffn_low = swap_low(ffn_half)
    qkv_half = add_parts(places, qkv_half, qkv_got, *out_halves, [ffn_half])
    qkv_low = swap_low(qkv_half)
    qkv_total = added(places, qkv_half, qkv_low, [])
    qkv_pieces = pieces_z(qkv_total)
    ffn_total = added(places, ffn_half, ffn_low, [qkv_total])
    ffn_pieces = pieces_z(ffn_total)

    block_out = block_out_of(places, middle_own, down_own, [qkv_total])
    input_grad = input_back(places, first_got, x_own, middle_grad, gain_attn, [qkv_total])
    grad_out = out_out(places, qkv_pieces)
    grad_query, grad_key, grad_value, qkv_gain = qkv_out(
        places, qkv_pieces, w_query, w_key, w_value, column_attn, []
    )
    grad_gate, grad_up, grad_down, ffn_gain = ffn_out(
        places, ffn_pieces, w_gate, w_up, column_ffn, [qkv_gain]
    )
    grad_norm_attn, grad_norm_ffn = qkv_gain[0], ffn_gain[0]
    return (
        block_out[None],
        input_grad[None],
        grad_norm_attn,
        grad_query,
        grad_key,
        grad_value,
        grad_out,
        grad_norm_ffn,
        grad_gate,
        grad_up,
        grad_down,
    )


def solution(mesh):
    rows = P("fsdp", None)
    tokens = P("fsdp", "sp", None)
    return jax.shard_map(
        body,
        mesh=mesh,
        in_specs=(tokens, P(), rows, rows, rows, rows, P(), rows, rows, rows, tokens),
        out_specs=(tokens, tokens, P("fsdp"), rows, rows, rows, rows, P("fsdp"), rows, rows, rows),
        check_vma=False,
    )
```

```python
import functools

import jax
import jax.numpy as jnp
import numpy as np
from jax import lax
from jax.experimental import pallas as pl
from jax.experimental.pallas import tpu as pltpu
from jax.sharding import PartitionSpec as P

D = 1536
HEADS = 16
KV_HEADS = 8
HEAD_DIM = 96
FF = 4096

EPSILON = 1e-05
ROPE_BASE = 100000.0
MASKED = -1e30

NX, NZ = 4, 4
ROWS = 128
TOKENS = ROWS * NZ
QW, KW = 384, 192
HALF = HEAD_DIM // 2
FFZ = FF // NZ
BF = jnp.bfloat16
F32 = jnp.float32
VMEM = pl.BlockSpec(memory_space=pltpu.VMEM)
SMEM = pl.BlockSpec(memory_space=pltpu.SMEM)
ANY = pl.BlockSpec(memory_space=pl.ANY)
LIMIT = pltpu.CompilerParams(vmem_limit_bytes=56 * 1024 * 1024)
X, YH, CORE, Z, YL = range(5)
SPLIT = 384
FIRST = 384
COST = {
    "norm": 54,
    "qkv": 0.1,
    "attend": 0.1,
    "down": 0.1,
    "middle": 4,
    "ffn": 17,
    "ffn_sent": 0.1,
    "middle_back": 60,
    "ffn_grad": 60,
    "ffn_grad_second": 0.1,
    "attend_back": 60,
    "turn": 0.1,
    "first": 0.1,
    "x_sum": 60,
    "y_sum": 0.1,
    "qkv_grad": 0.1,
    "add": 8,
}


Z_GROUPS = [[z * 2 + l for z in range(NZ)] for l in range(2)]


def scatter_z(v):
    return lax.psum_scatter(
        v, "sp", scatter_dimension=0, tiled=True, axis_index_groups=Z_GROUPS
    )


def gather_z(v):
    return lax.all_gather(v, "sp", axis=0, tiled=True, axis_index_groups=Z_GROUPS)


def shift_z(v, step):
    pairs = [(z * 2 + l, (z + step) % NZ * 2 + l) for z in range(NZ) for l in range(2)]
    return lax.ppermute(v, "sp", pairs)


def swap_low(v):
    return lax.ppermute(v, "sp", [(s, s ^ 1) for s in range(8)])


def shift_x(v, step):
    pairs = [(x * 4 + r, (x + step) % NX * 4 + r) for x in range(NX) for r in range(4)]
    return lax.ppermute(v, "fsdp", pairs)


def swap_core(v):
    return lax.ppermute(v, "fsdp", [(f, f ^ 1) for f in range(16)])


def mirror_y(v):
    pairs = [(f * 8 + s, (f ^ 2) * 8 + (s ^ 1)) for f in range(16) for s in range(8)]
    return lax.ppermute(v, ("fsdp", "sp"), pairs)


def pieces_z(v):
    far = [shift_z(v, -1), shift_z(v, 1), shift_z(v, 2)]
    return [v, far[0], far[2], far[1]]


def two_stage_z(v):
    above, below = shift_z(v, -1), shift_z(v, 1)
    return [v, above, shift_z(below, 1), below]


def two_stage_x(v):
    above, below = shift_x(v, -1), shift_x(v, 1)
    return [v, above, shift_x(below, 1), below]


def pieces_x(v):
    far = [shift_x(v, -1), shift_x(v, 1), shift_x(v, 2)]
    return [v, far[0], far[2], far[1]]


def part(v, index, size, dim=0):
    return lax.dynamic_slice_in_dim(v, index * size, size, dim)


def call(kernel, outs, ins, us, scratch=(), deps=(), grid=(), in_specs=None, out_specs=None):
    def run(*refs):
        kernel(*refs[: len(ins)], *refs[len(ins) + len(deps) :])

    return pl.pallas_call(
        run,
        name=kernel.__name__.replace("_kernel", ""),
        grid=grid,
        out_shape=[jax.ShapeDtypeStruct(s, t) for s, t in outs],
        in_specs=(in_specs or [SMEM] + [VMEM] * (len(ins) - 1)) + [ANY] * len(deps),
        out_specs=out_specs or [VMEM] * len(outs),
        scratch_shapes=scratch,
        compiler_params=LIMIT,
        cost_estimate=pl.CostEstimate(
            flops=int(us * 1e9), bytes_accessed=int(us * 3e6), transcendentals=0
        ),
    )(*ins, *deps)


def mm(a, b):
    return jnp.dot(a, b, preferred_element_type=F32)


def mm_t(a, b):
    return lax.dot_general(a, b, (((1,), (1,)), ((), ())), preferred_element_type=F32)


def t_mm(a, b):
    return lax.dot_general(a, b, (((0,), (0,)), ((), ())), preferred_element_type=F32)


def at_rows(index, size):
    return pl.ds(pl.multiple_of(index * size, size), size)


def rope(v, cosine, sine):
    width = v.shape[1]
    lane = lax.broadcasted_iota(jnp.int32, v.shape, 1) % HEAD_DIM
    partner = jnp.where(
        lane < HALF, pltpu.roll(v, width - HALF, 1), pltpu.roll(v, HALF, 1)
    )
    return v * cosine + partner * sine


def rope_keys(kv, cosine, sine):
    lane = lax.broadcasted_iota(jnp.int32, kv.shape, 1)
    return jnp.where(lane < KW, rope(kv, cosine, sine), kv)


def cut_kernel(places, wq, wk, wv, wg, wu, wd, wo, qkv_ref, rows_ref):
    z = places[Z]
    for t in range(3):
        cols = slice(t * 512, (t + 1) * 512)
        rows_ref[96 * t : 96 * (t + 1), :] = wo[:, cols]
        rows_ref[672 + 64 * t : 736 + 64 * t, :] = wd[at_rows(z, 64), cols]
    qkv_ref[:, :QW] = wq[:, pl.ds(pl.multiple_of(z * QW, 128), QW)]
    for at in range(NZ):

        @pl.when(z == at)
        def _():
            cols = slice(at * KW, (at + 1) * KW)
            qkv_ref[:, QW:] = jnp.concatenate([wk[:, cols], wv[:, cols]], axis=1)
            for k, w in enumerate((wg, wu)):
                for half in range(2):
                    starts = [(8 * half + i) * 256 + at * 64 for i in range(8)]
                    rows = slice(288 + (2 * half + k) * 96, 384 + (2 * half + k) * 96)
                    rows_ref[rows, :] = jnp.concatenate([w[:, b : b + 64] for b in starts], axis=1)


def cut(places, *arrays):
    return call(cut_kernel, [((96, 768), BF), ((864, 512), BF)], [places, *arrays], 3)


def copy_kernel(places, *refs):
    n = len(refs) // 2
    for i in range(n):
        refs[n + i][...] = refs[i][...]


def copied(places, arrays, deps):
    return call(copy_kernel, [(v.shape, v.dtype) for v in arrays], [places, *arrays], 0.1, deps=deps)


def pair_kernel(places, own, mirror, *outs):
    start = 0
    for out in outs:
        rows = slice(start, start + out.shape[1])
        out[places[YH]] = own[rows, :]
        out[1 - places[YH]] = mirror[rows, :]
        start += out.shape[1]


def paired(places, own, mirror, parts, deps):
    outs = [((2, n, own.shape[1]), BF) for n in parts]
    return call(pair_kernel, outs, [places, own, mirror], 0.1, deps=deps)


def norm_kernel(places, gain, og, *refs):
    xs, (normed_ref, x_ref, og_ref, mine_ref, sent_ref, turned_ref) = refs[:4], refs[4:]
    og_ref[...] = og[...]
    for i in range(NZ):
        x_ref[at_rows((places[Z] + i) % NZ, ROWS), :] = xs[i][...]
    for i in range(NZ):
        rows = pl.ds(i * ROWS, ROWS)
        v = x_ref[rows, :].astype(F32)
        r = lax.rsqrt(jnp.mean(v * v, axis=1, keepdims=True) + EPSILON)
        normed_ref[rows, :] = (v * r * gain[...]).astype(BF)
    turned_ref[...] = normed_ref[...].T
    split_cores(places, turned_ref, mine_ref, sent_ref, 96)


def split_cores(places, turned_ref, mine_ref, sent_ref, n):
    for k in range(8):
        rows = slice(k * n, (k + 1) * n)
        mine_ref[rows, :] = turned_ref[at_rows(2 * k + places[CORE], n), :]
        sent_ref[rows, :] = turned_ref[at_rows(2 * k + 1 - places[CORE], n), :]


def norm(places, gain, og, xs):
    return call(
        norm_kernel,
        [((TOKENS, D), BF)] * 2 + [((ROWS, D), BF)] + [((D // 2, TOKENS), BF)] * 2,
        [places, gain, og, *xs],
        COST["norm"],
        scratch=[pltpu.VMEM((D, TOKENS), BF)],
    )


def qkv_kernel(places, normed_ref, *refs):
    mine, other = refs[:4], refs[4:8]
    cosine, sine, q_ref, kv_ref, w_ref = refs[8:]
    for i in range(NX):
        for h in range(2):
            base = (places[X] + i) % NX * 4 + h * 2
            w_ref[at_rows(base + places[CORE], 96), :] = mine[i][h]
            w_ref[at_rows(base + 1 - places[CORE], 96), :] = other[i][h]
    for i in range(NZ):
        rows = pl.ds(i * ROWS, ROWS)
        lin = mm(normed_ref[rows, :], w_ref[...])
        q_ref[rows, :] = rope(lin[:, :QW], cosine[rows, :], sine[rows, :]).astype(BF)
        kv_ref[rows, :] = rope_keys(lin[:, QW:], cosine[rows, :], sine[rows, :]).astype(BF)


def qkv(places, normed, mine, other, cosine, sine):
    return call(
        qkv_kernel,
        [((TOKENS, QW), BF), ((TOKENS, 2 * KW), BF), ((D, QW + 2 * KW), BF)],
        [places, normed, *mine, *other, cosine, sine],
        COST["qkv"],
    )


def head(ref, rows, index):
    return ref[rows, index * HEAD_DIM : (index + 1) * HEAD_DIM]


def two_heads(ref, j, g):
    rows = slice(j * ROWS, (j + 1) * ROWS)
    return jnp.concatenate([head(ref, rows, 2 * g), head(ref, rows, 2 * g + 1)], axis=0)


def attend_kernel(places, q_ref, own_ref, other_ref, mixed_ref, p_ref):
    late = places[YL]
    factor = HEAD_DIM ** (-0.5)
    for g in range(2):
        for j in range(NZ):
            n = (j + 1) * ROWS
            q = two_heads(q_ref, j, g)
            s_own = mm_t(q, head(own_ref, slice(0, n), g)) * factor
            s_oth = mm_t(q, head(other_ref, slice(0, n), g)) * factor
            shape = (2 * ROWS, n)
            row = lax.broadcasted_iota(jnp.int32, shape, 0) % ROWS + j * ROWS
            col = lax.broadcasted_iota(jnp.int32, shape, 1)
            s_own = jnp.where(col <= row, s_own, MASKED)
            s_oth = jnp.where(col < (j + late) * ROWS, s_oth, MASKED)
            highest = jnp.maximum(
                jnp.max(s_own, axis=1, keepdims=True), jnp.max(s_oth, axis=1, keepdims=True)
            )
            p_own, p_oth = jnp.exp(s_own - highest), jnp.exp(s_oth - highest)
            total = jnp.sum(p_own, axis=1, keepdims=True) + jnp.sum(p_oth, axis=1, keepdims=True)
            scale = 1.0 / total
            p_own, p_oth = (p_own * scale).astype(BF), (p_oth * scale).astype(BF)
            p_ref[g, j, :, :n] = p_own
            p_ref[g, j, :, n : 2 * n] = p_oth
            out = mm(p_own, head(own_ref, slice(0, n), 2 + g)) + mm(
                p_oth, head(other_ref, slice(0, n), 2 + g)
            )
            out = out.astype(BF)
            for k in range(2):
                h = 2 * g + k
                mixed_ref[j * ROWS : (j + 1) * ROWS, h * HEAD_DIM : (h + 1) * HEAD_DIM] = out[
                    k * ROWS : (k + 1) * ROWS
                ]


def attend(places, q, kv, kv_other, deps):
    return call(
        attend_kernel,
        [((TOKENS, QW), BF), ((2, NZ, 2 * ROWS, 2 * TOKENS), BF)],
        [places, q, kv, kv_other],
        COST["attend"],
        deps=deps,
    )


def attend_back_kernel(places, *refs):
    grads = refs[:4]
    q_ref, own_ref, other_ref, p_ref = refs[4:8]
    dq_ref, down_ref, doth_ref = refs[8:11]
    do_ref, acc_own, acc_oth = refs[11:]
    factor = HEAD_DIM ** (-0.5)
    for i in range(NZ):
        do_ref[at_rows((places[Z] + i) % NZ, ROWS), :] = grads[i][...]
    for g in range(2):
        acc_own[...] = jnp.zeros_like(acc_own)
        acc_oth[...] = jnp.zeros_like(acc_oth)
        for j in range(NZ):
            n = (j + 1) * ROWS
            seen = slice(0, n)
            q = two_heads(q_ref, j, g)
            do = two_heads(do_ref, j, g)
            p_own, p_oth = p_ref[g, j, :, :n], p_ref[g, j, :, n : 2 * n]
            dp_own = mm_t(do, head(own_ref, seen, 2 + g))
            dp_oth = mm_t(do, head(other_ref, seen, 2 + g))
            f_own, f_oth = p_own.astype(F32), p_oth.astype(F32)
            dot = jnp.sum(f_own * dp_own, axis=1, keepdims=True) + jnp.sum(
                f_oth * dp_oth, axis=1, keepdims=True
            )
            ds_own = (f_own * (dp_own - dot)).astype(BF)
            ds_oth = (f_oth * (dp_oth - dot)).astype(BF)
            dq = mm(ds_own, head(own_ref, seen, g)) + mm(ds_oth, head(other_ref, seen, g))
            dq = (dq * factor).astype(BF)
            for k in range(2):
                h = 2 * g + k
                dq_ref[j * ROWS : (j + 1) * ROWS, h * HEAD_DIM : (h + 1) * HEAD_DIM] = dq[
                    k * ROWS : (k + 1) * ROWS
                ]
            acc_own[0, seen, :] += t_mm(ds_own, q)
            acc_own[1, seen, :] += t_mm(p_own, do)
            acc_oth[0, seen, :] += t_mm(ds_oth, q)
            acc_oth[1, seen, :] += t_mm(p_oth, do)
        for kind, scale in ((0, factor), (1, 1.0)):
            at = kind * KW + g * HEAD_DIM
            down_ref[:, at : at + HEAD_DIM] = acc_own[kind] * scale
            doth_ref[:, at : at + HEAD_DIM] = (acc_oth[kind] * scale).astype(BF)


def attend_back(places, grads, q, kv, kv_other, shares, deps):
    acc = pltpu.VMEM((2, TOKENS, HEAD_DIM), F32)
    return call(
        attend_back_kernel,
        [((TOKENS, QW), BF), ((TOKENS, 2 * KW), F32), ((TOKENS, 2 * KW), BF)],
        [places, *grads, q, kv, kv_other, shares],
        COST["attend_back"],
        scratch=[pltpu.VMEM((TOKENS, QW), BF), acc, acc],
        deps=deps,
    )


def send_chunks(refs, acc_ref, places):
    for i in range(NZ):
        rows = at_rows((places[Z] + i) % NZ, ROWS)
        refs[i][...] = acc_ref[rows, :].astype(refs[i].dtype)


CHUNKS = [((ROWS, D), F32)] + [((ROWS, D), BF)] * 3


def put_out(out_ref, places, core, ref):
    for k in range(8):
        rows = pl.ds(pl.multiple_of((k % 2 * 2 + core) * 96 + k // 2 * 24, 8), 24)
        tile = out_ref[rows, :]
        ref[k, 96:, :] = jnp.concatenate([tile[:, :768], tile[:, 768:]], axis=0).astype(BF)


def turn_kernel(
    places, dq_ref, own_ref, got_ref, cosine, sine, turned_ref, mixed_ref, branch_ref, *refs
):
    lin_ref, out_ref, sent_ref = refs
    for i in range(NZ):
        rows = slice(i * ROWS, (i + 1) * ROWS)
        dkv = (own_ref[rows, :] + got_ref[rows, :].astype(F32)).astype(BF)
        c, s = cosine[rows, :], -sine[rows, :]
        lin_ref[rows, :QW] = rope(dq_ref[rows, :].astype(F32), c, s).astype(BF)
        lin_ref[rows, QW:] = rope_keys(dkv.astype(F32), c, s).astype(BF)
    for k in range(8):
        sent_ref[k, :96, :] = mm(turned_ref[k * 96 : (k + 1) * 96, :], lin_ref[...]).astype(BF)
    out_ref[...] = t_mm(mixed_ref[...], branch_ref[...])
    put_out(out_ref, places, 1 - places[CORE], sent_ref)


def turn(places, dq, dkv_own, dkv_got, cosine, sine, turned, mixed, branch, deps):
    return call(
        turn_kernel,
        [((TOKENS, 768), BF), ((QW, D), F32), ((8, 144, 768), BF)],
        [places, dq, dkv_own, dkv_got, cosine, sine, turned, mixed, branch],
        COST["turn"],
        deps=deps,
    )


def first_kernel(places, lin_ref, w_ref, out_ref):
    out_ref[...] = mm_t(lin_ref[...], w_ref[...]).astype(BF)


def first(places, lin, w, deps):
    return call(first_kernel, [((TOKENS, D), BF)], [places, lin, w], COST["first"], deps=deps)[0]


def qkv_grad_kernel(places, lin_ref, turned_ref, out_ref, got_ref, *refs):
    outs, sum_ref = refs[:4], refs[4]
    for k in range(8):
        sum_ref[k, :96, :] = mm(turned_ref[k * 96 : (k + 1) * 96, :], lin_ref[...]).astype(BF)
    put_out(out_ref, places, places[CORE], sum_ref)
    for i in range(NX):
        for k in range(2):
            at = (places[X] + i) % NX * 2 + (places[YH] + k) % 2
            outs[i][k] = (sum_ref[at].astype(F32) + got_ref[at].astype(F32)).astype(BF)


def qkv_grad(places, lin, turned, out, got, deps):
    return call(
        qkv_grad_kernel,
        [((2, 144, 768), BF)] * 4,
        [places, lin, turned, out, got],
        COST["qkv_grad"],
        scratch=[pltpu.VMEM((8, 144, 768), BF)],
        deps=deps,
    )


def piece_rows(pieces, i, h, start, n):
    if i == 2:
        ref, start = (pieces[3], start) if start < SPLIT else (pieces[4], start - SPLIT)
    else:
        ref = pieces[(0, 1, None, 2)[i]]
    return ref[h, start : start + n, :]


def each_shard(places, pieces):
    for i in range(NX):
        for h in range(2):
            base = (places[X] + i) % NX * 4 + h * 2
            yield base + places[CORE], pieces[:5], i, h
            yield base + 1 - places[CORE], pieces[5:], i, h


def halves_kernel(places, below, *refs):
    above, first_ref, second_ref = refs[:-2], refs[-2], refs[-1]
    first_ref[...] = below[...]
    for i, ref in enumerate(above):
        second_ref[:, i * 96 : (i + 1) * 96] = ref[...]


def halves(places, above, below, deps):
    def block(n, at):
        return pl.BlockSpec((2, n, 512), lambda j: (0, at, 0))

    count = (864 - SPLIT) // 96
    return call(
        halves_kernel,
        [((2, SPLIT, 512), BF), ((2, 864 - SPLIT, 512), BF)],
        [places, below] + [above] * count,
        0.1,
        deps=deps,
        grid=(1,),
        in_specs=[SMEM, block(SPLIT, 0)] + [block(96, SPLIT // 96 + i) for i in range(count)],
    )


def lay_output(places, all_pieces, out_ref):
    for b, pieces, i, h in each_shard(places, all_pieces):
        for t in range(3):
            out_ref[at_rows(b, 96), t * 512 : (t + 1) * 512] = piece_rows(pieces, i, h, t * 96, 96)


def lay_down(places, all_pieces, out_ref):
    for b, pieces, i, h in each_shard(places, all_pieces):
        for t in range(3):
            tile = piece_rows(pieces, i, h, 672 + 64 * t, 64)
            out_ref[at_rows(b, 64), t * 512 : (t + 1) * 512] = tile


def down_kernel(places, hidden_ref, gain_a, gain_b, *refs):
    pieces, down_ref, col_a, col_b, wd_ref, turned_ref = refs[:10], *refs[10:]
    own = pl.ds(pl.multiple_of((places[X] * 4 + places[YH] * 2 + places[CORE]) * 96, 8), 96)
    for gain, col in ((gain_a, col_a), (gain_b, col_b)):
        turned_ref[...] = jnp.broadcast_to(gain[...], (128, D)).T
        col[...] = turned_ref[own, :1]
    lay_down(places, pieces, wd_ref)
    down_ref[...] = mm(hidden_ref[...], wd_ref[...]).astype(BF)


def down_of(places, hidden, gain_a, gain_b, pieces, deps):
    return call(
        down_kernel,
        [((TOKENS, D), BF), ((96, 1), F32), ((96, 1), F32)],
        [places, hidden, gain_a, gain_b, *pieces],
        COST["down"],
        scratch=[pltpu.VMEM((FFZ, D), BF), pltpu.VMEM((D, 128), F32)],
        deps=deps,
    )


def middle_kernel(places, x_ref, gain, mixed, *refs):
    pieces, (normed_ref, own_ref, w_ref, acc_ref, mixed_ref) = refs[:10], refs[10:]
    lay_output(places, pieces, w_ref)
    for z in range(NZ):
        mixed_ref[:, z * QW : (z + 1) * QW] = mixed[z]
    for t in range(3):
        cols = slice(t * 512, (t + 1) * 512)
        acc_ref[:, cols] = x_ref[:, cols].astype(F32) + mm(mixed_ref[...], w_ref[:, cols])
    for i in range(NZ):
        rows = slice(i * ROWS, (i + 1) * ROWS)
        v = acc_ref[rows, :]
        r = lax.rsqrt(jnp.mean(v * v, axis=1, keepdims=True) + EPSILON)
        normed_ref[rows, :] = (v * r * gain[...]).astype(BF)
    own_ref[...] = acc_ref[at_rows(places[Z], ROWS), :]


def middle_of(places, x_all, gain, mixed, pieces):
    def rows(n):
        return pl.BlockSpec((2, n, 512), lambda j: (0, 0, 0))

    used = [rows(288)] * 4 + [rows(16)]
    return call(
        middle_kernel,
        [((TOKENS, D), BF), ((ROWS, D), F32), ((D, D), BF)],
        [places, x_all, gain, mixed, *pieces],
        COST["middle"],
        scratch=[pltpu.VMEM((TOKENS, D), F32), pltpu.VMEM((TOKENS, D), BF)],
        grid=(1,),
        in_specs=[SMEM, VMEM, VMEM, VMEM] + used * 2,
    )


def ffn_kernel(places, n_ref, *refs):
    ogs, pieces, refs = refs[:4], refs[4:14], refs[14:]
    hidden_ref, gg_ref, ug_ref, og_ref = refs[:4]
    in_chunks = refs[4:8]
    in_acc, wg_ref, wu_ref, wd_ref = refs[8:]
    for i, g in enumerate(ogs):
        og_ref[at_rows((places[Z] + i) % NZ, ROWS), :] = g[...]
    lay_down(places, pieces, wd_ref)
    for j in range(2):
        cols = slice(j * 512, (j + 1) * 512)
        for b, some, i, h in each_shard(places, pieces):
            wg_ref[at_rows(b, 96), :] = piece_rows(some, i, h, 288 + 192 * j, 96)
            wu_ref[at_rows(b, 96), :] = piece_rows(some, i, h, 384 + 192 * j, 96)
        wg, wu, wd = wg_ref[...], wu_ref[...], wd_ref[cols, :]
        gate = mm(n_ref[...], wg)
        up = mm(n_ref[...], wu)
        hg = mm_t(og_ref[...], wd).astype(BF).astype(F32)
        sig = 1.0 / (1.0 + jnp.exp(-gate))
        silu = gate * sig
        hidden = (silu * up).astype(BF)
        gg = (hg * up * (sig * (1.0 + gate * (1.0 - sig)))).astype(BF)
        ug = (hg * silu).astype(BF)
        hidden_ref[:, cols] = hidden
        gg_ref[:, cols] = gg
        ug_ref[:, cols] = ug
        if j == 0:
            in_acc[...] = mm_t(gg, wg) + mm_t(ug, wu)
        else:
            in_acc[...] += mm_t(gg, wg) + mm_t(ug, wu)
    send_chunks(in_chunks, in_acc, places)


def ffn(places, normed, ogs, pieces):
    return call(
        ffn_kernel,
        [((TOKENS, FFZ), BF)] * 3 + [((TOKENS, D), BF)] + CHUNKS,
        [places, normed, *ogs, *pieces],
        COST["ffn"],
        scratch=[pltpu.VMEM((TOKENS, D), F32)]
        + [pltpu.VMEM((D, 512), BF)] * 2
        + [pltpu.VMEM((FFZ, D), BF)],
    )


def ffn_terms(n_ref, h_ref, gg_ref, ug_ref, og_ref, cols, put):
    for w, ref in enumerate((gg_ref, ug_ref)):
        for half in range(2):
            tile = mm(n_ref[...], ref[:, half * 512 + cols.start : half * 512 + cols.stop])
            r = (2 * w + half) * 96
            put(slice(r, r + 96), tile.reshape(8, 96, -1))
    for t in range(3):
        tile = mm(h_ref[...], og_ref[:, t * 512 + cols.start : t * 512 + cols.stop])
        put(slice(384 + 64 * t, 448 + 64 * t), tile.reshape(8, 64, -1))


def ffn_sent_kernel(places, n_ref, hidden_ref, gg_ref, ug_ref, og_ref, *refs):
    sent_refs, (n_mine, h_mine, n_turned, h_turned, n_sent, h_sent) = refs[:2], refs[2:]
    n_turned[...] = n_ref[...].T
    h_turned[...] = hidden_ref[...].T
    split_cores(places, n_turned, n_mine, n_sent, 96)
    split_cores(places, h_turned, h_mine, h_sent, 64)

    def put(rows, tile):
        for half, ref in enumerate(sent_refs):
            ref[:, rows, :] = tile[:, :, (0, FIRST)[half] : (FIRST, 512)[half]].astype(BF)

    ffn_terms(n_sent, h_sent, gg_ref, ug_ref, og_ref, slice(0, 512), put)


def ffn_sent_of(places, normed, hidden, gg, ug, og):
    return call(
        ffn_sent_kernel,
        [
            ((8, 576, FIRST), BF),
            ((8, 576, 512 - FIRST), BF),
            ((D // 2, TOKENS), BF),
            ((FFZ // 2, TOKENS), BF),
        ],
        [places, normed, hidden, gg, ug, og],
        COST["ffn_sent"],
        scratch=[
            pltpu.VMEM((D, TOKENS), BF),
            pltpu.VMEM((FFZ, TOKENS), BF),
            pltpu.VMEM((D // 2, TOKENS), BF),
            pltpu.VMEM((FFZ // 2, TOKENS), BF),
        ],
    )


def ffn_grad_kernel(cols, places, n_ref, h_ref, gg_ref, ug_ref, og_ref, got_ref, *refs):
    outs, sum_ref = refs[:-1], refs[-1]

    def put(rows, tile):
        sum_ref[:, rows, :] = (tile + got_ref[:, rows, :].astype(F32)).astype(BF)

    ffn_terms(n_ref, h_ref, gg_ref, ug_ref, og_ref, cols, put)
    for i in range(NX):
        for k in range(2):
            at = (places[X] + i) % NX * 2 + (places[YH] + k) % 2
            if len(outs) == 4:
                outs[i][k] = sum_ref[at]
            else:
                outs[k][i] = sum_ref[at]


def ffn_grad_first_kernel(*refs):
    ffn_grad_kernel(slice(0, FIRST), *refs)


def ffn_grad_second_kernel(*refs):
    ffn_grad_kernel(slice(FIRST, 512), *refs[:7], *refs[8:10], refs[11])
    refs[10][...] = refs[7][...]


def ffn_grad_first(places, args, deps):
    return call(
        ffn_grad_first_kernel,
        [((2, 576, FIRST), BF)] * 4,
        [places, *args],
        COST["ffn_grad"],
        scratch=[pltpu.VMEM((8, 576, FIRST), BF)],
        deps=deps,
    )


def ffn_grad_second(places, args, down_part, deps):
    return call(
        ffn_grad_second_kernel,
        [((4, 576, 512 - FIRST), BF)] * 2 + [((TOKENS, D), BF)],
        [places, *args, down_part],
        COST["ffn_grad_second"],
        scratch=[pltpu.VMEM((8, 576, 512 - FIRST), BF)],
        deps=deps,
    )


def y_sum_kernel(places, mine, got, *outs):
    for i in range(NX):
        outs[i][...] = (mine[i].astype(F32) + got[i].astype(F32)).astype(BF)


def y_sum(places, mine, got, deps):
    return call(
        y_sum_kernel,
        [(mine.shape[1:], BF)] * 4,
        [places, mine, got],
        COST["y_sum"],
        deps=deps,
    )


def ffn_join_kernel(places, mine, got, a, b, c, d, out):
    out[:, :FIRST] = (mine[...] + got[...].astype(F32)).astype(BF)
    total = a[...].astype(F32) + b[...].astype(F32) + c[...].astype(F32) + d[...].astype(F32)
    out[:, FIRST:] = total.astype(BF)


def ffn_join(places, mine, got, terms, deps):
    return call(
        ffn_join_kernel,
        [((576, 512), BF)],
        [places, mine, got, *terms],
        COST["add"],
        deps=deps,
    )[0]


def rms_back(grad, v, gain):
    r = lax.rsqrt(jnp.mean(v * v, axis=1, keepdims=True) + EPSILON)
    pulled = grad * gain
    return r * pulled - v * (r * r * r * jnp.mean(pulled * v, axis=1, keepdims=True))


def middle_back_kernel(places, own, g1, g2, g3, middle, og, gain, w_ref, mid_ref, branch_ref, *outs):
    grad = own[...] + g1[...].astype(F32) + g2[...].astype(F32) + g3[...].astype(F32)
    mid = og[...].astype(F32) + rms_back(grad, middle[...], gain[...])
    mid_ref[...] = mid
    branch = mid.astype(BF)
    branch_ref[...] = branch
    for i in range(NZ):
        outs[i][...] = mm_t(branch, w_ref[at_rows((places[Z] + i) % NZ, QW), :]).astype(BF)


def middle_back(places, chunks, middle, og, gain, w_out, deps):
    return call(
        middle_back_kernel,
        [((ROWS, D), F32), ((ROWS, D), BF)] + [((ROWS, QW), BF)] * 4,
        [places, *chunks, middle, og, gain, w_out],
        COST["middle_back"],
        deps=deps,
    )


def input_back_kernel(places, grad, x, mid, gain, out_ref):
    out_ref[...] = mid[...] + rms_back(grad[...].astype(F32), x[...].astype(F32), gain[...])


def input_back(places, grad, x, mid, gain, deps):
    return call(
        input_back_kernel, [((ROWS, D), F32)], [places, grad, x, mid, gain], 2, deps=deps
    )[0]


def scatter(chunks):
    far = [shift_z(chunks[1], 1), shift_z(chunks[3], -1), shift_z(chunks[2], 2)]
    return [chunks[0], *far]


def x_sum_kernel(places, a, b, c, d, mine, sent):
    mine[...] = a[0].astype(F32) + b[0].astype(F32) + c[0].astype(F32) + d[0].astype(F32)
    total = a[1].astype(F32) + b[1].astype(F32) + c[1].astype(F32) + d[1].astype(F32)
    sent[...] = total.astype(BF)


def x_sum(places, terms, us, deps):
    shape = terms[0].shape[1:]
    return call(x_sum_kernel, [(shape, F32), (shape, BF)], [places, *terms], us, deps=deps)


def qkv_x_sum_kernel(places, a, b, c, d, mine, sent, out_mine, out_sent):
    for k, (ref, out_ref) in enumerate(((mine, out_mine), (sent, out_sent))):
        total = a[k].astype(F32) + b[k].astype(F32) + c[k].astype(F32) + d[k].astype(F32)
        ref[...] = total[:96].astype(ref.dtype)
        out_ref[...] = total[96:].astype(BF)


def qkv_x_sum(places, terms):
    return call(
        qkv_x_sum_kernel,
        [((96, 768), F32), ((96, 768), BF), ((48, 768), BF), ((48, 768), BF)],
        [places, *terms],
        2,
    )


def add_parts_kernel(places, qkv, qkv_got, out_a, out_b, total):
    total[:96, :] = (qkv[...] + qkv_got[...].astype(F32)).astype(BF)
    total[96:, :] = (out_a[...].astype(F32) + out_b[...].astype(F32)).astype(BF)


def add_parts(places, qkv, qkv_got, out_a, out_b, deps):
    return call(
        add_parts_kernel,
        [((144, 768), BF)],
        [places, qkv, qkv_got, out_a, out_b],
        COST["add"],
        deps=deps,
    )[0]


def swap_xz(v, mirror):
    pairs = [
        (
            (a * 4 + r) * 8 + b * 2 + l,
            (b * 4 + (r ^ 2 * mirror)) * 8 + a * 2 + (l ^ mirror),
        )
        for a in range(NX)
        for b in range(NZ)
        for r in range(4)
        for l in range(2)
    ]
    return lax.ppermute(v, ("fsdp", "sp"), pairs)


def add_kernel(places, a, b, out):
    out[...] = (a[...].astype(F32) + b[...].astype(F32)).astype(BF)


def added(places, a, b, deps):
    return call(add_kernel, [(a.shape, BF)], [places, a, b], COST["add"], deps=deps)[0]


def over_x(chunks):
    far = [shift_x(chunks[1], 1), shift_x(chunks[3], -1), shift_x(chunks[2], 2)]
    return [chunks[0], *far]


def as_row(column):
    return jnp.broadcast_to(column, (column.shape[0], 128)).T[:1]


def ffn_out_kernel(
    places, p0, p1, p2, p3, wg, wu, gain, gate_ref, up_ref, down_ref, gain_ref, all_ref, acc_ref
):
    j = pl.program_id(0)

    @pl.when(j == 0)
    def _():
        for i, p in enumerate((p0, p1, p2, p3)):
            all_ref[(places[Z] + i) % NZ] = p[...]
        acc_ref[...] = jnp.zeros_like(acc_ref)

    cols = pl.ds(pl.multiple_of(j % 2 * 256, 256), 256)
    for k, (w, out) in enumerate(((wg, gate_ref), (wu, up_ref))):
        rows = pl.ds(pl.multiple_of((2 * k + j // 2) * 96, 96), 96)
        parts = [all_ref[q, rows, cols].astype(F32) for q in range(NZ)]
        for b in range(4):
            tile = jnp.concatenate([v[:, b * 64 : (b + 1) * 64] for v in parts], axis=1)
            at = slice(b * 256, (b + 1) * 256)
            out[:, at] = tile
            terms = tile * w[:, at].astype(F32)
            acc_ref[...] += terms[:, :128] + terms[:, 128:]
    for t in range(3):
        r = 384 + 64 * t
        down_ref[:, t * 512 : (t + 1) * 512] = all_ref[j, r : r + 64, :].astype(F32)

    @pl.when(j == 3)
    def _():
        total = jnp.sum(acc_ref[...], axis=1, keepdims=True)
        gain_ref[...] = as_row(total / gain[...])


def ffn_out(places, pieces, wg, wu, gain, deps):
    whole = lambda shape: pl.BlockSpec(shape, lambda j: (0,) * len(shape))
    cols = pl.BlockSpec((96, 1024), lambda j: (0, j))
    return call(
        ffn_out_kernel,
        [((96, FF), F32), ((96, FF), F32), ((256, D), F32), ((1, 96), F32)],
        [places, *pieces, wg, wu, gain],
        4,
        scratch=[pltpu.VMEM((NZ, 576, 512), BF), pltpu.VMEM((96, 128), F32)],
        deps=deps,
        grid=(4,),
        in_specs=[SMEM] + [whole((576, 512))] * 4 + [cols, cols, whole((96, 1))],
        out_specs=[cols, cols, pl.BlockSpec((64, D), lambda j: (j, 0)), whole((1, 96))],
    )


def qkv_out_kernel(
    places, p0, p1, p2, p3, wq, wk, wv, own_gain, q_ref, k_ref, v_ref, gain_ref, all_ref
):
    for i, p in enumerate((p0, p1, p2, p3)):
        all_ref[(places[Z] + i) % NZ] = p[:96, :]
    for q in range(NZ):
        q_ref[:, q * QW : (q + 1) * QW] = all_ref[q, :, :QW].astype(F32)
    gain = jnp.sum(q_ref[...] * wq[...].astype(F32), axis=1, keepdims=True)
    for out, w, at in ((k_ref, wk, QW), (v_ref, wv, QW + KW)):
        tile = jnp.concatenate(
            [all_ref[q, :, at : at + KW].astype(F32) for q in range(NZ)], axis=1
        )
        out[...] = tile
        gain += jnp.sum(tile * w[...].astype(F32), axis=1, keepdims=True)
    gain_ref[...] = as_row(gain / own_gain[...])


def qkv_out(places, pieces, wq, wk, wv, gain, deps):
    return call(
        qkv_out_kernel,
        [((96, 1536), F32), ((96, 768), F32), ((96, 768), F32), ((1, 96), F32)],
        [places, *pieces, wq, wk, wv, gain],
        2,
        scratch=[pltpu.VMEM((NZ, 96, 768), BF)],
        deps=deps,
    )


def out_out_kernel(places, p0, p1, p2, p3, out_ref):
    for i, p in enumerate((p0, p1, p2, p3)):
        tile = p[96:, :].astype(F32)
        rows = pl.ds(pl.multiple_of((places[Z] + i) % NZ * 24, 8), 24)
        out_ref[rows, :] = jnp.concatenate([tile[:24], tile[24:]], axis=1)


def out_out(places, pieces):
    return call(out_out_kernel, [((96, D), F32)], [places, *pieces], 1)[0]


def block_out_kernel(places, middle, down, out_ref):
    out_ref[...] = (middle[...] + down[...].astype(F32)).astype(BF)


def block_out_of(places, middle, down, deps):
    return call(block_out_kernel, [((ROWS, D), BF)], [places, middle, down], 1, deps=deps)[0]


def body(
    inputs, norm_attn, w_query, w_key, w_value, w_out, norm_ffn, w_gate, w_up, w_down, cotangent
):
    f, s = lax.axis_index("fsdp"), lax.axis_index("sp")
    x, yh, c, z, yl = f // 4, f // 2 % 2, f % 2, s // 2, s % 2
    places = jnp.stack([x, yh, c, z, yl]).astype(jnp.int32)
    x_own, og_own = inputs[0], cotangent[0]
    gain_attn, gain_ffn = norm_attn[None], norm_ffn[None]

    index = jnp.arange(TOKENS, dtype=jnp.int32)
    positions = (index // ROWS * 2 + yl) * ROWS + index % ROWS
    lane = np.arange(QW) % HEAD_DIM
    frequency = ROPE_BASE ** (-(jnp.arange(HALF, dtype=F32) * 2.0 / HEAD_DIM))
    frequency = jnp.concatenate([frequency] * (QW // HALF))
    angles = positions.astype(F32)[:, None] * frequency[None, :]
    sign = np.where(lane < HALF, -1.0, 1.0).astype(np.float32)
    cosine, sine = jnp.cos(angles), jnp.sin(angles) * sign[None, :]

    qkv_shard, row_shard = cut(
        places, w_query, w_key, w_value, w_gate, w_up, w_down, w_out
    )
    qkv_mirror, row_mirror = mirror_y(qkv_shard), mirror_y(row_shard)
    xs = two_stage_z(x_own)
    (qkv_pair,) = paired(places, qkv_shard, qkv_mirror, [96], [cosine, sine, gain_attn])
    qkv_mine = two_stage_x(qkv_pair)
    qkv_other = [swap_core(p) for p in qkv_mine]
    (rows_pair,) = paired(
        places, row_shard, row_mirror, [864], [qkv_mine[1], qkv_mine[2], xs[1], xs[2]]
    )
    above, below = shift_x(rows_pair, -1), shift_x(rows_pair, 1)

    normed, x_all, og_copy, turned_mine, turned_sent = norm(places, gain_attn, og_own, xs)
    ogs = two_stage_z(og_copy)
    q, kv, held_qkv = qkv(places, normed, qkv_mine, qkv_other, cosine, sine)
    kv_other = swap_low(kv)
    mixed, shares = attend(places, q, kv, kv_other, [ogs[1], ogs[2]])
    half_up, half_down = halves(places, above, below, [mixed])
    far = [shift_x(half_up, 1), shift_x(half_down, -1)]
    mixed_all = gather_z(mixed).reshape(NZ, TOKENS, QW)
    pieces = [rows_pair, above, below, *far]
    pieces += [swap_core(p) for p in pieces]
    normed_ffn, middle_own, held_out = middle_of(places, x_all, gain_ffn, mixed_all, pieces)
    outs = ffn(places, normed_ffn, ogs, pieces)
    hidden, gate_grad, up_grad, og_all = outs[:4]
    in_chunks = outs[4:8]

    in_got = scatter(in_chunks)
    a_sent, b_sent, n_mine, h_mine = ffn_sent_of(
        places, normed_ffn, hidden, gate_grad, up_grad, og_all
    )
    down_part, column_attn, column_ffn = down_of(
        places, hidden, gain_attn, gain_ffn, pieces, [n_mine]
    )
    back = middle_back(
        places, in_got, middle_own, og_own, gain_ffn, held_out, [n_mine, down_part]
    )
    middle_grad, branch = back[:2]
    head_grads = [back[2], shift_z(back[5], -1), shift_z(back[4], 2), shift_z(back[3], 1)]
    branch_all = gather_z(branch)
    a_got, b_got = swap_core(a_sent), swap_core(b_sent)
    ffn_args = (n_mine, h_mine, gate_grad, up_grad, og_all)
    a_chunks = ffn_grad_first(places, (*ffn_args, a_got), [branch])
    a_terms = over_x(a_chunks)

    dq, dkv_own, dkv_sent = attend_back(
        places, head_grads, q, kv, kv_other, shares, [a_chunks[0]]
    )
    b_mine, b_sent, down_part = ffn_grad_second(places, (*ffn_args, b_got), down_part, [dq])
    down_own = scatter_z(down_part)
    b_got = mirror_y(b_sent)
    dkv_got = swap_low(dkv_sent)
    lin, out_part, qkv_sent = turn(
        places, dq, dkv_own, dkv_got, cosine, sine, turned_sent, mixed, branch_all, [b_sent]
    )
    qkv_got = swap_core(qkv_sent)
    first_part = first(places, lin, held_qkv, [])
    first_got = scatter_z(first_part)
    a_half, a_sent = x_sum(places, a_terms, COST["x_sum"], [first_part])
    a_got = mirror_y(a_sent)
    qkv_chunks = qkv_grad(places, lin, turned_mine, out_part, qkv_got, [a_sent])
    qkv_terms = over_x(qkv_chunks)
    b_terms = over_x(y_sum(places, b_mine, b_got, [qkv_chunks[0]]))

    qkv_half, qkv_sent, out_half, out_sent = qkv_x_sum(places, qkv_terms)
    qkv_got = mirror_y(qkv_sent)
    out_halves = swap_xz(out_half, 0), swap_xz(out_sent, 1)
    ffn_half = ffn_join(places, a_half, a_got, b_terms, [qkv_sent])
    ffn_low = swap_low(ffn_half)
    qkv_half = add_parts(places, qkv_half, qkv_got, *out_halves, [ffn_half])
    qkv_low = swap_low(qkv_half)
    input_grad = input_back(places, first_got, x_own, middle_grad, gain_attn, [qkv_half])
    qkv_total = added(places, qkv_half, qkv_low, [input_grad])
    qkv_pieces = pieces_z(qkv_total)
    ffn_total = added(places, ffn_half, ffn_low, [qkv_total])
    ffn_pieces = pieces_z(ffn_total)

    block_out = block_out_of(places, middle_own, down_own, [qkv_total])
    grad_out = out_out(places, qkv_pieces)
    grad_query, grad_key, grad_value, qkv_gain = qkv_out(
        places, qkv_pieces, w_query, w_key, w_value, column_attn, []
    )
    grad_gate, grad_up, grad_down, ffn_gain = ffn_out(
        places, ffn_pieces, w_gate, w_up, column_ffn, [qkv_gain]
    )
    grad_norm_attn, grad_norm_ffn = qkv_gain[0], ffn_gain[0]
    return (
        block_out[None],
        input_grad[None],
        grad_norm_attn,
        grad_query,
        grad_key,
        grad_value,
        grad_out,
        grad_norm_ffn,
        grad_gate,
        grad_up,
        grad_down,
    )


def solution(mesh):
    rows = P("fsdp", None)
    tokens = P("fsdp", "sp", None)
    return jax.shard_map(
        body,
        mesh=mesh,
        in_specs=(tokens, P(), rows, rows, rows, rows, P(), rows, rows, rows, tokens),
        out_specs=(tokens, tokens, P("fsdp"), rows, rows, rows, rows, P("fsdp"), rows, rows, rows),
        check_vma=False,
    )
```

```python
import functools

import jax
import jax.numpy as jnp
import numpy as np
from jax import lax
from jax.experimental import pallas as pl
from jax.experimental.pallas import tpu as pltpu
from jax.sharding import PartitionSpec as P

D = 1536
HEADS = 16
KV_HEADS = 8
HEAD_DIM = 96
FF = 4096

EPSILON = 1e-05
ROPE_BASE = 100000.0
MASKED = -1e30

NX, NZ = 4, 4
ROWS = 128
TOKENS = ROWS * NZ
QW, KW = 384, 192
HALF = HEAD_DIM // 2
FFZ = FF // NZ
BF = jnp.bfloat16
F32 = jnp.float32
VMEM = pl.BlockSpec(memory_space=pltpu.VMEM)
SMEM = pl.BlockSpec(memory_space=pltpu.SMEM)
ANY = pl.BlockSpec(memory_space=pl.ANY)
LIMIT = pltpu.CompilerParams(vmem_limit_bytes=56 * 1024 * 1024)
X, YH, CORE, Z, YL = range(5)
SPLIT = 384
FIRST = 384
COST = {
    "norm": 54,
    "qkv": 0.1,
    "attend": 0.1,
    "down": 0.1,
    "middle": 4,
    "ffn": 17,
    "ffn_sent": 0.1,
    "middle_back": 60,
    "ffn_grad": 60,
    "ffn_grad_second": 0.1,
    "attend_back": 60,
    "turn": 0.1,
    "first": 0.1,
    "x_sum": 60,
    "y_sum": 0.1,
    "qkv_grad": 0.1,
    "add": 8,
}


Z_GROUPS = [[z * 2 + l for z in range(NZ)] for l in range(2)]


def scatter_z(v):
    return lax.psum_scatter(
        v, "sp", scatter_dimension=0, tiled=True, axis_index_groups=Z_GROUPS
    )


def gather_z(v):
    return lax.all_gather(v, "sp", axis=0, tiled=True, axis_index_groups=Z_GROUPS)


def shift_z(v, step):
    pairs = [(z * 2 + l, (z + step) % NZ * 2 + l) for z in range(NZ) for l in range(2)]
    return lax.ppermute(v, "sp", pairs)


def swap_low(v):
    return lax.ppermute(v, "sp", [(s, s ^ 1) for s in range(8)])


def shift_x(v, step):
    pairs = [(x * 4 + r, (x + step) % NX * 4 + r) for x in range(NX) for r in range(4)]
    return lax.ppermute(v, "fsdp", pairs)


def swap_core(v):
    return lax.ppermute(v, "fsdp", [(f, f ^ 1) for f in range(16)])


def mirror_y(v):
    pairs = [(f * 8 + s, (f ^ 2) * 8 + (s ^ 1)) for f in range(16) for s in range(8)]
    return lax.ppermute(v, ("fsdp", "sp"), pairs)


def pieces_z(v):
    far = [shift_z(v, -1), shift_z(v, 1), shift_z(v, 2)]
    return [v, far[0], far[2], far[1]]


def two_stage_z(v):
    above, below = shift_z(v, -1), shift_z(v, 1)
    return [v, above, shift_z(below, 1), below]


def two_stage_x(v):
    above, below = shift_x(v, -1), shift_x(v, 1)
    return [v, above, shift_x(below, 1), below]


def pieces_x(v):
    far = [shift_x(v, -1), shift_x(v, 1), shift_x(v, 2)]
    return [v, far[0], far[2], far[1]]


def part(v, index, size, dim=0):
    return lax.dynamic_slice_in_dim(v, index * size, size, dim)


def call(kernel, outs, ins, us, scratch=(), deps=(), grid=(), in_specs=None, out_specs=None):
    def run(*refs):
        kernel(*refs[: len(ins)], *refs[len(ins) + len(deps) :])

    return pl.pallas_call(
        run,
        name=kernel.__name__.replace("_kernel", ""),
        grid=grid,
        out_shape=[jax.ShapeDtypeStruct(s, t) for s, t in outs],
        in_specs=(in_specs or [SMEM] + [VMEM] * (len(ins) - 1)) + [ANY] * len(deps),
        out_specs=out_specs or [VMEM] * len(outs),
        scratch_shapes=scratch,
        compiler_params=LIMIT,
        cost_estimate=pl.CostEstimate(
            flops=int(us * 1e9), bytes_accessed=int(us * 3e6), transcendentals=0
        ),
    )(*ins, *deps)


def mm(a, b):
    return jnp.dot(a, b, preferred_element_type=F32)


def mm_t(a, b):
    return lax.dot_general(a, b, (((1,), (1,)), ((), ())), preferred_element_type=F32)


def t_mm(a, b):
    return lax.dot_general(a, b, (((0,), (0,)), ((), ())), preferred_element_type=F32)


def at_rows(index, size):
    return pl.ds(pl.multiple_of(index * size, size), size)


def rope(v, cosine, sine):
    width = v.shape[1]
    lane = lax.broadcasted_iota(jnp.int32, v.shape, 1) % HEAD_DIM
    partner = jnp.where(
        lane < HALF, pltpu.roll(v, width - HALF, 1), pltpu.roll(v, HALF, 1)
    )
    return v * cosine + partner * sine


def rope_keys(kv, cosine, sine):
    lane = lax.broadcasted_iota(jnp.int32, kv.shape, 1)
    return jnp.where(lane < KW, rope(kv, cosine, sine), kv)


def cut_kernel(places, wq, wk, wv, wg, wu, wd, wo, qkv_ref, rows_ref):
    z = places[Z]
    for t in range(3):
        cols = slice(t * 512, (t + 1) * 512)
        rows_ref[96 * t : 96 * (t + 1), :] = wo[:, cols]
        rows_ref[672 + 64 * t : 736 + 64 * t, :] = wd[at_rows(z, 64), cols]
    qkv_ref[:, :QW] = wq[:, pl.ds(pl.multiple_of(z * QW, 128), QW)]
    for at in range(NZ):

        @pl.when(z == at)
        def _():
            cols = slice(at * KW, (at + 1) * KW)
            qkv_ref[:, QW:] = jnp.concatenate([wk[:, cols], wv[:, cols]], axis=1)
            for k, w in enumerate((wg, wu)):
                for half in range(2):
                    starts = [(8 * half + i) * 256 + at * 64 for i in range(8)]
                    rows = slice(288 + (2 * half + k) * 96, 384 + (2 * half + k) * 96)
                    rows_ref[rows, :] = jnp.concatenate([w[:, b : b + 64] for b in starts], axis=1)


def cut(places, *arrays):
    return call(cut_kernel, [((96, 768), BF), ((864, 512), BF)], [places, *arrays], 3)


def copy_kernel(places, *refs):
    n = len(refs) // 2
    for i in range(n):
        refs[n + i][...] = refs[i][...]


def copied(places, arrays, deps):
    return call(copy_kernel, [(v.shape, v.dtype) for v in arrays], [places, *arrays], 0.1, deps=deps)


def pair_kernel(places, own, mirror, *outs):
    start = 0
    for out in outs:
        rows = slice(start, start + out.shape[1])
        out[places[YH]] = own[rows, :]
        out[1 - places[YH]] = mirror[rows, :]
        start += out.shape[1]


def paired(places, own, mirror, parts, deps):
    outs = [((2, n, own.shape[1]), BF) for n in parts]
    return call(pair_kernel, outs, [places, own, mirror], 0.1, deps=deps)


def norm_kernel(places, gain, og, *refs):
    xs, (normed_ref, x_ref, og_ref, mine_ref, sent_ref, turned_ref) = refs[:4], refs[4:]
    og_ref[...] = og[...]
    for i in range(NZ):
        x_ref[at_rows((places[Z] + i) % NZ, ROWS), :] = xs[i][...]
    for i in range(NZ):
        rows = pl.ds(i * ROWS, ROWS)
        v = x_ref[rows, :].astype(F32)
        r = lax.rsqrt(jnp.mean(v * v, axis=1, keepdims=True) + EPSILON)
        normed_ref[rows, :] = (v * r * gain[...]).astype(BF)
    turned_ref[...] = normed_ref[...].T
    split_cores(places, turned_ref, mine_ref, sent_ref, 96)


def split_cores(places, turned_ref, mine_ref, sent_ref, n):
    for k in range(8):
        rows = slice(k * n, (k + 1) * n)
        mine_ref[rows, :] = turned_ref[at_rows(2 * k + places[CORE], n), :]
        sent_ref[rows, :] = turned_ref[at_rows(2 * k + 1 - places[CORE], n), :]


def norm(places, gain, og, xs):
    return call(
        norm_kernel,
        [((TOKENS, D), BF)] * 2 + [((ROWS, D), BF)] + [((D // 2, TOKENS), BF)] * 2,
        [places, gain, og, *xs],
        COST["norm"],
        scratch=[pltpu.VMEM((D, TOKENS), BF)],
    )


def qkv_kernel(places, normed_ref, *refs):
    mine, other = refs[:4], refs[4:8]
    cosine, sine, q_ref, kv_ref, w_ref = refs[8:]
    for i in range(NX):
        for h in range(2):
            base = (places[X] + i) % NX * 4 + h * 2
            w_ref[at_rows(base + places[CORE], 96), :] = mine[i][h]
            w_ref[at_rows(base + 1 - places[CORE], 96), :] = other[i][h]
    for i in range(NZ):
        rows = pl.ds(i * ROWS, ROWS)
        lin = mm(normed_ref[rows, :], w_ref[...])
        q_ref[rows, :] = rope(lin[:, :QW], cosine[rows, :], sine[rows, :]).astype(BF)
        kv_ref[rows, :] = rope_keys(lin[:, QW:], cosine[rows, :], sine[rows, :]).astype(BF)


def qkv(places, normed, mine, other, cosine, sine):
    return call(
        qkv_kernel,
        [((TOKENS, QW), BF), ((TOKENS, 2 * KW), BF), ((D, QW + 2 * KW), BF)],
        [places, normed, *mine, *other, cosine, sine],
        COST["qkv"],
    )


def head(ref, rows, index):
    return ref[rows, index * HEAD_DIM : (index + 1) * HEAD_DIM]


def two_heads(ref, j, g):
    rows = slice(j * ROWS, (j + 1) * ROWS)
    return jnp.concatenate([head(ref, rows, 2 * g), head(ref, rows, 2 * g + 1)], axis=0)


def attend_kernel(places, q_ref, own_ref, other_ref, mixed_ref, p_ref):
    late = places[YL]
    factor = HEAD_DIM ** (-0.5)
    for g in range(2):
        for j in range(NZ):
            n = (j + 1) * ROWS
            q = two_heads(q_ref, j, g)
            s_own = mm_t(q, head(own_ref, slice(0, n), g)) * factor
            s_oth = mm_t(q, head(other_ref, slice(0, n), g)) * factor
            shape = (2 * ROWS, n)
            row = lax.broadcasted_iota(jnp.int32, shape, 0) % ROWS + j * ROWS
            col = lax.broadcasted_iota(jnp.int32, shape, 1)
            s_own = jnp.where(col <= row, s_own, MASKED)
            s_oth = jnp.where(col < (j + late) * ROWS, s_oth, MASKED)
            highest = jnp.maximum(
                jnp.max(s_own, axis=1, keepdims=True), jnp.max(s_oth, axis=1, keepdims=True)
            )
            p_own, p_oth = jnp.exp(s_own - highest), jnp.exp(s_oth - highest)
            total = jnp.sum(p_own, axis=1, keepdims=True) + jnp.sum(p_oth, axis=1, keepdims=True)
            scale = 1.0 / total
            p_own, p_oth = (p_own * scale).astype(BF), (p_oth * scale).astype(BF)
            p_ref[g, j, :, :n] = p_own
            p_ref[g, j, :, n : 2 * n] = p_oth
            out = mm(p_own, head(own_ref, slice(0, n), 2 + g)) + mm(
                p_oth, head(other_ref, slice(0, n), 2 + g)
            )
            out = out.astype(BF)
            for k in range(2):
                h = 2 * g + k
                mixed_ref[j * ROWS : (j + 1) * ROWS, h * HEAD_DIM : (h + 1) * HEAD_DIM] = out[
                    k * ROWS : (k + 1) * ROWS
                ]


def attend(places, q, kv, kv_other, deps):
    return call(
        attend_kernel,
        [((TOKENS, QW), BF), ((2, NZ, 2 * ROWS, 2 * TOKENS), BF)],
        [places, q, kv, kv_other],
        COST["attend"],
        deps=deps,
    )


def attend_back_kernel(places, *refs):
    grads = refs[:4]
    q_ref, own_ref, other_ref, p_ref = refs[4:8]
    dq_ref, down_ref, doth_ref = refs[8:11]
    do_ref, acc_own, acc_oth = refs[11:]
    factor = HEAD_DIM ** (-0.5)
    for i in range(NZ):
        do_ref[at_rows((places[Z] + i) % NZ, ROWS), :] = grads[i][...]
    for g in range(2):
        acc_own[...] = jnp.zeros_like(acc_own)
        acc_oth[...] = jnp.zeros_like(acc_oth)
        for j in range(NZ):
            n = (j + 1) * ROWS
            seen = slice(0, n)
            q = two_heads(q_ref, j, g)
            do = two_heads(do_ref, j, g)
            p_own, p_oth = p_ref[g, j, :, :n], p_ref[g, j, :, n : 2 * n]
            dp_own = mm_t(do, head(own_ref, seen, 2 + g))
            dp_oth = mm_t(do, head(other_ref, seen, 2 + g))
            f_own, f_oth = p_own.astype(F32), p_oth.astype(F32)
            dot = jnp.sum(f_own * dp_own, axis=1, keepdims=True) + jnp.sum(
                f_oth * dp_oth, axis=1, keepdims=True
            )
            ds_own = (f_own * (dp_own - dot)).astype(BF)
            ds_oth = (f_oth * (dp_oth - dot)).astype(BF)
            dq = mm(ds_own, head(own_ref, seen, g)) + mm(ds_oth, head(other_ref, seen, g))
            dq = (dq * factor).astype(BF)
            for k in range(2):
                h = 2 * g + k
                dq_ref[j * ROWS : (j + 1) * ROWS, h * HEAD_DIM : (h + 1) * HEAD_DIM] = dq[
                    k * ROWS : (k + 1) * ROWS
                ]
            acc_own[0, seen, :] += t_mm(ds_own, q)
            acc_own[1, seen, :] += t_mm(p_own, do)
            acc_oth[0, seen, :] += t_mm(ds_oth, q)
            acc_oth[1, seen, :] += t_mm(p_oth, do)
        for kind, scale in ((0, factor), (1, 1.0)):
            at = kind * KW + g * HEAD_DIM
            down_ref[:, at : at + HEAD_DIM] = acc_own[kind] * scale
            doth_ref[:, at : at + HEAD_DIM] = (acc_oth[kind] * scale).astype(BF)


def attend_back(places, grads, q, kv, kv_other, shares, deps):
    acc = pltpu.VMEM((2, TOKENS, HEAD_DIM), F32)
    return call(
        attend_back_kernel,
        [((TOKENS, QW), BF), ((TOKENS, 2 * KW), F32), ((TOKENS, 2 * KW), BF)],
        [places, *grads, q, kv, kv_other, shares],
        COST["attend_back"],
        scratch=[pltpu.VMEM((TOKENS, QW), BF), acc, acc],
        deps=deps,
    )


def send_chunks(refs, acc_ref, places):
    for i in range(NZ):
        rows = at_rows((places[Z] + i) % NZ, ROWS)
        refs[i][...] = acc_ref[rows, :].astype(refs[i].dtype)


CHUNKS = [((ROWS, D), F32)] + [((ROWS, D), BF)] * 3


def put_out(out_ref, places, core, ref):
    for k in range(8):
        rows = pl.ds(pl.multiple_of((k % 2 * 2 + core) * 96 + k // 2 * 24, 8), 24)
        tile = out_ref[rows, :]
        ref[k, 96:, :] = jnp.concatenate([tile[:, :768], tile[:, 768:]], axis=0).astype(BF)


def turn_kernel(
    places, dq_ref, own_ref, got_ref, cosine, sine, turned_ref, mixed_ref, branch_ref, *refs
):
    lin_ref, out_ref, sent_ref = refs
    for i in range(NZ):
        rows = slice(i * ROWS, (i + 1) * ROWS)
        dkv = (own_ref[rows, :] + got_ref[rows, :].astype(F32)).astype(BF)
        c, s = cosine[rows, :], -sine[rows, :]
        lin_ref[rows, :QW] = rope(dq_ref[rows, :].astype(F32), c, s).astype(BF)
        lin_ref[rows, QW:] = rope_keys(dkv.astype(F32), c, s).astype(BF)
    for k in range(8):
        sent_ref[k, :96, :] = mm(turned_ref[k * 96 : (k + 1) * 96, :], lin_ref[...]).astype(BF)
    out_ref[...] = t_mm(mixed_ref[...], branch_ref[...])
    put_out(out_ref, places, 1 - places[CORE], sent_ref)


def turn(places, dq, dkv_own, dkv_got, cosine, sine, turned, mixed, branch, deps):
    return call(
        turn_kernel,
        [((TOKENS, 768), BF), ((QW, D), F32), ((8, 144, 768), BF)],
        [places, dq, dkv_own, dkv_got, cosine, sine, turned, mixed, branch],
        COST["turn"],
        deps=deps,
    )


def first_kernel(places, lin_ref, w_ref, out_ref):
    out_ref[...] = mm_t(lin_ref[...], w_ref[...]).astype(BF)


def first(places, lin, w, deps):
    return call(first_kernel, [((TOKENS, D), BF)], [places, lin, w], COST["first"], deps=deps)[0]


def qkv_grad_kernel(places, lin_ref, turned_ref, out_ref, got_ref, *refs):
    outs, sum_ref = refs[:4], refs[4]
    for k in range(8):
        sum_ref[k, :96, :] = mm(turned_ref[k * 96 : (k + 1) * 96, :], lin_ref[...]).astype(BF)
    put_out(out_ref, places, places[CORE], sum_ref)
    for i in range(NX):
        for k in range(2):
            at = (places[X] + i) % NX * 2 + (places[YH] + k) % 2
            outs[i][k] = (sum_ref[at].astype(F32) + got_ref[at].astype(F32)).astype(BF)


def qkv_grad(places, lin, turned, out, got, deps):
    return call(
        qkv_grad_kernel,
        [((2, 144, 768), BF)] * 4,
        [places, lin, turned, out, got],
        COST["qkv_grad"],
        scratch=[pltpu.VMEM((8, 144, 768), BF)],
        deps=deps,
    )


def piece_rows(pieces, i, h, start, n):
    if i == 2:
        ref, start = (pieces[3], start) if start < SPLIT else (pieces[4], start - SPLIT)
    else:
        ref = pieces[(0, 1, None, 2)[i]]
    return ref[h, start : start + n, :]


def each_shard(places, pieces):
    for i in range(NX):
        for h in range(2):
            base = (places[X] + i) % NX * 4 + h * 2
            yield base + places[CORE], pieces[:5], i, h
            yield base + 1 - places[CORE], pieces[5:], i, h


def halves_kernel(places, below, *refs):
    above, first_ref, second_ref = refs[:-2], refs[-2], refs[-1]
    first_ref[...] = below[...]
    for i, ref in enumerate(above):
        second_ref[:, i * 96 : (i + 1) * 96] = ref[...]


def halves(places, above, below, deps):
    def block(n, at):
        return pl.BlockSpec((2, n, 512), lambda j: (0, at, 0))

    count = (864 - SPLIT) // 96
    return call(
        halves_kernel,
        [((2, SPLIT, 512), BF), ((2, 864 - SPLIT, 512), BF)],
        [places, below] + [above] * count,
        0.1,
        deps=deps,
        grid=(1,),
        in_specs=[SMEM, block(SPLIT, 0)] + [block(96, SPLIT // 96 + i) for i in range(count)],
    )


def lay_output(places, all_pieces, out_ref):
    for b, pieces, i, h in each_shard(places, all_pieces):
        for t in range(3):
            out_ref[at_rows(b, 96), t * 512 : (t + 1) * 512] = piece_rows(pieces, i, h, t * 96, 96)


def lay_down(places, all_pieces, out_ref):
    for b, pieces, i, h in each_shard(places, all_pieces):
        for t in range(3):
            tile = piece_rows(pieces, i, h, 672 + 64 * t, 64)
            out_ref[at_rows(b, 64), t * 512 : (t + 1) * 512] = tile


def down_kernel(places, hidden_ref, gain_a, gain_b, *refs):
    blocks, (down_ref, col_a, col_b, wd_ref, turned_ref) = refs[:16], refs[16:]
    for side in range(2):
        core = places[CORE] if side == 0 else 1 - places[CORE]
        for i in range(NX):
            for h in range(2):
                b = (places[X] + i) % NX * 4 + h * 2 + core
                for block, row, at, n in ((0, 0, 0, 64), (0, 64, 64, 32), (1, 0, 96, 32), (1, 32, 128, 64)):
                    tile = blocks[8 * side + 2 * i + block][h, row : row + n, :]
                    to = pl.ds(pl.multiple_of(b * 64 + at % 64, 32), n)
                    wd_ref[to, at // 64 * 512 : (at // 64 + 1) * 512] = tile
    down_ref[...] = mm(hidden_ref[...], wd_ref[...]).astype(BF)
    own = pl.ds(pl.multiple_of((places[X] * 4 + places[YH] * 2 + places[CORE]) * 96, 8), 96)
    for gain, col in ((gain_a, col_a), (gain_b, col_b)):
        turned_ref[...] = jnp.broadcast_to(gain[...], (128, D)).T
        col[...] = turned_ref[own, :1]


def down_of(places, hidden, gain_a, gain_b, pieces, deps):
    def block(at):
        return pl.BlockSpec((2, 96, 512), lambda j: (0, at, 0))

    ins, specs = [], []
    for side in (pieces[:5], pieces[5:]):
        for i in range(NX):
            first = 3 if i == 2 else 7
            ins += [side[(0, 1, 4, 2)[i]]] * 2
            specs += [block(first), block(first + 1)]
    return call(
        down_kernel,
        [((TOKENS, D), BF), ((96, 1), F32), ((96, 1), F32)],
        [places, hidden, gain_a, gain_b, *ins],
        COST["down"],
        scratch=[pltpu.VMEM((FFZ, D), BF), pltpu.VMEM((D, 128), F32)],
        deps=deps,
        grid=(1,),
        in_specs=[SMEM, VMEM, VMEM, VMEM] + specs,
    )


def middle_kernel(places, x_ref, gain, mixed, *refs):
    pieces, (normed_ref, own_ref, w_ref, acc_ref, mixed_ref) = refs[:10], refs[10:]
    lay_output(places, pieces, w_ref)
    for z in range(NZ):
        mixed_ref[:, z * QW : (z + 1) * QW] = mixed[z]
    for t in range(3):
        cols = slice(t * 512, (t + 1) * 512)
        acc_ref[:, cols] = x_ref[:, cols].astype(F32) + mm(mixed_ref[...], w_ref[:, cols])
    for i in range(NZ):
        rows = slice(i * ROWS, (i + 1) * ROWS)
        v = acc_ref[rows, :]
        r = lax.rsqrt(jnp.mean(v * v, axis=1, keepdims=True) + EPSILON)
        normed_ref[rows, :] = (v * r * gain[...]).astype(BF)
    own_ref[...] = acc_ref[at_rows(places[Z], ROWS), :]


def middle_of(places, x_all, gain, mixed, pieces):
    def rows(n):
        return pl.BlockSpec((2, n, 512), lambda j: (0, 0, 0))

    used = [rows(288)] * 4 + [rows(16)]
    return call(
        middle_kernel,
        [((TOKENS, D), BF), ((ROWS, D), F32), ((D, D), BF)],
        [places, x_all, gain, mixed, *pieces],
        COST["middle"],
        scratch=[pltpu.VMEM((TOKENS, D), F32), pltpu.VMEM((TOKENS, D), BF)],
        grid=(1,),
        in_specs=[SMEM, VMEM, VMEM, VMEM] + used * 2,
    )


def ffn_kernel(places, n_ref, *refs):
    ogs, pieces, refs = refs[:4], refs[4:14], refs[14:]
    hidden_ref, gg_ref, ug_ref, og_ref = refs[:4]
    in_chunks = refs[4:8]
    in_acc, wg_ref, wu_ref, wd_ref = refs[8:]
    for i, g in enumerate(ogs):
        og_ref[at_rows((places[Z] + i) % NZ, ROWS), :] = g[...]
    lay_down(places, pieces, wd_ref)
    for j in range(2):
        cols = slice(j * 512, (j + 1) * 512)
        for b, some, i, h in each_shard(places, pieces):
            wg_ref[at_rows(b, 96), :] = piece_rows(some, i, h, 288 + 192 * j, 96)
            wu_ref[at_rows(b, 96), :] = piece_rows(some, i, h, 384 + 192 * j, 96)
        wg, wu, wd = wg_ref[...], wu_ref[...], wd_ref[cols, :]
        gate = mm(n_ref[...], wg)
        up = mm(n_ref[...], wu)
        hg = mm_t(og_ref[...], wd).astype(BF).astype(F32)
        sig = 1.0 / (1.0 + jnp.exp(-gate))
        silu = gate * sig
        hidden = (silu * up).astype(BF)
        gg = (hg * up * (sig * (1.0 + gate * (1.0 - sig)))).astype(BF)
        ug = (hg * silu).astype(BF)
        hidden_ref[:, cols] = hidden
        gg_ref[:, cols] = gg
        ug_ref[:, cols] = ug
        if j == 0:
            in_acc[...] = mm_t(gg, wg) + mm_t(ug, wu)
        else:
            in_acc[...] += mm_t(gg, wg) + mm_t(ug, wu)
    send_chunks(in_chunks, in_acc, places)


def ffn(places, normed, ogs, pieces):
    return call(
        ffn_kernel,
        [((TOKENS, FFZ), BF)] * 3 + [((TOKENS, D), BF)] + CHUNKS,
        [places, normed, *ogs, *pieces],
        COST["ffn"],
        scratch=[pltpu.VMEM((TOKENS, D), F32)]
        + [pltpu.VMEM((D, 512), BF)] * 2
        + [pltpu.VMEM((FFZ, D), BF)],
    )


def ffn_terms(n_ref, h_ref, gg_ref, ug_ref, og_ref, cols, put):
    for w, ref in enumerate((gg_ref, ug_ref)):
        for half in range(2):
            tile = mm(n_ref[...], ref[:, half * 512 + cols.start : half * 512 + cols.stop])
            r = (2 * w + half) * 96
            put(slice(r, r + 96), tile.reshape(8, 96, -1))
    for t in range(3):
        tile = mm(h_ref[...], og_ref[:, t * 512 + cols.start : t * 512 + cols.stop])
        put(slice(384 + 64 * t, 448 + 64 * t), tile.reshape(8, 64, -1))


def ffn_sent_kernel(places, n_ref, hidden_ref, gg_ref, ug_ref, og_ref, *refs):
    sent_refs, (n_mine, h_mine, n_turned, h_turned, n_sent, h_sent) = refs[:2], refs[2:]
    n_turned[...] = n_ref[...].T
    h_turned[...] = hidden_ref[...].T
    split_cores(places, n_turned, n_mine, n_sent, 96)
    split_cores(places, h_turned, h_mine, h_sent, 64)

    def put(rows, tile):
        for half, ref in enumerate(sent_refs):
            ref[:, rows, :] = tile[:, :, (0, FIRST)[half] : (FIRST, 512)[half]].astype(BF)

    ffn_terms(n_sent, h_sent, gg_ref, ug_ref, og_ref, slice(0, 512), put)


def ffn_sent_of(places, normed, hidden, gg, ug, og):
    return call(
        ffn_sent_kernel,
        [
            ((8, 576, FIRST), BF),
            ((8, 576, 512 - FIRST), BF),
            ((D // 2, TOKENS), BF),
            ((FFZ // 2, TOKENS), BF),
        ],
        [places, normed, hidden, gg, ug, og],
        COST["ffn_sent"],
        scratch=[
            pltpu.VMEM((D, TOKENS), BF),
            pltpu.VMEM((FFZ, TOKENS), BF),
            pltpu.VMEM((D // 2, TOKENS), BF),
            pltpu.VMEM((FFZ // 2, TOKENS), BF),
        ],
    )


def ffn_grad_kernel(cols, places, n_ref, h_ref, gg_ref, ug_ref, og_ref, got_ref, *refs):
    outs, sum_ref = refs[:-1], refs[-1]

    def put(rows, tile):
        sum_ref[:, rows, :] = (tile + got_ref[:, rows, :].astype(F32)).astype(BF)

    ffn_terms(n_ref, h_ref, gg_ref, ug_ref, og_ref, cols, put)
    for i in range(NX):
        for k in range(2):
            at = (places[X] + i) % NX * 2 + (places[YH] + k) % 2
            if len(outs) == 4:
                outs[i][k] = sum_ref[at]
            else:
                outs[k][i] = sum_ref[at]


def ffn_grad_first_kernel(*refs):
    ffn_grad_kernel(slice(0, FIRST), *refs)


def ffn_grad_second_kernel(*refs):
    ffn_grad_kernel(slice(FIRST, 512), *refs[:7], *refs[8:10], refs[11])
    refs[10][...] = refs[7][...]


def ffn_grad_first(places, args, deps):
    return call(
        ffn_grad_first_kernel,
        [((2, 576, FIRST), BF)] * 4,
        [places, *args],
        COST["ffn_grad"],
        scratch=[pltpu.VMEM((8, 576, FIRST), BF)],
        deps=deps,
    )


def ffn_grad_second(places, args, down_part, deps):
    return call(
        ffn_grad_second_kernel,
        [((4, 576, 512 - FIRST), BF)] * 2 + [((TOKENS, D), BF)],
        [places, *args, down_part],
        COST["ffn_grad_second"],
        scratch=[pltpu.VMEM((8, 576, 512 - FIRST), BF)],
        deps=deps,
    )


def y_sum_kernel(places, mine, got, *outs):
    for i in range(NX):
        outs[i][...] = (mine[i].astype(F32) + got[i].astype(F32)).astype(BF)


def y_sum(places, mine, got, deps):
    return call(
        y_sum_kernel,
        [(mine.shape[1:], BF)] * 4,
        [places, mine, got],
        COST["y_sum"],
        deps=deps,
    )


def ffn_join_kernel(places, mine, got, a, b, c, d, out):
    out[:, :FIRST] = (mine[...] + got[...].astype(F32)).astype(BF)
    total = a[...].astype(F32) + b[...].astype(F32) + c[...].astype(F32) + d[...].astype(F32)
    out[:, FIRST:] = total.astype(BF)


def ffn_join(places, mine, got, terms, deps):
    return call(
        ffn_join_kernel,
        [((576, 512), BF)],
        [places, mine, got, *terms],
        COST["add"],
        deps=deps,
    )[0]


def rms_back(grad, v, gain):
    r = lax.rsqrt(jnp.mean(v * v, axis=1, keepdims=True) + EPSILON)
    pulled = grad * gain
    return r * pulled - v * (r * r * r * jnp.mean(pulled * v, axis=1, keepdims=True))


def middle_back_kernel(places, own, g1, g2, g3, middle, og, gain, w_ref, mid_ref, branch_ref, *outs):
    grad = own[...] + g1[...].astype(F32) + g2[...].astype(F32) + g3[...].astype(F32)
    mid = og[...].astype(F32) + rms_back(grad, middle[...], gain[...])
    mid_ref[...] = mid
    branch = mid.astype(BF)
    branch_ref[...] = branch
    for i in range(NZ):
        outs[i][...] = mm_t(branch, w_ref[at_rows((places[Z] + i) % NZ, QW), :]).astype(BF)


def middle_back(places, chunks, middle, og, gain, w_out, deps):
    return call(
        middle_back_kernel,
        [((ROWS, D), F32), ((ROWS, D), BF)] + [((ROWS, QW), BF)] * 4,
        [places, *chunks, middle, og, gain, w_out],
        COST["middle_back"],
        deps=deps,
    )


def input_back_kernel(places, grad, x, mid, gain, out_ref):
    out_ref[...] = mid[...] + rms_back(grad[...].astype(F32), x[...].astype(F32), gain[...])


def input_back(places, grad, x, mid, gain, deps):
    return call(
        input_back_kernel, [((ROWS, D), F32)], [places, grad, x, mid, gain], 2, deps=deps
    )[0]


def scatter(chunks):
    far = [shift_z(chunks[1], 1), shift_z(chunks[3], -1), shift_z(chunks[2], 2)]
    return [chunks[0], *far]


def x_sum_kernel(places, a, b, c, d, mine, sent):
    mine[...] = a[0].astype(F32) + b[0].astype(F32) + c[0].astype(F32) + d[0].astype(F32)
    total = a[1].astype(F32) + b[1].astype(F32) + c[1].astype(F32) + d[1].astype(F32)
    sent[...] = total.astype(BF)


def x_sum(places, terms, us, deps):
    shape = terms[0].shape[1:]
    return call(x_sum_kernel, [(shape, F32), (shape, BF)], [places, *terms], us, deps=deps)


def qkv_x_sum_kernel(places, a, b, c, d, mine, sent, out_mine, out_sent):
    for k, (ref, out_ref) in enumerate(((mine, out_mine), (sent, out_sent))):
        total = a[k].astype(F32) + b[k].astype(F32) + c[k].astype(F32) + d[k].astype(F32)
        ref[...] = total[:96].astype(ref.dtype)
        out_ref[...] = total[96:].astype(BF)


def qkv_x_sum(places, terms):
    return call(
        qkv_x_sum_kernel,
        [((96, 768), F32), ((96, 768), BF), ((48, 768), BF), ((48, 768), BF)],
        [places, *terms],
        2,
    )


def add_parts_kernel(places, qkv, qkv_got, out_a, out_b, total):
    total[:96, :] = (qkv[...] + qkv_got[...].astype(F32)).astype(BF)
    total[96:, :] = (out_a[...].astype(F32) + out_b[...].astype(F32)).astype(BF)


def add_parts(places, qkv, qkv_got, out_a, out_b, deps):
    return call(
        add_parts_kernel,
        [((144, 768), BF)],
        [places, qkv, qkv_got, out_a, out_b],
        COST["add"],
        deps=deps,
    )[0]


def swap_xz(v, mirror):
    pairs = [
        (
            (a * 4 + r) * 8 + b * 2 + l,
            (b * 4 + (r ^ 2 * mirror)) * 8 + a * 2 + (l ^ mirror),
        )
        for a in range(NX)
        for b in range(NZ)
        for r in range(4)
        for l in range(2)
    ]
    return lax.ppermute(v, ("fsdp", "sp"), pairs)


def add_kernel(places, a, b, out):
    out[...] = (a[...].astype(F32) + b[...].astype(F32)).astype(BF)


def added(places, a, b, deps):
    return call(add_kernel, [(a.shape, BF)], [places, a, b], COST["add"], deps=deps)[0]


def over_x(chunks):
    far = [shift_x(chunks[1], 1), shift_x(chunks[3], -1), shift_x(chunks[2], 2)]
    return [chunks[0], *far]


def as_row(column):
    return jnp.broadcast_to(column, (column.shape[0], 128)).T[:1]


def ffn_out_kernel(
    places, p0, p1, p2, p3, wg, wu, gain, gate_ref, up_ref, down_ref, gain_ref, all_ref, acc_ref
):
    j = pl.program_id(0)

    @pl.when(j == 0)
    def _():
        for i, p in enumerate((p0, p1, p2, p3)):
            all_ref[(places[Z] + i) % NZ] = p[...]
        acc_ref[...] = jnp.zeros_like(acc_ref)

    cols = pl.ds(pl.multiple_of(j % 2 * 256, 256), 256)
    for k, (w, out) in enumerate(((wg, gate_ref), (wu, up_ref))):
        rows = pl.ds(pl.multiple_of((2 * k + j // 2) * 96, 96), 96)
        parts = [all_ref[q, rows, cols].astype(F32) for q in range(NZ)]
        for b in range(4):
            tile = jnp.concatenate([v[:, b * 64 : (b + 1) * 64] for v in parts], axis=1)
            at = slice(b * 256, (b + 1) * 256)
            out[:, at] = tile
            terms = tile * w[:, at].astype(F32)
            acc_ref[...] += terms[:, :128] + terms[:, 128:]
    for t in range(3):
        r = 384 + 64 * t
        down_ref[:, t * 512 : (t + 1) * 512] = all_ref[j, r : r + 64, :].astype(F32)

    @pl.when(j == 3)
    def _():
        total = jnp.sum(acc_ref[...], axis=1, keepdims=True)
        gain_ref[...] = as_row(total / gain[...])


def ffn_out(places, pieces, wg, wu, gain, deps):
    whole = lambda shape: pl.BlockSpec(shape, lambda j: (0,) * len(shape))
    cols = pl.BlockSpec((96, 1024), lambda j: (0, j))
    return call(
        ffn_out_kernel,
        [((96, FF), F32), ((96, FF), F32), ((256, D), F32), ((1, 96), F32)],
        [places, *pieces, wg, wu, gain],
        4,
        scratch=[pltpu.VMEM((NZ, 576, 512), BF), pltpu.VMEM((96, 128), F32)],
        deps=deps,
        grid=(4,),
        in_specs=[SMEM] + [whole((576, 512))] * 4 + [cols, cols, whole((96, 1))],
        out_specs=[cols, cols, pl.BlockSpec((64, D), lambda j: (j, 0)), whole((1, 96))],
    )


def qkv_out_kernel(
    places, p0, p1, p2, p3, wq, wk, wv, own_gain, q_ref, k_ref, v_ref, gain_ref, all_ref
):
    for i, p in enumerate((p0, p1, p2, p3)):
        all_ref[(places[Z] + i) % NZ] = p[:96, :]
    for q in range(NZ):
        q_ref[:, q * QW : (q + 1) * QW] = all_ref[q, :, :QW].astype(F32)
    gain = jnp.sum(q_ref[...] * wq[...].astype(F32), axis=1, keepdims=True)
    for out, w, at in ((k_ref, wk, QW), (v_ref, wv, QW + KW)):
        tile = jnp.concatenate(
            [all_ref[q, :, at : at + KW].astype(F32) for q in range(NZ)], axis=1
        )
        out[...] = tile
        gain += jnp.sum(tile * w[...].astype(F32), axis=1, keepdims=True)
    gain_ref[...] = as_row(gain / own_gain[...])


def qkv_out(places, pieces, wq, wk, wv, gain, deps):
    return call(
        qkv_out_kernel,
        [((96, 1536), F32), ((96, 768), F32), ((96, 768), F32), ((1, 96), F32)],
        [places, *pieces, wq, wk, wv, gain],
        2,
        scratch=[pltpu.VMEM((NZ, 96, 768), BF)],
        deps=deps,
    )


def out_out_kernel(places, p0, p1, p2, p3, out_ref):
    for i, p in enumerate((p0, p1, p2, p3)):
        tile = p[96:, :].astype(F32)
        rows = pl.ds(pl.multiple_of((places[Z] + i) % NZ * 24, 8), 24)
        out_ref[rows, :] = jnp.concatenate([tile[:24], tile[24:]], axis=1)


def out_out(places, pieces):
    return call(out_out_kernel, [((96, D), F32)], [places, *pieces], 1)[0]


def block_out_kernel(places, middle, down, out_ref):
    out_ref[...] = (middle[...] + down[...].astype(F32)).astype(BF)


def block_out_of(places, middle, down, deps):
    return call(block_out_kernel, [((ROWS, D), BF)], [places, middle, down], 1, deps=deps)[0]


def body(
    inputs, norm_attn, w_query, w_key, w_value, w_out, norm_ffn, w_gate, w_up, w_down, cotangent
):
    f, s = lax.axis_index("fsdp"), lax.axis_index("sp")
    x, yh, c, z, yl = f // 4, f // 2 % 2, f % 2, s // 2, s % 2
    places = jnp.stack([x, yh, c, z, yl]).astype(jnp.int32)
    x_own, og_own = inputs[0], cotangent[0]
    gain_attn, gain_ffn = norm_attn[None], norm_ffn[None]

    index = jnp.arange(TOKENS, dtype=jnp.int32)
    positions = (index // ROWS * 2 + yl) * ROWS + index % ROWS
    lane = np.arange(QW) % HEAD_DIM
    frequency = ROPE_BASE ** (-(jnp.arange(HALF, dtype=F32) * 2.0 / HEAD_DIM))
    frequency = jnp.concatenate([frequency] * (QW // HALF))
    angles = positions.astype(F32)[:, None] * frequency[None, :]
    sign = np.where(lane < HALF, -1.0, 1.0).astype(np.float32)
    cosine, sine = jnp.cos(angles), jnp.sin(angles) * sign[None, :]

    qkv_shard, row_shard = cut(
        places, w_query, w_key, w_value, w_gate, w_up, w_down, w_out
    )
    qkv_mirror, row_mirror = mirror_y(qkv_shard), mirror_y(row_shard)
    xs = two_stage_z(x_own)
    (qkv_pair,) = paired(places, qkv_shard, qkv_mirror, [96], [cosine, sine, gain_attn])
    qkv_mine = two_stage_x(qkv_pair)
    qkv_other = [swap_core(p) for p in qkv_mine]
    (rows_pair,) = paired(
        places, row_shard, row_mirror, [864], [qkv_mine[1], qkv_mine[2], xs[1], xs[2]]
    )
    above, below = shift_x(rows_pair, -1), shift_x(rows_pair, 1)

    normed, x_all, og_copy, turned_mine, turned_sent = norm(places, gain_attn, og_own, xs)
    ogs = two_stage_z(og_copy)
    q, kv, held_qkv = qkv(places, normed, qkv_mine, qkv_other, cosine, sine)
    kv_other = swap_low(kv)
    mixed, shares = attend(places, q, kv, kv_other, [ogs[1], ogs[2]])
    half_up, half_down = halves(places, above, below, [mixed])
    far = [shift_x(half_up, 1), shift_x(half_down, -1)]
    mixed_all = gather_z(mixed).reshape(NZ, TOKENS, QW)
    pieces = [rows_pair, above, below, *far]
    pieces += [swap_core(p) for p in pieces]
    normed_ffn, middle_own, held_out = middle_of(places, x_all, gain_ffn, mixed_all, pieces)
    outs = ffn(places, normed_ffn, ogs, pieces)
    hidden, gate_grad, up_grad, og_all = outs[:4]
    in_chunks = outs[4:8]

    in_got = scatter(in_chunks)
    a_sent, b_sent, n_mine, h_mine = ffn_sent_of(
        places, normed_ffn, hidden, gate_grad, up_grad, og_all
    )
    down_part, column_attn, column_ffn = down_of(
        places, hidden, gain_attn, gain_ffn, pieces, [n_mine]
    )
    back = middle_back(
        places, in_got, middle_own, og_own, gain_ffn, held_out, [n_mine, down_part]
    )
    middle_grad, branch = back[:2]
    head_grads = [back[2], shift_z(back[5], -1), shift_z(back[4], 2), shift_z(back[3], 1)]
    branch_all = gather_z(branch)
    a_got, b_got = swap_core(a_sent), swap_core(b_sent)
    ffn_args = (n_mine, h_mine, gate_grad, up_grad, og_all)
    a_chunks = ffn_grad_first(places, (*ffn_args, a_got), [branch])
    a_terms = over_x(a_chunks)

    dq, dkv_own, dkv_sent = attend_back(
        places, head_grads, q, kv, kv_other, shares, [a_chunks[0]]
    )
    b_mine, b_sent, down_part = ffn_grad_second(places, (*ffn_args, b_got), down_part, [dq])
    down_own = scatter_z(down_part)
    b_got = mirror_y(b_sent)
    dkv_got = swap_low(dkv_sent)
    lin, out_part, qkv_sent = turn(
        places, dq, dkv_own, dkv_got, cosine, sine, turned_sent, mixed, branch_all, [b_sent]
    )
    qkv_got = swap_core(qkv_sent)
    first_part = first(places, lin, held_qkv, [])
    first_got = scatter_z(first_part)
    a_half, a_sent = x_sum(places, a_terms, COST["x_sum"], [first_part])
    a_got = mirror_y(a_sent)
    qkv_chunks = qkv_grad(places, lin, turned_mine, out_part, qkv_got, [a_sent])
    qkv_terms = over_x(qkv_chunks)
    b_terms = over_x(y_sum(places, b_mine, b_got, [qkv_chunks[0]]))

    qkv_half, qkv_sent, out_half, out_sent = qkv_x_sum(places, qkv_terms)
    qkv_got = mirror_y(qkv_sent)
    out_halves = swap_xz(out_half, 0), swap_xz(out_sent, 1)
    ffn_half = ffn_join(places, a_half, a_got, b_terms, [qkv_sent])
    ffn_low = swap_low(ffn_half)
    qkv_half = add_parts(places, qkv_half, qkv_got, *out_halves, [ffn_half])
    qkv_low = swap_low(qkv_half)
    qkv_total = added(places, qkv_half, qkv_low, [])
    qkv_pieces = pieces_z(qkv_total)
    ffn_total = added(places, ffn_half, ffn_low, [qkv_total])
    ffn_pieces = pieces_z(ffn_total)

    block_out = block_out_of(places, middle_own, down_own, [qkv_total])
    input_grad = input_back(places, first_got, x_own, middle_grad, gain_attn, [qkv_total])
    grad_out = out_out(places, qkv_pieces)
    grad_query, grad_key, grad_value, qkv_gain = qkv_out(
        places, qkv_pieces, w_query, w_key, w_value, column_attn, []
    )
    grad_gate, grad_up, grad_down, ffn_gain = ffn_out(
        places, ffn_pieces, w_gate, w_up, column_ffn, [qkv_gain]
    )
    grad_norm_attn, grad_norm_ffn = qkv_gain[0], ffn_gain[0]
    return (
        block_out[None],
        input_grad[None],
        grad_norm_attn,
        grad_query,
        grad_key,
        grad_value,
        grad_out,
        grad_norm_ffn,
        grad_gate,
        grad_up,
        grad_down,
    )


def solution(mesh):
    rows = P("fsdp", None)
    tokens = P("fsdp", "sp", None)
    return jax.shard_map(
        body,
        mesh=mesh,
        in_specs=(tokens, P(), rows, rows, rows, rows, P(), rows, rows, rows, tokens),
        out_specs=(tokens, tokens, P("fsdp"), rows, rows, rows, rows, P("fsdp"), rows, rows, rows),
        check_vma=False,
    )
```
